32 devices in a mesh: branch: 4 (over y, x), seq: 8 (over z, core).
Axes of the slice: x: 2, y: 2, z: 4, core: 2. Of those that a mesh axis runs over, the one named last changes fastest.
Arguments:
- tokens: bfloat16 [2, 4096, 768], P(None, 'seq'), may hold values from -6 to 6
- cotangent: bfloat16 [2, 4096, 768], P(None, 'seq'), may hold values from -6 to 6
- lengths: int32 [2], replicated, may hold values from 512 to 4096, as said below
- query_index: int32 [2, 512], P(None, 'seq'), may hold values from -1 to 4095, as said below
- key_index: int32 [2, 512], P(None, 'seq'), may hold values from -1 to 4095, as said below
- gain_attn: bfloat16 [768], replicated, may hold values from 0.5 to 1.5
- router_query: bfloat16 [768], replicated, may hold values from -0.15625 to 0.15625
- router_key: bfloat16 [768], replicated, may hold values from -0.15625 to 0.15625
- wq_light: bfloat16 [768, 512], P(None, 'branch'), may hold values from -0.21875 to 0.21875
- wk_light: bfloat16 [768, 512], P(None, 'branch'), may hold values from -0.21875 to 0.21875
- wv_light: bfloat16 [768, 512], P(None, 'branch'), may hold values from -0.21875 to 0.21875
- wo_light: bfloat16 [768, 512], P(None, 'branch'), may hold values from -0.75 to 0.75
- wq_heavy: bfloat16 [768, 768], P(None, 'branch'), may hold values from -0.21875 to 0.21875
- wk_heavy: bfloat16 [768, 768], P(None, 'branch'), may hold values from -0.21875 to 0.21875
- wv_heavy: bfloat16 [768, 768], P(None, 'branch'), may hold values from -0.21875 to 0.21875
- wo_heavy: bfloat16 [768, 768], P(None, 'branch'), may hold values from -0.875 to 0.875
- gain_ffn: bfloat16 [768], replicated, may hold values from 0.5 to 1.5
- router_ffn: bfloat16 [768], replicated, may hold values from -0.15625 to 0.15625
- gate_light: bfloat16 [768, 1024], P(None, 'branch'), may hold values from -0.21875 to 0.21875
- up_light: bfloat16 [768, 1024], P(None, 'branch'), may hold values from -0.21875 to 0.21875
- down_light: bfloat16 [768, 1024], P(None, 'branch'), may hold values from -0.1875 to 0.1875
- gate_heavy: bfloat16 [768, 4096], P(None, 'branch'), may hold values from -0.21875 to 0.21875
- up_heavy: bfloat16 [768, 4096], P(None, 'branch'), may hold values from -0.21875 to 0.21875
- down_heavy: bfloat16 [768, 4096], P(None, 'branch'), may hold values from -0.09375 to 0.09375
Outputs:
- mixed: float32 [2, 4096, 768], P(None, 'seq', 'branch')
- grad_tokens: float32 [2, 4096, 768], P(None, 'seq')
- grad_gain_attn: float32 [768], P('seq')
- grad_router_query: float32 [768], P('seq')
- grad_router_key: float32 [768], P('seq')
- grad_wq_light: float32 [768, 512], P('seq', 'branch')
- grad_wk_light: float32 [768, 512], P('seq', 'branch')
- grad_wv_light: float32 [768, 512], P('seq', 'branch')
- grad_wo_light: float32 [768, 512], P('seq', 'branch')
- grad_wq_heavy: float32 [768, 768], P('seq', 'branch')
- grad_wk_heavy: float32 [768, 768], P('seq', 'branch')
- grad_wv_heavy: float32 [768, 768], P('seq', 'branch')
- grad_wo_heavy: float32 [768, 768], P('seq', 'branch')
- grad_gain_ffn: float32 [768], P('seq')
- grad_router_ffn: float32 [768], P('seq')
- grad_gate_light: float32 [768, 1024], P('seq', 'branch')
- grad_up_light: float32 [768, 1024], P('seq', 'branch')
- grad_down_light: float32 [768, 1024], P('seq', 'branch')
- grad_gate_heavy: float32 [768, 4096], P('seq', 'branch')
- grad_up_heavy: float32 [768, 4096], P('seq', 'branch')
- grad_down_heavy: float32 [768, 4096], P('seq', 'branch')
The draws below stay inside these ranges and needn't reach their ends.
Inputs may be any that keep to these rules, and one draw needn't show every extreme that they name: `lengths`: one document, a different one from seed to seed, has exactly 4096 tokens; every other one has at most 3584. `query_index`: slots k * 64 to (k + 1) * 64 - 1 of a document hold distinct positions from k * 512 to (k + 1) * 512 - 1 that are below the document's length, as many as one eighth of that range's positions below the length, rounded up, always including the last such position; the other slots hold -1. `key_index`: built as query_index, drawn independently.
All inputs are finite; a program needn't handle non-finite values.
Results may differ from the reference program's by a relative error of at most 0.02.
Values may be sent and summed in bfloat16 or wider, within the bound.
A program may use at most 192 MiB of HBM per device.

```python
import math
import jax
import jax.numpy as jnp
from jax import lax

D = 768
HD = 64
HEADS_L = 8
HEADS_H = 12
FF_L = 1024
FF_H = 4096
WINDOW = 128
SEQ_DEV = 512
DOCS = 2
LENGTH = 4096


def shared_lengths(key):
    key = jax.random.fold_in(key, 101)
    length_key, choice_key = jax.random.split(key)
    drawn_lengths = jax.random.randint(length_key, (DOCS,), LENGTH // 8, LENGTH - SEQ_DEV + 1)
    longest = jax.random.randint(choice_key, (), 0, DOCS)
    return jnp.where(jnp.arange(DOCS) == longest, LENGTH, drawn_lengths).astype(jnp.int32)


def routed_positions(key, lengths_now):
    blocks = LENGTH // SEQ_DEV
    starts = jnp.arange(blocks, dtype=jnp.int32) * SEQ_DEV
    live_rows = jnp.clip(lengths_now[:, None] - starts[None, :], 0, SEQ_DEV)
    counts = (live_rows + 7) // 8
    local_rows = jnp.arange(SEQ_DEV, dtype=jnp.int32)
    scores = jax.random.randint(key, (DOCS, blocks, SEQ_DEV), 0, 2 ** 16) * SEQ_DEV + local_rows
    scores = jnp.where(local_rows[None, None, :] < live_rows[:, :, None], scores, scores + 2 ** 28)
    scores = jnp.where(local_rows[None, None, :] == live_rows[:, :, None] - 1, -1, scores)
    order = jnp.argsort(scores, axis=-1, stable=True)[:, :, :SEQ_DEV // 8].astype(jnp.int32)
    slots = jnp.arange(SEQ_DEV // 8, dtype=jnp.int32)
    chosen = jnp.where(slots[None, None, :] < counts[:, :, None], order + starts[None, :, None], -1)
    return chosen.reshape(DOCS, -1).astype(jnp.int32)


def draw_lengths(key, part):
    return shared_lengths(key)


def draw_query_index(key, part):
    lengths_now = shared_lengths(key)
    key = jax.random.fold_in(key, 7)
    return routed_positions(key, lengths_now)


def draw_key_index(key, part):
    lengths_now = shared_lengths(key)
    key = jax.random.fold_in(key, 13)
    return routed_positions(key, lengths_now)


def steps_of(own_key, shape, pieces, smallest, largest):
    def one(axis_at, blocks):
        draws = jax.random.uniform(jax.random.fold_in(jax.random.fold_in(own_key, 6), axis_at), (blocks,), jnp.float32, smallest / len(pieces), largest / len(pieces))
        return jnp.repeat(jnp.exp(draws), shape[axis_at] // blocks).reshape((-1,) + (1,) * (len(shape) - axis_at - 1))

    factor_of = one(*pieces[0])
    for cut in pieces[1:]:
        factor_of = factor_of * one(*cut)
    return factor_of


def centred(key, extent, deviation, reach, shards=(), held_as=jnp.bfloat16):
    values = deviation * jax.random.normal(key, extent, jnp.float32)
    if shards:
        values = values * steps_of(key, extent, shards, -0.22, 0.18)
    return jnp.clip(values, -reach, reach).astype(held_as)


def setup_inputs(seed: int = 0) -> dict:
    seeds = jax.random.split(jax.random.key(seed), 25)
    tokens = centred(seeds[0], (DOCS, LENGTH, D), 1.0, 6.0, ((1, 8),))
    cotangent = centred(seeds[1], (DOCS, LENGTH, D), 1.0, 6.0, ((1, 8),))
    lengths = draw_lengths(jax.random.fold_in(seeds[24], 71), 0)
    query_index = draw_query_index(jax.random.fold_in(seeds[24], 71), 0)
    key_index = draw_key_index(jax.random.fold_in(seeds[24], 71), 0)
    gain_attn = jnp.clip(1.0 + 0.1 * jax.random.normal(seeds[5], (D,), jnp.float32), 0.5, 1.5).astype(jnp.bfloat16)
    router_query = centred(seeds[6], (D,), (2 * D) ** -0.5, 0.15625)
    router_key = centred(seeds[7], (D,), (2 * D) ** -0.5, 0.15625)
    wq_light = centred(seeds[8], (D, HEADS_L * HD), D ** -0.5, 0.21875, ((1, 4),))
    wk_light = centred(seeds[9], (D, HEADS_L * HD), D ** -0.5, 0.21875, ((1, 4),))
    wv_light = centred(seeds[10], (D, HEADS_L * HD), D ** -0.5, 0.21875, ((1, 4),))
    wo_light = centred(seeds[11], (D, HEADS_L * HD), (HEADS_L * HD // 8) ** -0.5, 0.75, ((1, 4),))
    wq_heavy = centred(seeds[12], (D, HEADS_H * HD), D ** -0.5, 0.21875, ((1, 4),))
    wk_heavy = centred(seeds[13], (D, HEADS_H * HD), D ** -0.5, 0.21875, ((1, 4),))
    wv_heavy = centred(seeds[14], (D, HEADS_H * HD), D ** -0.5, 0.21875, ((1, 4),))
    wo_heavy = centred(seeds[15], (D, HEADS_H * HD), (HEADS_H * HD // 16) ** -0.5, 0.875, ((1, 4),))
    gain_ffn = jnp.clip(1.0 + 0.1 * jax.random.normal(seeds[16], (D,), jnp.float32), 0.5, 1.5).astype(jnp.bfloat16)
    router_ffn = centred(seeds[17], (D,), (2 * D) ** -0.5, 0.15625)
    gate_light = centred(seeds[18], (D, FF_L), D ** -0.5, 0.21875, ((1, 4),))
    up_light = centred(seeds[19], (D, FF_L), D ** -0.5, 0.21875, ((1, 4),))
    down_light = centred(seeds[20], (D, FF_L), FF_L ** -0.5, 0.1875, ((1, 4),))
    gate_heavy = centred(seeds[21], (D, FF_H), D ** -0.5, 0.21875, ((1, 4),))
    up_heavy = centred(seeds[22], (D, FF_H), D ** -0.5, 0.21875, ((1, 4),))
    down_heavy = centred(seeds[23], (D, FF_H), FF_H ** -0.5, 0.09375, ((1, 4),))
    return dict(tokens=tokens, cotangent=cotangent, lengths=lengths, query_index=query_index, key_index=key_index, gain_attn=gain_attn, router_query=router_query, router_key=router_key, wq_light=wq_light, wk_light=wk_light, wv_light=wv_light, wo_light=wo_light, wq_heavy=wq_heavy, wk_heavy=wk_heavy, wv_heavy=wv_heavy, wo_heavy=wo_heavy, gain_ffn=gain_ffn, router_ffn=router_ffn, gate_light=gate_light, up_light=up_light, down_light=down_light, gate_heavy=gate_heavy, up_heavy=up_heavy, down_heavy=down_heavy)


@jax.custom_vjp
def low(v):
    return lax.optimization_barrier(v.astype(jnp.bfloat16)).astype(jnp.float32)

@jax.custom_vjp
def low_back(v):
    return v

def low_keep(v):
    return (low(v), None)

def low_pass(kept, grad):
    return (grad,)

def back_keep(v):
    return (v, None)

def back_low(kept, grad):
    return (low(grad),)
low.defvjp(low_keep, low_pass)
low_back.defvjp(back_keep, back_low)
masked_value = -1000000000.0

def both(values):
    return low_back(low(values))

def matmul(operand, matrix):
    return jnp.dot(operand, matrix, precision=lax.Precision.HIGHEST)

def rms_norm(values, gains):
    inverse = lax.rsqrt(lax.optimization_barrier(jnp.mean(values * values, axis=-1, keepdims=True)) + 1e-06)
    return values * inverse * gains

def heads_first(values):
    return values.reshape(values.shape[0], -1, HD).transpose(1, 0, 2)

def heads_last(values):
    return values.transpose(1, 0, 2).reshape(values.shape[1], -1)

def attend(queries, keys, values, mask_bias):
    raw_scores = low_back(jnp.einsum('hqe,hke->hqk', queries, keys, precision=lax.Precision.HIGHEST))
    scores = raw_scores * HD ** (-0.5) + mask_bias
    probs = jax.nn.softmax(scores, axis=-1)
    return jnp.einsum('hqk,hke->hqe', low(probs), values, precision=lax.Precision.HIGHEST)

def local_attention(queries, keys, values, length):
    radius = WINDOW // 2
    total_rows = queries.shape[0]
    block_rows = math.gcd(total_rows, 512)
    keys_padded = jnp.pad(keys, ((radius, radius), (0, 0)))
    values_padded = jnp.pad(values, ((radius, radius), (0, 0)))

    def one_block(block_index):
        first_row = (block_index * block_rows).astype(jnp.int32)
        query_block = lax.dynamic_slice_in_dim(queries, first_row, block_rows, 0)
        key_block = lax.dynamic_slice_in_dim(keys_padded, first_row, block_rows + 2 * radius, 0)
        value_block = lax.dynamic_slice_in_dim(values_padded, first_row, block_rows + 2 * radius, 0)
        query_pos = first_row + jnp.arange(block_rows, dtype=jnp.int32)
        key_pos = first_row - radius + jnp.arange(block_rows + 2 * radius, dtype=jnp.int32)
        in_window = (jnp.abs(query_pos[:, None] - key_pos[None, :]) <= radius) & (key_pos[None, :] >= 0) & (key_pos[None, :] < length)
        mask_bias = jnp.where(in_window, 0.0, masked_value)
        result = attend(heads_first(query_block), heads_first(key_block), heads_first(value_block), mask_bias[None])
        return heads_last(result)
    blocks = lax.map(jax.checkpoint(one_block), jnp.arange(total_rows // block_rows, dtype=jnp.int32))
    return blocks.reshape(total_rows, -1)

def layer_doc(weight_set, document, length, query_slots, key_slots):
    gain_attn, router_query, router_key, wq_light, wk_light, wv_light, wo_light, wq_heavy, wk_heavy, wv_heavy, wo_heavy, gain_ffn, router_ffn, gate_light, up_light, down_light, gate_heavy, up_heavy, down_heavy = weight_set
    total_rows = document.shape[0]
    valid_rows = (jnp.arange(total_rows, dtype=jnp.int32) < length).astype(document.dtype)[:, None]
    query_rows = jnp.maximum(query_slots, 0)
    query_live = (query_slots >= 0).astype(document.dtype)
    key_rows = jnp.maximum(key_slots, 0)
    key_live = (key_slots >= 0).astype(document.dtype)
    normed = rms_norm(document, gain_attn)
    normed_low = low(normed)
    light_q = both(matmul(normed_low, wq_light))
    light_k = both(matmul(normed_low, wk_light))
    light_v = both(matmul(normed_low, wv_light))
    light = local_attention(light_q, light_k, light_v, length)
    light_attn = low_back(matmul(both(light), wo_light.T)) * valid_rows
    score_query = jax.nn.sigmoid(matmul(normed, router_query))[query_rows] * query_live
    score_key = jax.nn.sigmoid(matmul(normed, router_key))[key_rows] * key_live
    picked_query = low(normed[query_rows] * query_live[:, None])
    picked_key = normed[key_rows] * key_live[:, None]
    heavy_q = both(matmul(picked_query, wq_heavy))
    heavy_k = both(matmul(low(picked_key), wk_heavy))
    heavy_v = both(matmul(low(picked_key * score_key[:, None]), wv_heavy))
    key_bias = jnp.where(key_live > 0, 0.0, masked_value)[None, None, :]
    heavy = heads_last(attend(heads_first(heavy_q), heads_first(heavy_k), heads_first(heavy_v), key_bias))
    heavy_proj = low_back(matmul(both(heavy), wo_heavy.T)) * score_query[:, None]
    hidden = document + light_attn + jnp.zeros_like(document).at[query_rows].add(heavy_proj)
    normed_ffn = rms_norm(hidden, gain_ffn)
    ffn_low = low(normed_ffn)
    gate_l = both(matmul(ffn_low, gate_light))
    up_l = both(matmul(ffn_low, up_light))
    middle_l = low(jax.nn.gelu(gate_l) * up_l)
    light_ffn = low_back(matmul(middle_l, down_light.T)) * valid_rows
    score_ffn = jax.nn.sigmoid(matmul(normed_ffn, router_ffn))[query_rows] * query_live
    ffn_rows = low(normed_ffn[query_rows] * query_live[:, None])
    gate_h = both(matmul(ffn_rows, gate_heavy))
    up_h = both(matmul(ffn_rows, up_heavy))
    middle_h = low(jax.nn.gelu(gate_h) * up_h)
    heavy_ffn = low_back(matmul(middle_h, down_heavy.T)) * score_ffn[:, None]
    return hidden + light_ffn + jnp.zeros_like(hidden).at[query_rows].add(heavy_ffn)

def reference(tokens, cotangent, lengths, query_index, key_index, gain_attn, router_query, router_key, wq_light, wk_light, wv_light, wo_light, wq_heavy, wk_heavy, wv_heavy, wo_heavy, gain_ffn, router_ffn, gate_light, up_light, down_light, gate_heavy, up_heavy, down_heavy):
    weights = tuple((array.astype(jnp.float32) for array in (gain_attn, router_query, router_key, wq_light, wk_light, wv_light, wo_light, wq_heavy, wk_heavy, wv_heavy, wo_heavy, gain_ffn, router_ffn, gate_light, up_light, down_light, gate_heavy, up_heavy, down_heavy)))

    def forward(weight_set, inputs):

        def doc_step(unused_carry, doc_item):
            document, doc_length, query_slots, key_slots = doc_item
            return (unused_carry, layer_doc(weight_set, document, doc_length, query_slots, key_slots))
        return lax.scan(doc_step, jnp.zeros((), jnp.float32), (inputs, lengths, query_index, key_index))[1]
    mixed, pullback = jax.vjp(forward, weights, tokens.astype(jnp.float32))
    weight_grads, grad_tokens = pullback(cotangent.astype(jnp.float32))
    grad_gain_attn, grad_router_query, grad_router_key, grad_wq_light, grad_wk_light, grad_wv_light, grad_wo_light, grad_wq_heavy, grad_wk_heavy, grad_wv_heavy, grad_wo_heavy, grad_gain_ffn, grad_router_ffn, grad_gate_light, grad_up_light, grad_down_light, grad_gate_heavy, grad_up_heavy, grad_down_heavy = weight_grads
    return (mixed, grad_tokens, grad_gain_attn, grad_router_query, grad_router_key, grad_wq_light, grad_wk_light, grad_wv_light, grad_wo_light, grad_wq_heavy, grad_wk_heavy, grad_wv_heavy, grad_wo_heavy, grad_gain_ffn, grad_router_ffn, grad_gate_light, grad_up_light, grad_down_light, grad_gate_heavy, grad_up_heavy, grad_down_heavy)
```

```python
import math

import jax
import jax.numpy as jnp
from jax import lax
from jax.sharding import PartitionSpec as P

HD = 64
WINDOW = 128


highest = lax.Precision.HIGHEST
masked_value = -1000000000.0
epsilon = 1e-06


def with_halo(cells, sides, width):
    for axis, dim in sides:
        count = lax.axis_size(axis)
        ends = count - 1
        head = lax.slice_in_dim(cells, 0, width, axis=dim)
        tail = lax.slice_in_dim(cells, cells.shape[dim] - width, cells.shape[dim], axis=dim)
        cells = jnp.concatenate(
            [
                lax.ppermute(tail, axis, [(i, (i + 1) % count) for i in range(ends)]),
                cells,
                lax.ppermute(head, axis, [((i + 1) % count, i) for i in range(ends)]),
            ],
            axis=dim,
        )
    return cells


def project(operand, matrix):
    return jnp.einsum("dsc,ch->dsh", operand, matrix, preferred_element_type=jnp.float32)


def unproject(operand, matrix):
    return jnp.einsum("dsh,ch->dsc", operand, matrix, preferred_element_type=jnp.float32)


def weight_grad(operand, gradient):
    return jnp.einsum("dsc,dsh->ch", operand, gradient, preferred_element_type=jnp.float32)


def pick_rows(selector, values):
    return jnp.einsum("drs,dsc->drc", selector, values, precision=highest)


def put_rows(selector, values):
    return jnp.einsum("drs,drc->dsc", selector, values, precision=highest)


def pick_scalar(selector, values):
    return jnp.einsum("drs,ds->dr", selector, values, precision=highest)


def put_scalar(selector, values):
    return jnp.einsum("drs,dr->ds", selector, values, precision=highest)


def split_heads(values):
    return values.reshape(values.shape[0], values.shape[1], -1, HD)


def attention_scores(queries, keys, mask_bias):
    raw_scores = jnp.einsum("dqhe,dkhe->dhqk", queries, keys, preferred_element_type=jnp.float32)
    return raw_scores * HD ** (-0.5) + mask_bias


def forward_attention(queries, keys, values, mask_bias):
    scores = attention_scores(queries, keys, mask_bias)
    highest_score = jnp.max(scores, axis=-1, keepdims=True)
    exponent = jnp.exp(scores - highest_score)
    totals = jnp.sum(exponent, axis=-1, keepdims=True)
    probs_low = (exponent / totals).astype(jnp.bfloat16)
    result = jnp.einsum("dhqk,dkhe->dqhe", probs_low, values, preferred_element_type=jnp.float32)
    result = result.reshape(result.shape[0], result.shape[1], -1).astype(jnp.bfloat16)
    return (result, highest_score + jnp.log(totals))


def score_grads(queries, keys, values, mask_bias, logsum, grad_out, row_delta):
    probs = jnp.exp(attention_scores(queries, keys, mask_bias) - logsum)
    grad_probs = jnp.einsum("dqhe,dkhe->dhqk", grad_out, values, preferred_element_type=jnp.float32)
    row_delta = jnp.sum(grad_probs * probs, axis=-1, keepdims=True)
    grad_raw = (probs * (grad_probs - row_delta) * HD ** (-0.5)).astype(jnp.bfloat16)
    return (grad_raw, probs.astype(jnp.bfloat16), row_delta)


def contract_query(grad_raw, keys):
    result = jnp.einsum("dhqk,dkhe->dqhe", grad_raw, keys, preferred_element_type=jnp.float32)
    return result.reshape(result.shape[0], result.shape[1], -1)


def contract_key(grad_raw, queries):
    result = jnp.einsum("dhqk,dqhe->dkhe", grad_raw, queries, preferred_element_type=jnp.float32)
    return result.reshape(result.shape[0], result.shape[1], -1)


def geglu_back(gate_vals, up_vals, grad_mid):
    activated, gelu_pull = jax.vjp(jax.nn.gelu, gate_vals.astype(jnp.float32))
    grad_gate = gelu_pull(grad_mid * up_vals.astype(jnp.float32))[0].astype(jnp.bfloat16)
    grad_up = (grad_mid * activated).astype(jnp.bfloat16)
    return (grad_gate, grad_up)


def geglu(gate_vals, up_vals):
    return (jax.nn.gelu(gate_vals.astype(jnp.float32)) * up_vals.astype(jnp.float32)).astype(
        jnp.bfloat16
    )


def shards(
    tokens,
    cotangent,
    lengths,
    query_index,
    key_index,
    gain_attn,
    router_query,
    router_key,
    wq_light,
    wk_light,
    wv_light,
    wo_light,
    wq_heavy,
    wk_heavy,
    wv_heavy,
    wo_heavy,
    gain_ffn,
    router_ffn,
    gate_light,
    up_light,
    down_light,
    gate_heavy,
    up_heavy,
    down_heavy,
):
    documents, local_len, model_width = tokens.shape
    radius = WINDOW // 2
    block_rows = math.gcd(local_len, 512)
    key_span = block_rows + 2 * radius
    offset = lax.axis_index("seq") * local_len
    positions = offset + jnp.arange(local_len, dtype=jnp.int32)
    valid_rows = (positions[None, :] < lengths[:, None]).astype(jnp.float32)[:, :, None]
    pick_query = (query_index[:, :, None] == positions[None, None, :]).astype(jnp.float32)
    pick_key = (key_index[:, :, None] == positions[None, None, :]).astype(jnp.float32)
    inputs = tokens.astype(jnp.float32)
    inv_attn = lax.rsqrt(jnp.mean(inputs * inputs, axis=-1, keepdims=True) + epsilon)
    unit_attn = inputs * inv_attn
    gain_attn_f = gain_attn.astype(jnp.float32)
    normed = unit_attn * gain_attn_f
    normed_low = normed.astype(jnp.bfloat16)
    light_q = project(normed_low, wq_light).astype(jnp.bfloat16)
    light_k = project(normed_low, wk_light).astype(jnp.bfloat16)
    light_v = project(normed_low, wv_light).astype(jnp.bfloat16)
    light_width = light_q.shape[2]
    rim_block = with_halo(jnp.concatenate([light_k, light_v], axis=2), (("seq", 1),), radius)
    wide_k = split_heads(rim_block[:, :, :light_width])
    wide_v = split_heads(rim_block[:, :, light_width:])
    heads_q = split_heads(light_q)
    key_pos = offset - radius + jnp.arange(local_len + 2 * radius, dtype=jnp.int32)
    in_window = (jnp.abs(positions[:, None] - key_pos[None, :]) <= radius)[None]
    in_window = (
        in_window
        & (key_pos[None, None, :] >= 0)
        & (key_pos[None, None, :] < lengths[:, None, None])
    )
    light_bias = jnp.where(in_window, 0.0, masked_value)[:, None]
    piece_out, piece_lse = forward_attention(heads_q, wide_k, wide_v, light_bias)
    router_query_f = router_query.astype(jnp.float32)
    router_key_f = router_key.astype(jnp.float32)
    score_query = pick_scalar(
        pick_query,
        jax.nn.sigmoid(jnp.einsum("dsc,c->ds", normed, router_query_f, precision=highest)),
    )
    score_key = pick_scalar(
        pick_key, jax.nn.sigmoid(jnp.einsum("dsc,c->ds", normed, router_key_f, precision=highest))
    )
    heavy_in = pick_rows(pick_query, normed).astype(jnp.bfloat16)
    key_rows = pick_rows(pick_key, normed)
    key_in = key_rows.astype(jnp.bfloat16)
    scaled_in = (key_rows * score_key[:, :, None]).astype(jnp.bfloat16)
    heavy_q = project(heavy_in, wq_heavy).astype(jnp.bfloat16)
    heavy_k = project(key_in, wk_heavy).astype(jnp.bfloat16)
    heavy_v = project(scaled_in, wv_heavy).astype(jnp.bfloat16)
    heavy_width = heavy_q.shape[2]
    key_alive = (key_index >= 0).astype(jnp.bfloat16)
    routed_kv, alive_all = (
        lax.all_gather(jnp.concatenate([heavy_k, heavy_v], axis=2), "seq", axis=1, tiled=True),
        lax.all_gather(key_alive, "seq", axis=1, tiled=True),
    )
    all_k = routed_kv[:, :, :heavy_width]
    all_v = routed_kv[:, :, heavy_width:]
    heavy_bias = jnp.where(alive_all > 0, 0.0, masked_value)[:, None, None, :]
    heavy_out, heavy_lse = forward_attention(
        split_heads(heavy_q), split_heads(all_k), split_heads(all_v), heavy_bias
    )
    heavy_proj = unproject(heavy_out, wo_heavy)
    light_attn = unproject(piece_out, wo_light) * valid_rows
    heavy_attn = put_rows(pick_query, heavy_proj * score_query[:, :, None])
    attn_total = lax.psum((light_attn + heavy_attn).astype(jnp.bfloat16), "branch").astype(
        jnp.float32
    )
    hidden = inputs + attn_total
    inv_ffn = lax.rsqrt(jnp.mean(hidden * hidden, axis=-1, keepdims=True) + epsilon)
    unit_ffn = hidden * inv_ffn
    gain_ffn_f = gain_ffn.astype(jnp.float32)
    normed_ffn = unit_ffn * gain_ffn_f
    ffn_low = normed_ffn.astype(jnp.bfloat16)
    gate_l = project(ffn_low, gate_light).astype(jnp.bfloat16)
    up_l = project(ffn_low, up_light).astype(jnp.bfloat16)
    middle_l = geglu(gate_l, up_l)
    light_ffn = unproject(middle_l, down_light) * valid_rows
    router_ffn_f = router_ffn.astype(jnp.float32)
    score_ffn = pick_scalar(
        pick_query,
        jax.nn.sigmoid(jnp.einsum("dsc,c->ds", normed_ffn, router_ffn_f, precision=highest)),
    )
    ffn_rows = pick_rows(pick_query, normed_ffn).astype(jnp.bfloat16)
    gate_h = project(ffn_rows, gate_heavy).astype(jnp.bfloat16)
    up_h = project(ffn_rows, up_heavy).astype(jnp.bfloat16)
    middle_h = geglu(gate_h, up_h)
    heavy_fproj = unproject(middle_h, down_heavy)
    heavy_ffn = put_rows(pick_query, heavy_fproj * score_ffn[:, :, None])
    share = model_width // lax.axis_size("branch")
    own_cols = lax.axis_index("branch") * share
    mixed = lax.dynamic_slice_in_dim(hidden, own_cols, share, 2) + lax.psum_scatter(
        (light_ffn + heavy_ffn).astype(jnp.bfloat16), "branch", scatter_dimension=2, tiled=True
    ).astype(jnp.float32)
    grad_out = cotangent.astype(jnp.float32)
    grad_light = (grad_out * valid_rows).astype(jnp.bfloat16)
    grad_down_light = weight_grad(grad_light, middle_l)
    grad_gate_l, grad_up_l = geglu_back(gate_l, up_l, project(grad_light, down_light))
    grad_gate_light = weight_grad(ffn_low, grad_gate_l)
    grad_up_light = weight_grad(ffn_low, grad_up_l)
    grad_rows = pick_rows(pick_query, grad_out)
    grad_heavy = (grad_rows * score_ffn[:, :, None]).astype(jnp.bfloat16)
    score_ffn_part = jnp.sum(grad_rows * heavy_fproj, axis=-1)
    grad_down_heavy = weight_grad(grad_heavy, middle_h)
    grad_gate_h, grad_up_h = geglu_back(gate_h, up_h, project(grad_heavy, down_heavy))
    grad_gate_heavy = weight_grad(ffn_rows, grad_gate_h)
    grad_up_heavy = weight_grad(ffn_rows, grad_up_h)
    heavy_ffn_rows = unproject(grad_gate_h, gate_heavy) + unproject(grad_up_h, up_heavy)
    ffn_part = (
        unproject(grad_gate_l, gate_light)
        + unproject(grad_up_l, up_light)
        + put_rows(pick_query, heavy_ffn_rows)
    )
    grad_normed_ffn, grad_score_ffn = (
        lax.psum(ffn_part.astype(jnp.bfloat16), "branch").astype(jnp.float32),
        lax.psum(score_ffn_part.astype(jnp.bfloat16), "branch").astype(jnp.float32),
    )
    pre_ffn = put_scalar(pick_query, grad_score_ffn * score_ffn * (1.0 - score_ffn))
    grad_normed_ffn = grad_normed_ffn + pre_ffn[:, :, None] * router_ffn_f
    grad_router_ffn = jnp.einsum("ds,dsc->c", pre_ffn, normed_ffn, precision=highest)
    grad_gain_ffn = jnp.sum(grad_normed_ffn * unit_ffn, axis=(0, 1))
    grad_unit_f = grad_normed_ffn * gain_ffn_f
    grad_hidden = grad_out + inv_ffn * (
        grad_unit_f - unit_ffn * jnp.mean(grad_unit_f * unit_ffn, axis=-1, keepdims=True)
    )
    grad_light_attn = (grad_hidden * valid_rows).astype(jnp.bfloat16)
    grad_wo_light = weight_grad(grad_light_attn, piece_out)
    grad_light_out = split_heads(project(grad_light_attn, wo_light).astype(jnp.bfloat16))
    wide_grad = jnp.zeros((documents, local_len + 2 * radius, 2 * light_width), jnp.float32)
    light_raw, light_plow, unused_delta = score_grads(
        heads_q, wide_k, wide_v, light_bias, piece_lse, grad_light_out, None
    )
    query_pieces = contract_query(light_raw, wide_k)
    key_terms = jnp.concatenate(
        [contract_key(light_raw, heads_q), contract_key(light_plow, grad_light_out)], axis=2
    )
    wide_grad = wide_grad.at[:, 0:key_span].add(key_terms)
    grad_light_q = query_pieces.astype(jnp.bfloat16)
    outer_rims = jnp.concatenate(
        [wide_grad[:, :radius], wide_grad[:, radius + local_len :]], axis=1
    )
    returned = with_halo(outer_rims.astype(jnp.bfloat16), (("seq", 1),), radius).astype(
        outer_rims.dtype
    )
    inner = wide_grad[:, radius : radius + local_len]
    inner = inner + jnp.pad(returned[:, :radius], ((0, 0), (0, local_len - radius), (0, 0)))
    inner = inner + jnp.pad(returned[:, 3 * radius :], ((0, 0), (local_len - radius, 0), (0, 0)))
    grad_light_k = inner[:, :, :light_width].astype(jnp.bfloat16)
    grad_light_v = inner[:, :, light_width:].astype(jnp.bfloat16)
    grad_wq_light = weight_grad(normed_low, grad_light_q)
    grad_wk_light = weight_grad(normed_low, grad_light_k)
    grad_wv_light = weight_grad(normed_low, grad_light_v)
    light_part = (
        unproject(grad_light_q, wq_light)
        + unproject(grad_light_k, wk_light)
        + unproject(grad_light_v, wv_light)
    )
    grad_hrows = pick_rows(pick_query, grad_hidden)
    grad_heavy_attn = (grad_hrows * score_query[:, :, None]).astype(jnp.bfloat16)
    score_query_part = jnp.sum(grad_hrows * heavy_proj, axis=-1)
    grad_wo_heavy = weight_grad(grad_heavy_attn, heavy_out)
    grad_heavy_out = project(grad_heavy_attn, wo_heavy).astype(jnp.bfloat16)
    heavy_raw, heavy_plow, heavy_delta = score_grads(
        split_heads(heavy_q),
        split_heads(all_k),
        split_heads(all_v),
        heavy_bias,
        heavy_lse,
        split_heads(grad_heavy_out),
        None,
    )
    grad_heavy_q = contract_query(heavy_raw, split_heads(all_k)).astype(jnp.bfloat16)
    every_kv = jnp.concatenate(
        [
            contract_key(heavy_raw, split_heads(heavy_q)),
            contract_key(heavy_plow, split_heads(grad_heavy_out)),
        ],
        axis=2,
    )
    own_kv = lax.psum_scatter(every_kv, "seq", scatter_dimension=1, tiled=True)
    grad_heavy_k = own_kv[:, :, :heavy_width].astype(jnp.bfloat16)
    grad_heavy_v = own_kv[:, :, heavy_width:].astype(jnp.bfloat16)
    grad_scaled = unproject(grad_heavy_v, wv_heavy)
    score_key_part = jnp.sum(grad_scaled * key_rows, axis=-1)
    grad_key_rows = unproject(grad_heavy_k, wk_heavy) + grad_scaled * score_key[:, :, None]
    grad_wq_heavy = weight_grad(heavy_in, grad_heavy_q)
    grad_wk_heavy = weight_grad(key_in, grad_heavy_k)
    grad_wv_heavy = weight_grad(scaled_in, grad_heavy_v)
    attn_part = (
        light_part
        + put_rows(pick_query, unproject(grad_heavy_q, wq_heavy))
        + put_rows(pick_key, grad_key_rows)
    )
    grad_normed, grad_score_query, grad_score_key = (
        lax.psum(attn_part.astype(jnp.bfloat16), "branch").astype(jnp.float32),
        lax.psum(score_query_part.astype(jnp.bfloat16), "branch").astype(jnp.float32),
        lax.psum(score_key_part.astype(jnp.bfloat16), "branch").astype(jnp.float32),
    )
    pre_query = put_scalar(pick_query, grad_score_query * score_query * (1.0 - score_query))
    pre_key = put_scalar(pick_key, grad_score_key * score_key * (1.0 - score_key))
    grad_normed = (
        grad_normed + pre_query[:, :, None] * router_query_f + pre_key[:, :, None] * router_key_f
    )
    grad_router_query = jnp.einsum("ds,dsc->c", pre_query, normed, precision=highest)
    grad_router_key = jnp.einsum("ds,dsc->c", pre_key, normed, precision=highest)
    grad_gain_attn = jnp.sum(grad_normed * unit_attn, axis=(0, 1))
    grad_unit_a = grad_normed * gain_attn_f
    grad_tokens = grad_hidden + inv_attn * (
        grad_unit_a - unit_attn * jnp.mean(grad_unit_a * unit_attn, axis=-1, keepdims=True)
    )
    names = (
        grad_wq_light, grad_wk_light, grad_wv_light, grad_wo_light,
        grad_wq_heavy, grad_wk_heavy, grad_wv_heavy, grad_wo_heavy,
        grad_gate_light, grad_up_light, grad_down_light,
        grad_gate_heavy, grad_up_heavy, grad_down_heavy,
    )
    vectors = jnp.stack(
        [grad_gain_attn, grad_router_query, grad_router_key, grad_gain_ffn, grad_router_ffn], axis=1
    )
    packed = jnp.concatenate([g.astype(jnp.bfloat16) for g in names + (vectors,)], axis=1)
    summed = lax.psum_scatter(packed, "seq", scatter_dimension=0, tiled=True).astype(jnp.float32)
    widths = [g.shape[1] for g in names]
    cuts = [sum(widths[:i]) for i in range(len(widths) + 1)]
    (
        grad_wq_light, grad_wk_light, grad_wv_light, grad_wo_light,
        grad_wq_heavy, grad_wk_heavy, grad_wv_heavy, grad_wo_heavy,
        grad_gate_light, grad_up_light, grad_down_light,
        grad_gate_heavy, grad_up_heavy, grad_down_heavy,
    ) = [summed[:, cuts[i] : cuts[i + 1]] for i in range(len(widths))]
    grad_gain_attn, grad_router_query, grad_router_key, grad_gain_ffn, grad_router_ffn = [
        summed[:, cuts[-1] + i] for i in range(5)
    ]
    return (
        mixed,
        grad_tokens,
        grad_gain_attn,
        grad_router_query,
        grad_router_key,
        grad_wq_light,
        grad_wk_light,
        grad_wv_light,
        grad_wo_light,
        grad_wq_heavy,
        grad_wk_heavy,
        grad_wv_heavy,
        grad_wo_heavy,
        grad_gain_ffn,
        grad_router_ffn,
        grad_gate_light,
        grad_up_light,
        grad_down_light,
        grad_gate_heavy,
        grad_up_heavy,
        grad_down_heavy,
    )


def solution(mesh):
    return jax.shard_map(
        shards,
        mesh=mesh,
        in_specs=(
            P(None, "seq", None),
            P(None, "seq", None),
            P(),
            P(None, "seq"),
            P(None, "seq"),
            P(),
            P(),
            P(),
            P(None, "branch"),
            P(None, "branch"),
            P(None, "branch"),
            P(None, "branch"),
            P(None, "branch"),
            P(None, "branch"),
            P(None, "branch"),
            P(None, "branch"),
            P(),
            P(),
            P(None, "branch"),
            P(None, "branch"),
            P(None, "branch"),
            P(None, "branch"),
            P(None, "branch"),
            P(None, "branch"),
        ),
        out_specs=(
            P(None, "seq", "branch"),
            P(None, "seq", None),
            P("seq"),
            P("seq"),
            P("seq"),
            P("seq", "branch"),
            P("seq", "branch"),
            P("seq", "branch"),
            P("seq", "branch"),
            P("seq", "branch"),
            P("seq", "branch"),
            P("seq", "branch"),
            P("seq", "branch"),
            P("seq"),
            P("seq"),
            P("seq", "branch"),
            P("seq", "branch"),
            P("seq", "branch"),
            P("seq", "branch"),
            P("seq", "branch"),
            P("seq", "branch"),
        ),
        check_vma=False,
    )
```

```python
import functools
import math

import jax
import jax.numpy as jnp
from jax import lax
from jax.experimental import pallas as pl
from jax.experimental.pallas import tpu as pltpu
from jax.sharding import PartitionSpec as P

HD = 64
WINDOW = 128


highest = lax.Precision.HIGHEST
masked_value = -1000000000.0
epsilon = 1e-06


def with_halo(cells, sides, width):
    for axis, dim in sides:
        count = lax.axis_size(axis)
        ends = count - 1
        head = lax.slice_in_dim(cells, 0, width, axis=dim)
        tail = lax.slice_in_dim(cells, cells.shape[dim] - width, cells.shape[dim], axis=dim)
        cells = jnp.concatenate(
            [
                lax.ppermute(tail, axis, [(i, (i + 1) % count) for i in range(ends)]),
                cells,
                lax.ppermute(head, axis, [((i + 1) % count, i) for i in range(ends)]),
            ],
            axis=dim,
        )
    return cells


def project(operand, matrix):
    return jnp.einsum("dsc,ch->dsh", operand, matrix, preferred_element_type=jnp.float32)


def unproject(operand, matrix):
    return jnp.einsum("dsh,ch->dsc", operand, matrix, preferred_element_type=jnp.float32)


def weight_grad(operand, gradient):
    return jnp.einsum("dsc,dsh->ch", operand, gradient, preferred_element_type=jnp.float32)


def pick_rows(selector, values):
    return jnp.einsum("drs,dsc->drc", selector, values, precision=highest)


def put_rows(selector, values):
    return jnp.einsum("drs,drc->dsc", selector, values, precision=highest)


def pick_scalar(selector, values):
    return jnp.einsum("drs,ds->dr", selector, values, precision=highest)


def put_scalar(selector, values):
    return jnp.einsum("drs,dr->ds", selector, values, precision=highest)


def split_heads(values):
    return values.reshape(values.shape[0], values.shape[1], -1, HD)


def attention_scores(queries, keys, mask_bias):
    raw_scores = jnp.einsum("dqhe,dkhe->dhqk", queries, keys, preferred_element_type=jnp.float32)
    return raw_scores * HD ** (-0.5) + mask_bias


def forward_attention(queries, keys, values, mask_bias):
    scores = attention_scores(queries, keys, mask_bias)
    highest_score = jnp.max(scores, axis=-1, keepdims=True)
    exponent = jnp.exp(scores - highest_score)
    totals = jnp.sum(exponent, axis=-1, keepdims=True)
    probs_low = (exponent / totals).astype(jnp.bfloat16)
    result = jnp.einsum("dhqk,dkhe->dqhe", probs_low, values, preferred_element_type=jnp.float32)
    result = result.reshape(result.shape[0], result.shape[1], -1).astype(jnp.bfloat16)
    return (result, highest_score + jnp.log(totals))


def score_grads(queries, keys, values, mask_bias, logsum, grad_out, row_delta):
    probs = jnp.exp(attention_scores(queries, keys, mask_bias) - logsum)
    grad_probs = jnp.einsum("dqhe,dkhe->dhqk", grad_out, values, preferred_element_type=jnp.float32)
    row_delta = jnp.sum(grad_probs * probs, axis=-1, keepdims=True)
    grad_raw = (probs * (grad_probs - row_delta) * HD ** (-0.5)).astype(jnp.bfloat16)
    return (grad_raw, probs.astype(jnp.bfloat16), row_delta)


def contract_query(grad_raw, keys):
    result = jnp.einsum("dhqk,dkhe->dqhe", grad_raw, keys, preferred_element_type=jnp.float32)
    return result.reshape(result.shape[0], result.shape[1], -1)


def contract_key(grad_raw, queries):
    result = jnp.einsum("dhqk,dqhe->dkhe", grad_raw, queries, preferred_element_type=jnp.float32)
    return result.reshape(result.shape[0], result.shape[1], -1)


def geglu_back(gate_vals, up_vals, grad_mid):
    activated, gelu_pull = jax.vjp(jax.nn.gelu, gate_vals.astype(jnp.float32))
    grad_gate = gelu_pull(grad_mid * up_vals.astype(jnp.float32))[0].astype(jnp.bfloat16)
    grad_up = (grad_mid * activated).astype(jnp.bfloat16)
    return (grad_gate, grad_up)


def geglu(gate_vals, up_vals):
    return (jax.nn.gelu(gate_vals.astype(jnp.float32)) * up_vals.astype(jnp.float32)).astype(
        jnp.bfloat16
    )


def plain_shards(
    tokens,
    cotangent,
    lengths,
    query_index,
    key_index,
    gain_attn,
    router_query,
    router_key,
    wq_light,
    wk_light,
    wv_light,
    wo_light,
    wq_heavy,
    wk_heavy,
    wv_heavy,
    wo_heavy,
    gain_ffn,
    router_ffn,
    gate_light,
    up_light,
    down_light,
    gate_heavy,
    up_heavy,
    down_heavy,
):
    documents, local_len, model_width = tokens.shape
    radius = WINDOW // 2
    block_rows = math.gcd(local_len, 512)
    key_span = block_rows + 2 * radius
    offset = lax.axis_index("seq") * local_len
    positions = offset + jnp.arange(local_len, dtype=jnp.int32)
    valid_rows = (positions[None, :] < lengths[:, None]).astype(jnp.float32)[:, :, None]
    pick_query = (query_index[:, :, None] == positions[None, None, :]).astype(jnp.float32)
    pick_key = (key_index[:, :, None] == positions[None, None, :]).astype(jnp.float32)
    inputs = tokens.astype(jnp.float32)
    inv_attn = lax.rsqrt(jnp.mean(inputs * inputs, axis=-1, keepdims=True) + epsilon)
    unit_attn = inputs * inv_attn
    gain_attn_f = gain_attn.astype(jnp.float32)
    normed = unit_attn * gain_attn_f
    normed_low = normed.astype(jnp.bfloat16)
    light_q = project(normed_low, wq_light).astype(jnp.bfloat16)
    light_k = project(normed_low, wk_light).astype(jnp.bfloat16)
    light_v = project(normed_low, wv_light).astype(jnp.bfloat16)
    light_width = light_q.shape[2]
    rim_block = with_halo(jnp.concatenate([light_k, light_v], axis=2), (("seq", 1),), radius)
    wide_k = split_heads(rim_block[:, :, :light_width])
    wide_v = split_heads(rim_block[:, :, light_width:])
    heads_q = split_heads(light_q)
    key_pos = offset - radius + jnp.arange(local_len + 2 * radius, dtype=jnp.int32)
    in_window = (jnp.abs(positions[:, None] - key_pos[None, :]) <= radius)[None]
    in_window = (
        in_window
        & (key_pos[None, None, :] >= 0)
        & (key_pos[None, None, :] < lengths[:, None, None])
    )
    light_bias = jnp.where(in_window, 0.0, masked_value)[:, None]
    piece_out, piece_lse = forward_attention(heads_q, wide_k, wide_v, light_bias)
    router_query_f = router_query.astype(jnp.float32)
    router_key_f = router_key.astype(jnp.float32)
    score_query = pick_scalar(
        pick_query,
        jax.nn.sigmoid(jnp.einsum("dsc,c->ds", normed, router_query_f, precision=highest)),
    )
    score_key = pick_scalar(
        pick_key, jax.nn.sigmoid(jnp.einsum("dsc,c->ds", normed, router_key_f, precision=highest))
    )
    heavy_in = pick_rows(pick_query, normed).astype(jnp.bfloat16)
    key_rows = pick_rows(pick_key, normed)
    key_in = key_rows.astype(jnp.bfloat16)
    scaled_in = (key_rows * score_key[:, :, None]).astype(jnp.bfloat16)
    heavy_q = project(heavy_in, wq_heavy).astype(jnp.bfloat16)
    heavy_k = project(key_in, wk_heavy).astype(jnp.bfloat16)
    heavy_v = project(scaled_in, wv_heavy).astype(jnp.bfloat16)
    heavy_width = heavy_q.shape[2]
    key_alive = (key_index >= 0).astype(jnp.bfloat16)
    routed_kv, alive_all = (
        lax.all_gather(jnp.concatenate([heavy_k, heavy_v], axis=2), "seq", axis=1, tiled=True),
        lax.all_gather(key_alive, "seq", axis=1, tiled=True),
    )
    all_k = routed_kv[:, :, :heavy_width]
    all_v = routed_kv[:, :, heavy_width:]
    heavy_bias = jnp.where(alive_all > 0, 0.0, masked_value)[:, None, None, :]
    heavy_out, heavy_lse = forward_attention(
        split_heads(heavy_q), split_heads(all_k), split_heads(all_v), heavy_bias
    )
    heavy_proj = unproject(heavy_out, wo_heavy)
    light_attn = unproject(piece_out, wo_light) * valid_rows
    heavy_attn = put_rows(pick_query, heavy_proj * score_query[:, :, None])
    attn_total = lax.psum((light_attn + heavy_attn).astype(jnp.bfloat16), "branch").astype(
        jnp.float32
    )
    hidden = inputs + attn_total
    inv_ffn = lax.rsqrt(jnp.mean(hidden * hidden, axis=-1, keepdims=True) + epsilon)
    unit_ffn = hidden * inv_ffn
    gain_ffn_f = gain_ffn.astype(jnp.float32)
    normed_ffn = unit_ffn * gain_ffn_f
    ffn_low = normed_ffn.astype(jnp.bfloat16)
    gate_l = project(ffn_low, gate_light).astype(jnp.bfloat16)
    up_l = project(ffn_low, up_light).astype(jnp.bfloat16)
    middle_l = geglu(gate_l, up_l)
    light_ffn = unproject(middle_l, down_light) * valid_rows
    router_ffn_f = router_ffn.astype(jnp.float32)
    score_ffn = pick_scalar(
        pick_query,
        jax.nn.sigmoid(jnp.einsum("dsc,c->ds", normed_ffn, router_ffn_f, precision=highest)),
    )
    ffn_rows = pick_rows(pick_query, normed_ffn).astype(jnp.bfloat16)
    gate_h = project(ffn_rows, gate_heavy).astype(jnp.bfloat16)
    up_h = project(ffn_rows, up_heavy).astype(jnp.bfloat16)
    middle_h = geglu(gate_h, up_h)
    heavy_fproj = unproject(middle_h, down_heavy)
    heavy_ffn = put_rows(pick_query, heavy_fproj * score_ffn[:, :, None])
    share = model_width // lax.axis_size("branch")
    own_cols = lax.axis_index("branch") * share
    mixed = lax.dynamic_slice_in_dim(hidden, own_cols, share, 2) + lax.psum_scatter(
        (light_ffn + heavy_ffn).astype(jnp.bfloat16), "branch", scatter_dimension=2, tiled=True
    ).astype(jnp.float32)
    grad_out = cotangent.astype(jnp.float32)
    grad_light = (grad_out * valid_rows).astype(jnp.bfloat16)
    grad_down_light = weight_grad(grad_light, middle_l)
    grad_gate_l, grad_up_l = geglu_back(gate_l, up_l, project(grad_light, down_light))
    grad_gate_light = weight_grad(ffn_low, grad_gate_l)
    grad_up_light = weight_grad(ffn_low, grad_up_l)
    grad_rows = pick_rows(pick_query, grad_out)
    grad_heavy = (grad_rows * score_ffn[:, :, None]).astype(jnp.bfloat16)
    score_ffn_part = jnp.sum(grad_rows * heavy_fproj, axis=-1)
    grad_down_heavy = weight_grad(grad_heavy, middle_h)
    grad_gate_h, grad_up_h = geglu_back(gate_h, up_h, project(grad_heavy, down_heavy))
    grad_gate_heavy = weight_grad(ffn_rows, grad_gate_h)
    grad_up_heavy = weight_grad(ffn_rows, grad_up_h)
    heavy_ffn_rows = unproject(grad_gate_h, gate_heavy) + unproject(grad_up_h, up_heavy)
    ffn_part = (
        unproject(grad_gate_l, gate_light)
        + unproject(grad_up_l, up_light)
        + put_rows(pick_query, heavy_ffn_rows)
    )
    grad_normed_ffn, grad_score_ffn = (
        lax.psum(ffn_part.astype(jnp.bfloat16), "branch").astype(jnp.float32),
        lax.psum(score_ffn_part.astype(jnp.bfloat16), "branch").astype(jnp.float32),
    )
    pre_ffn = put_scalar(pick_query, grad_score_ffn * score_ffn * (1.0 - score_ffn))
    grad_normed_ffn = grad_normed_ffn + pre_ffn[:, :, None] * router_ffn_f
    grad_router_ffn = jnp.einsum("ds,dsc->c", pre_ffn, normed_ffn, precision=highest)
    grad_gain_ffn = jnp.sum(grad_normed_ffn * unit_ffn, axis=(0, 1))
    grad_unit_f = grad_normed_ffn * gain_ffn_f
    grad_hidden = grad_out + inv_ffn * (
        grad_unit_f - unit_ffn * jnp.mean(grad_unit_f * unit_ffn, axis=-1, keepdims=True)
    )
    grad_light_attn = (grad_hidden * valid_rows).astype(jnp.bfloat16)
    grad_wo_light = weight_grad(grad_light_attn, piece_out)
    grad_light_out = split_heads(project(grad_light_attn, wo_light).astype(jnp.bfloat16))
    wide_grad = jnp.zeros((documents, local_len + 2 * radius, 2 * light_width), jnp.float32)
    light_raw, light_plow, unused_delta = score_grads(
        heads_q, wide_k, wide_v, light_bias, piece_lse, grad_light_out, None
    )
    query_pieces = contract_query(light_raw, wide_k)
    key_terms = jnp.concatenate(
        [contract_key(light_raw, heads_q), contract_key(light_plow, grad_light_out)], axis=2
    )
    wide_grad = wide_grad.at[:, 0:key_span].add(key_terms)
    grad_light_q = query_pieces.astype(jnp.bfloat16)
    outer_rims = jnp.concatenate(
        [wide_grad[:, :radius], wide_grad[:, radius + local_len :]], axis=1
    )
    returned = with_halo(outer_rims.astype(jnp.bfloat16), (("seq", 1),), radius).astype(
        outer_rims.dtype
    )
    inner = wide_grad[:, radius : radius + local_len]
    inner = inner + jnp.pad(returned[:, :radius], ((0, 0), (0, local_len - radius), (0, 0)))
    inner = inner + jnp.pad(returned[:, 3 * radius :], ((0, 0), (local_len - radius, 0), (0, 0)))
    grad_light_k = inner[:, :, :light_width].astype(jnp.bfloat16)
    grad_light_v = inner[:, :, light_width:].astype(jnp.bfloat16)
    grad_wq_light = weight_grad(normed_low, grad_light_q)
    grad_wk_light = weight_grad(normed_low, grad_light_k)
    grad_wv_light = weight_grad(normed_low, grad_light_v)
    light_part = (
        unproject(grad_light_q, wq_light)
        + unproject(grad_light_k, wk_light)
        + unproject(grad_light_v, wv_light)
    )
    grad_hrows = pick_rows(pick_query, grad_hidden)
    grad_heavy_attn = (grad_hrows * score_query[:, :, None]).astype(jnp.bfloat16)
    score_query_part = jnp.sum(grad_hrows * heavy_proj, axis=-1)
    grad_wo_heavy = weight_grad(grad_heavy_attn, heavy_out)
    grad_heavy_out = project(grad_heavy_attn, wo_heavy).astype(jnp.bfloat16)
    heavy_raw, heavy_plow, heavy_delta = score_grads(
        split_heads(heavy_q),
        split_heads(all_k),
        split_heads(all_v),
        heavy_bias,
        heavy_lse,
        split_heads(grad_heavy_out),
        None,
    )
    grad_heavy_q = contract_query(heavy_raw, split_heads(all_k)).astype(jnp.bfloat16)
    every_kv = jnp.concatenate(
        [
            contract_key(heavy_raw, split_heads(heavy_q)),
            contract_key(heavy_plow, split_heads(grad_heavy_out)),
        ],
        axis=2,
    )
    own_kv = lax.psum_scatter(every_kv, "seq", scatter_dimension=1, tiled=True)
    grad_heavy_k = own_kv[:, :, :heavy_width].astype(jnp.bfloat16)
    grad_heavy_v = own_kv[:, :, heavy_width:].astype(jnp.bfloat16)
    grad_scaled = unproject(grad_heavy_v, wv_heavy)
    score_key_part = jnp.sum(grad_scaled * key_rows, axis=-1)
    grad_key_rows = unproject(grad_heavy_k, wk_heavy) + grad_scaled * score_key[:, :, None]
    grad_wq_heavy = weight_grad(heavy_in, grad_heavy_q)
    grad_wk_heavy = weight_grad(key_in, grad_heavy_k)
    grad_wv_heavy = weight_grad(scaled_in, grad_heavy_v)
    attn_part = (
        light_part
        + put_rows(pick_query, unproject(grad_heavy_q, wq_heavy))
        + put_rows(pick_key, grad_key_rows)
    )
    grad_normed, grad_score_query, grad_score_key = (
        lax.psum(attn_part.astype(jnp.bfloat16), "branch").astype(jnp.float32),
        lax.psum(score_query_part.astype(jnp.bfloat16), "branch").astype(jnp.float32),
        lax.psum(score_key_part.astype(jnp.bfloat16), "branch").astype(jnp.float32),
    )
    pre_query = put_scalar(pick_query, grad_score_query * score_query * (1.0 - score_query))
    pre_key = put_scalar(pick_key, grad_score_key * score_key * (1.0 - score_key))
    grad_normed = (
        grad_normed + pre_query[:, :, None] * router_query_f + pre_key[:, :, None] * router_key_f
    )
    grad_router_query = jnp.einsum("ds,dsc->c", pre_query, normed, precision=highest)
    grad_router_key = jnp.einsum("ds,dsc->c", pre_key, normed, precision=highest)
    grad_gain_attn = jnp.sum(grad_normed * unit_attn, axis=(0, 1))
    grad_unit_a = grad_normed * gain_attn_f
    grad_tokens = grad_hidden + inv_attn * (
        grad_unit_a - unit_attn * jnp.mean(grad_unit_a * unit_attn, axis=-1, keepdims=True)
    )
    names = (
        grad_wq_light, grad_wk_light, grad_wv_light, grad_wo_light,
        grad_wq_heavy, grad_wk_heavy, grad_wv_heavy, grad_wo_heavy,
        grad_gate_light, grad_up_light, grad_down_light,
        grad_gate_heavy, grad_up_heavy, grad_down_heavy,
    )
    vectors = jnp.stack(
        [grad_gain_attn, grad_router_query, grad_router_key, grad_gain_ffn, grad_router_ffn], axis=1
    )
    packed = jnp.concatenate([g.astype(jnp.bfloat16) for g in names + (vectors,)], axis=1)
    summed = lax.psum_scatter(packed, "seq", scatter_dimension=0, tiled=True).astype(jnp.float32)
    widths = [g.shape[1] for g in names]
    cuts = [sum(widths[:i]) for i in range(len(widths) + 1)]
    (
        grad_wq_light, grad_wk_light, grad_wv_light, grad_wo_light,
        grad_wq_heavy, grad_wk_heavy, grad_wv_heavy, grad_wo_heavy,
        grad_gate_light, grad_up_light, grad_down_light,
        grad_gate_heavy, grad_up_heavy, grad_down_heavy,
    ) = [summed[:, cuts[i] : cuts[i + 1]] for i in range(len(widths))]
    grad_gain_attn, grad_router_query, grad_router_key, grad_gain_ffn, grad_router_ffn = [
        summed[:, cuts[-1] + i] for i in range(5)
    ]
    return (
        mixed,
        grad_tokens,
        grad_gain_attn,
        grad_router_query,
        grad_router_key,
        grad_wq_light,
        grad_wk_light,
        grad_wv_light,
        grad_wo_light,
        grad_wq_heavy,
        grad_wk_heavy,
        grad_wv_heavy,
        grad_wo_heavy,
        grad_gain_ffn,
        grad_router_ffn,
        grad_gate_light,
        grad_up_light,
        grad_down_light,
        grad_gate_heavy,
        grad_up_heavy,
        grad_down_heavy,
    )


BF = jnp.bfloat16
F32 = jnp.float32
MESH = pl.DeviceIdType.MESH


def mm(a, b):
    return jnp.dot(a, b, preferred_element_type=F32)


def mmt(a, b):
    return lax.dot_general(a, b, (((1,), (1,)), ((), ())), preferred_element_type=F32)


def tmm(a, b):
    return lax.dot_general(a, b, (((0,), (0,)), ((), ())), preferred_element_type=F32)


def row_sum(values):
    return jnp.sum(values, axis=-1, keepdims=True)


def gelu_parts(v):
    c = math.sqrt(2.0 / math.pi)
    square = v * v
    t = jnp.tanh(c * v * (1.0 + 0.044715 * square))
    act = 0.5 * v * (1.0 + t)
    slope = 0.5 * (1.0 + t) + (0.5 * c) * v * (1.0 - t * t) * (1.0 + 0.134145 * square)
    return act, slope


def layer_kernel(dims, *refs):
    docs, rows, width, slots, n_seq, wl, wh, fl_n, fh_n = dims
    nz = n_seq // 2
    chunk = width // n_seq
    half = rows // 2
    quarter = rows // 4
    eighth = rows // 8
    radius = WINDOW // 2
    share = width // 4
    it = iter(refs)

    def take(count):
        return [next(it) for _ in range(count)]

    lens, vec, idxc, idxr = take(4)
    (tok_h, cot_h, wql_h, wkl_h, wvl_h, wol_h, wqh_h, wkh_h, wvh_h, woh_h,
     gl_h, ul_h, dl_h, gh_h, uh_h, dh_h) = take(16)
    gt_o, mix_o, tot_o, pack_o = take(4)
    (tok, cot, wqkv, wol, whq, whk, whv, who, wgul, wdl, wguh, wdh) = take(12)
    (nl, inva, hin, kin, sin, qbuf, kvw, pbuf, lo, hqx, kvall, ph, hox) = take(13)
    (pqk, pqkt, parts, tot1, tot2, r1, r2, cols) = take(8)
    (dm, dmh, grow, fl, invf, mid, dgu, frow, ghr, midh, dguh) = take(11)
    (mixb, mixr, ghf, ghb, dol, dox, gah, dqh, dkvw, rims, rimr, dqkv) = take(12)
    (hb, h1, h2, dkvh, gains) = take(5)
    (g_h, g_l, ra_h, ra_l, ra_a, rb_h, rb_l, rb_a, packed, vbuf, vr) = take(11)
    g_a = wguh
    (load_s, ar_s, ar_r, ag_s, ag_r, fw_s, fw_r, halo_s, halo_r, rim_s, rim_r, ha_s, ha_r, hz_s, hz_r,
     mx_s, mx_r, wa_s, wa_r, wz_s, wz_r, v_s, v_r, out_s) = take(24)

    b = lax.axis_index("branch")
    s = lax.axis_index("seq")
    bit_x = b % 2
    bit_y = b // 2
    core = s % 2
    z = s // 2
    offset = s * rows
    dev_x = (b + 1 - 2 * bit_x, s)
    dev_y = (b + 2 - 4 * bit_y, s)
    sibling = (b, s + 1 - 2 * core)

    def zpeer(k):
        return (z + k) % nz

    def same_core(k):
        return (b, 2 * zpeer(k) + core)

    late = []

    def send(src, dst, ssem, rsem, dev, when=None):
        copy = pltpu.make_async_remote_copy(
            src_ref=src, dst_ref=dst, send_sem=ssem, recv_sem=rsem, device_id=dev, device_id_type=MESH
        )
        if when is None:
            copy.start()
        else:
            pl.when(when)(copy.start)
        return copy

    def arrived(dst, ssem, rsem, dev):
        pltpu.make_async_remote_copy(
            src_ref=dst, dst_ref=dst, send_sem=ssem, recv_sem=rsem, device_id=dev, device_id_type=MESH
        ).wait_recv()

    loads = {}

    def load(name, src, dst, i):
        copy = pltpu.make_async_copy(src, dst, load_s.at[i])
        copy.start()
        loads[name] = copy

    load("tok", tok_h, tok, 0)
    load("whq", wqh_h, whq, 1)
    load("whk", wkh_h, whk, 2)
    load("whv", wvh_h, whv, 3)
    load("wq", wql_h, wqkv.at[:, 0:wl], 4)
    load("wk", wkl_h, wqkv.at[:, wl : 2 * wl], 5)
    load("wv", wvl_h, wqkv.at[:, 2 * wl : 3 * wl], 6)
    load("wol", wol_h, wol, 7)
    load("who", woh_h, who, 8)
    load("cot", cot_h, cot, 9)
    load("wdl", dl_h, wdl, 10)
    load("wdh", dh_h, wdh, 11)
    load("gl", gl_h, wgul.at[:, 0:fl_n], 12)
    load("ul", ul_h, wgul.at[:, fl_n : 2 * fl_n], 13)
    load("gh", gh_h, wguh.at[:, 0:fh_n], 14)
    load("uh", uh_h, wguh.at[:, fh_n : 2 * fh_n], 15)

    barrier = pltpu.get_barrier_semaphore()
    for k in range(1, 4):
        pl.semaphore_signal(barrier, inc=1, device_id=((b + k) % 4, s), device_id_type=MESH)

    def greet(k, carry):
        pl.semaphore_signal(barrier, inc=1, device_id=(b, (s + k) % n_seq), device_id_type=MESH)
        return carry

    lax.fori_loop(1, n_seq, greet, 0)
    pl.semaphore_wait(barrier, 3 + n_seq - 1)

    gain_a = vec[0:1, :]
    router_q = vec[1:2, :]
    router_k = vec[2:3, :]
    gain_f = vec[3:4, :]
    router_f = vec[4:5, :]

    def valid_rows(d, first, count):
        at = lax.broadcasted_iota(jnp.int32, (count, 1), 0) + (offset + first)
        return jnp.where(at < lens[d], 1.0, 0.0).astype(F32)

    def tiles(count, size, body):
        def step(t, carry):
            body(pl.multiple_of(t * size, size))
            return carry

        lax.fori_loop(0, count // size, step, 0)

    def geometry(h):
        first, second = ((dev_x, bit_x), (dev_y, bit_y))[:: 1 if h == 0 else -1]
        base = half * h
        keep1 = base + quarter * first[1]
        send1 = base + quarter * (1 - first[1])
        keep2 = keep1 + eighth * second[1]
        send2 = keep1 + eighth * (1 - second[1])
        return (first[0], second[0]) + tuple(pl.multiple_of(v, eighth) for v in (keep1, send1, keep2, send2))

    flights = {}

    def ar_start(a, d, h):
        first, second, keep1, send1, keep2, send2 = geometry(h)
        flights[a, d, h, 0] = send(
            parts.at[d, pl.ds(send1, quarter)], r1.at[d, h], ar_s.at[a, d, h, 0], ar_r.at[a, d, h, 0], first
        )

    def add_rows(d, at, buf, base, total):
        def body(t, carry):
            r = pl.multiple_of(t * 32, 32)
            here = pl.ds(pl.multiple_of(at + r, 32), 32)
            value = parts[d, here, :].astype(F32) + buf[pl.ds(base + r, 32), :].astype(F32)
            total[d, here, :] = value.astype(BF)
            return carry

        lax.fori_loop(0, eighth // 32, body, 0)

    def ar_step(a, d, step, total):
        for h in range(2):
            first, second, keep1, send1, keep2, send2 = geometry(h)
            at = (a, d, h)
            if step == 1:
                arrived(r1.at[d, h], ar_s.at[a, d, h, 0], ar_r.at[a, d, h, 0], first)
                add_rows(d, send2, r1.at[d, h], pl.multiple_of(send2 - keep1, eighth), parts)
                flights[at + (1,)] = send(
                    parts.at[d, pl.ds(send2, eighth)], r2.at[d, h], ar_s.at[a, d, h, 1], ar_r.at[a, d, h, 1], second
                )
                add_rows(d, keep2, r1.at[d, h], pl.multiple_of(keep2 - keep1, eighth), parts)
            elif step == 2:
                arrived(r2.at[d, h], ar_s.at[a, d, h, 1], ar_r.at[a, d, h, 1], second)
                add_rows(d, keep2, r2.at[d, h], 0, total)
                own = total.at[d, pl.ds(keep2, eighth)]
                flights[at + (2,)] = send(own, own, ar_s.at[a, d, h, 2], ar_r.at[a, d, h, 2], second)
            elif step == 3:
                arrived(total.at[d, pl.ds(send2, eighth)], ar_s.at[a, d, h, 2], ar_r.at[a, d, h, 2], second)
                own = total.at[d, pl.ds(keep1, quarter)]
                flights[at + (3,)] = send(own, own, ar_s.at[a, d, h, 3], ar_r.at[a, d, h, 3], first)
            else:
                arrived(total.at[d, pl.ds(send1, quarter)], ar_s.at[a, d, h, 3], ar_r.at[a, d, h, 3], first)
                flights[at + (0,)].wait_send()
                flights[at + (1,)].wait_send()

    def ar_sent(a, d):
        for h in range(2):
            flights[a, d, h, 2].wait_send()
            flights[a, d, h, 3].wait_send()

    loads["tok"].wait()
    for d in range(docs):

        def norm_body(t, d=d):
            r = pl.ds(t, 32)
            x = tok[d, r, :].astype(F32)
            inv = lax.rsqrt(row_sum(x * x) * (1.0 / width) + epsilon)
            inva[d, r, :] = inv
            nl[d, r, :] = (x * inv * gain_a).astype(BF)

        tiles(rows, 32, norm_body)

    for d in range(docs):
        lane_pos = lax.broadcasted_iota(jnp.int32, (2 * slots, rows), 1) + offset
        pqk[d] = jnp.where(idxc[:, d : d + 1] == lane_pos, 1.0, 0.0).astype(BF)
        sub_pos = lax.broadcasted_iota(jnp.int32, (rows, 2 * slots), 0) + offset
        pqkt[d] = jnp.where(idxr[d : d + 1, :] == sub_pos, 1.0, 0.0).astype(BF)

    SQ, SK, SF, PREQ, PREF, PREK = range(6)

    def mine(d):
        return slice(d * slots, (d + 1) * slots)

    for d in range(docs):
        live = jnp.where(idxc[:, d : d + 1] >= 0, 1.0, 0.0).astype(F32)
        picked = mm(pqk[d], nl[d])
        score_q = jax.nn.sigmoid(row_sum(picked[:slots] * router_q)) * live[:slots]
        score_k = jax.nn.sigmoid(row_sum(picked[slots:] * router_k)) * live[slots:]
        cols[SQ, mine(d), :] = score_q
        cols[SK, mine(d), :] = score_k
        hin[mine(d), :] = picked[:slots].astype(BF)
        kin[mine(d), :] = picked[slots:].astype(BF)
        sin[mine(d), :] = (picked[slots:] * score_k).astype(BF)
        pad_lane = lax.broadcasted_iota(jnp.int32, (slots, 256 - wh), 1)
        kvall[s, mine(d), wh:256] = jnp.where(
            pad_lane == 0, (1.0 - live[slots:]) * masked_value, 0.0
        ).astype(BF)
        kvall[s, mine(d), 256 + wh : 512] = jnp.zeros((slots, 256 - wh), BF)
    loads["whk"].wait()
    kvall[s, :, 0:wh] = mm(kin[...], whk[...]).astype(BF)
    loads["whv"].wait()
    kvall[s, :, 256 : 256 + wh] = mm(sin[...], whv[...]).astype(BF)

    own_block = kvall.at[s]
    late.append(send(own_block, own_block, ag_s.at[0], ag_r.at[0], sibling))
    for k in range(1, nz):
        late.append(send(own_block, own_block, ag_s.at[k], ag_r.at[k], same_core(k)))

    loads["whq"].wait()
    hqx[:, 0:wh] = mm(hin[...], whq[...]).astype(BF)
    pad_lane = lax.broadcasted_iota(jnp.int32, (docs * slots, 256 - wh), 1)
    hqx[:, wh:256] = jnp.where(pad_lane == 0, 8.0, 0.0).astype(BF)

    for name in ("wq", "wk", "wv"):
        loads[name].wait()
    last = n_seq - 1
    left = (b, (s + last) % n_seq)
    right = (b, (s + 1) % n_seq)
    for d in range(docs):

        def qkv_body(t, d=d):
            r = mm(nl[d, pl.ds(t, half), :], wqkv[...]).astype(BF)
            qbuf[d, pl.ds(t, half), :] = r[:, 0:wl]
            kvw[d, pl.ds(pl.multiple_of(t + radius, 32), half), :] = r[:, wl : 3 * wl]

        tiles(rows, half, qkv_body)

        @pl.when(s == 0)
        def _(d=d):
            kvw[d, 0:radius, :] = jnp.zeros((radius, 2 * wl), BF)

        @pl.when(s == last)
        def _(d=d):
            kvw[d, rows + radius : rows + 2 * radius, :] = jnp.zeros((radius, 2 * wl), BF)

        late.append((s > 0, send(
            kvw.at[d, pl.ds(radius, radius)], kvw.at[d, pl.ds(rows + radius, radius)],
            halo_s.at[d, 0], halo_r.at[d, 0], left, s > 0,
        )))
        late.append((s < last, send(
            kvw.at[d, pl.ds(rows, radius)], kvw.at[d, pl.ds(0, radius)],
            halo_s.at[d, 1], halo_r.at[d, 1], right, s < last,
        )))

    def halo_wait(d):
        @pl.when(s < last)
        def _():
            arrived(kvw.at[d, pl.ds(rows + radius, radius)], halo_s.at[d, 0], halo_r.at[d, 0], right)

        @pl.when(s > 0)
        def _():
            arrived(kvw.at[d, pl.ds(0, radius)], halo_s.at[d, 1], halo_r.at[d, 1], left)

    blk = WINDOW
    span = 2 * WINDOW
    n_blk = rows // blk

    def two_heads(v):
        lane = lax.broadcasted_iota(jnp.int32, v.shape, 1)
        zero = jnp.zeros_like(v)
        return jnp.concatenate([jnp.where(lane < HD, v, zero), jnp.where(lane < HD, zero, v)], axis=0)

    def one_of_two(v):
        lane = lax.broadcasted_iota(jnp.int32, (blk, 2 * HD), 1)
        return jnp.where(lane < HD, v[:blk], v[blk:])

    def light_attention(d):
        def body(i, carry):
            at = pl.multiple_of(i * blk, blk)
            q2 = two_heads(qbuf[d, pl.ds(at, blk), :])
            k = kvw[d, pl.ds(at, span), 0:wl]
            v = kvw[d, pl.ds(at, span), wl : 2 * wl]
            row = lax.broadcasted_iota(jnp.int32, (2 * blk, span), 0) % blk
            col = lax.broadcasted_iota(jnp.int32, (2 * blk, span), 1)
            pos = col + (offset + at - radius)
            seen = (col >= row) & (col <= row + WINDOW) & (pos >= 0) & (pos < lens[d])
            scores = jnp.where(seen, mmt(q2, k) * HD ** (-0.5), masked_value)
            e = jnp.exp(scores - jnp.max(scores, axis=-1, keepdims=True))
            p = (e * (1.0 / row_sum(e))).astype(BF)
            pbuf[d * n_blk + i] = p
            out = one_of_two(mm(p, v))
            lo[d, pl.ds(at, blk), :] = (out * valid_rows(d, at, blk)).astype(BF)
            return carry

        lax.fori_loop(0, n_blk, body, 0)

    def three_heads(v):
        lane = lax.broadcasted_iota(jnp.int32, v.shape, 1)
        zero = jnp.zeros_like(v)
        return jnp.concatenate(
            [jnp.where((lane // HD == h) | (lane >= wh), v, zero) for h in range(wh // HD)], axis=0
        )

    def one_of_three(v):
        lane = lax.broadcasted_iota(jnp.int32, (slots, 256), 1)
        total = jnp.zeros((slots, 256), F32)
        for h in range(wh // HD):
            total = jnp.where(lane // HD == h, v[h * slots : (h + 1) * slots], total)
        return total

    def keys_of(d, at):
        return kvall[:, mine(d), at : at + 256].reshape(n_seq * slots, 256)

    def heavy_attention(d):
        q3 = three_heads(hqx[mine(d), :])
        scores = mmt(q3, keys_of(d, 0)) * HD ** (-0.5)
        e = jnp.exp(scores - jnp.max(scores, axis=-1, keepdims=True))
        p = (e * (1.0 / row_sum(e))).astype(BF)
        ph[d] = p
        hox[mine(d), :] = one_of_three(mm(p, keys_of(d, 256))).astype(BF)

    halo_wait(0)
    light_attention(0)
    forwards = []
    for k in range(1, nz):
        block = kvall.at[2 * zpeer(nz - k) + core]
        arrived(block, ag_s.at[k], ag_r.at[k], same_core(nz - k))
        late.append(send(block, block, fw_s.at[k], fw_r.at[k], sibling))
    halo_wait(1)
    light_attention(1)
    arrived(kvall.at[s + 1 - 2 * core], ag_s.at[0], ag_r.at[0], sibling)
    for k in range(1, nz):
        block = kvall.at[2 * zpeer(nz - k) + 1 - core]
        arrived(block, fw_s.at[k], fw_r.at[k], sibling)

    loads["who"].wait()
    loads["wol"].wait()

    def attention_terms(d):
        heavy_attention(d)
        proj = (mmt(hox[mine(d), 0:wh], who[...]) * cols[SQ, mine(d), :]).astype(BF)
        for h in range(2):
            r = pl.ds(h * half, half)
            value = mmt(lo[d, r, :], wol[...]) + mm(pqkt[d, r, 0:slots], proj)
            parts[d, r, :] = value.astype(BF)
            ar_start(0, d, h)

    attention_terms(0)
    attention_terms(1)
    ar_step(0, 0, 1, tot1)

    for name in ("cot", "wdl", "wdh"):
        loads[name].wait()

    def light_pre(d):
        def body(t):
            r = pl.ds(t, half)
            dm[d, r, :] = mm(cot[d, r, :], wdl[...]) * valid_rows(d, t, half)

        tiles(rows, half, body)
        grow[mine(d), :] = mm(pqk[d, 0:slots, :], cot[d]).astype(BF)

    light_pre(0)
    ar_step(0, 0, 2, tot1)
    ar_step(0, 1, 1, tot1)
    light_pre(1)
    dmh[...] = mm(grow[...], wdh[...])
    ar_step(0, 0, 3, tot1)
    ar_step(0, 1, 2, tot1)
    for name in ("gl", "ul", "gh", "uh"):
        loads[name].wait()

    gains[...] = jnp.zeros(gains.shape, F32)

    def hidden_rows(d, r):
        return tok[d, r, :].astype(F32) + tot1[d, r, :].astype(F32)

    def ffn_norm(d):
        def body(t):
            r = pl.ds(t, 32)
            hidden = hidden_rows(d, r)
            inv = lax.rsqrt(row_sum(hidden * hidden) * (1.0 / width) + epsilon)
            invf[d, r, :] = inv
            fl[d, r, :] = (hidden * inv * gain_f).astype(BF)

        tiles(rows, 32, body)

    def ffn_heavy(d):
        live = jnp.where(idxc[0:slots, d : d + 1] >= 0, 1.0, 0.0).astype(F32)
        rowsf = mm(pqk[d, 0:slots, :], fl[d])
        score = jax.nn.sigmoid(row_sum(rowsf * router_f)) * live
        cols[SF, mine(d), :] = score
        frow[mine(d), :] = rowsf.astype(BF)
        ghr[mine(d), :] = (grow[mine(d), :].astype(F32) * score).astype(BF)
        step = 256

        def body(t, dscore):
            c = pl.ds(pl.multiple_of(t * step, step), step)
            c2 = pl.ds(pl.multiple_of(fh_n + t * step, step), step)
            gate = mm(frow[mine(d), :], wguh[:, c]).astype(BF).astype(F32)
            up = mm(frow[mine(d), :], wguh[:, c2]).astype(BF).astype(F32)
            act, slope = gelu_parts(gate)
            middle = (act * up).astype(BF)
            raw = dmh[mine(d), c]
            grad_mid = raw * score
            midh[mine(d), c] = middle
            dguh[mine(d), c] = (grad_mid * up * slope).astype(BF)
            dguh[mine(d), c2] = (grad_mid * act).astype(BF)
            return dscore + row_sum(middle.astype(F32) * raw)

        dscore = lax.fori_loop(0, fh_n // step, body, jnp.zeros((slots, 1), F32))
        pre = dscore * score * (1.0 - score)
        cols[PREF, mine(d), :] = pre
        return (mmt(dguh[mine(d), :], wguh[...]) + pre * router_f).astype(BF)

    def add_gain(which, values):
        count = values.shape[0]
        gains[which] += jnp.sum(values.reshape(count // 8, 8, width), axis=0)

    def ffn_light(d, back_rows, between):
        for h in range(2):
            r = pl.ds(h * half, half)
            gu = mm(fl[d, r, :], wgul[...]).astype(BF)
            gate = gu[:, 0:fl_n].astype(F32)
            up = gu[:, fl_n : 2 * fl_n].astype(F32)
            act, slope = gelu_parts(gate)
            mid[d, r, :] = (act * up * valid_rows(d, h * half, half)).astype(BF)
            grad_mid = dm[d, r, :]
            dgu[d, r, 0:fl_n] = (grad_mid * up * slope).astype(BF)
            dgu[d, r, fl_n : 2 * fl_n] = (grad_mid * act).astype(BF)
            value = mmt(dgu[d, r, :], wgul[...]) + mm(pqkt[d, r, 0:slots], back_rows)
            parts[d, r, :] = value.astype(BF)
            ar_start(1, d, h)

            def gain_body(t, d=d, h=h):
                rr = pl.ds(pl.multiple_of(h * half + t, 32), 32)
                unit = hidden_rows(d, rr) * invf[d, rr, :]
                add_gain(1, parts[d, rr, :].astype(F32) * unit)

            tiles(half, 32, gain_body)
            if h == 0:
                between()

    def nothing():
        pass

    ar_step(0, 0, 4, tot1)
    ffn_norm(0)
    back0 = ffn_heavy(0)
    ar_step(0, 1, 3, tot1)
    ffn_light(0, back0, nothing)
    ar_step(0, 1, 4, tot1)
    ffn_norm(1)
    back1 = ffn_heavy(1)
    ar_step(1, 0, 1, tot2)
    ffn_light(1, back1, nothing)
    ar_step(1, 0, 2, tot2)
    tot_copy = pltpu.make_async_copy(tot1, tot_o, out_s.at[0])
    tot_copy.start()

    grads = ((g_h, ra_h, rb_h), (g_l, ra_l, rb_l), (g_a, ra_a, rb_a))
    packed_at = (0, g_h.shape[1], g_h.shape[1] + g_l.shape[1])

    def chunk_rows(zz, cc):
        return pl.ds(pl.multiple_of(chunk * (2 * zz + cc), chunk), chunk)

    def rs_start(p):
        grad, ra, rb = grads[p]
        for zz in range(nz):
            late.append(send(
                grad.at[chunk_rows(zz, 1 - core), pl.ds(0, ra.shape[2])], ra.at[zz],
                wa_s.at[p, zz], wa_r.at[p, zz], sibling,
            ))

    def rs_middle(p):
        grad, ra, rb = grads[p]
        cut = ra.shape[2]
        for k in range(1, nz + 1):
            zz = zpeer(k)
            arrived(ra.at[zz], wa_s.at[p, zz], wa_r.at[p, zz], sibling)

            def add_body(t, carry):
                r = pl.ds(pl.multiple_of(chunk * (2 * zz + core) + 16 * t, 16), 16)
                value = grad[r, 0:cut].astype(F32) + ra[zz, pl.ds(pl.multiple_of(16 * t, 16), 16), :].astype(F32)
                grad[r, 0:cut] = value.astype(BF)
                return carry

            lax.fori_loop(0, chunk // 16, add_body, 0)
            if k < nz:
                late.append(send(
                    grad.at[chunk_rows(zz, core), pl.ds(0, cut)], rb.at[k - 1],
                    wz_s.at[p, k - 1], wz_r.at[p, k - 1], same_core(k),
                ))

    def rs_end(p):
        grad, ra, rb = grads[p]
        cut = ra.shape[2]
        for k in range(1, nz):
            arrived(rb.at[k - 1], wz_s.at[p, k - 1], wz_r.at[p, k - 1], same_core(nz - k))

        def add_body(t, carry):
            r = pl.ds(pl.multiple_of(16 * t, 16), 16)
            value = grad[pl.ds(pl.multiple_of(chunk * s + 16 * t, 16), 16), 0:cut].astype(F32)
            for k in range(1, nz):
                value = value + rb[k - 1, r, :].astype(F32)
            packed[r, packed_at[p] : packed_at[p] + cut] = value
            return carry

        lax.fori_loop(0, chunk // 16, add_body, 0)

    def heavy_ffn_grads():
        step = 512
        for src, gr, base, total in ((frow, dguh, 0, 2 * fh_n), (ghr, midh, 2 * fh_n, fh_n)):
            for t in range(2):
                f = slice(t * (width // 2), (t + 1) * (width // 2))
                left_t = src[:, f].T

                def body(i, carry, gr=gr, f=f, base=base, left_t=left_t):
                    c = pl.ds(pl.multiple_of(i * step, step), step)
                    o = pl.ds(pl.multiple_of(base + i * step, step), step)
                    g_h[f, o] = mm(left_t, gr[:, c]).astype(BF)
                    return carry

                lax.fori_loop(0, total // step, body, 0)

    def all_rows(ref, f):
        return ref[:, :, f].reshape(docs * rows, ref[:, :, f].shape[2])

    def light_grad(src, gr, ref, base):
        for t in range(2):
            f = slice(t * (width // 2), (t + 1) * (width // 2))
            right_side = gr[...].reshape(docs * rows, gr.shape[2])
            ref[f, base : base + gr.shape[2]] = tmm(all_rows(src, f), right_side).astype(BF)

    heavy_ffn_grads()
    rs_start(0)
    ar_step(1, 1, 1, tot2)
    ar_step(1, 0, 3, tot2)
    light_grad(fl, dgu, g_l, 0)
    light_grad(cot, mid, g_l, 2 * fl_n)
    rs_start(1)
    rs_middle(0)
    ar_step(1, 1, 2, tot2)

    def mixed_terms(d):
        def body(j, carry):
            w = pl.ds(pl.multiple_of(j * share, share), share)
            heavy = (mmt(midh[mine(d), :], wdh[w, :]) * cols[SF, mine(d), :]).astype(BF)
            for h in range(2):
                r = pl.ds(h * half, half)
                value = mmt(mid[d, r, :], wdl[w, :]) + mm(pqkt[d, r, 0:slots], heavy)
                mixb[j, d, r, :] = value.astype(BF)
            return carry

        lax.fori_loop(0, 4, body, 0)

    mixed_terms(0)
    mixed_terms(1)
    rs_middle(1)

    def hidden_grad(d):
        def body(t):
            r = pl.ds(t, 32)
            unit = hidden_rows(d, r) * invf[d, r, :]
            w = tot2[d, r, :].astype(F32) * gain_f
            inner = row_sum(w * unit) * (1.0 / width)
            value = cot[d, r, :].astype(F32) + invf[d, r, :] * (w - unit * inner)
            ghf[d, r, :] = value
            ghb[d, r, :] = value.astype(BF)

        tiles(rows, 32, body)

    def heavy_back(d):
        picked = mm(pqk[d, 0:slots, :], ghb[d])
        score = cols[SQ, mine(d), :]
        gah[mine(d), :] = (picked * score).astype(BF)
        raw = mm(picked.astype(BF), who[...])
        pre = row_sum(hox[mine(d), 0:wh].astype(F32) * raw) * score * (1.0 - score)
        cols[PREQ, mine(d), :] = pre
        dox[mine(d), 0:wh] = (raw * score).astype(BF)
        dox[mine(d), wh:256] = jnp.zeros((slots, 256 - wh), BF)
        do3 = three_heads(dox[mine(d), :])
        q3 = three_heads(hqx[mine(d), :])
        p = ph[d]
        pf = p.astype(F32)
        dp = mmt(do3, keys_of(d, 256))
        ds = (pf * (dp - row_sum(dp * pf)) * HD ** (-0.5)).astype(BF)
        dqh[mine(d), :] = one_of_three(mm(ds, keys_of(d, 0))).astype(BF)
        dk = tmm(ds, q3).astype(BF).reshape(nz, 2, slots, 256)
        dv = tmm(p, do3).astype(BF).reshape(nz, 2, slots, 256)
        for c in range(2):
            for zz in range(nz):
                hb[d, c, zz, :, 0:256] = dk[zz, c]
                hb[d, c, zz, :, 256:512] = dv[zz, c]
        late.append(send(hb.at[d, 1 - core], h1.at[d], ha_s.at[d], ha_r.at[d], sibling))

    def heavy_back_middle(d):
        arrived(h1.at[d], ha_s.at[d], ha_r.at[d], sibling)
        for k in range(1, nz + 1):
            zz = zpeer(k)
            value = hb[d, core, zz].astype(F32) + h1[d, zz].astype(F32)
            hb[d, core, zz] = value.astype(BF)
            if k < nz:
                late.append(send(
                    hb.at[d, core, zz], h2.at[d, k - 1], hz_s.at[d, k - 1], hz_r.at[d, k - 1], same_core(k)
                ))

    def heavy_back_end(d):
        for k in range(1, nz):
            arrived(h2.at[d, k - 1], hz_s.at[d, k - 1], hz_r.at[d, k - 1], same_core(nz - k))
        value = hb[d, core, z].astype(F32)
        for k in range(1, nz):
            value = value + h2[d, k - 1].astype(F32)
        dkvh[mine(d), :] = value.astype(BF)

    def light_back(d):
        dkvw[d] = jnp.zeros((rows + 2 * radius, 2 * wl), F32)

        def dol_body(t):
            r = pl.ds(t, half)
            dol[d, r, :] = (mm(ghb[d, r, :], wol[...]) * valid_rows(d, t, half)).astype(BF)

        tiles(rows, half, dol_body)

        def body(i, carry):
            at = pl.multiple_of(i * blk, blk)
            q2 = two_heads(qbuf[d, pl.ds(at, blk), :])
            do2 = two_heads(dol[d, pl.ds(at, blk), :])
            k = kvw[d, pl.ds(at, span), 0:wl]
            v = kvw[d, pl.ds(at, span), wl : 2 * wl]
            p = pbuf[d * n_blk + i]
            pf = p.astype(F32)
            dp = mmt(do2, v)
            ds = (pf * (dp - row_sum(dp * pf)) * HD ** (-0.5)).astype(BF)
            dqkv[d, pl.ds(at, blk), 0:wl] = one_of_two(mm(ds, k)).astype(BF)
            dkvw[d, pl.ds(at, span), 0:wl] += tmm(ds, q2)
            dkvw[d, pl.ds(at, span), wl : 2 * wl] += tmm(p, do2)
            return carry

        lax.fori_loop(0, n_blk, body, 0)
        rims[d, 0] = dkvw[d, 0:radius, :].astype(BF)
        rims[d, 1] = dkvw[d, rows + radius : rows + 2 * radius, :].astype(BF)

        @pl.when(s == 0)
        def _():
            rimr[d, 0] = jnp.zeros((radius, 2 * wl), BF)

        @pl.when(s == last)
        def _():
            rimr[d, 1] = jnp.zeros((radius, 2 * wl), BF)

        late.append((s > 0, send(rims.at[d, 0], rimr.at[d, 1], rim_s.at[d, 0], rim_r.at[d, 0], left, s > 0)))
        late.append((s < last, send(rims.at[d, 1], rimr.at[d, 0], rim_s.at[d, 1], rim_r.at[d, 1], right, s < last)))

    def rim_wait(d):
        @pl.when(s < last)
        def _():
            arrived(rimr.at[d, 1], rim_s.at[d, 0], rim_r.at[d, 0], right)

        @pl.when(s > 0)
        def _():
            arrived(rimr.at[d, 0], rim_s.at[d, 1], rim_r.at[d, 1], left)

    def attention_back_terms(d):
        heavy_back_end(d)
        ds_in = mmt(dkvh[mine(d), 256 : 256 + wh], whv[...])
        score = cols[SK, mine(d), :]
        pre_k = row_sum(ds_in * kin[mine(d), :].astype(F32)) * score * (1.0 - score)
        cols[PREK, mine(d), :] = pre_k
        key_rows = mmt(dkvh[mine(d), 0:wh], whk[...]) + ds_in * score + pre_k * router_k
        query_rows = mmt(dqh[mine(d), 0:wh], whq[...]) + cols[PREQ, mine(d), :] * router_q
        both = jnp.concatenate([query_rows, key_rows], axis=0).astype(BF)
        rim_wait(d)
        dkvw[d, radius : 2 * radius, :] += rimr[d, 0].astype(F32)
        dkvw[d, rows : rows + radius, :] += rimr[d, 1].astype(F32)
        for h in range(2):
            r = pl.ds(h * half, half)
            dqkv[d, r, wl : 3 * wl] = dkvw[d, pl.ds(h * half + radius, half), :].astype(BF)
            value = mmt(dqkv[d, r, :], wqkv[...]) + mm(pqkt[d, r, :], both)
            parts[d, r, :] = value.astype(BF)
            ar_start(2, d, h)

            def gain_body(t, d=d, h=h):
                rr = pl.ds(pl.multiple_of(h * half + t, 32), 32)
                unit = tok[d, rr, :].astype(F32) * inva[d, rr, :]
                add_gain(0, parts[d, rr, :].astype(F32) * unit)

            tiles(half, 32, gain_body)

    def token_grad(d):
        def body(t):
            r = pl.ds(t, 32)
            inv = inva[d, r, :]
            unit = tok[d, r, :].astype(F32) * inv
            w = tot2[d, r, :].astype(F32) * gain_a
            inner = row_sum(w * unit) * (1.0 / width)
            ghf[d, r, :] = ghf[d, r, :] + inv * (w - unit * inner)

        tiles(rows, 32, body)
        copy = pltpu.make_async_copy(ghf.at[d], gt_o.at[d], out_s.at[1 + d])
        copy.start()
        return copy

    ar_step(1, 0, 4, tot2)
    hidden_grad(0)
    heavy_back(0)
    ar_step(1, 1, 3, tot2)
    light_back(0)
    heavy_back_middle(0)
    ar_step(1, 1, 4, tot2)
    for k in range(1, 4):
        to = (b + k) % 4
        late.append(send(mixb.at[to], mixr.at[k - 1], mx_s.at[k - 1], mx_r.at[k - 1], (to, s)))
    hidden_grad(1)
    heavy_back(1)
    ar_sent(1, 0)
    attention_back_terms(0)
    light_back(1)
    heavy_back_middle(1)
    ar_step(2, 0, 1, tot2)
    ar_sent(1, 1)
    attention_back_terms(1)
    ar_step(2, 0, 2, tot2)
    ar_step(2, 1, 1, tot2)

    light_grad(nl, dqkv, g_a, 0)
    light_grad(ghb, lo, g_a, 3 * wl)
    at = 4 * wl
    for src, gr in (
        (hin, dqh[:, 0:wh]), (kin, dkvh[:, 0:wh]), (sin, dkvh[:, 256 : 256 + wh]), (gah, hox[:, 0:wh])
    ):
        g_a[:, at : at + wh] = tmm(src[...], gr).astype(BF)
        at += 256
    vector_lane = lax.broadcasted_iota(jnp.int32, (width, 128), 1)
    lane = lax.broadcasted_iota(jnp.int32, (docs * slots, 128), 1)
    vectors = jnp.zeros((width, 128), F32)
    for src, which, at_lane in ((hin, PREQ, 1), (kin, PREK, 2), (frow, PREF, 4)):
        vectors = vectors + tmm(src[...], jnp.where(lane == at_lane, cols[which], 0.0).astype(BF))
    for which, at_lane in ((0, 0), (1, 3)):
        vectors = jnp.where(vector_lane == at_lane, row_sum(gains[which].T), vectors)
    g_a[:, at : at + 128] = vectors.astype(BF)
    rs_start(2)
    ar_step(2, 0, 3, tot2)
    ar_step(2, 1, 2, tot2)
    rs_end(0)
    rs_middle(2)
    ar_step(2, 0, 4, tot2)
    out_copies = [tot_copy, token_grad(0)]
    ar_step(2, 1, 3, tot2)
    rs_end(1)

    for k in range(1, 4):
        frm = (b + 4 - k) % 4
        arrived(mixr.at[k - 1], mx_s.at[k - 1], mx_r.at[k - 1], (frm, s))
    for d in range(docs):

        def mix_body(t, d=d):
            r = pl.ds(t, 64)
            value = mixb[b, d, r, :].astype(F32)
            for k in range(3):
                value = value + mixr[k, d, r, :].astype(F32)
            dm[d, r, 0:share] = value

        tiles(rows, 64, mix_body)
    mix_copy = pltpu.make_async_copy(dm, mix_o, out_s.at[3])
    mix_copy.start()
    out_copies.append(mix_copy)
    ar_step(2, 1, 4, tot2)
    out_copies.append(token_grad(1))
    rs_end(2)
    va = packed.shape[1] - 128
    vbuf[...] = packed[:, va : va + 128]
    for k in range(1, 4):
        late.append(send(vbuf, vr.at[k - 1], v_s.at[k - 1], v_r.at[k - 1], ((b + k) % 4, s)))
    for k in range(1, 4):
        arrived(vr.at[k - 1], v_s.at[k - 1], v_r.at[k - 1], ((b + 4 - k) % 4, s))
    packed[:, va : va + 128] = vbuf[...] + vr[0] + vr[1] + vr[2]
    pack_copy = pltpu.make_async_copy(packed, pack_o, out_s.at[4])
    pack_copy.start()
    out_copies.append(pack_copy)

    for entry in late:
        if isinstance(entry, tuple):
            pl.when(entry[0])(entry[1].wait_send)
        else:
            entry.wait_send()
    for d in range(docs):
        ar_sent(0, d)
        ar_sent(2, d)
    for copy in out_copies:
        copy.wait()


def kernel_scratch(docs, rows, width, slots, n_seq, wl, wh, fl_n, fh_n):
    nz = n_seq // 2
    chunk = width // n_seq
    routed = docs * slots
    keys = n_seq * slots
    pad = -(-wh // 256) * 256
    ga_n = 4 * wl + 4 * pad + 128
    h_n, l_n = 3 * fh_n, 3 * fl_n
    radius = WINDOW // 2
    span = rows + 2 * radius
    vmem = [
        ((docs, rows, width), BF), ((docs, rows, width), BF), ((width, 3 * wl), BF), ((width, wl), BF),
        ((width, wh), BF), ((width, wh), BF), ((width, wh), BF), ((width, wh), BF),
        ((width, 2 * fl_n), BF), ((width, fl_n), BF), ((width, 2 * fh_n), BF), ((width, fh_n), BF),
        ((docs, rows, width), BF), ((docs, rows, 1), F32), ((routed, width), BF), ((routed, width), BF),
        ((routed, width), BF), ((docs, rows, wl), BF), ((docs, span, 2 * wl), BF),
        ((docs * rows // WINDOW, 2 * WINDOW, 2 * WINDOW), BF), ((docs, rows, wl), BF), ((routed, pad), BF),
        ((n_seq, routed, 2 * pad), BF), ((docs, wh // HD * slots, keys), BF), ((routed, pad), BF),
        ((docs, 2 * slots, rows), BF), ((docs, rows, 2 * slots), BF), ((docs, rows, width), BF),
        ((docs, rows, width), BF), ((docs, rows, width), BF), ((docs, 2, rows // 4, width), BF),
        ((docs, 2, rows // 8, width), BF), ((6, routed, 1), F32),
        ((docs, rows, fl_n), F32), ((routed, fh_n), F32), ((routed, width), BF), ((docs, rows, width), BF),
        ((docs, rows, 1), F32), ((docs, rows, fl_n), BF), ((docs, rows, 2 * fl_n), BF), ((routed, width), BF),
        ((routed, width), BF), ((routed, fh_n), BF), ((routed, 2 * fh_n), BF),
        ((4, docs, rows, width // 4), BF), ((3, docs, rows, width // 4), BF), ((docs, rows, width), F32),
        ((docs, rows, width), BF), ((docs, rows, wl), BF), ((routed, pad), BF), ((routed, width), BF),
        ((routed, pad), BF), ((docs, span, 2 * wl), F32), ((docs, 2, radius, 2 * wl), BF),
        ((docs, 2, radius, 2 * wl), BF), ((docs, rows, 3 * wl), BF),
        ((docs, 2, nz, slots, 2 * pad), BF), ((docs, nz, slots, 2 * pad), BF),
        ((docs, nz - 1, slots, 2 * pad), BF), ((routed, 2 * pad), BF), ((2, 8, width), F32),
        ((width, h_n), BF), ((width, l_n), BF),
        ((nz, chunk, h_n), BF), ((nz, chunk, l_n), BF), ((nz, chunk, ga_n), BF),
        ((nz - 1, chunk, h_n), BF), ((nz - 1, chunk, l_n), BF), ((nz - 1, chunk, ga_n), BF),
        ((chunk, h_n + l_n + ga_n), F32), ((chunk, 128), F32), ((3, chunk, 128), F32),
    ]
    sems = [
        (16,), (3, docs, 2, 4), (3, docs, 2, 4), (nz,), (nz,), (nz,), (nz,), (docs, 2), (docs, 2),
        (docs, 2), (docs, 2), (docs,), (docs,), (docs, nz - 1), (docs, nz - 1), (3,), (3,),
        (3, nz), (3, nz), (3, nz - 1), (3, nz - 1), (3,), (3,), (5,),
    ]
    total = 0
    for shape, kind in vmem:
        lanes = -(-shape[-1] // 128) * 128
        total += math.prod(shape[:-1]) * lanes * jnp.dtype(kind).itemsize
    return vmem, sems, total


def shards(sizes, *args):
    (tokens, cotangent, lengths, query_index, key_index, gain_attn, router_query, router_key, wq_light,
     wk_light, wv_light, wo_light, wq_heavy, wk_heavy, wv_heavy, wo_heavy, gain_ffn, router_ffn,
     gate_light, up_light, down_light, gate_heavy, up_heavy, down_heavy) = args
    n_seq = sizes["seq"]
    docs, rows, width = tokens.shape
    slots = query_index.shape[1]
    wl, wh = wq_light.shape[1], wq_heavy.shape[1]
    fl_n, fh_n = gate_light.shape[1], gate_heavy.shape[1]
    dims = (docs, rows, width, slots, n_seq, wl, wh, fl_n, fh_n)
    vmem, sems, total = kernel_scratch(*dims)
    fits = (
        total <= 60 * 2**20
        and sizes["branch"] == 4
        and n_seq % 2 == 0
        and width % (16 * n_seq) == 0
        and wl == 2 * HD
        and wh == 3 * HD
        and slots % 16 == 0
        and rows % 256 == 0
    )
    if not fits:
        return plain_shards(*args)
    share = width // 4
    chunk = width // n_seq
    ga_n = 4 * wl + 4 * 256 + 128
    pack_n = 3 * fh_n + 3 * fl_n + ga_n
    idx_rows = jnp.concatenate([query_index, key_index], axis=1)
    vec = jnp.stack(
        [gain_attn, router_query, router_key, gain_ffn, router_ffn, gain_ffn, gain_ffn, gain_ffn]
    ).astype(F32)
    in_hbm = [
        tokens, cotangent, wq_light, wk_light, wv_light, wo_light, wq_heavy, wk_heavy, wv_heavy, wo_heavy,
        gate_light, up_light, down_light, gate_heavy, up_heavy, down_heavy,
    ]
    whole = pl.BlockSpec(memory_space=pltpu.VMEM)
    outside = pl.BlockSpec(memory_space=pl.ANY)
    grad_tokens, mix, attn_total, packed = pl.pallas_call(
        functools.partial(layer_kernel, dims),
        out_shape=[
            jax.ShapeDtypeStruct((docs, rows, width), F32),
            jax.ShapeDtypeStruct((docs, rows, fl_n), F32),
            jax.ShapeDtypeStruct((docs, rows, width), BF),
            jax.ShapeDtypeStruct((chunk, pack_n), F32),
        ],
        in_specs=[pl.BlockSpec(memory_space=pltpu.SMEM), whole, whole, whole] + [outside] * 16,
        out_specs=[outside] * 4,
        scratch_shapes=[pltpu.VMEM(shape, kind) for shape, kind in vmem]
        + [pltpu.SemaphoreType.DMA(shape) for shape in sems],
        compiler_params=pltpu.CompilerParams(
            collective_id=0, has_side_effects=True, vmem_limit_bytes=64 * 2**20 - 2**16
        ),
    )(lengths, vec, idx_rows.T, idx_rows, *in_hbm)
    own = lax.axis_index("branch") * share
    mixed = mix[:, :, :share] + (
        lax.dynamic_slice_in_dim(tokens, own, share, 2).astype(F32)
        + lax.dynamic_slice_in_dim(attn_total, own, share, 2).astype(F32)
    )

    def part(at, wide):
        return packed[:, at : at + wide]

    l_at = 3 * fh_n
    a_at = l_at + 3 * fl_n
    h_at = a_at + 4 * wl
    v_at = h_at + 4 * 256
    return (
        mixed, grad_tokens,
        packed[:, v_at], packed[:, v_at + 1], packed[:, v_at + 2],
        part(a_at, wl), part(a_at + wl, wl), part(a_at + 2 * wl, wl), part(a_at + 3 * wl, wl),
        part(h_at, wh), part(h_at + 256, wh), part(h_at + 512, wh), part(h_at + 768, wh),
        packed[:, v_at + 3], packed[:, v_at + 4],
        part(l_at, fl_n), part(l_at + fl_n, fl_n), part(l_at + 2 * fl_n, fl_n),
        part(0, fh_n), part(fh_n, fh_n), part(2 * fh_n, fh_n),
    )


def solution(mesh):
    return jax.shard_map(
        functools.partial(shards, dict(mesh.shape)),
        mesh=mesh,
        in_specs=(
            P(None, "seq", None),
            P(None, "seq", None),
            P(),
            P(None, "seq"),
            P(None, "seq"),
            P(),
            P(),
            P(),
            P(None, "branch"),
            P(None, "branch"),
            P(None, "branch"),
            P(None, "branch"),
            P(None, "branch"),
            P(None, "branch"),
            P(None, "branch"),
            P(None, "branch"),
            P(),
            P(),
            P(None, "branch"),
            P(None, "branch"),
            P(None, "branch"),
            P(None, "branch"),
            P(None, "branch"),
            P(None, "branch"),
        ),
        out_specs=(
            P(None, "seq", "branch"),
            P(None, "seq", None),
            P("seq"),
            P("seq"),
            P("seq"),
            P("seq", "branch"),
            P("seq", "branch"),
            P("seq", "branch"),
            P("seq", "branch"),
            P("seq", "branch"),
            P("seq", "branch"),
            P("seq", "branch"),
            P("seq", "branch"),
            P("seq"),
            P("seq"),
            P("seq", "branch"),
            P("seq", "branch"),
            P("seq", "branch"),
            P("seq", "branch"),
            P("seq", "branch"),
            P("seq", "branch"),
        ),
        check_vma=False,
    )
```

```python
import functools
import math

import jax
import jax.numpy as jnp
from jax import lax
from jax.experimental import pallas as pl
from jax.experimental.pallas import tpu as pltpu
from jax.sharding import PartitionSpec as P

HD = 64
WINDOW = 128


highest = lax.Precision.HIGHEST
masked_value = -1000000000.0
epsilon = 1e-06


def with_halo(cells, sides, width):
    for axis, dim in sides:
        count = lax.axis_size(axis)
        ends = count - 1
        head = lax.slice_in_dim(cells, 0, width, axis=dim)
        tail = lax.slice_in_dim(cells, cells.shape[dim] - width, cells.shape[dim], axis=dim)
        cells = jnp.concatenate(
            [
                lax.ppermute(tail, axis, [(i, (i + 1) % count) for i in range(ends)]),
                cells,
                lax.ppermute(head, axis, [((i + 1) % count, i) for i in range(ends)]),
            ],
            axis=dim,
        )
    return cells


def project(operand, matrix):
    return jnp.einsum("dsc,ch->dsh", operand, matrix, preferred_element_type=jnp.float32)


def unproject(operand, matrix):
    return jnp.einsum("dsh,ch->dsc", operand, matrix, preferred_element_type=jnp.float32)


def weight_grad(operand, gradient):
    return jnp.einsum("dsc,dsh->ch", operand, gradient, preferred_element_type=jnp.float32)


def pick_rows(selector, values):
    return jnp.einsum("drs,dsc->drc", selector, values, precision=highest)


def put_rows(selector, values):
    return jnp.einsum("drs,drc->dsc", selector, values, precision=highest)


def pick_scalar(selector, values):
    return jnp.einsum("drs,ds->dr", selector, values, precision=highest)


def put_scalar(selector, values):
    return jnp.einsum("drs,dr->ds", selector, values, precision=highest)


def split_heads(values):
    return values.reshape(values.shape[0], values.shape[1], -1, HD)


def attention_scores(queries, keys, mask_bias):
    raw_scores = jnp.einsum("dqhe,dkhe->dhqk", queries, keys, preferred_element_type=jnp.float32)
    return raw_scores * HD ** (-0.5) + mask_bias


def forward_attention(queries, keys, values, mask_bias):
    scores = attention_scores(queries, keys, mask_bias)
    highest_score = jnp.max(scores, axis=-1, keepdims=True)
    exponent = jnp.exp(scores - highest_score)
    totals = jnp.sum(exponent, axis=-1, keepdims=True)
    probs_low = (exponent / totals).astype(jnp.bfloat16)
    result = jnp.einsum("dhqk,dkhe->dqhe", probs_low, values, preferred_element_type=jnp.float32)
    result = result.reshape(result.shape[0], result.shape[1], -1).astype(jnp.bfloat16)
    return (result, highest_score + jnp.log(totals))


def score_grads(queries, keys, values, mask_bias, logsum, grad_out, row_delta):
    probs = jnp.exp(attention_scores(queries, keys, mask_bias) - logsum)
    grad_probs = jnp.einsum("dqhe,dkhe->dhqk", grad_out, values, preferred_element_type=jnp.float32)
    row_delta = jnp.sum(grad_probs * probs, axis=-1, keepdims=True)
    grad_raw = (probs * (grad_probs - row_delta) * HD ** (-0.5)).astype(jnp.bfloat16)
    return (grad_raw, probs.astype(jnp.bfloat16), row_delta)


def contract_query(grad_raw, keys):
    result = jnp.einsum("dhqk,dkhe->dqhe", grad_raw, keys, preferred_element_type=jnp.float32)
    return result.reshape(result.shape[0], result.shape[1], -1)


def contract_key(grad_raw, queries):
    result = jnp.einsum("dhqk,dqhe->dkhe", grad_raw, queries, preferred_element_type=jnp.float32)
    return result.reshape(result.shape[0], result.shape[1], -1)


def geglu_back(gate_vals, up_vals, grad_mid):
    activated, gelu_pull = jax.vjp(jax.nn.gelu, gate_vals.astype(jnp.float32))
    grad_gate = gelu_pull(grad_mid * up_vals.astype(jnp.float32))[0].astype(jnp.bfloat16)
    grad_up = (grad_mid * activated).astype(jnp.bfloat16)
    return (grad_gate, grad_up)


def geglu(gate_vals, up_vals):
    return (jax.nn.gelu(gate_vals.astype(jnp.float32)) * up_vals.astype(jnp.float32)).astype(
        jnp.bfloat16
    )


def plain_shards(
    tokens,
    cotangent,
    lengths,
    query_index,
    key_index,
    gain_attn,
    router_query,
    router_key,
    wq_light,
    wk_light,
    wv_light,
    wo_light,
    wq_heavy,
    wk_heavy,
    wv_heavy,
    wo_heavy,
    gain_ffn,
    router_ffn,
    gate_light,
    up_light,
    down_light,
    gate_heavy,
    up_heavy,
    down_heavy,
):
    documents, local_len, model_width = tokens.shape
    radius = WINDOW // 2
    block_rows = math.gcd(local_len, 512)
    key_span = block_rows + 2 * radius
    offset = lax.axis_index("seq") * local_len
    positions = offset + jnp.arange(local_len, dtype=jnp.int32)
    valid_rows = (positions[None, :] < lengths[:, None]).astype(jnp.float32)[:, :, None]
    pick_query = (query_index[:, :, None] == positions[None, None, :]).astype(jnp.float32)
    pick_key = (key_index[:, :, None] == positions[None, None, :]).astype(jnp.float32)
    inputs = tokens.astype(jnp.float32)
    inv_attn = lax.rsqrt(jnp.mean(inputs * inputs, axis=-1, keepdims=True) + epsilon)
    unit_attn = inputs * inv_attn
    gain_attn_f = gain_attn.astype(jnp.float32)
    normed = unit_attn * gain_attn_f
    normed_low = normed.astype(jnp.bfloat16)
    light_q = project(normed_low, wq_light).astype(jnp.bfloat16)
    light_k = project(normed_low, wk_light).astype(jnp.bfloat16)
    light_v = project(normed_low, wv_light).astype(jnp.bfloat16)
    light_width = light_q.shape[2]
    rim_block = with_halo(jnp.concatenate([light_k, light_v], axis=2), (("seq", 1),), radius)
    wide_k = split_heads(rim_block[:, :, :light_width])
    wide_v = split_heads(rim_block[:, :, light_width:])
    heads_q = split_heads(light_q)
    key_pos = offset - radius + jnp.arange(local_len + 2 * radius, dtype=jnp.int32)
    in_window = (jnp.abs(positions[:, None] - key_pos[None, :]) <= radius)[None]
    in_window = (
        in_window
        & (key_pos[None, None, :] >= 0)
        & (key_pos[None, None, :] < lengths[:, None, None])
    )
    light_bias = jnp.where(in_window, 0.0, masked_value)[:, None]
    piece_out, piece_lse = forward_attention(heads_q, wide_k, wide_v, light_bias)
    router_query_f = router_query.astype(jnp.float32)
    router_key_f = router_key.astype(jnp.float32)
    score_query = pick_scalar(
        pick_query,
        jax.nn.sigmoid(jnp.einsum("dsc,c->ds", normed, router_query_f, precision=highest)),
    )
    score_key = pick_scalar(
        pick_key, jax.nn.sigmoid(jnp.einsum("dsc,c->ds", normed, router_key_f, precision=highest))
    )
    heavy_in = pick_rows(pick_query, normed).astype(jnp.bfloat16)
    key_rows = pick_rows(pick_key, normed)
    key_in = key_rows.astype(jnp.bfloat16)
    scaled_in = (key_rows * score_key[:, :, None]).astype(jnp.bfloat16)
    heavy_q = project(heavy_in, wq_heavy).astype(jnp.bfloat16)
    heavy_k = project(key_in, wk_heavy).astype(jnp.bfloat16)
    heavy_v = project(scaled_in, wv_heavy).astype(jnp.bfloat16)
    heavy_width = heavy_q.shape[2]
    key_alive = (key_index >= 0).astype(jnp.bfloat16)
    routed_kv, alive_all = (
        lax.all_gather(jnp.concatenate([heavy_k, heavy_v], axis=2), "seq", axis=1, tiled=True),
        lax.all_gather(key_alive, "seq", axis=1, tiled=True),
    )
    all_k = routed_kv[:, :, :heavy_width]
    all_v = routed_kv[:, :, heavy_width:]
    heavy_bias = jnp.where(alive_all > 0, 0.0, masked_value)[:, None, None, :]
    heavy_out, heavy_lse = forward_attention(
        split_heads(heavy_q), split_heads(all_k), split_heads(all_v), heavy_bias
    )
    heavy_proj = unproject(heavy_out, wo_heavy)
    light_attn = unproject(piece_out, wo_light) * valid_rows
    heavy_attn = put_rows(pick_query, heavy_proj * score_query[:, :, None])
    attn_total = lax.psum((light_attn + heavy_attn).astype(jnp.bfloat16), "branch").astype(
        jnp.float32
    )
    hidden = inputs + attn_total
    inv_ffn = lax.rsqrt(jnp.mean(hidden * hidden, axis=-1, keepdims=True) + epsilon)
    unit_ffn = hidden * inv_ffn
    gain_ffn_f = gain_ffn.astype(jnp.float32)
    normed_ffn = unit_ffn * gain_ffn_f
    ffn_low = normed_ffn.astype(jnp.bfloat16)
    gate_l = project(ffn_low, gate_light).astype(jnp.bfloat16)
    up_l = project(ffn_low, up_light).astype(jnp.bfloat16)
    middle_l = geglu(gate_l, up_l)
    light_ffn = unproject(middle_l, down_light) * valid_rows
    router_ffn_f = router_ffn.astype(jnp.float32)
    score_ffn = pick_scalar(
        pick_query,
        jax.nn.sigmoid(jnp.einsum("dsc,c->ds", normed_ffn, router_ffn_f, precision=highest)),
    )
    ffn_rows = pick_rows(pick_query, normed_ffn).astype(jnp.bfloat16)
    gate_h = project(ffn_rows, gate_heavy).astype(jnp.bfloat16)
    up_h = project(ffn_rows, up_heavy).astype(jnp.bfloat16)
    middle_h = geglu(gate_h, up_h)
    heavy_fproj = unproject(middle_h, down_heavy)
    heavy_ffn = put_rows(pick_query, heavy_fproj * score_ffn[:, :, None])
    share = model_width // lax.axis_size("branch")
    own_cols = lax.axis_index("branch") * share
    mixed = lax.dynamic_slice_in_dim(hidden, own_cols, share, 2) + lax.psum_scatter(
        (light_ffn + heavy_ffn).astype(jnp.bfloat16), "branch", scatter_dimension=2, tiled=True
    ).astype(jnp.float32)
    grad_out = cotangent.astype(jnp.float32)
    grad_light = (grad_out * valid_rows).astype(jnp.bfloat16)
    grad_down_light = weight_grad(grad_light, middle_l)
    grad_gate_l, grad_up_l = geglu_back(gate_l, up_l, project(grad_light, down_light))
    grad_gate_light = weight_grad(ffn_low, grad_gate_l)
    grad_up_light = weight_grad(ffn_low, grad_up_l)
    grad_rows = pick_rows(pick_query, grad_out)
    grad_heavy = (grad_rows * score_ffn[:, :, None]).astype(jnp.bfloat16)
    score_ffn_part = jnp.sum(grad_rows * heavy_fproj, axis=-1)
    grad_down_heavy = weight_grad(grad_heavy, middle_h)
    grad_gate_h, grad_up_h = geglu_back(gate_h, up_h, project(grad_heavy, down_heavy))
    grad_gate_heavy = weight_grad(ffn_rows, grad_gate_h)
    grad_up_heavy = weight_grad(ffn_rows, grad_up_h)
    heavy_ffn_rows = unproject(grad_gate_h, gate_heavy) + unproject(grad_up_h, up_heavy)
    ffn_part = (
        unproject(grad_gate_l, gate_light)
        + unproject(grad_up_l, up_light)
        + put_rows(pick_query, heavy_ffn_rows)
    )
    grad_normed_ffn, grad_score_ffn = (
        lax.psum(ffn_part.astype(jnp.bfloat16), "branch").astype(jnp.float32),
        lax.psum(score_ffn_part.astype(jnp.bfloat16), "branch").astype(jnp.float32),
    )
    pre_ffn = put_scalar(pick_query, grad_score_ffn * score_ffn * (1.0 - score_ffn))
    grad_normed_ffn = grad_normed_ffn + pre_ffn[:, :, None] * router_ffn_f
    grad_router_ffn = jnp.einsum("ds,dsc->c", pre_ffn, normed_ffn, precision=highest)
    grad_gain_ffn = jnp.sum(grad_normed_ffn * unit_ffn, axis=(0, 1))
    grad_unit_f = grad_normed_ffn * gain_ffn_f
    grad_hidden = grad_out + inv_ffn * (
        grad_unit_f - unit_ffn * jnp.mean(grad_unit_f * unit_ffn, axis=-1, keepdims=True)
    )
    grad_light_attn = (grad_hidden * valid_rows).astype(jnp.bfloat16)
    grad_wo_light = weight_grad(grad_light_attn, piece_out)
    grad_light_out = split_heads(project(grad_light_attn, wo_light).astype(jnp.bfloat16))
    wide_grad = jnp.zeros((documents, local_len + 2 * radius, 2 * light_width), jnp.float32)
    light_raw, light_plow, unused_delta = score_grads(
        heads_q, wide_k, wide_v, light_bias, piece_lse, grad_light_out, None
    )
    query_pieces = contract_query(light_raw, wide_k)
    key_terms = jnp.concatenate(
        [contract_key(light_raw, heads_q), contract_key(light_plow, grad_light_out)], axis=2
    )
    wide_grad = wide_grad.at[:, 0:key_span].add(key_terms)
    grad_light_q = query_pieces.astype(jnp.bfloat16)
    outer_rims = jnp.concatenate(
        [wide_grad[:, :radius], wide_grad[:, radius + local_len :]], axis=1
    )
    returned = with_halo(outer_rims.astype(jnp.bfloat16), (("seq", 1),), radius).astype(
        outer_rims.dtype
    )
    inner = wide_grad[:, radius : radius + local_len]
    inner = inner + jnp.pad(returned[:, :radius], ((0, 0), (0, local_len - radius), (0, 0)))
    inner = inner + jnp.pad(returned[:, 3 * radius :], ((0, 0), (local_len - radius, 0), (0, 0)))
    grad_light_k = inner[:, :, :light_width].astype(jnp.bfloat16)
    grad_light_v = inner[:, :, light_width:].astype(jnp.bfloat16)
    grad_wq_light = weight_grad(normed_low, grad_light_q)
    grad_wk_light = weight_grad(normed_low, grad_light_k)
    grad_wv_light = weight_grad(normed_low, grad_light_v)
    light_part = (
        unproject(grad_light_q, wq_light)
        + unproject(grad_light_k, wk_light)
        + unproject(grad_light_v, wv_light)
    )
    grad_hrows = pick_rows(pick_query, grad_hidden)
    grad_heavy_attn = (grad_hrows * score_query[:, :, None]).astype(jnp.bfloat16)
    score_query_part = jnp.sum(grad_hrows * heavy_proj, axis=-1)
    grad_wo_heavy = weight_grad(grad_heavy_attn, heavy_out)
    grad_heavy_out = project(grad_heavy_attn, wo_heavy).astype(jnp.bfloat16)
    heavy_raw, heavy_plow, heavy_delta = score_grads(
        split_heads(heavy_q),
        split_heads(all_k),
        split_heads(all_v),
        heavy_bias,
        heavy_lse,
        split_heads(grad_heavy_out),
        None,
    )
    grad_heavy_q = contract_query(heavy_raw, split_heads(all_k)).astype(jnp.bfloat16)
    every_kv = jnp.concatenate(
        [
            contract_key(heavy_raw, split_heads(heavy_q)),
            contract_key(heavy_plow, split_heads(grad_heavy_out)),
        ],
        axis=2,
    )
    own_kv = lax.psum_scatter(every_kv, "seq", scatter_dimension=1, tiled=True)
    grad_heavy_k = own_kv[:, :, :heavy_width].astype(jnp.bfloat16)
    grad_heavy_v = own_kv[:, :, heavy_width:].astype(jnp.bfloat16)
    grad_scaled = unproject(grad_heavy_v, wv_heavy)
    score_key_part = jnp.sum(grad_scaled * key_rows, axis=-1)
    grad_key_rows = unproject(grad_heavy_k, wk_heavy) + grad_scaled * score_key[:, :, None]
    grad_wq_heavy = weight_grad(heavy_in, grad_heavy_q)
    grad_wk_heavy = weight_grad(key_in, grad_heavy_k)
    grad_wv_heavy = weight_grad(scaled_in, grad_heavy_v)
    attn_part = (
        light_part
        + put_rows(pick_query, unproject(grad_heavy_q, wq_heavy))
        + put_rows(pick_key, grad_key_rows)
    )
    grad_normed, grad_score_query, grad_score_key = (
        lax.psum(attn_part.astype(jnp.bfloat16), "branch").astype(jnp.float32),
        lax.psum(score_query_part.astype(jnp.bfloat16), "branch").astype(jnp.float32),
        lax.psum(score_key_part.astype(jnp.bfloat16), "branch").astype(jnp.float32),
    )
    pre_query = put_scalar(pick_query, grad_score_query * score_query * (1.0 - score_query))
    pre_key = put_scalar(pick_key, grad_score_key * score_key * (1.0 - score_key))
    grad_normed = (
        grad_normed + pre_query[:, :, None] * router_query_f + pre_key[:, :, None] * router_key_f
    )
    grad_router_query = jnp.einsum("ds,dsc->c", pre_query, normed, precision=highest)
    grad_router_key = jnp.einsum("ds,dsc->c", pre_key, normed, precision=highest)
    grad_gain_attn = jnp.sum(grad_normed * unit_attn, axis=(0, 1))
    grad_unit_a = grad_normed * gain_attn_f
    grad_tokens = grad_hidden + inv_attn * (
        grad_unit_a - unit_attn * jnp.mean(grad_unit_a * unit_attn, axis=-1, keepdims=True)
    )
    names = (
        grad_wq_light, grad_wk_light, grad_wv_light, grad_wo_light,
        grad_wq_heavy, grad_wk_heavy, grad_wv_heavy, grad_wo_heavy,
        grad_gate_light, grad_up_light, grad_down_light,
        grad_gate_heavy, grad_up_heavy, grad_down_heavy,
    )
    vectors = jnp.stack(
        [grad_gain_attn, grad_router_query, grad_router_key, grad_gain_ffn, grad_router_ffn], axis=1
    )
    packed = jnp.concatenate([g.astype(jnp.bfloat16) for g in names + (vectors,)], axis=1)
    summed = lax.psum_scatter(packed, "seq", scatter_dimension=0, tiled=True).astype(jnp.float32)
    widths = [g.shape[1] for g in names]
    cuts = [sum(widths[:i]) for i in range(len(widths) + 1)]
    (
        grad_wq_light, grad_wk_light, grad_wv_light, grad_wo_light,
        grad_wq_heavy, grad_wk_heavy, grad_wv_heavy, grad_wo_heavy,
        grad_gate_light, grad_up_light, grad_down_light,
        grad_gate_heavy, grad_up_heavy, grad_down_heavy,
    ) = [summed[:, cuts[i] : cuts[i + 1]] for i in range(len(widths))]
    grad_gain_attn, grad_router_query, grad_router_key, grad_gain_ffn, grad_router_ffn = [
        summed[:, cuts[-1] + i] for i in range(5)
    ]
    return (
        mixed,
        grad_tokens,
        grad_gain_attn,
        grad_router_query,
        grad_router_key,
        grad_wq_light,
        grad_wk_light,
        grad_wv_light,
        grad_wo_light,
        grad_wq_heavy,
        grad_wk_heavy,
        grad_wv_heavy,
        grad_wo_heavy,
        grad_gain_ffn,
        grad_router_ffn,
        grad_gate_light,
        grad_up_light,
        grad_down_light,
        grad_gate_heavy,
        grad_up_heavy,
        grad_down_heavy,
    )


BF = jnp.bfloat16
F32 = jnp.float32
MESH = pl.DeviceIdType.MESH


def mm(a, b):
    return jnp.dot(a, b, preferred_element_type=F32)


def mmt(a, b):
    return lax.dot_general(a, b, (((1,), (1,)), ((), ())), preferred_element_type=F32)


def tmm(a, b):
    return lax.dot_general(a, b, (((0,), (0,)), ((), ())), preferred_element_type=F32)


def row_sum(values):
    return jnp.sum(values, axis=-1, keepdims=True)


def gelu_parts(v):
    c = math.sqrt(2.0 / math.pi)
    square = v * v
    t = jnp.tanh(c * v * (1.0 + 0.044715 * square))
    act = 0.5 * v * (1.0 + t)
    slope = 0.5 * (1.0 + t) + (0.5 * c) * v * (1.0 - t * t) * (1.0 + 0.134145 * square)
    return act, slope


def layer_kernel(dims, *refs):
    docs, rows, width, slots, n_seq, wl, wh, fl_n, fh_n = dims
    nz = n_seq // 2
    chunk = width // n_seq
    half = rows // 2
    quarter = rows // 4
    eighth = rows // 8
    radius = WINDOW // 2
    share = width // 4
    it = iter(refs)

    def take(count):
        return [next(it) for _ in range(count)]

    lens, qi, ki, ga_v, rq_v, rk_v, gf_v, rf_v = take(8)
    (tok_h, cot_h, wql_h, wkl_h, wvl_h, wol_h, wqh_h, wkh_h, wvh_h, woh_h,
     gl_h, ul_h, dl_h, gh_h, uh_h, dh_h) = take(16)
    gt_o, mix_o, pack_o, vec_o = take(4)
    (tok, cot, wqkv, wol, whq, whk, whv, who, wgul, wdl, wguh, wdh, wkeep) = take(13)
    (nl, inva, hin, kin, sin, qbuf, kvw, pbuf, lo, hqx, kvall, ph, hox, qall, doall) = take(15)
    (pqk, pqkt, parts, tot1, tot2, r1, r2, cols) = take(8)
    (dm, dmh, grow, fl, invf, mid, dgu, frow, ghr, midh, dguh) = take(11)
    (mixb, mixr, mixa, ghf, ghb, dol, dox, gah, dqh, dkvw, rims, rimr, dqkv, dkvh) = take(14)
    (g_h, g_l, ra_h, ra_l, ra_a, rb_h, rb_l, rb_a, rl_h, rl_l, rl_a, packed, vbuf, vr, vect) = take(15)
    g_a = wguh
    (load_s, ar_s, ar_r, ag_s, ag_r, fw_s, fw_r, halo_s, halo_r, rim_s, rim_r,
     mx_s, mx_r, wa_s, wa_r, wz_s, wz_r, rl_s, rl_r, v_s, v_r, out_s) = take(22)

    b = lax.axis_index("branch")
    s = lax.axis_index("seq")
    bit_x = b % 2
    bit_y = b // 2
    core = s % 2
    z = s // 2
    offset = s * rows
    dev_x = (b + 1 - 2 * bit_x, s)
    dev_y = (b + 2 - 4 * bit_y, s)
    sibling = (b, s + 1 - 2 * core)

    def zpeer(k):
        return (z + k) % nz

    def same_core(k):
        return (b, 2 * zpeer(k) + core)

    late = []

    def send(src, dst, ssem, rsem, dev, when=None):
        copy = pltpu.make_async_remote_copy(
            src_ref=src, dst_ref=dst, send_sem=ssem, recv_sem=rsem, device_id=dev, device_id_type=MESH
        )
        if when is None:
            copy.start()
        else:
            pl.when(when)(copy.start)
        return copy

    def arrived(dst, ssem, rsem, dev):
        pltpu.make_async_remote_copy(
            src_ref=dst, dst_ref=dst, send_sem=ssem, recv_sem=rsem, device_id=dev, device_id_type=MESH
        ).wait_recv()

    loads = {}

    def load(name, src, dst, i):
        copy = pltpu.make_async_copy(src, dst, load_s.at[i])
        copy.start()
        loads[name] = copy

    load("tok", tok_h, tok, 0)
    load("whq", wqh_h, whq, 1)
    load("whk", wkh_h, whk, 2)
    load("whv", wvh_h, whv, 3)
    load("wq", wql_h, wqkv.at[:, 0:wl], 4)
    load("wk", wkl_h, wqkv.at[:, wl : 2 * wl], 5)
    load("wv", wvl_h, wqkv.at[:, 2 * wl : 3 * wl], 6)
    load("wol", wol_h, wol, 7)
    load("who", woh_h, who, 8)
    load("cot", cot_h, cot, 9)
    load("wdl", dl_h, wdl, 10)
    load("wdh", dh_h, wdh, 11)
    load("gl", gl_h, wgul.at[:, 0:fl_n], 12)
    load("ul", ul_h, wgul.at[:, fl_n : 2 * fl_n], 13)
    load("gh", gh_h, wguh.at[:, 0:fh_n], 14)
    load("uh", uh_h, wguh.at[:, fh_n : 2 * fh_n], 15)
    own_rows = pl.ds(pl.multiple_of(chunk * s, chunk), chunk)
    load("gk", gh_h.at[own_rows], wkeep.at[:, 0:fh_n], 16)
    load("uk", uh_h.at[own_rows], wkeep.at[:, fh_n : 2 * fh_n], 17)

    barrier = pltpu.get_barrier_semaphore()
    for k in range(1, 4):
        pl.semaphore_signal(barrier, inc=1, device_id=((b + k) % 4, s), device_id_type=MESH)

    def greet(k, carry):
        pl.semaphore_signal(barrier, inc=1, device_id=(b, (s + k) % n_seq), device_id_type=MESH)
        return carry

    lax.fori_loop(1, n_seq, greet, 0)
    pl.semaphore_wait(barrier, 3 + n_seq - 1)

    gain_a, router_q, router_k, gain_f, router_f = [
        ref[...].astype(F32).reshape(1, width) for ref in (ga_v, rq_v, rk_v, gf_v, rf_v)
    ]

    def as_column(row):
        count = row.shape[1]
        square = lax.broadcasted_iota(jnp.int32, (count, count), 0)
        same = square == lax.broadcasted_iota(jnp.int32, (count, count), 1)
        return row_sum(jnp.where(same, row.astype(F32), 0.0)).astype(jnp.int32)

    idx_row = [[ref[d : d + 1, :] for ref in (qi, ki)] for d in range(docs)]
    idx_col = [[as_column(row) for row in idx_row[d]] for d in range(docs)]

    def valid_rows(d, first, count):
        at = lax.broadcasted_iota(jnp.int32, (count, 1), 0) + (offset + first)
        return jnp.where(at < lens[d], 1.0, 0.0).astype(F32)

    big = 64

    def tiles(count, size, body):
        def step(t, carry):
            body(pl.multiple_of(t * size, size))
            return carry

        lax.fori_loop(0, count // size, step, 0)

    def geometry(h):
        first, second = ((dev_x, bit_x), (dev_y, bit_y))[:: 1 if h == 0 else -1]
        base = half * h
        keep1 = base + quarter * first[1]
        send1 = base + quarter * (1 - first[1])
        keep2 = keep1 + eighth * second[1]
        send2 = keep1 + eighth * (1 - second[1])
        return (first[0], second[0]) + tuple(pl.multiple_of(v, eighth) for v in (keep1, send1, keep2, send2))

    flights = {}

    def ar_start(a, d, h):
        first, second, keep1, send1, keep2, send2 = geometry(h)
        flights[a, d, h, 0] = send(
            parts.at[d, pl.ds(send1, quarter)], r1.at[d, h], ar_s.at[a, d, h, 0], ar_r.at[a, d, h, 0], first
        )

    def add_rows(d, at, buf, base, total):
        def body(t, carry):
            r = pl.multiple_of(t * 32, 32)
            here = pl.ds(pl.multiple_of(at + r, 32), 32)
            value = parts[d, here, :].astype(F32) + buf[pl.ds(base + r, 32), :].astype(F32)
            total[d, here, :] = value.astype(BF)
            return carry

        lax.fori_loop(0, eighth // 32, body, 0)

    def ar_step(a, d, step, total):
        for h in range(2):
            first, second, keep1, send1, keep2, send2 = geometry(h)
            at = (a, d, h)
            if step == 1:
                arrived(r1.at[d, h], ar_s.at[a, d, h, 0], ar_r.at[a, d, h, 0], first)
                add_rows(d, send2, r1.at[d, h], pl.multiple_of(send2 - keep1, eighth), parts)
                flights[at + (1,)] = send(
                    parts.at[d, pl.ds(send2, eighth)], r2.at[d, h], ar_s.at[a, d, h, 1], ar_r.at[a, d, h, 1], second
                )
                add_rows(d, keep2, r1.at[d, h], pl.multiple_of(keep2 - keep1, eighth), parts)
            elif step == 2:
                arrived(r2.at[d, h], ar_s.at[a, d, h, 1], ar_r.at[a, d, h, 1], second)
                add_rows(d, keep2, r2.at[d, h], 0, total)
                own = total.at[d, pl.ds(keep2, eighth)]
                flights[at + (2,)] = send(own, own, ar_s.at[a, d, h, 2], ar_r.at[a, d, h, 2], second)
            elif step == 3:
                arrived(total.at[d, pl.ds(send2, eighth)], ar_s.at[a, d, h, 2], ar_r.at[a, d, h, 2], second)
                own = total.at[d, pl.ds(keep1, quarter)]
                flights[at + (3,)] = send(own, own, ar_s.at[a, d, h, 3], ar_r.at[a, d, h, 3], first)
            else:
                arrived(total.at[d, pl.ds(send1, quarter)], ar_s.at[a, d, h, 3], ar_r.at[a, d, h, 3], first)
                flights[at + (0,)].wait_send()
                flights[at + (1,)].wait_send()

    def ar_sent(a, d):
        for h in range(2):
            flights[a, d, h, 2].wait_send()
            flights[a, d, h, 3].wait_send()

    loads["tok"].wait()
    for d in range(docs):

        def norm_body(t, d=d):
            r = pl.ds(t, big)
            x = tok[d, r, :].astype(F32)
            inv = lax.rsqrt(row_sum(x * x) * (1.0 / width) + epsilon)
            inva[d, r, :] = inv
            nl[d, r, :] = (x * inv * gain_a).astype(BF)

        tiles(rows, big, norm_body)

    for d in range(docs):
        lane_pos = lax.broadcasted_iota(jnp.int32, (slots, rows), 1) + offset
        sub_pos = lax.broadcasted_iota(jnp.int32, (rows, slots), 0) + offset
        for i in range(2):
            here = slice(i * slots, (i + 1) * slots)
            pqk[d, here, :] = jnp.where(idx_col[d][i] == lane_pos, 1.0, 0.0).astype(BF)
            pqkt[d, :, here] = jnp.where(idx_row[d][i] == sub_pos, 1.0, 0.0).astype(BF)

    def alive(d, i):
        return jnp.where(idx_col[d][i] >= 0, 1.0, 0.0).astype(F32)

    SQ, SK, SF, PREQ, PREF, PREK = range(6)

    def mine(d):
        return slice(d * slots, (d + 1) * slots)

    for d in range(docs):
        picked = mm(pqk[d], nl[d])
        score_q = jax.nn.sigmoid(row_sum(picked[:slots] * router_q)) * alive(d, 0)
        score_k = jax.nn.sigmoid(row_sum(picked[slots:] * router_k)) * alive(d, 1)
        cols[SQ, mine(d), :] = score_q
        cols[SK, mine(d), :] = score_k
        hin[mine(d), :] = picked[:slots].astype(BF)
        kin[mine(d), :] = picked[slots:].astype(BF)
        sin[mine(d), :] = (picked[slots:] * score_k).astype(BF)
        pad_lane = lax.broadcasted_iota(jnp.int32, (slots, 256 - wh), 1)
        kvall[s, mine(d), wh:256] = jnp.where(
            pad_lane == 0, (1.0 - alive(d, 1)) * masked_value, 0.0
        ).astype(BF)
        kvall[s, mine(d), 256 + wh : 512] = jnp.zeros((slots, 256 - wh), BF)
    loads["whk"].wait()
    kvall[s, :, 0:wh] = mmt(kin[...], whk[...]).astype(BF)
    loads["whv"].wait()
    kvall[s, :, 256 : 256 + wh] = mmt(sin[...], whv[...]).astype(BF)

    def gather_start(g, ref, part):
        block = ref.at[s, part]
        late.append(send(block, block, ag_s.at[g, 0], ag_r.at[g, 0], sibling))
        for k in range(1, nz):
            late.append(send(block, block, ag_s.at[g, k], ag_r.at[g, k], same_core(k)))

    def gather_pass(g, ref, part):
        for k in range(1, nz):
            block = ref.at[2 * zpeer(nz - k) + core, part]
            arrived(block, ag_s.at[g, k], ag_r.at[g, k], same_core(nz - k))
            late.append(send(block, block, fw_s.at[g, k], fw_r.at[g, k], sibling))

    def gather_end(g, ref, part):
        arrived(ref.at[s + 1 - 2 * core, part], ag_s.at[g, 0], ag_r.at[g, 0], sibling)
        for k in range(1, nz):
            block = ref.at[2 * zpeer(nz - k) + 1 - core, part]
            arrived(block, fw_s.at[g, k], fw_r.at[g, k], sibling)

    def routed(d):
        return pl.ds(d * slots, slots)

    every = pl.ds(0, docs * slots)
    gather_start(0, kvall, every)

    loads["whq"].wait()
    hqx[:, 0:wh] = mmt(hin[...], whq[...]).astype(BF)
    pad_lane = lax.broadcasted_iota(jnp.int32, (docs * slots, 256 - wh), 1)
    hqx[:, wh:256] = jnp.where(pad_lane == 0, 8.0, 0.0).astype(BF)

    for name in ("wq", "wk", "wv"):
        loads[name].wait()
    last = n_seq - 1
    left = (b, (s + last) % n_seq)
    right = (b, (s + 1) % n_seq)
    for d in range(docs):

        def qkv_body(t, d=d):
            r = mm(nl[d, pl.ds(t, half), :], wqkv[...]).astype(BF)
            qbuf[d, pl.ds(t, half), :] = r[:, 0:wl]
            kvw[d, pl.ds(pl.multiple_of(t + radius, 32), half), :] = r[:, wl : 3 * wl]

        tiles(rows, half, qkv_body)

        @pl.when(s == 0)
        def _(d=d):
            kvw[d, 0:radius, :] = jnp.zeros((radius, 2 * wl), BF)

        @pl.when(s == last)
        def _(d=d):
            kvw[d, rows + radius : rows + 2 * radius, :] = jnp.zeros((radius, 2 * wl), BF)

        late.append((s > 0, send(
            kvw.at[d, pl.ds(radius, radius)], kvw.at[d, pl.ds(rows + radius, radius)],
            halo_s.at[d, 0], halo_r.at[d, 0], left, s > 0,
        )))
        late.append((s < last, send(
            kvw.at[d, pl.ds(rows, radius)], kvw.at[d, pl.ds(0, radius)],
            halo_s.at[d, 1], halo_r.at[d, 1], right, s < last,
        )))

    def halo_wait(d):
        @pl.when(s < last)
        def _():
            arrived(kvw.at[d, pl.ds(rows + radius, radius)], halo_s.at[d, 0], halo_r.at[d, 0], right)

        @pl.when(s > 0)
        def _():
            arrived(kvw.at[d, pl.ds(0, radius)], halo_s.at[d, 1], halo_r.at[d, 1], left)

    blk = WINDOW
    span = 2 * WINDOW
    n_blk = rows // blk

    def two_heads(v):
        lane = lax.broadcasted_iota(jnp.int32, v.shape, 1)
        zero = jnp.zeros_like(v)
        return jnp.concatenate([jnp.where(lane < HD, v, zero), jnp.where(lane < HD, zero, v)], axis=0)

    def one_of_two(v):
        lane = lax.broadcasted_iota(jnp.int32, (blk, 2 * HD), 1)
        return jnp.where(lane < HD, v[:blk], v[blk:])

    def light_attention(d):
        def body(i, carry):
            at = pl.multiple_of(i * blk, blk)
            q2 = two_heads(qbuf[d, pl.ds(at, blk), :])
            k = kvw[d, pl.ds(at, span), 0:wl]
            v = kvw[d, pl.ds(at, span), wl : 2 * wl]
            row = lax.broadcasted_iota(jnp.int32, (2 * blk, span), 0) % blk
            col = lax.broadcasted_iota(jnp.int32, (2 * blk, span), 1)
            pos = col + (offset + at - radius)
            seen = (col >= row) & (col <= row + WINDOW) & (pos >= 0) & (pos < lens[d])
            scores = jnp.where(seen, mmt(q2, k) * HD ** (-0.5), masked_value)
            e = jnp.exp(scores - jnp.max(scores, axis=-1, keepdims=True))
            p = (e * (1.0 / row_sum(e))).astype(BF)
            pbuf[d * n_blk + i] = p
            out = one_of_two(mm(p, v))
            lo[d, pl.ds(at, blk), :] = (out * valid_rows(d, at, blk)).astype(BF)
            return carry

        lax.fori_loop(0, n_blk, body, 0)

    def three_heads(v):
        lane = lax.broadcasted_iota(jnp.int32, v.shape, 1)
        zero = jnp.zeros_like(v)
        return jnp.concatenate(
            [jnp.where((lane // HD == h) | (lane >= wh), v, zero) for h in range(wh // HD)], axis=0
        )

    def one_of_three(v):
        lane = lax.broadcasted_iota(jnp.int32, (slots, 256), 1)
        total = jnp.zeros((slots, 256), F32)
        for h in range(wh // HD):
            total = jnp.where(lane // HD == h, v[h * slots : (h + 1) * slots], total)
        return total

    def keys_of(d, at):
        return kvall[:, mine(d), at : at + 256].reshape(n_seq * slots, 256)

    def spread(column):
        lane = lax.broadcasted_iota(jnp.int32, (slots, 256 - wh), 1)
        out = jnp.zeros((slots, 256 - wh), F32)
        for h in range(wh // HD):
            value = column[h * slots : (h + 1) * slots]
            high = value.astype(BF).astype(F32)
            low = value - high
            out = jnp.where(lane == 2 * h, high, jnp.where(lane == 2 * h + 1, low, out))
        return out.astype(BF)

    def own_keys(d, at):
        v = kvall[s, mine(d), at : at + 256]
        lane = lax.broadcasted_iota(jnp.int32, v.shape, 1)
        zero = jnp.zeros_like(v)
        one = jnp.ones_like(v)
        return jnp.concatenate(
            [
                jnp.where(
                    lane // HD == h, v, jnp.where((lane == wh + 2 * h) | (lane == wh + 2 * h + 1), one, zero)
                )
                for h in range(wh // HD)
            ],
            axis=0,
        )

    def heavy_attention(d):
        q3 = three_heads(hqx[mine(d), :])
        scores = mmt(q3, keys_of(d, 0)) * HD ** (-0.5)
        top = jnp.max(scores, axis=-1, keepdims=True)
        e = jnp.exp(scores - top)
        sums = row_sum(e)
        p = (e * (1.0 / sums)).astype(BF)
        ph[d] = p
        qall[s, mine(d), 0:wh] = hqx[mine(d), 0:wh]
        qall[s, mine(d), wh:256] = spread((top + jnp.log(sums)) * -(HD**0.5))
        hox[mine(d), :] = one_of_three(mm(p, keys_of(d, 256))).astype(BF)

    halo_wait(0)
    light_attention(0)
    gather_pass(0, kvall, every)
    halo_wait(1)
    light_attention(1)
    gather_end(0, kvall, every)

    loads["who"].wait()
    loads["wol"].wait()

    def attention_terms(d):
        heavy_attention(d)
        proj = (mm(hox[mine(d), 0:wh], who[...]) * cols[SQ, mine(d), :]).astype(BF)
        for h in range(2):
            r = pl.ds(h * half, half)
            value = mmt(lo[d, r, :], wol[...]) + mm(pqkt[d, r, 0:slots], proj)
            parts[d, r, :] = value.astype(BF)
            ar_start(0, d, h)

    attention_terms(0)
    attention_terms(1)
    gather_start(1, qall, every)
    ar_step(0, 0, 1, tot1)

    for name in ("cot", "wdl", "wdh"):
        loads[name].wait()

    def light_pre(d):
        def body(t):
            r = pl.ds(t, half)
            dm[d, r, :] = mm(cot[d, r, :], wdl[...]) * valid_rows(d, t, half)

        tiles(rows, half, body)
        grow[mine(d), :] = mm(pqk[d, 0:slots, :], cot[d]).astype(BF)

    light_pre(0)
    ar_step(0, 0, 2, tot1)
    ar_step(0, 1, 1, tot1)
    light_pre(1)
    dmh[...] = mm(grow[...], wdh[...])
    ar_step(0, 0, 3, tot1)
    ar_step(0, 1, 2, tot1)
    for name in ("gl", "ul", "gh", "uh"):
        loads[name].wait()

    def hidden_rows(d, r):
        return tok[d, r, :].astype(F32) + tot1[d, r, :].astype(F32)

    def ffn_norm(d):
        def body(t):
            r = pl.ds(t, big)
            hidden = hidden_rows(d, r)
            inv = lax.rsqrt(row_sum(hidden * hidden) * (1.0 / width) + epsilon)
            invf[d, r, :] = inv
            fl[d, r, :] = (hidden * inv * gain_f).astype(BF)

        tiles(rows, big, body)

    def ffn_heavy(d):
        rowsf = mm(pqk[d, 0:slots, :], fl[d])
        score = jax.nn.sigmoid(row_sum(rowsf * router_f)) * alive(d, 0)
        cols[SF, mine(d), :] = score
        frow[mine(d), :] = rowsf.astype(BF)
        ghr[mine(d), :] = (grow[mine(d), :].astype(F32) * score).astype(BF)
        step = 256

        def body(t, dscore):
            c = pl.ds(pl.multiple_of(t * step, step), step)
            c2 = pl.ds(pl.multiple_of(fh_n + t * step, step), step)
            gate = mm(frow[mine(d), :], wguh[:, c]).astype(BF).astype(F32)
            up = mm(frow[mine(d), :], wguh[:, c2]).astype(BF).astype(F32)
            act, slope = gelu_parts(gate)
            middle = (act * up).astype(BF)
            raw = dmh[mine(d), c]
            grad_mid = raw * score
            midh[mine(d), c] = middle
            dguh[mine(d), c] = (grad_mid * up * slope).astype(BF)
            dguh[mine(d), c2] = (grad_mid * act).astype(BF)
            return dscore + row_sum(middle.astype(F32) * raw)

        dscore = lax.fori_loop(0, fh_n // step, body, jnp.zeros((slots, 1), F32))
        pre = dscore * score * (1.0 - score)
        cols[PREF, mine(d), :] = pre
        return (mmt(dguh[mine(d), :], wguh[...]) + pre * router_f).astype(BF)

    def ffn_light(d, back_rows):
        for h in range(2):
            r = pl.ds(h * half, half)
            gu = mm(fl[d, r, :], wgul[...]).astype(BF)
            gate = gu[:, 0:fl_n].astype(F32)
            up = gu[:, fl_n : 2 * fl_n].astype(F32)
            act, slope = gelu_parts(gate)
            mid[d, r, :] = (act * up * valid_rows(d, h * half, half)).astype(BF)
            grad_mid = dm[d, r, :]
            dgu[d, r, 0:fl_n] = (grad_mid * up * slope).astype(BF)
            dgu[d, r, fl_n : 2 * fl_n] = (grad_mid * act).astype(BF)
            value = mmt(dgu[d, r, :], wgul[...]) + mm(pqkt[d, r, 0:slots], back_rows)
            parts[d, r, :] = value.astype(BF)
            ar_start(1, d, h)

    grads = ((g_h, ra_h, rb_h, rl_h), (g_l, ra_l, rb_l, rl_l), (g_a, ra_a, rb_a, rl_a))
    packed_at = (0, g_h.shape[1], g_h.shape[1] + g_l.shape[1])
    at_end = (z == 0) | (z == nz - 1)
    inner = (z > 0) & (z < nz - 1)
    low_side = jnp.where(z < nz // 2, 1, 0)

    def chunk_rows(zz, cc):
        return pl.ds(pl.multiple_of(chunk * (2 * zz + cc), chunk), chunk)

    def rs_start(p):
        grad, ra, rb, rl = grads[p]
        for zz in range(nz):
            late.append(send(
                grad.at[chunk_rows(zz, 1 - core), pl.ds(0, ra.shape[2])], ra.at[zz],
                wa_s.at[p, zz], wa_r.at[p, zz], sibling,
            ))

    def add_chunk(grad, zz, other):
        cut = other.shape[1]

        def add_body(t, carry):
            r = pl.ds(pl.multiple_of(chunk * (2 * zz + core) + 16 * t, 16), 16)
            value = grad[r, 0:cut].astype(F32) + other[pl.ds(pl.multiple_of(16 * t, 16), 16), :].astype(F32)
            grad[r, 0:cut] = value.astype(BF)
            return carry

        lax.fori_loop(0, chunk // 16, add_body, 0)

    def rs_direct(p, k, when):
        grad, ra, rb, rl = grads[p]
        late.append((when, send(
            grad.at[chunk_rows(zpeer(k), core), pl.ds(0, ra.shape[2])], rb.at[k - 1],
            wz_s.at[p, k - 1], wz_r.at[p, k - 1], same_core(k), when,
        )))

    def rs_middle(p):
        grad, ra, rb, rl = grads[p]
        for i in range(1, nz + 1):
            k = low_side * (nz - i) + (1 - low_side) * i if i < nz else nz
            zz = zpeer(k)
            arrived(ra.at[zz], wa_s.at[p, zz], wa_r.at[p, zz], sibling)
            add_chunk(grad, zz, ra.at[zz])
            if i == 1:
                neighbour = (b, 2 * (z + 2 * low_side - 1) + core)
                late.append((at_end, send(
                    grad.at[chunk_rows(zz, core), pl.ds(0, ra.shape[2])], rl, rl_s.at[p], rl_r.at[p],
                    neighbour, at_end,
                )))
                rs_direct(p, k, inner)
            elif i == 2:
                rs_direct(p, k, at_end)
            elif i == 3:
                rs_direct(p, k, z >= 0)

    def rs_relay(p):
        grad, ra, rb, rl = grads[p]

        @pl.when(inner)
        def _():
            arrived(rl, rl_s.at[p], rl_r.at[p], same_core(1))
            add_chunk(grad, zpeer(2), rl)

        rs_direct(p, 2, inner)

    def rs_end(p):
        grad, ra, rb, rl = grads[p]
        cut = ra.shape[2]
        for k, when in ((1, z > 0), (2, z >= 0), (3, z < nz - 1)):

            @pl.when(when)
            def _(k=k):
                arrived(rb.at[k - 1], wz_s.at[p, k - 1], wz_r.at[p, k - 1], same_core(nz - k))

        def add_body(t, carry):
            r = pl.ds(pl.multiple_of(16 * t, 16), 16)
            value = grad[pl.ds(pl.multiple_of(chunk * s + 16 * t, 16), 16), 0:cut].astype(F32)
            for k in range(1, nz):
                value = value + rb[k - 1, r, :].astype(F32)
            packed[r, packed_at[p] : packed_at[p] + cut] = value
            return carry

        lax.fori_loop(0, chunk // 16, add_body, 0)

    @pl.when(z == 0)
    def _():
        for grad, ra, rb, rl in grads:
            rb[0] = jnp.zeros(rb.shape[1:], BF)

    @pl.when(z == nz - 1)
    def _():
        for grad, ra, rb, rl in grads:
            rb[2] = jnp.zeros(rb.shape[1:], BF)

    def heavy_ffn_grads():
        step = 512
        for src, gr, base, total in ((frow, dguh, 0, 2 * fh_n), (ghr, midh, 2 * fh_n, fh_n)):
            for t in range(2):
                f = slice(t * (width // 2), (t + 1) * (width // 2))
                left_t = src[:, f].T

                def body(i, carry, gr=gr, f=f, base=base, left_t=left_t):
                    c = pl.ds(pl.multiple_of(i * step, step), step)
                    o = pl.ds(pl.multiple_of(base + i * step, step), step)
                    g_h[f, o] = mm(left_t, gr[:, c]).astype(BF)
                    return carry

                lax.fori_loop(0, total // step, body, 0)

    def all_rows(ref, f):
        return ref[:, :, f].reshape(docs * rows, ref[:, :, f].shape[2])

    def light_grad(src, gr, ref, base):
        for t in range(2):
            f = slice(t * (width // 2), (t + 1) * (width // 2))
            right_side = gr[...].reshape(docs * rows, gr.shape[2])
            ref[f, base : base + gr.shape[2]] = tmm(all_rows(src, f), right_side).astype(BF)

    def mixed_terms(d):
        def body(j, carry):
            w = pl.ds(pl.multiple_of(j * share, share), share)
            heavy = (mmt(midh[mine(d), :], wdh[w, :]) * cols[SF, mine(d), :]).astype(BF)
            value = mmt(wdl[w, :], mid[d]) + tmm(heavy, pqk[d, 0:slots, :])
            mixb[j, d] = value.astype(BF)
            return carry

        lax.fori_loop(0, 4, body, 0)

    def mixed_start(d):
        column = lax.broadcasted_iota(jnp.int32, (share, width), 1) - b * share
        own = jnp.where(column == lax.broadcasted_iota(jnp.int32, (share, width), 0), 1.0, 0.0).astype(BF)
        mixa[d] = mmt(own, tok[d]) + mmt(own, tot1[d]) + mixb[b, d].astype(F32)

    def hidden_grad(d):
        def body(t):
            r = pl.ds(t, big)
            unit = hidden_rows(d, r) * invf[d, r, :]
            w = tot2[d, r, :].astype(F32) * gain_f
            inner = row_sum(w * unit) * (1.0 / width)
            value = cot[d, r, :].astype(F32) + invf[d, r, :] * (w - unit * inner)
            ghf[d, r, :] = value
            ghb[d, r, :] = value.astype(BF)

        tiles(rows, big, body)

    def heavy_back(d):
        picked = mm(pqk[d, 0:slots, :], ghb[d])
        score = cols[SQ, mine(d), :]
        gah[mine(d), :] = (picked * score).astype(BF)
        raw = mmt(picked.astype(BF), who[...])
        pre = row_sum(hox[mine(d), 0:wh].astype(F32) * raw) * score * (1.0 - score)
        cols[PREQ, mine(d), :] = pre
        dox[mine(d), 0:wh] = (raw * score).astype(BF)
        dox[mine(d), wh:256] = jnp.zeros((slots, 256 - wh), BF)
        do3 = three_heads(dox[mine(d), :])
        pf = ph[d].astype(F32)
        dp = mmt(do3, keys_of(d, 256))
        delta = row_sum(dp * pf)
        doall[s, mine(d), 0:wh] = dox[mine(d), 0:wh]
        doall[s, mine(d), wh:256] = spread(-delta)
        gather_start(2 + d, doall, routed(d))
        ds = (pf * (dp - delta) * HD ** (-0.5)).astype(BF)
        dqh[mine(d), :] = one_of_three(mm(ds, keys_of(d, 0))).astype(BF)

    def heavy_back_keys(d):
        q = qall[:, mine(d), :].reshape(n_seq * slots, 256)
        do = doall[:, mine(d), :].reshape(n_seq * slots, 256)
        live = jnp.concatenate([alive(d, 1)] * (wh // HD), axis=0) > 0
        p = jnp.exp(jnp.where(live, mmt(own_keys(d, 0), q) * HD ** (-0.5), masked_value))
        ds = (p * mmt(own_keys(d, 256), do) * HD ** (-0.5)).astype(BF)
        dkvh[mine(d), 0:256] = one_of_three(mm(ds, q)).astype(BF)
        dkvh[mine(d), 256:512] = one_of_three(mm(p.astype(BF), do)).astype(BF)

    def light_back(d):
        dkvw[d] = jnp.zeros((rows + 2 * radius, 2 * wl), F32)

        def dol_body(t):
            r = pl.ds(t, half)
            dol[d, r, :] = (mm(ghb[d, r, :], wol[...]) * valid_rows(d, t, half)).astype(BF)

        tiles(rows, half, dol_body)

        def body(i, carry):
            at = pl.multiple_of(i * blk, blk)
            q2 = two_heads(qbuf[d, pl.ds(at, blk), :])
            do2 = two_heads(dol[d, pl.ds(at, blk), :])
            k = kvw[d, pl.ds(at, span), 0:wl]
            v = kvw[d, pl.ds(at, span), wl : 2 * wl]
            p = pbuf[d * n_blk + i]
            pf = p.astype(F32)
            dp = mmt(do2, v)
            ds = (pf * (dp - row_sum(dp * pf)) * HD ** (-0.5)).astype(BF)
            dqkv[d, pl.ds(at, blk), 0:wl] = one_of_two(mm(ds, k)).astype(BF)
            dkvw[d, pl.ds(at, span), 0:wl] += tmm(ds, q2)
            dkvw[d, pl.ds(at, span), wl : 2 * wl] += tmm(p, do2)
            return carry

        lax.fori_loop(0, n_blk, body, 0)
        rims[d, 0] = dkvw[d, 0:radius, :].astype(BF)
        rims[d, 1] = dkvw[d, rows + radius : rows + 2 * radius, :].astype(BF)

        @pl.when(s == 0)
        def _():
            rimr[d, 0] = jnp.zeros((radius, 2 * wl), BF)

        @pl.when(s == last)
        def _():
            rimr[d, 1] = jnp.zeros((radius, 2 * wl), BF)

        late.append((s > 0, send(rims.at[d, 0], rimr.at[d, 1], rim_s.at[d, 0], rim_r.at[d, 0], left, s > 0)))
        late.append((s < last, send(rims.at[d, 1], rimr.at[d, 0], rim_s.at[d, 1], rim_r.at[d, 1], right, s < last)))

    def rim_wait(d):
        @pl.when(s < last)
        def _():
            arrived(rimr.at[d, 1], rim_s.at[d, 0], rim_r.at[d, 0], right)

        @pl.when(s > 0)
        def _():
            arrived(rimr.at[d, 0], rim_s.at[d, 1], rim_r.at[d, 1], left)

    def attention_back_terms(d):
        heavy_back_keys(d)
        ds_in = mm(dkvh[mine(d), 256 : 256 + wh], whv[...])
        score = cols[SK, mine(d), :]
        pre_k = row_sum(ds_in * kin[mine(d), :].astype(F32)) * score * (1.0 - score)
        cols[PREK, mine(d), :] = pre_k
        key_rows = mm(dkvh[mine(d), 0:wh], whk[...]) + ds_in * score + pre_k * router_k
        query_rows = mm(dqh[mine(d), 0:wh], whq[...]) + cols[PREQ, mine(d), :] * router_q
        both = jnp.concatenate([query_rows, key_rows], axis=0).astype(BF)
        rim_wait(d)
        dkvw[d, radius : 2 * radius, :] += rimr[d, 0].astype(F32)
        dkvw[d, rows : rows + radius, :] += rimr[d, 1].astype(F32)
        for h in range(2):
            r = pl.ds(h * half, half)
            dqkv[d, r, wl : 3 * wl] = dkvw[d, pl.ds(h * half + radius, half), :].astype(BF)
            value = mmt(dqkv[d, r, :], wqkv[...]) + mm(pqkt[d, r, :], both)
            parts[d, r, :] = value.astype(BF)
            ar_start(2, d, h)

    def token_grad(d):
        def body(t):
            r = pl.ds(t, big)
            inv = inva[d, r, :]
            unit = tok[d, r, :].astype(F32) * inv
            w = tot2[d, r, :].astype(F32) * gain_a
            inner = row_sum(w * unit) * (1.0 / width)
            ghf[d, r, :] = ghf[d, r, :] + inv * (w - unit * inner)

        tiles(rows, big, body)
        copy = pltpu.make_async_copy(ghf.at[d], gt_o.at[d], out_s.at[1 + d])
        copy.start()
        return copy

    gather_pass(1, qall, every)
    ar_step(0, 0, 4, tot1)
    ffn_norm(0)
    back0 = ffn_heavy(0)
    ar_step(0, 1, 3, tot1)
    ffn_light(0, back0)
    ar_step(0, 1, 4, tot1)
    ffn_norm(1)
    back1 = ffn_heavy(1)
    ar_step(1, 0, 1, tot2)
    heavy_ffn_grads()
    rs_start(0)
    ffn_light(1, back1)
    ar_step(1, 0, 2, tot2)
    rs_middle(0)
    light_grad(fl, dgu, g_l, 0)
    ar_step(1, 1, 1, tot2)
    ar_step(1, 0, 3, tot2)
    light_grad(cot, mid, g_l, 2 * fl_n)
    rs_start(1)
    ar_step(1, 1, 2, tot2)
    mixed_terms(0)
    ar_step(1, 0, 4, tot2)
    hidden_grad(0)
    heavy_back(0)
    ar_step(1, 1, 3, tot2)
    rs_middle(1)
    light_back(0)
    mixed_terms(1)
    ar_step(1, 1, 4, tot2)
    for k in range(1, 4):
        to = (b + k) % 4
        late.append(send(mixb.at[to], mixr.at[k - 1], mx_s.at[k - 1], mx_r.at[k - 1], (to, s)))
    hidden_grad(1)
    gather_end(1, qall, every)
    gather_pass(2, doall, routed(0))
    heavy_back(1)
    ar_sent(1, 0)
    gather_end(2, doall, routed(0))
    attention_back_terms(0)
    rs_relay(0)
    light_back(1)
    gather_pass(3, doall, routed(1))
    ar_step(2, 0, 1, tot2)
    ar_sent(1, 1)
    gather_end(3, doall, routed(1))
    attention_back_terms(1)
    ar_step(2, 0, 2, tot2)
    ar_step(2, 1, 1, tot2)
    rs_relay(1)

    light_grad(nl, dqkv, g_a, 0)
    light_grad(ghb, lo, g_a, 3 * wl)
    at = 4 * wl
    for src, gr in (
        (hin, dqh[:, 0:wh]), (kin, dkvh[:, 0:wh]), (sin, dkvh[:, 256 : 256 + wh]), (gah, hox[:, 0:wh])
    ):
        g_a[:, at : at + wh] = tmm(src[...], gr).astype(BF)
        at += 256
    lane = lax.broadcasted_iota(jnp.int32, (docs * slots, 128), 1)
    vectors = jnp.zeros((width, 128), F32)
    for src, which, at_lane in ((hin, PREQ, 1), (kin, PREK, 2), (frow, PREF, 4)):
        vectors = vectors + tmm(src[...], jnp.where(lane == at_lane, cols[which], 0.0).astype(BF))
    g_a[:, at : at + 128] = vectors.astype(BF)
    rs_start(2)
    mixed_start(0)
    mixed_start(1)
    ar_step(2, 0, 3, tot2)
    ar_step(2, 1, 2, tot2)
    rs_middle(2)
    rs_end(0)
    ar_step(2, 0, 4, tot2)
    out_copies = [token_grad(0)]
    ar_step(2, 1, 3, tot2)
    rs_end(1)
    rs_relay(2)

    for name in ("gk", "uk"):
        loads[name].wait()
    vlane = lax.broadcasted_iota(jnp.int32, (chunk, 128), 1)
    eye = lax.broadcasted_iota(jnp.int32, (chunk, width), 1) - chunk * s
    eye = eye == lax.broadcasted_iota(jnp.int32, (chunk, width), 0)

    def own_column(row):
        return row_sum(jnp.where(eye, row, 0.0))

    gf_sum = row_sum(packed[:, 0 : 2 * fh_n] * wkeep[...].astype(F32))
    gf_sum = gf_sum + row_sum(
        packed[:, packed_at[1] : packed_at[1] + 2 * fl_n] * wgul[own_rows, :].astype(F32)
    )
    for k in range(1, 4):
        frm = (b + 4 - k) % 4
        arrived(mixr.at[k - 1], mx_s.at[k - 1], mx_r.at[k - 1], (frm, s))
    for d in range(docs):

        def mix_body(t, d=d):
            r = pl.ds(t, 32)
            value = mixa[d, r, :]
            for k in range(3):
                value = value + mixr[k, d, r, :].astype(F32)
            mixa[d, r, :] = value

        tiles(share, 32, mix_body)
    mix_copy = pltpu.make_async_copy(mixa, mix_o, out_s.at[3])
    mix_copy.start()
    out_copies.append(mix_copy)
    ar_step(2, 1, 4, tot2)
    out_copies.append(token_grad(1))
    rs_end(2)
    a_at = packed_at[2]
    va = packed.shape[1] - 128
    ga_sum = row_sum(packed[:, a_at : a_at + 3 * wl] * wqkv[own_rows, :].astype(F32))
    eye_b = eye.astype(F32).astype(BF)
    for i, w in enumerate((whq, whk, whv)):
        h_at = a_at + 4 * wl + 256 * i
        ga_sum = ga_sum + row_sum(packed[:, h_at : h_at + wh] * mmt(eye_b, w[...]))
    vectors = packed[:, va : va + 128]

    def lane_of(i):
        return row_sum(jnp.where(vlane == i, vectors, 0.0))

    ga_sum = ga_sum + own_column(router_q) * lane_of(1) + own_column(router_k) * lane_of(2)
    gf_sum = gf_sum + own_column(router_f) * lane_of(4)
    vectors = jnp.where(vlane == 0, ga_sum / own_column(gain_a), vectors)
    vectors = jnp.where(vlane == 3, gf_sum / own_column(gain_f), vectors)
    vbuf[...] = vectors
    pack_copy = pltpu.make_async_copy(packed, pack_o, out_s.at[4])
    pack_copy.start()
    out_copies.append(pack_copy)
    for k in range(1, 4):
        late.append(send(vbuf, vr.at[k - 1], v_s.at[k - 1], v_r.at[k - 1], ((b + k) % 4, s)))
    for k in range(1, 4):
        arrived(vr.at[k - 1], v_s.at[k - 1], v_r.at[k - 1], ((b + 4 - k) % 4, s))
    vect[...] = (vbuf[...] + vr[0] + vr[1] + vr[2]).T
    vec_copy = pltpu.make_async_copy(vect, vec_o, out_s.at[0])
    vec_copy.start()
    out_copies.append(vec_copy)

    for entry in late:
        if isinstance(entry, tuple):
            pl.when(entry[0])(entry[1].wait_send)
        else:
            entry.wait_send()
    for d in range(docs):
        ar_sent(0, d)
        ar_sent(2, d)
    for copy in out_copies:
        copy.wait()


def kernel_scratch(docs, rows, width, slots, n_seq, wl, wh, fl_n, fh_n):
    nz = n_seq // 2
    chunk = width // n_seq
    routed = docs * slots
    keys = n_seq * slots
    pad = -(-wh // 256) * 256
    ga_n = 4 * wl + 4 * pad + 128
    h_n, l_n = 3 * fh_n, 3 * fl_n
    radius = WINDOW // 2
    span = rows + 2 * radius
    vmem = [
        ((docs, rows, width), BF), ((docs, rows, width), BF), ((width, 3 * wl), BF), ((width, wl), BF),
        ((wh, width), BF), ((wh, width), BF), ((wh, width), BF), ((wh, width), BF),
        ((width, 2 * fl_n), BF), ((width, fl_n), BF), ((width, 2 * fh_n), BF), ((width, fh_n), BF),
        ((chunk, 2 * fh_n), BF),
        ((docs, rows, width), BF), ((docs, rows, 1), F32), ((routed, width), BF), ((routed, width), BF),
        ((routed, width), BF), ((docs, rows, wl), BF), ((docs, span, 2 * wl), BF),
        ((docs * rows // WINDOW, 2 * WINDOW, 2 * WINDOW), BF), ((docs, rows, wl), BF), ((routed, pad), BF),
        ((n_seq, routed, 2 * pad), BF), ((docs, wh // HD * slots, keys), BF), ((routed, pad), BF),
        ((n_seq, routed, pad), BF), ((n_seq, routed, pad), BF),
        ((docs, 2 * slots, rows), BF), ((docs, rows, 2 * slots), BF), ((docs, rows, width), BF),
        ((docs, rows, width), BF), ((docs, rows, width), BF), ((docs, 2, rows // 4, width), BF),
        ((docs, 2, rows // 8, width), BF), ((6, routed, 1), F32),
        ((docs, rows, fl_n), F32), ((routed, fh_n), F32), ((routed, width), BF), ((docs, rows, width), BF),
        ((docs, rows, 1), F32), ((docs, rows, fl_n), BF), ((docs, rows, 2 * fl_n), BF), ((routed, width), BF),
        ((routed, width), BF), ((routed, fh_n), BF), ((routed, 2 * fh_n), BF),
        ((4, docs, width // 4, rows), BF), ((3, docs, width // 4, rows), BF), ((docs, width // 4, rows), F32),
        ((docs, rows, width), F32), ((docs, rows, width), BF), ((docs, rows, wl), BF), ((routed, pad), BF),
        ((routed, width), BF), ((routed, pad), BF), ((docs, span, 2 * wl), F32),
        ((docs, 2, radius, 2 * wl), BF), ((docs, 2, radius, 2 * wl), BF), ((docs, rows, 3 * wl), BF),
        ((routed, 2 * pad), BF),
        ((width, h_n), BF), ((width, l_n), BF),
        ((nz, chunk, h_n), BF), ((nz, chunk, l_n), BF), ((nz, chunk, ga_n), BF),
        ((nz - 1, chunk, h_n), BF), ((nz - 1, chunk, l_n), BF), ((nz - 1, chunk, ga_n), BF),
        ((chunk, h_n), BF), ((chunk, l_n), BF), ((chunk, ga_n), BF),
        ((chunk, h_n + l_n + ga_n), F32), ((chunk, 128), F32), ((3, chunk, 128), F32), ((128, chunk), F32),
    ]
    sems = [
        (18,), (3, docs, 2, 4), (3, docs, 2, 4), (2 + docs, nz), (2 + docs, nz), (2 + docs, nz), (2 + docs, nz),
        (docs, 2), (docs, 2), (docs, 2), (docs, 2), (3,), (3,),
        (3, nz), (3, nz), (3, nz - 1), (3, nz - 1), (3,), (3,), (3,), (3,), (5,),
    ]
    total = 0
    for shape, kind in vmem:
        lanes = -(-shape[-1] // 128) * 128
        total += math.prod(shape[:-1]) * lanes * jnp.dtype(kind).itemsize
    return vmem, sems, total


def shards(sizes, *args):
    (tokens, cotangent, lengths, query_index, key_index, gain_attn, router_query, router_key, wq_light,
     wk_light, wv_light, wo_light, wq_heavy, wk_heavy, wv_heavy, wo_heavy, gain_ffn, router_ffn,
     gate_light, up_light, down_light, gate_heavy, up_heavy, down_heavy) = args
    n_seq = sizes["seq"]
    docs, rows, width = tokens.shape
    slots = query_index.shape[1]
    wl, wh = wq_light.shape[1], wq_heavy.shape[1]
    fl_n, fh_n = gate_light.shape[1], gate_heavy.shape[1]
    dims = (docs, rows, width, slots, n_seq, wl, wh, fl_n, fh_n)
    vmem, sems, total = kernel_scratch(*dims)
    fits = (
        total <= 60 * 2**20
        and sizes["branch"] == 4
        and n_seq == 8
        and width % (16 * n_seq) == 0
        and wl == 2 * HD
        and wh == 3 * HD
        and slots % 16 == 0
        and rows % 256 == 0
    )
    if not fits:
        return plain_shards(*args)
    share = width // 4
    chunk = width // n_seq
    ga_n = 4 * wl + 4 * 256 + 128
    pack_n = 3 * fh_n + 3 * fl_n + ga_n
    in_hbm = [
        tokens, cotangent, wq_light, wk_light, wv_light, wo_light, wq_heavy.T, wk_heavy.T, wv_heavy.T, wo_heavy.T,
        gate_light, up_light, down_light, gate_heavy, up_heavy, down_heavy,
    ]
    whole = pl.BlockSpec(memory_space=pltpu.VMEM)
    outside = pl.BlockSpec(memory_space=pl.ANY)
    grad_tokens, mix, packed, vectors = pl.pallas_call(
        functools.partial(layer_kernel, dims),
        out_shape=[
            jax.ShapeDtypeStruct((docs, rows, width), F32),
            jax.ShapeDtypeStruct((docs, share, rows), F32),
            jax.ShapeDtypeStruct((chunk, pack_n), F32),
            jax.ShapeDtypeStruct((128, chunk), F32),
        ],
        in_specs=[pl.BlockSpec(memory_space=pltpu.SMEM)] + [whole] * 7 + [outside] * 16,
        out_specs=[outside] * 4,
        scratch_shapes=[pltpu.VMEM(shape, kind) for shape, kind in vmem]
        + [pltpu.SemaphoreType.DMA(shape) for shape in sems],
        compiler_params=pltpu.CompilerParams(
            collective_id=0, has_side_effects=True, vmem_limit_bytes=64 * 2**20 - 2**16
        ),
    )(lengths, query_index, key_index, gain_attn, router_query, router_key, gain_ffn, router_ffn, *in_hbm)

    l_at = 3 * fh_n
    a_at = l_at + 3 * fl_n
    h_at = a_at + 4 * wl
    parts = [(a_at + i * wl, wl) for i in range(4)] + [(h_at + i * 256, wh) for i in range(4)]
    parts += [(l_at + i * fl_n, fl_n) for i in range(3)] + [(i * fh_n, fh_n) for i in range(3)]
    outs = pl.pallas_call(
        functools.partial(hand_out, parts),
        out_shape=[jax.ShapeDtypeStruct(grad_tokens.shape, F32), jax.ShapeDtypeStruct(mix.shape, F32)]
        + [jax.ShapeDtypeStruct((chunk, wide), F32) for at, wide in parts],
        in_specs=[pl.BlockSpec(memory_space=pltpu.HBM)] * 3,
        out_specs=[outside] * 2 + [outside if wide % 128 == 0 else whole for at, wide in parts],
        scratch_shapes=[
            pltpu.SemaphoreType.DMA((3 + docs,)), pltpu.SemaphoreType.DMA((1 + docs + len(parts),)),
            pltpu.VMEM(grad_tokens.shape, F32), pltpu.VMEM(mix.shape, F32), pltpu.VMEM(packed.shape, F32),
        ],
        compiler_params=pltpu.CompilerParams(vmem_limit_bytes=60 * 2**20),
    )(grad_tokens, mix, packed)
    grad_tokens, mix = outs[:2]
    mixed = jnp.swapaxes(mix, 1, 2)
    vec = [vectors[i] for i in range(5)]
    return (mixed, grad_tokens, *vec[:3], *outs[2:10], *vec[3:], *outs[10:])


def hand_out(parts, tokens_in, mix_in, packed_in, tokens_out, mix_out, *rest):
    in_sems, out_sems, tokens, mix, packed = rest[-5:]
    docs = tokens.shape[0]
    arriving = [pltpu.make_async_copy(packed_in, packed, in_sems.at[0])]
    arriving += [pltpu.make_async_copy(tokens_in.at[d], tokens.at[d], in_sems.at[1 + d]) for d in range(docs)]
    arriving += [pltpu.make_async_copy(mix_in, mix, in_sems.at[1 + docs])]
    for copy in arriving:
        copy.start()
    leaving = [pltpu.make_async_copy(mix, mix_out, out_sems.at[0])]
    leaving += [pltpu.make_async_copy(tokens.at[d], tokens_out.at[d], out_sems.at[1 + d]) for d in range(docs)]
    arriving[0].wait()
    for i, (at, wide) in enumerate(parts):
        if wide % 128 == 0:
            copy = pltpu.make_async_copy(packed.at[:, at : at + wide], rest[i], out_sems.at[1 + docs + i])
            copy.start()
            leaving.append(copy)
    for d in range(docs):
        arriving[1 + d].wait()
        leaving[1 + d].start()
    arriving[1 + docs].wait()
    leaving[0].start()
    for i, (at, wide) in enumerate(parts):
        if wide % 128 != 0:
            rest[i][...] = packed[:, at : at + wide]
    for copy in leaving:
        copy.wait()


def solution(mesh):
    return jax.shard_map(
        functools.partial(shards, dict(mesh.shape)),
        mesh=mesh,
        in_specs=(
            P(None, "seq", None),
            P(None, "seq", None),
            P(),
            P(None, "seq"),
            P(None, "seq"),
            P(),
            P(),
            P(),
            P(None, "branch"),
            P(None, "branch"),
            P(None, "branch"),
            P(None, "branch"),
            P(None, "branch"),
            P(None, "branch"),
            P(None, "branch"),
            P(None, "branch"),
            P(),
            P(),
            P(None, "branch"),
            P(None, "branch"),
            P(None, "branch"),
            P(None, "branch"),
            P(None, "branch"),
            P(None, "branch"),
        ),
        out_specs=(
            P(None, "seq", "branch"),
            P(None, "seq", None),
            P("seq"),
            P("seq"),
            P("seq"),
            P("seq", "branch"),
            P("seq", "branch"),
            P("seq", "branch"),
            P("seq", "branch"),
            P("seq", "branch"),
            P("seq", "branch"),
            P("seq", "branch"),
            P("seq", "branch"),
            P("seq"),
            P("seq"),
            P("seq", "branch"),
            P("seq", "branch"),
            P("seq", "branch"),
            P("seq", "branch"),
            P("seq", "branch"),
            P("seq", "branch"),
        ),
        check_vma=False,
    )
```

```python
import functools
import math

import jax
import jax.numpy as jnp
from jax import lax
from jax.experimental import pallas as pl
from jax.experimental.pallas import tpu as pltpu
from jax.sharding import PartitionSpec as P

HD = 64
WINDOW = 128


highest = lax.Precision.HIGHEST
masked_value = -1000000000.0
epsilon = 1e-06


def with_halo(cells, sides, width):
    for axis, dim in sides:
        count = lax.axis_size(axis)
        ends = count - 1
        head = lax.slice_in_dim(cells, 0, width, axis=dim)
        tail = lax.slice_in_dim(cells, cells.shape[dim] - width, cells.shape[dim], axis=dim)
        cells = jnp.concatenate(
            [
                lax.ppermute(tail, axis, [(i, (i + 1) % count) for i in range(ends)]),
                cells,
                lax.ppermute(head, axis, [((i + 1) % count, i) for i in range(ends)]),
            ],
            axis=dim,
        )
    return cells


def project(operand, matrix):
    return jnp.einsum("dsc,ch->dsh", operand, matrix, preferred_element_type=jnp.float32)


def unproject(operand, matrix):
    return jnp.einsum("dsh,ch->dsc", operand, matrix, preferred_element_type=jnp.float32)


def weight_grad(operand, gradient):
    return jnp.einsum("dsc,dsh->ch", operand, gradient, preferred_element_type=jnp.float32)


def pick_rows(selector, values):
    return jnp.einsum("drs,dsc->drc", selector, values, precision=highest)


def put_rows(selector, values):
    return jnp.einsum("drs,drc->dsc", selector, values, precision=highest)


def pick_scalar(selector, values):
    return jnp.einsum("drs,ds->dr", selector, values, precision=highest)


def put_scalar(selector, values):
    return jnp.einsum("drs,dr->ds", selector, values, precision=highest)


def split_heads(values):
    return values.reshape(values.shape[0], values.shape[1], -1, HD)


def attention_scores(queries, keys, mask_bias):
    raw_scores = jnp.einsum("dqhe,dkhe->dhqk", queries, keys, preferred_element_type=jnp.float32)
    return raw_scores * HD ** (-0.5) + mask_bias


def forward_attention(queries, keys, values, mask_bias):
    scores = attention_scores(queries, keys, mask_bias)
    highest_score = jnp.max(scores, axis=-1, keepdims=True)
    exponent = jnp.exp(scores - highest_score)
    totals = jnp.sum(exponent, axis=-1, keepdims=True)
    probs_low = (exponent / totals).astype(jnp.bfloat16)
    result = jnp.einsum("dhqk,dkhe->dqhe", probs_low, values, preferred_element_type=jnp.float32)
    result = result.reshape(result.shape[0], result.shape[1], -1).astype(jnp.bfloat16)
    return (result, highest_score + jnp.log(totals))


def score_grads(queries, keys, values, mask_bias, logsum, grad_out, row_delta):
    probs = jnp.exp(attention_scores(queries, keys, mask_bias) - logsum)
    grad_probs = jnp.einsum("dqhe,dkhe->dhqk", grad_out, values, preferred_element_type=jnp.float32)
    row_delta = jnp.sum(grad_probs * probs, axis=-1, keepdims=True)
    grad_raw = (probs * (grad_probs - row_delta) * HD ** (-0.5)).astype(jnp.bfloat16)
    return (grad_raw, probs.astype(jnp.bfloat16), row_delta)


def contract_query(grad_raw, keys):
    result = jnp.einsum("dhqk,dkhe->dqhe", grad_raw, keys, preferred_element_type=jnp.float32)
    return result.reshape(result.shape[0], result.shape[1], -1)


def contract_key(grad_raw, queries):
    result = jnp.einsum("dhqk,dqhe->dkhe", grad_raw, queries, preferred_element_type=jnp.float32)
    return result.reshape(result.shape[0], result.shape[1], -1)


def geglu_back(gate_vals, up_vals, grad_mid):
    activated, gelu_pull = jax.vjp(jax.nn.gelu, gate_vals.astype(jnp.float32))
    grad_gate = gelu_pull(grad_mid * up_vals.astype(jnp.float32))[0].astype(jnp.bfloat16)
    grad_up = (grad_mid * activated).astype(jnp.bfloat16)
    return (grad_gate, grad_up)


def geglu(gate_vals, up_vals):
    return (jax.nn.gelu(gate_vals.astype(jnp.float32)) * up_vals.astype(jnp.float32)).astype(
        jnp.bfloat16
    )


def plain_shards(
    tokens,
    cotangent,
    lengths,
    query_index,
    key_index,
    gain_attn,
    router_query,
    router_key,
    wq_light,
    wk_light,
    wv_light,
    wo_light,
    wq_heavy,
    wk_heavy,
    wv_heavy,
    wo_heavy,
    gain_ffn,
    router_ffn,
    gate_light,
    up_light,
    down_light,
    gate_heavy,
    up_heavy,
    down_heavy,
):
    documents, local_len, model_width = tokens.shape
    radius = WINDOW // 2
    block_rows = math.gcd(local_len, 512)
    key_span = block_rows + 2 * radius
    offset = lax.axis_index("seq") * local_len
    positions = offset + jnp.arange(local_len, dtype=jnp.int32)
    valid_rows = (positions[None, :] < lengths[:, None]).astype(jnp.float32)[:, :, None]
    pick_query = (query_index[:, :, None] == positions[None, None, :]).astype(jnp.float32)
    pick_key = (key_index[:, :, None] == positions[None, None, :]).astype(jnp.float32)
    inputs = tokens.astype(jnp.float32)
    inv_attn = lax.rsqrt(jnp.mean(inputs * inputs, axis=-1, keepdims=True) + epsilon)
    unit_attn = inputs * inv_attn
    gain_attn_f = gain_attn.astype(jnp.float32)
    normed = unit_attn * gain_attn_f
    normed_low = normed.astype(jnp.bfloat16)
    light_q = project(normed_low, wq_light).astype(jnp.bfloat16)
    light_k = project(normed_low, wk_light).astype(jnp.bfloat16)
    light_v = project(normed_low, wv_light).astype(jnp.bfloat16)
    light_width = light_q.shape[2]
    rim_block = with_halo(jnp.concatenate([light_k, light_v], axis=2), (("seq", 1),), radius)
    wide_k = split_heads(rim_block[:, :, :light_width])
    wide_v = split_heads(rim_block[:, :, light_width:])
    heads_q = split_heads(light_q)
    key_pos = offset - radius + jnp.arange(local_len + 2 * radius, dtype=jnp.int32)
    in_window = (jnp.abs(positions[:, None] - key_pos[None, :]) <= radius)[None]
    in_window = (
        in_window
        & (key_pos[None, None, :] >= 0)
        & (key_pos[None, None, :] < lengths[:, None, None])
    )
    light_bias = jnp.where(in_window, 0.0, masked_value)[:, None]
    piece_out, piece_lse = forward_attention(heads_q, wide_k, wide_v, light_bias)
    router_query_f = router_query.astype(jnp.float32)
    router_key_f = router_key.astype(jnp.float32)
    score_query = pick_scalar(
        pick_query,
        jax.nn.sigmoid(jnp.einsum("dsc,c->ds", normed, router_query_f, precision=highest)),
    )
    score_key = pick_scalar(
        pick_key, jax.nn.sigmoid(jnp.einsum("dsc,c->ds", normed, router_key_f, precision=highest))
    )
    heavy_in = pick_rows(pick_query, normed).astype(jnp.bfloat16)
    key_rows = pick_rows(pick_key, normed)
    key_in = key_rows.astype(jnp.bfloat16)
    scaled_in = (key_rows * score_key[:, :, None]).astype(jnp.bfloat16)
    heavy_q = project(heavy_in, wq_heavy).astype(jnp.bfloat16)
    heavy_k = project(key_in, wk_heavy).astype(jnp.bfloat16)
    heavy_v = project(scaled_in, wv_heavy).astype(jnp.bfloat16)
    heavy_width = heavy_q.shape[2]
    key_alive = (key_index >= 0).astype(jnp.bfloat16)
    routed_kv, alive_all = (
        lax.all_gather(jnp.concatenate([heavy_k, heavy_v], axis=2), "seq", axis=1, tiled=True),
        lax.all_gather(key_alive, "seq", axis=1, tiled=True),
    )
    all_k = routed_kv[:, :, :heavy_width]
    all_v = routed_kv[:, :, heavy_width:]
    heavy_bias = jnp.where(alive_all > 0, 0.0, masked_value)[:, None, None, :]
    heavy_out, heavy_lse = forward_attention(
        split_heads(heavy_q), split_heads(all_k), split_heads(all_v), heavy_bias
    )
    heavy_proj = unproject(heavy_out, wo_heavy)
    light_attn = unproject(piece_out, wo_light) * valid_rows
    heavy_attn = put_rows(pick_query, heavy_proj * score_query[:, :, None])
    attn_total = lax.psum((light_attn + heavy_attn).astype(jnp.bfloat16), "branch").astype(
        jnp.float32
    )
    hidden = inputs + attn_total
    inv_ffn = lax.rsqrt(jnp.mean(hidden * hidden, axis=-1, keepdims=True) + epsilon)
    unit_ffn = hidden * inv_ffn
    gain_ffn_f = gain_ffn.astype(jnp.float32)
    normed_ffn = unit_ffn * gain_ffn_f
    ffn_low = normed_ffn.astype(jnp.bfloat16)
    gate_l = project(ffn_low, gate_light).astype(jnp.bfloat16)
    up_l = project(ffn_low, up_light).astype(jnp.bfloat16)
    middle_l = geglu(gate_l, up_l)
    light_ffn = unproject(middle_l, down_light) * valid_rows
    router_ffn_f = router_ffn.astype(jnp.float32)
    score_ffn = pick_scalar(
        pick_query,
        jax.nn.sigmoid(jnp.einsum("dsc,c->ds", normed_ffn, router_ffn_f, precision=highest)),
    )
    ffn_rows = pick_rows(pick_query, normed_ffn).astype(jnp.bfloat16)
    gate_h = project(ffn_rows, gate_heavy).astype(jnp.bfloat16)
    up_h = project(ffn_rows, up_heavy).astype(jnp.bfloat16)
    middle_h = geglu(gate_h, up_h)
    heavy_fproj = unproject(middle_h, down_heavy)
    heavy_ffn = put_rows(pick_query, heavy_fproj * score_ffn[:, :, None])
    share = model_width // lax.axis_size("branch")
    own_cols = lax.axis_index("branch") * share
    mixed = lax.dynamic_slice_in_dim(hidden, own_cols, share, 2) + lax.psum_scatter(
        (light_ffn + heavy_ffn).astype(jnp.bfloat16), "branch", scatter_dimension=2, tiled=True
    ).astype(jnp.float32)
    grad_out = cotangent.astype(jnp.float32)
    grad_light = (grad_out * valid_rows).astype(jnp.bfloat16)
    grad_down_light = weight_grad(grad_light, middle_l)
    grad_gate_l, grad_up_l = geglu_back(gate_l, up_l, project(grad_light, down_light))
    grad_gate_light = weight_grad(ffn_low, grad_gate_l)
    grad_up_light = weight_grad(ffn_low, grad_up_l)
    grad_rows = pick_rows(pick_query, grad_out)
    grad_heavy = (grad_rows * score_ffn[:, :, None]).astype(jnp.bfloat16)
    score_ffn_part = jnp.sum(grad_rows * heavy_fproj, axis=-1)
    grad_down_heavy = weight_grad(grad_heavy, middle_h)
    grad_gate_h, grad_up_h = geglu_back(gate_h, up_h, project(grad_heavy, down_heavy))
    grad_gate_heavy = weight_grad(ffn_rows, grad_gate_h)
    grad_up_heavy = weight_grad(ffn_rows, grad_up_h)
    heavy_ffn_rows = unproject(grad_gate_h, gate_heavy) + unproject(grad_up_h, up_heavy)
    ffn_part = (
        unproject(grad_gate_l, gate_light)
        + unproject(grad_up_l, up_light)
        + put_rows(pick_query, heavy_ffn_rows)
    )
    grad_normed_ffn, grad_score_ffn = (
        lax.psum(ffn_part.astype(jnp.bfloat16), "branch").astype(jnp.float32),
        lax.psum(score_ffn_part.astype(jnp.bfloat16), "branch").astype(jnp.float32),
    )
    pre_ffn = put_scalar(pick_query, grad_score_ffn * score_ffn * (1.0 - score_ffn))
    grad_normed_ffn = grad_normed_ffn + pre_ffn[:, :, None] * router_ffn_f
    grad_router_ffn = jnp.einsum("ds,dsc->c", pre_ffn, normed_ffn, precision=highest)
    grad_gain_ffn = jnp.sum(grad_normed_ffn * unit_ffn, axis=(0, 1))
    grad_unit_f = grad_normed_ffn * gain_ffn_f
    grad_hidden = grad_out + inv_ffn * (
        grad_unit_f - unit_ffn * jnp.mean(grad_unit_f * unit_ffn, axis=-1, keepdims=True)
    )
    grad_light_attn = (grad_hidden * valid_rows).astype(jnp.bfloat16)
    grad_wo_light = weight_grad(grad_light_attn, piece_out)
    grad_light_out = split_heads(project(grad_light_attn, wo_light).astype(jnp.bfloat16))
    wide_grad = jnp.zeros((documents, local_len + 2 * radius, 2 * light_width), jnp.float32)
    light_raw, light_plow, unused_delta = score_grads(
        heads_q, wide_k, wide_v, light_bias, piece_lse, grad_light_out, None
    )
    query_pieces = contract_query(light_raw, wide_k)
    key_terms = jnp.concatenate(
        [contract_key(light_raw, heads_q), contract_key(light_plow, grad_light_out)], axis=2
    )
    wide_grad = wide_grad.at[:, 0:key_span].add(key_terms)
    grad_light_q = query_pieces.astype(jnp.bfloat16)
    outer_rims = jnp.concatenate(
        [wide_grad[:, :radius], wide_grad[:, radius + local_len :]], axis=1
    )
    returned = with_halo(outer_rims.astype(jnp.bfloat16), (("seq", 1),), radius).astype(
        outer_rims.dtype
    )
    inner = wide_grad[:, radius : radius + local_len]
    inner = inner + jnp.pad(returned[:, :radius], ((0, 0), (0, local_len - radius), (0, 0)))
    inner = inner + jnp.pad(returned[:, 3 * radius :], ((0, 0), (local_len - radius, 0), (0, 0)))
    grad_light_k = inner[:, :, :light_width].astype(jnp.bfloat16)
    grad_light_v = inner[:, :, light_width:].astype(jnp.bfloat16)
    grad_wq_light = weight_grad(normed_low, grad_light_q)
    grad_wk_light = weight_grad(normed_low, grad_light_k)
    grad_wv_light = weight_grad(normed_low, grad_light_v)
    light_part = (
        unproject(grad_light_q, wq_light)
        + unproject(grad_light_k, wk_light)
        + unproject(grad_light_v, wv_light)
    )
    grad_hrows = pick_rows(pick_query, grad_hidden)
    grad_heavy_attn = (grad_hrows * score_query[:, :, None]).astype(jnp.bfloat16)
    score_query_part = jnp.sum(grad_hrows * heavy_proj, axis=-1)
    grad_wo_heavy = weight_grad(grad_heavy_attn, heavy_out)
    grad_heavy_out = project(grad_heavy_attn, wo_heavy).astype(jnp.bfloat16)
    heavy_raw, heavy_plow, heavy_delta = score_grads(
        split_heads(heavy_q),
        split_heads(all_k),
        split_heads(all_v),
        heavy_bias,
        heavy_lse,
        split_heads(grad_heavy_out),
        None,
    )
    grad_heavy_q = contract_query(heavy_raw, split_heads(all_k)).astype(jnp.bfloat16)
    every_kv = jnp.concatenate(
        [
            contract_key(heavy_raw, split_heads(heavy_q)),
            contract_key(heavy_plow, split_heads(grad_heavy_out)),
        ],
        axis=2,
    )
    own_kv = lax.psum_scatter(every_kv, "seq", scatter_dimension=1, tiled=True)
    grad_heavy_k = own_kv[:, :, :heavy_width].astype(jnp.bfloat16)
    grad_heavy_v = own_kv[:, :, heavy_width:].astype(jnp.bfloat16)
    grad_scaled = unproject(grad_heavy_v, wv_heavy)
    score_key_part = jnp.sum(grad_scaled * key_rows, axis=-1)
    grad_key_rows = unproject(grad_heavy_k, wk_heavy) + grad_scaled * score_key[:, :, None]
    grad_wq_heavy = weight_grad(heavy_in, grad_heavy_q)
    grad_wk_heavy = weight_grad(key_in, grad_heavy_k)
    grad_wv_heavy = weight_grad(scaled_in, grad_heavy_v)
    attn_part = (
        light_part
        + put_rows(pick_query, unproject(grad_heavy_q, wq_heavy))
        + put_rows(pick_key, grad_key_rows)
    )
    grad_normed, grad_score_query, grad_score_key = (
        lax.psum(attn_part.astype(jnp.bfloat16), "branch").astype(jnp.float32),
        lax.psum(score_query_part.astype(jnp.bfloat16), "branch").astype(jnp.float32),
        lax.psum(score_key_part.astype(jnp.bfloat16), "branch").astype(jnp.float32),
    )
    pre_query = put_scalar(pick_query, grad_score_query * score_query * (1.0 - score_query))
    pre_key = put_scalar(pick_key, grad_score_key * score_key * (1.0 - score_key))
    grad_normed = (
        grad_normed + pre_query[:, :, None] * router_query_f + pre_key[:, :, None] * router_key_f
    )
    grad_router_query = jnp.einsum("ds,dsc->c", pre_query, normed, precision=highest)
    grad_router_key = jnp.einsum("ds,dsc->c", pre_key, normed, precision=highest)
    grad_gain_attn = jnp.sum(grad_normed * unit_attn, axis=(0, 1))
    grad_unit_a = grad_normed * gain_attn_f
    grad_tokens = grad_hidden + inv_attn * (
        grad_unit_a - unit_attn * jnp.mean(grad_unit_a * unit_attn, axis=-1, keepdims=True)
    )
    names = (
        grad_wq_light, grad_wk_light, grad_wv_light, grad_wo_light,
        grad_wq_heavy, grad_wk_heavy, grad_wv_heavy, grad_wo_heavy,
        grad_gate_light, grad_up_light, grad_down_light,
        grad_gate_heavy, grad_up_heavy, grad_down_heavy,
    )
    vectors = jnp.stack(
        [grad_gain_attn, grad_router_query, grad_router_key, grad_gain_ffn, grad_router_ffn], axis=1
    )
    packed = jnp.concatenate([g.astype(jnp.bfloat16) for g in names + (vectors,)], axis=1)
    summed = lax.psum_scatter(packed, "seq", scatter_dimension=0, tiled=True).astype(jnp.float32)
    widths = [g.shape[1] for g in names]
    cuts = [sum(widths[:i]) for i in range(len(widths) + 1)]
    (
        grad_wq_light, grad_wk_light, grad_wv_light, grad_wo_light,
        grad_wq_heavy, grad_wk_heavy, grad_wv_heavy, grad_wo_heavy,
        grad_gate_light, grad_up_light, grad_down_light,
        grad_gate_heavy, grad_up_heavy, grad_down_heavy,
    ) = [summed[:, cuts[i] : cuts[i + 1]] for i in range(len(widths))]
    grad_gain_attn, grad_router_query, grad_router_key, grad_gain_ffn, grad_router_ffn = [
        summed[:, cuts[-1] + i] for i in range(5)
    ]
    return (
        mixed,
        grad_tokens,
        grad_gain_attn,
        grad_router_query,
        grad_router_key,
        grad_wq_light,
        grad_wk_light,
        grad_wv_light,
        grad_wo_light,
        grad_wq_heavy,
        grad_wk_heavy,
        grad_wv_heavy,
        grad_wo_heavy,
        grad_gain_ffn,
        grad_router_ffn,
        grad_gate_light,
        grad_up_light,
        grad_down_light,
        grad_gate_heavy,
        grad_up_heavy,
        grad_down_heavy,
    )


ORDER = (
    "load", "rowskv", "pre0", "norm", "qkv", "pre1", "gp0_2", "la0", "predmh", "gp0_1", "gp0_3", "wgp",
    "hattn", "la1", "hproj", "nf00", "nf01", "fh0", "fl00", "nf10", "nf11", "fh1", "hgrA1", "hgrA0", "fl01",
    "hgrB0", "rs0a", "fl11", "hgrB1", "rs0b", "ar101_1", "fl10", "rs1a", "lgA", "ar100_1", "lgB", "ar101_2",
    "rs0r", "ar110_1", "ar100_2", "ar111_1", "rs1b", "hgrB2", "mixt1", "rs3a", "ar110_2", "ar100_3",
    "ar111_2", "rs3b", "mixt0", "rs1c", "ar101_3", "gp1_1", "ar110_3", "gp1_2", "ar111_3", "ar101_4", "mx1",
    "ar100_4", "hg00", "hg01", "rs3r", "hb0", "mx0", "rs1d", "rs1r", "lb0", "rs0c", "gp1_3", "ar110_4",
    "mixs1", "ar111_4", "hg10", "hg11", "hgrA2", "gp2_3", "rs3c", "hb1", "gp2_1", "gp2_2", "mixs0", "awgB",
    "lb1", "hk0", "rs2a", "rs2b", "abt00", "abt01", "gp3_1", "blank", "gp3_2", "gp3_3", "rs2r", "rs2c",
    "ar200_1", "hk1", "rs0d", "awgA", "rs2d", "rs4a", "ar201_1", "ar200_2", "rs4b", "abt10", "ar201_2",
    "abt11", "ar200_3", "rs4c", "aqgA", "aqgB", "rs5a", "ar210_1", "rs5b", "rs4r", "rs5d", "rs5c",
    "ar210_2", "ar211_1", "ar201_3", "rs3d", "mixf0", "ar210_3", "rs2e", "ar211_2", "ar201_4", "rs5r",
    "rs4d", "ar210_4", "tok10", "rs4e", "rs1e", "ar211_3", "rs3e", "rs0e", "gains", "rs5e", "vec", "tok01",
    "ar211_4", "mixf1", "tok11", "ar200_4", "tok00", "vece",
)
BF = jnp.bfloat16
F32 = jnp.float32
MESH = pl.DeviceIdType.MESH


def mm(a, b):
    return jnp.dot(a, b, preferred_element_type=F32)


def mmt(a, b):
    return lax.dot_general(a, b, (((1,), (1,)), ((), ())), preferred_element_type=F32)


def tmm(a, b):
    return lax.dot_general(a, b, (((0,), (0,)), ((), ())), preferred_element_type=F32)


def row_sum(values):
    return jnp.sum(values, axis=-1, keepdims=True)


def gelu_parts(v):
    c = math.sqrt(2.0 / math.pi)
    square = v * v
    t = jnp.tanh(c * v * (1.0 + 0.044715 * square))
    act = 0.5 * v * (1.0 + t)
    slope = 0.5 * (1.0 + t) + (0.5 * c) * v * (1.0 - t * t) * (1.0 + 0.134145 * square)
    return act, slope


def layer_kernel(dims, *refs):
    docs, rows, width, slots, n_seq, wl, wh, fl_n, fh_n = dims
    nz = n_seq // 2
    chunk = width // n_seq
    half = rows // 2
    quarter = rows // 4
    eighth = rows // 8
    radius = WINDOW // 2
    share = width // 4
    it = iter(refs)

    def take(count):
        return [next(it) for _ in range(count)]

    lens, qi, ki, ga_v, rq_v, rk_v, gf_v, rf_v = take(8)
    (tok_h, cot_h, wql_h, wkl_h, wvl_h, wol_h, wqh_h, wkh_h, wvh_h, woh_h,
     gl_h, ul_h, dl_h, gh_h, uh_h, dh_h) = take(16)
    gt_o, mix_o, pack_o, vec_o = take(4)
    (tok, cot, wqkv, wola, whq, whk, whv, woha, wgul, wdl, wguh, wdh, wkeep) = take(13)
    (nl, inva, hin, kin, sin, qbuf, kvw, pbuf, loall, hqx, kvall, ph, hoall, qall, doall, hproj, backr, bothr) = take(18)
    (pqk, pqkt, parts, tot1, tot2, r1, r2, cols) = take(8)
    (dm, dmh, grow, fl, invf, mid, dgu, frow, ghr, midh, dguh) = take(11)
    (mixb, mixr, mixa, ghf, ghb, dol, dox, gah, dqh, dkvw, rims, rimr, dqkv, dkvh) = take(14)
    (g_h, g_l, ra, rb, rl, packed, vbuf, vr, vect) = take(2) + [take(6), take(6), take(6)] + take(4)
    g_a = wguh
    (load_s, wg_s, wg_r, wf_s, wf_r, lo_s, lo_r, ho_s, ho_r, ar_s, ar_r, ag_s, ag_r, fw_s, fw_r, halo_s, halo_r, rim_s, rim_r,
     mx_s, mx_r, wa_s, wa_r, wz_s, wz_r, rl_s, rl_r, v_s, v_r, out_s) = take(30)

    b = lax.axis_index("branch")
    s = lax.axis_index("seq")
    bit_x = b % 2
    bit_y = b // 2
    core = s % 2
    z = s // 2
    offset = s * rows
    dev_x = (b + 1 - 2 * bit_x, s)
    dev_y = (b + 2 - 4 * bit_y, s)
    sibling = (b, s + 1 - 2 * core)

    def zpeer(k):
        return (z + k) % nz

    def same_core(k):
        return (b, 2 * zpeer(k) + core)

    late = []

    def send(src, dst, ssem, rsem, dev, when=None):
        copy = pltpu.make_async_remote_copy(
            src_ref=src, dst_ref=dst, send_sem=ssem, recv_sem=rsem, device_id=dev, device_id_type=MESH
        )
        if when is None:
            copy.start()
        else:
            pl.when(when)(copy.start)
        return copy

    def arrived(dst, ssem, rsem, dev):
        pltpu.make_async_remote_copy(
            src_ref=dst, dst_ref=dst, send_sem=ssem, recv_sem=rsem, device_id=dev, device_id_type=MESH
        ).wait_recv()

    loads = {}

    def load(name, src, dst, i):
        copy = pltpu.make_async_copy(src, dst, load_s.at[i])
        copy.start()
        loads[name] = copy

    load("tok", tok_h, tok, 0)
    load("whq", wqh_h, whq, 1)
    load("whk", wkh_h, whk, 2)
    load("whv", wvh_h, whv, 3)
    load("wq", wql_h, wqkv.at[:, 0:wl], 4)
    load("wk", wkl_h, wqkv.at[:, wl : 2 * wl], 5)
    load("wv", wvl_h, wqkv.at[:, 2 * wl : 3 * wl], 6)
    load("wol", wol_h, wola.at[b], 7)
    load("who", woh_h, woha.at[b], 8)
    load("cot", cot_h, cot, 9)
    load("wdl", dl_h, wdl, 10)
    load("wdh", dh_h, wdh, 11)
    load("gl", gl_h, wgul.at[:, 0:fl_n], 12)
    load("ul", ul_h, wgul.at[:, fl_n : 2 * fl_n], 13)
    load("gh", gh_h, wguh.at[:, 0:fh_n], 14)
    load("uh", uh_h, wguh.at[:, fh_n : 2 * fh_n], 15)
    own_rows = pl.ds(pl.multiple_of(chunk * s, chunk), chunk)
    load("gk", gh_h.at[own_rows], wkeep.at[:, 0:fh_n], 16)
    load("uk", uh_h.at[own_rows], wkeep.at[:, fh_n : 2 * fh_n], 17)

    barrier = pltpu.get_barrier_semaphore()
    for k in range(1, 4):
        pl.semaphore_signal(barrier, inc=1, device_id=((b + k) % 4, s), device_id_type=MESH)

    def greet(k, carry):
        pl.semaphore_signal(barrier, inc=1, device_id=(b, (s + k) % n_seq), device_id_type=MESH)
        return carry

    lax.fori_loop(1, n_seq, greet, 0)
    pl.semaphore_wait(barrier, 3 + n_seq - 1)

    gain_a, router_q, router_k, gain_f, router_f = [
        ref[...].astype(F32).reshape(1, width) for ref in (ga_v, rq_v, rk_v, gf_v, rf_v)
    ]

    def as_column(row):
        count = row.shape[1]
        square = lax.broadcasted_iota(jnp.int32, (count, count), 0)
        same = square == lax.broadcasted_iota(jnp.int32, (count, count), 1)
        return row_sum(jnp.where(same, row.astype(F32), 0.0)).astype(jnp.int32)

    idx_row = [[ref[d : d + 1, :] for ref in (qi, ki)] for d in range(docs)]
    idx_col = [[as_column(row) for row in idx_row[d]] for d in range(docs)]

    def valid_rows(d, first, count):
        at = lax.broadcasted_iota(jnp.int32, (count, 1), 0) + (offset + first)
        return jnp.where(at < lens[d], 1.0, 0.0).astype(F32)

    big = 64

    def tiles(count, size, body):
        def step(t, carry):
            body(pl.multiple_of(t * size, size))
            return carry

        lax.fori_loop(0, count // size, step, 0)

    def geometry(h):
        first, second = ((dev_x, bit_x), (dev_y, bit_y))[:: 1 if h == 0 else -1]
        base = half * h
        keep1 = base + quarter * first[1]
        send1 = base + quarter * (1 - first[1])
        keep2 = keep1 + eighth * second[1]
        send2 = keep1 + eighth * (1 - second[1])
        return (first[0], second[0]) + tuple(pl.multiple_of(v, eighth) for v in (keep1, send1, keep2, send2))

    flights = {}

    def ar_start(a, d, h):
        first, second, keep1, send1, keep2, send2 = geometry(h)
        flights[a, d, h, 0] = send(
            parts.at[d, pl.ds(send1, quarter)], r1.at[d, h], ar_s.at[a, d, h, 0], ar_r.at[a, d, h, 0], first
        )

    def add_rows(d, at, buf, base, total):
        def body(t, carry):
            r = pl.multiple_of(t * 32, 32)
            here = pl.ds(pl.multiple_of(at + r, 32), 32)
            value = parts[d, here, :].astype(F32) + buf[pl.ds(base + r, 32), :].astype(F32)
            total[d, here, :] = value.astype(BF)
            return carry

        lax.fori_loop(0, eighth // 32, body, 0)

    def ar_step(a, d, h, step, total):
        first, second, keep1, send1, keep2, send2 = geometry(h)
        at = (a, d, h)
        if step == 1:
            arrived(r1.at[d, h], ar_s.at[a, d, h, 0], ar_r.at[a, d, h, 0], first)
            add_rows(d, send2, r1.at[d, h], pl.multiple_of(send2 - keep1, eighth), parts)
            flights[at + (1,)] = send(
                parts.at[d, pl.ds(send2, eighth)], r2.at[d, h], ar_s.at[a, d, h, 1], ar_r.at[a, d, h, 1], second
            )
            add_rows(d, keep2, r1.at[d, h], pl.multiple_of(keep2 - keep1, eighth), parts)
        elif step == 2:
            arrived(r2.at[d, h], ar_s.at[a, d, h, 1], ar_r.at[a, d, h, 1], second)
            add_rows(d, keep2, r2.at[d, h], 0, total)
            own = total.at[d, pl.ds(keep2, eighth)]
            flights[at + (2,)] = send(own, own, ar_s.at[a, d, h, 2], ar_r.at[a, d, h, 2], second)
        elif step == 3:
            arrived(total.at[d, pl.ds(send2, eighth)], ar_s.at[a, d, h, 2], ar_r.at[a, d, h, 2], second)
            own = total.at[d, pl.ds(keep1, quarter)]
            flights[at + (3,)] = send(own, own, ar_s.at[a, d, h, 3], ar_r.at[a, d, h, 3], first)
        else:
            arrived(total.at[d, pl.ds(send1, quarter)], ar_s.at[a, d, h, 3], ar_r.at[a, d, h, 3], first)
            flights[at + (0,)].wait_send()
            flights[at + (1,)].wait_send()

    def ar_sent(a, d):
        for h in range(2):
            flights[a, d, h, 2].wait_send()
            flights[a, d, h, 3].wait_send()

    steps = {}

    def step(name):
        def keep(body):
            steps[name] = body
            return body

        return keep

    def halves(core_of):
        return (
            (wola, pl.ds(pl.multiple_of(width // 2 * core_of, 16), width // 2)),
            (woha, pl.ds(pl.multiple_of(wh // 2 * core_of, 16), wh // 2)),
        )

    @step("load")
    def _():
        loads["wol"].wait()
        loads["who"].wait()
        for k in range(1, 4):
            for i, (ref, part) in enumerate(halves(core)):
                block = ref.at[b, part]
                late.append(send(block, block, wg_s.at[k - 1, i], wg_r.at[k - 1, i], ((b + k) % 4, s)))
        loads["tok"].wait()

    @step("wgp")
    def _():
        for k in range(1, 4):
            frm = (b + 4 - k) % 4
            for i, (ref, part) in enumerate(halves(core)):
                block = ref.at[frm, part]
                arrived(block, wg_s.at[k - 1, i], wg_r.at[k - 1, i], (frm, s))
                late.append(send(block, block, wf_s.at[k - 1, i], wf_r.at[k - 1, i], sibling))

    def projections_wait():
        for k in range(1, 4):
            frm = (b + 4 - k) % 4
            for i, (ref, part) in enumerate(halves(1 - core)):
                arrived(ref.at[frm, part], wf_s.at[k - 1, i], wf_r.at[k - 1, i], sibling)

    @step("norm")
    def _():
        for d in range(docs):

            def norm_body(t, d=d):
                r = pl.ds(t, big)
                x = tok[d, r, :].astype(F32)
                inv = lax.rsqrt(row_sum(x * x) * (1.0 / width) + epsilon)
                inva[d, r, :] = inv
                nl[d, r, :] = (x * inv * gain_a).astype(BF)

            tiles(rows, big, norm_body)

    def selectors():
        for d in range(docs):
            lane_pos = lax.broadcasted_iota(jnp.int32, (slots, rows), 1) + offset
            sub_pos = lax.broadcasted_iota(jnp.int32, (rows, slots), 0) + offset
            for i in range(2):
                here = slice(i * slots, (i + 1) * slots)
                pqk[d, here, :] = jnp.where(idx_col[d][i] == lane_pos, 1.0, 0.0).astype(BF)
                pqkt[d, :, here] = jnp.where(idx_row[d][i] == sub_pos, 1.0, 0.0).astype(BF)

    def alive(d, i):
        return jnp.where(idx_col[d][i] >= 0, 1.0, 0.0).astype(F32)

    SQ, SK, SF, PREQ, PREF, PREK = range(6)

    def mine(d):
        return slice(d * slots, (d + 1) * slots)

    def routed_rows():
        for d in range(docs):
            x = mm(pqk[d], tok[d])
            picked = x * lax.rsqrt(row_sum(x * x) * (1.0 / width) + epsilon) * gain_a
            score_q = jax.nn.sigmoid(row_sum(picked[:slots] * router_q)) * alive(d, 0)
            score_k = jax.nn.sigmoid(row_sum(picked[slots:] * router_k)) * alive(d, 1)
            cols[SQ, mine(d), :] = score_q
            cols[SK, mine(d), :] = score_k
            hin[mine(d), :] = picked[:slots].astype(BF)
            kin[mine(d), :] = picked[slots:].astype(BF)
            sin[mine(d), :] = (picked[slots:] * score_k).astype(BF)
            pad_lane = lax.broadcasted_iota(jnp.int32, (slots, 256 - wh), 1)
            kvall[s, mine(d), wh:256] = jnp.where(
                pad_lane == 0, (1.0 - alive(d, 1)) * masked_value, 0.0
            ).astype(BF)
            kvall[s, mine(d), 256 + wh : 512] = jnp.zeros((slots, 256 - wh), BF)
        loads["whk"].wait()
        kvall[s, :, 0:wh] = mmt(kin[...], whk[...]).astype(BF)
        loads["whv"].wait()
        kvall[s, :, 256 : 256 + wh] = mmt(sin[...], whv[...]).astype(BF)

    at_end = (z == 0) | (z == nz - 1)
    inner = (z > 0) & (z < nz - 1)
    low_side = jnp.where(z < nz // 2, 1, 0)

    def gather_start(g, ref, part):
        block = ref.at[s, part]
        late.append(send(block, block, ag_s.at[g, 0], ag_r.at[g, 0], sibling))
        for k in (2, 1, 3):
            near = (z != 0) if k == 3 else (z != 3) if k == 1 else (z >= 0)
            late.append((near, send(block, block, ag_s.at[g, k], ag_r.at[g, k], same_core(k), near)))

    def gather_pass(g, ref, part, k):
        block = ref.at[2 * zpeer(nz - k) + core, part]
        arrived(block, ag_s.at[g, k], ag_r.at[g, k], same_core(nz - k))
        late.append(send(block, block, fw_s.at[g, k], fw_r.at[g, k], sibling))
        if k == 2:
            onward = (b, 2 * (z + 1 - 2 * low_side) + core)
            slot = 3 - 2 * low_side
            late.append((inner, send(block, block, fw_s.at[g, 0], ag_r.at[g, slot], onward, inner)))

    def gather_end(g, ref, part):
        arrived(ref.at[s + 1 - 2 * core, part], ag_s.at[g, 0], ag_r.at[g, 0], sibling)
        for k in range(1, nz):
            block = ref.at[2 * zpeer(nz - k) + 1 - core, part]
            arrived(block, fw_s.at[g, k], fw_r.at[g, k], sibling)

    def routed(d):
        return pl.ds(d * slots, slots)

    every = pl.ds(0, docs * slots)

    @step("rowskv")
    def _():
        selectors()
        routed_rows()
        gather_start(0, kvall, every)


    last = n_seq - 1
    left = (b, (s + last) % n_seq)
    right = (b, (s + 1) % n_seq)

    @step("qkv")
    def _():
        for name in ("wq", "wk", "wv"):
            loads[name].wait()
        for d in range(docs):

            def qkv_body(t, d=d):
                r = mm(nl[d, pl.ds(t, half), :], wqkv[...]).astype(BF)
                qbuf[d, pl.ds(t, half), :] = r[:, 0:wl]
                kvw[d, pl.ds(pl.multiple_of(t + radius, 32), half), :] = r[:, wl : 3 * wl]

            tiles(rows, half, qkv_body)

            @pl.when(s == 0)
            def _(d=d):
                kvw[d, 0:radius, :] = jnp.zeros((radius, 2 * wl), BF)

            @pl.when(s == last)
            def _(d=d):
                kvw[d, rows + radius : rows + 2 * radius, :] = jnp.zeros((radius, 2 * wl), BF)

            late.append((s > 0, send(
                kvw.at[d, pl.ds(radius, radius)], kvw.at[d, pl.ds(rows + radius, radius)],
                halo_s.at[d, 0], halo_r.at[d, 0], left, s > 0,
            )))
            late.append((s < last, send(
                kvw.at[d, pl.ds(rows, radius)], kvw.at[d, pl.ds(0, radius)],
                halo_s.at[d, 1], halo_r.at[d, 1], right, s < last,
            )))
        loads["whq"].wait()
        hqx[:, 0:wh] = mmt(hin[...], whq[...]).astype(BF)
        pad_lane = lax.broadcasted_iota(jnp.int32, (docs * slots, 256 - wh), 1)
        hqx[:, wh:256] = jnp.where(pad_lane == 0, 8.0, 0.0).astype(BF)

    def halo_wait(d):
        @pl.when(s < last)
        def _():
            arrived(kvw.at[d, pl.ds(rows + radius, radius)], halo_s.at[d, 0], halo_r.at[d, 0], right)

        @pl.when(s > 0)
        def _():
            arrived(kvw.at[d, pl.ds(0, radius)], halo_s.at[d, 1], halo_r.at[d, 1], left)

    blk = WINDOW
    span = 2 * WINDOW
    n_blk = rows // blk

    def two_heads(v):
        lane = lax.broadcasted_iota(jnp.int32, v.shape, 1)
        zero = jnp.zeros_like(v)
        return jnp.concatenate([jnp.where(lane < HD, v, zero), jnp.where(lane < HD, zero, v)], axis=0)

    def one_of_two(v):
        lane = lax.broadcasted_iota(jnp.int32, (blk, 2 * HD), 1)
        return jnp.where(lane < HD, v[:blk], v[blk:])

    def light_attention(d):
        def body(i, carry):
            at = pl.multiple_of(i * blk, blk)
            q2 = two_heads(qbuf[d, pl.ds(at, blk), :])
            k = kvw[d, pl.ds(at, span), 0:wl]
            v = kvw[d, pl.ds(at, span), wl : 2 * wl]
            row = lax.broadcasted_iota(jnp.int32, (2 * blk, span), 0) % blk
            col = lax.broadcasted_iota(jnp.int32, (2 * blk, span), 1)
            pos = col + (offset + at - radius)
            seen = (col >= row) & (col <= row + WINDOW) & (pos >= 0) & (pos < lens[d])
            scores = jnp.where(seen, mmt(q2, k) * HD ** (-0.5), masked_value)
            e = jnp.exp(scores - jnp.max(scores, axis=-1, keepdims=True))
            p = (e * (1.0 / row_sum(e))).astype(BF)
            pbuf[d * n_blk + i] = p
            out = one_of_two(mm(p, v))
            loall[b, d, pl.ds(at, blk), :] = (out * valid_rows(d, at, blk)).astype(BF)
            return carry

        lax.fori_loop(0, n_blk, body, 0)

    def three_heads(v):
        lane = lax.broadcasted_iota(jnp.int32, v.shape, 1)
        zero = jnp.zeros_like(v)
        return jnp.concatenate(
            [jnp.where((lane // HD == h) | (lane >= wh), v, zero) for h in range(wh // HD)], axis=0
        )

    def one_of_three(v):
        lane = lax.broadcasted_iota(jnp.int32, (slots, 256), 1)
        total = jnp.zeros((slots, 256), F32)
        for h in range(wh // HD):
            total = jnp.where(lane // HD == h, v[h * slots : (h + 1) * slots], total)
        return total

    def keys_of(d, at):
        return kvall[:, mine(d), at : at + 256].reshape(n_seq * slots, 256)

    def spread(column):
        lane = lax.broadcasted_iota(jnp.int32, (slots, 256 - wh), 1)
        out = jnp.zeros((slots, 256 - wh), F32)
        for h in range(wh // HD):
            value = column[h * slots : (h + 1) * slots]
            high = value.astype(BF).astype(F32)
            low = value - high
            out = jnp.where(lane == 2 * h, high, jnp.where(lane == 2 * h + 1, low, out))
        return out.astype(BF)

    def own_keys(d, at):
        v = kvall[s, mine(d), at : at + 256]
        lane = lax.broadcasted_iota(jnp.int32, v.shape, 1)
        zero = jnp.zeros_like(v)
        one = jnp.ones_like(v)
        return jnp.concatenate(
            [
                jnp.where(
                    lane // HD == h, v, jnp.where((lane == wh + 2 * h) | (lane == wh + 2 * h + 1), one, zero)
                )
                for h in range(wh // HD)
            ],
            axis=0,
        )

    def heavy_attention(d):
        q3 = three_heads(hqx[mine(d), :])
        scores = mmt(q3, keys_of(d, 0)) * HD ** (-0.5)
        top = jnp.max(scores, axis=-1, keepdims=True)
        e = jnp.exp(scores - top)
        sums = row_sum(e)
        p = (e * (1.0 / sums)).astype(BF)
        ph[d] = p
        qall[s, mine(d), 0:wh] = hqx[mine(d), 0:wh]
        qall[s, mine(d), wh:256] = spread((top + jnp.log(sums)) * -(HD**0.5))
        hoall[b, mine(d), :] = one_of_three(mm(p, keys_of(d, 256))).astype(BF)

    def to_branches(block, ssem, rsem, k):
        return send(block, block, ssem, rsem, ((b + k) % 4, s))

    def from_branch(ref, ssem, rsem, k):
        frm = (b + 4 - k) % 4
        arrived(ref.at[frm], ssem, rsem, (frm, s))

    for d in range(docs):

        @step("la%d" % d)
        def _(d=d):
            halo_wait(d)
            light_attention(d)
            for k in range(1, 4):
                late.append(to_branches(loall.at[b, d], lo_s.at[d, k - 1], lo_r.at[d, k - 1], k))

    @step("hattn")
    def _():
        gather_end(0, kvall, every)
        for d in range(docs):
            heavy_attention(d)
        for k in range(1, 4):
            late.append(to_branches(hoall.at[b], ho_s.at[k - 1], ho_r.at[k - 1], k))
        gather_start(1, qall, every)

    gathers = ((0, kvall, every), (1, qall, every)) + tuple((2 + d, doall, routed(d)) for d in range(docs))
    for g, ref, part in gathers:
        for k in range(1, nz):

            @step("gp%d_%d" % (g, k))
            def _(g=g, ref=ref, part=part, k=k):
                gather_pass(g, ref, part, k)

    @step("hproj")
    def _():
        projections_wait()
        for k in range(1, 4):
            from_branch(hoall, ho_s.at[k - 1], ho_r.at[k - 1], k)
        total = mm(hoall[0, :, 0:wh], woha[0])
        for j in range(1, 4):
            total = total + mm(hoall[j, :, 0:wh], woha[j])
        hproj[...] = (total * cols[SQ]).astype(BF)

    def attention_total(d, h):
        r = pl.ds(h * half, half)
        heads = jnp.concatenate([loall[j, d, r, :] for j in range(4)], axis=1)
        out_weights = jnp.concatenate([wola[j] for j in range(4)], axis=1)
        value = mmt(heads, out_weights) + mm(pqkt[d, r, 0:slots], hproj[mine(d), :])
        tot1[d, r, :] = value.astype(BF)

    def light_pre(d):
        def body(t):
            r = pl.ds(t, half)
            dm[d, r, :] = mm(cot[d, r, :], wdl[...]) * valid_rows(d, t, half)

        tiles(rows, half, body)
        grow[mine(d), :] = mm(pqk[d, 0:slots, :], cot[d]).astype(BF)

    for d in range(docs):

        @step("pre%d" % d)
        def _(d=d):
            if d == 0:
                for name in ("cot", "wdl"):
                    loads[name].wait()
            light_pre(d)

    @step("predmh")
    def _():
        loads["wdh"].wait()
        dmh[...] = mm(grow[...], wdh[...])

    def hidden_rows(d, r):
        return tok[d, r, :].astype(F32) + tot1[d, r, :].astype(F32)

    def ffn_norm(d, h):
        def body(t):
            r = pl.ds(pl.multiple_of(h * half + t, big), big)
            hidden = hidden_rows(d, r)
            inv = lax.rsqrt(row_sum(hidden * hidden) * (1.0 / width) + epsilon)
            invf[d, r, :] = inv
            fl[d, r, :] = (hidden * inv * gain_f).astype(BF)

        tiles(half, big, body)

    for d in range(docs):
        for h in range(2):

            @step("nf%d%d" % (d, h))
            def _(d=d, h=h):
                if h == 0:
                    for k in range(1, 4):
                        frm = (b + 4 - k) % 4
                        arrived(loall.at[frm, d], lo_s.at[d, k - 1], lo_r.at[d, k - 1], (frm, s))
                attention_total(d, h)
                ffn_norm(d, h)

    def ffn_heavy(d):
        rowsf = mm(pqk[d, 0:slots, :], fl[d])
        score = jax.nn.sigmoid(row_sum(rowsf * router_f)) * alive(d, 0)
        cols[SF, mine(d), :] = score
        frow[mine(d), :] = rowsf.astype(BF)
        ghr[mine(d), :] = (grow[mine(d), :].astype(F32) * score).astype(BF)
        step = 256

        def body(t, dscore):
            c = pl.ds(pl.multiple_of(t * step, step), step)
            c2 = pl.ds(pl.multiple_of(fh_n + t * step, step), step)
            gate = mm(frow[mine(d), :], wguh[:, c]).astype(BF).astype(F32)
            up = mm(frow[mine(d), :], wguh[:, c2]).astype(BF).astype(F32)
            act, slope = gelu_parts(gate)
            middle = (act * up).astype(BF)
            raw = dmh[mine(d), c]
            grad_mid = raw * score
            midh[mine(d), c] = middle
            dguh[mine(d), c] = (grad_mid * up * slope).astype(BF)
            dguh[mine(d), c2] = (grad_mid * act).astype(BF)
            return dscore + row_sum(middle.astype(F32) * raw)

        dscore = lax.fori_loop(0, fh_n // step, body, jnp.zeros((slots, 1), F32))
        pre = dscore * score * (1.0 - score)
        cols[PREF, mine(d), :] = pre
        backr[mine(d), :] = (mmt(dguh[mine(d), :], wguh[...]) + pre * router_f).astype(BF)

    for d in range(docs):

        @step("fh%d" % d)
        def _(d=d):
            if d == 0:
                for name in ("gh", "uh"):
                    loads[name].wait()
            ffn_heavy(d)


    def ffn_light(d, h):
        r = pl.ds(h * half, half)
        gu = mm(fl[d, r, :], wgul[...]).astype(BF)
        gate = gu[:, 0:fl_n].astype(F32)
        up = gu[:, fl_n : 2 * fl_n].astype(F32)
        act, slope = gelu_parts(gate)
        mid[d, r, :] = (act * up * valid_rows(d, h * half, half)).astype(BF)
        grad_mid = dm[d, r, :]
        dgu[d, r, 0:fl_n] = (grad_mid * up * slope).astype(BF)
        dgu[d, r, fl_n : 2 * fl_n] = (grad_mid * act).astype(BF)
        value = mmt(dgu[d, r, :], wgul[...]) + mm(pqkt[d, r, 0:slots], backr[mine(d), :])
        parts[d, r, :] = value.astype(BF)
        ar_start(1, d, h)

    for d in range(docs):
        for h in range(2):

            @step("fl%d%d" % (d, h))
            def _(d=d, h=h):
                if d == 0 and h == 0:
                    for name in ("gl", "ul"):
                        loads[name].wait()
                ffn_light(d, h)

            for a in (1, 2):
                for i in range(1, 5):

                    @step("ar%d%d%d_%d" % (a, d, h, i))
                    def _(a=a, d=d, h=h, i=i):
                        ar_step(a, d, h, i, tot2)

    pieces = (
        (g_h, 0, fh_n), (g_h, fh_n, fh_n), (g_h, 2 * fh_n, fh_n), (g_l, 0, 3 * fl_n),
        (g_a, 0, wl + 512), (g_a, wl + 512, 3 * wl + 640),
    )
    packed_at = [sum(piece[2] for piece in pieces[:p]) for p in range(len(pieces))]

    def chunk_rows(zz, cc):
        return pl.ds(pl.multiple_of(chunk * (2 * zz + cc), chunk), chunk)

    def chunk_of(p, zz, cc):
        grad, base, wide = pieces[p]
        return grad.at[chunk_rows(zz, cc), pl.ds(base, wide)]

    def rs_start(p, t):
        for zz in (2 * t, 2 * t + 1):
            late.append(send(
                chunk_of(p, zz, 1 - core), ra[p].at[zz], wa_s.at[p, zz], wa_r.at[p, zz], sibling
            ))

    def add_chunk(p, zz, other):
        grad, base, wide = pieces[p]

        def add_body(t, carry):
            r = pl.ds(pl.multiple_of(chunk * (2 * zz + core) + 16 * t, 16), 16)
            value = grad[r, base : base + wide].astype(F32)
            value = value + other[pl.ds(pl.multiple_of(16 * t, 16), 16), :].astype(F32)
            grad[r, base : base + wide] = value.astype(BF)
            return carry

        lax.fori_loop(0, chunk // 16, add_body, 0)

    def rs_direct(p, k, when):
        late.append((when, send(
            chunk_of(p, zpeer(k), core), rb[p].at[k - 1], wz_s.at[p, k - 1], wz_r.at[p, k - 1],
            same_core(k), when,
        )))

    def rs_own(p, k):
        zz = zpeer(k)
        arrived(ra[p].at[zz], wa_s.at[p, zz], wa_r.at[p, zz], sibling)
        add_chunk(p, zz, ra[p].at[zz])

    def rs_far(p):
        k = 1 + 2 * low_side
        rs_own(p, k)
        neighbour = (b, 2 * (z + 2 * low_side - 1) + core)
        late.append((at_end, send(
            chunk_of(p, zpeer(k), core), rl[p], rl_s.at[p], rl_r.at[p], neighbour, at_end
        )))
        rs_direct(p, k, inner)

    def rs_two(p):
        rs_own(p, 2)
        rs_direct(p, 2, at_end)

    def rs_near(p):
        k = 3 - 2 * low_side
        rs_own(p, k)
        rs_direct(p, k, z >= 0)

    def rs_relay(p):
        @pl.when(inner)
        def _():
            arrived(rl[p], rl_s.at[p], rl_r.at[p], same_core(1))
            add_chunk(p, zpeer(2), rl[p])

        rs_direct(p, 2, inner)

    for p in range(len(pieces)):
        steps["rs%da" % p] = functools.partial(rs_far, p)
        steps["rs%db" % p] = functools.partial(rs_two, p)
        steps["rs%dc" % p] = functools.partial(rs_near, p)
        steps["rs%dd" % p] = functools.partial(rs_own, p, nz)
        steps["rs%dr" % p] = functools.partial(rs_relay, p)

    def rs_end(p):
        grad, base, wide = pieces[p]
        for k, when in ((1, z > 0), (2, z >= 0), (3, z < nz - 1)):

            @pl.when(when)
            def _(k=k):
                arrived(rb[p].at[k - 1], wz_s.at[p, k - 1], wz_r.at[p, k - 1], same_core(nz - k))

        at = packed_at[p]

        def add_body(t, carry):
            r = pl.ds(pl.multiple_of(16 * t, 16), 16)
            value = grad[pl.ds(pl.multiple_of(chunk * s + 16 * t, 16), 16), base : base + wide].astype(F32)
            for k in range(1, nz):
                value = value + rb[p][k - 1, r, :].astype(F32)
            packed[r, at : at + wide] = value
            return carry

        lax.fori_loop(0, chunk // 16, add_body, 0)
        leave(packed.at[:, at : at + wide], pack_o.at[:, at : at + wide], 7 + p)

    @step("blank")
    def _():
        @pl.when(z == 0)
        def _():
            for buf in rb:
                buf[0] = jnp.zeros(buf.shape[1:], BF)

        @pl.when(z == nz - 1)
        def _():
            for buf in rb:
                buf[2] = jnp.zeros(buf.shape[1:], BF)

    def half_features(t):
        return slice(t * (width // 2), (t + 1) * (width // 2))

    def heavy_ffn_grads(t, p):
        size = 512
        f = half_features(t)
        src, gr, first = ((frow, dguh, 0), (frow, dguh, fh_n), (ghr, midh, 0))[p]
        left_t = src[:, f].T

        def body(i, carry):
            c = pl.ds(pl.multiple_of(first + i * size, size), size)
            o = pl.ds(pl.multiple_of(p * fh_n + i * size, size), size)
            g_h[f, o] = mm(left_t, gr[:, c]).astype(BF)
            return carry

        lax.fori_loop(0, fh_n // size, body, 0)

    def light_grad(t, src, gr, ref, base):
        f = half_features(t)
        wide = gr.shape[2]
        value = tmm(src[:, :, f].reshape(docs * rows, width // 2), gr[...].reshape(docs * rows, wide))
        ref[f, base : base + wide] = value.astype(BF)

    def rows_grad(t, src, gr, at):
        g_a[half_features(t), at : at + wh] = tmm(src[:, half_features(t)], gr).astype(BF)

    def early_grads(t):
        light_grad(t, ghb, loall.at[b], g_a, 0)
        rows_grad(t, gah, hoall[b, :, 0:wh], wl)
        rows_grad(t, hin, dqh[:, 0:wh], wl + 256)

    def late_grads(t):
        f = half_features(t)
        at = wl + 512
        light_grad(t, nl, dqkv, g_a, at)
        rows_grad(t, kin, dkvh[:, 0:wh], at + 3 * wl)
        rows_grad(t, sin, dkvh[:, 256 : 256 + wh], at + 3 * wl + 256)
        lane = lax.broadcasted_iota(jnp.int32, (docs * slots, 128), 1)
        vectors = jnp.zeros((width // 2, 128), F32)
        for src, which, at_lane in ((hin, PREQ, 1), (kin, PREK, 2), (frow, PREF, 4)):
            vectors = vectors + tmm(src[:, f], jnp.where(lane == at_lane, cols[which], 0.0).astype(BF))
        at = at + 3 * wl + 512
        g_a[f, at : at + 128] = vectors.astype(BF)

    for t in range(2):

        for p in range(3):

            @step("hgr%s%d" % ("AB"[t], p))
            def _(t=t, p=p):
                heavy_ffn_grads(t, p)
                rs_start(p, t)

        @step("lg" + "AB"[t])
        def _(t=t):
            light_grad(t, fl, dgu, g_l, 0)
            light_grad(t, cot, mid, g_l, 2 * fl_n)
            rs_start(3, t)

        @step("awg" + "AB"[t])
        def _(t=t):
            early_grads(t)
            rs_start(4, t)

        @step("aqg" + "AB"[t])
        def _(t=t):
            late_grads(t)
            rs_start(5, t)

    def mixed_terms(d):
        def body(j, carry):
            w = pl.ds(pl.multiple_of(j * share, share), share)
            heavy = (mmt(midh[mine(d), :], wdh[w, :]) * cols[SF, mine(d), :]).astype(BF)
            value = mmt(wdl[w, :], mid[d]) + tmm(heavy, pqk[d, 0:slots, :])
            mixb[j, d] = value.astype(BF)
            return carry

        lax.fori_loop(0, 4, body, 0)

    def mixed_start(d):
        column = lax.broadcasted_iota(jnp.int32, (share, width), 1) - b * share
        own = jnp.where(column == lax.broadcasted_iota(jnp.int32, (share, width), 0), 1.0, 0.0).astype(BF)
        mixa[d] = mmt(own, tok[d]) + mmt(own, tot1[d]) + mixb[b, d].astype(F32)

    def hidden_grad(d, h):
        def body(t):
            r = pl.ds(pl.multiple_of(h * half + t, big), big)
            unit = hidden_rows(d, r) * invf[d, r, :]
            w = tot2[d, r, :].astype(F32) * gain_f
            inner = row_sum(w * unit) * (1.0 / width)
            value = cot[d, r, :].astype(F32) + invf[d, r, :] * (w - unit * inner)
            ghf[d, r, :] = value
            ghb[d, r, :] = value.astype(BF)

        tiles(half, big, body)

    def heavy_back(d):
        picked = mm(pqk[d, 0:slots, :], ghb[d])
        score = cols[SQ, mine(d), :]
        gah[mine(d), :] = (picked * score).astype(BF)
        raw = mmt(picked.astype(BF), woha[b])
        pre = row_sum(hoall[b, mine(d), 0:wh].astype(F32) * raw) * score * (1.0 - score)
        cols[PREQ, mine(d), :] = pre
        dox[mine(d), 0:wh] = (raw * score).astype(BF)
        dox[mine(d), wh:256] = jnp.zeros((slots, 256 - wh), BF)
        do3 = three_heads(dox[mine(d), :])
        pf = ph[d].astype(F32)
        dp = mmt(do3, keys_of(d, 256))
        delta = row_sum(dp * pf)
        doall[s, mine(d), 0:wh] = dox[mine(d), 0:wh]
        doall[s, mine(d), wh:256] = spread(-delta)
        gather_start(2 + d, doall, routed(d))
        ds = (pf * (dp - delta) * HD ** (-0.5)).astype(BF)
        dqh[mine(d), :] = one_of_three(mm(ds, keys_of(d, 0))).astype(BF)

    def heavy_back_keys(d):
        q = qall[:, mine(d), :].reshape(n_seq * slots, 256)
        do = doall[:, mine(d), :].reshape(n_seq * slots, 256)
        live = jnp.concatenate([alive(d, 1)] * (wh // HD), axis=0) > 0
        p = jnp.exp(jnp.where(live, mmt(own_keys(d, 0), q) * HD ** (-0.5), masked_value))
        ds = (p * mmt(own_keys(d, 256), do) * HD ** (-0.5)).astype(BF)
        dkvh[mine(d), 0:256] = one_of_three(mm(ds, q)).astype(BF)
        dkvh[mine(d), 256:512] = one_of_three(mm(p.astype(BF), do)).astype(BF)

    def light_back(d):
        dkvw[d] = jnp.zeros((rows + 2 * radius, 2 * wl), F32)

        def dol_body(t):
            r = pl.ds(t, half)
            dol[d, r, :] = (mm(ghb[d, r, :], wola[b]) * valid_rows(d, t, half)).astype(BF)

        tiles(rows, half, dol_body)

        def body(i, carry):
            at = pl.multiple_of(i * blk, blk)
            q2 = two_heads(qbuf[d, pl.ds(at, blk), :])
            do2 = two_heads(dol[d, pl.ds(at, blk), :])
            k = kvw[d, pl.ds(at, span), 0:wl]
            v = kvw[d, pl.ds(at, span), wl : 2 * wl]
            p = pbuf[d * n_blk + i]
            pf = p.astype(F32)
            dp = mmt(do2, v)
            ds = (pf * (dp - row_sum(dp * pf)) * HD ** (-0.5)).astype(BF)
            dqkv[d, pl.ds(at, blk), 0:wl] = one_of_two(mm(ds, k)).astype(BF)
            dkvw[d, pl.ds(at, span), 0:wl] += tmm(ds, q2)
            dkvw[d, pl.ds(at, span), wl : 2 * wl] += tmm(p, do2)
            return carry

        lax.fori_loop(0, n_blk, body, 0)
        rims[d, 0] = dkvw[d, 0:radius, :].astype(BF)
        rims[d, 1] = dkvw[d, rows + radius : rows + 2 * radius, :].astype(BF)

        @pl.when(s == 0)
        def _():
            rimr[d, 0] = jnp.zeros((radius, 2 * wl), BF)

        @pl.when(s == last)
        def _():
            rimr[d, 1] = jnp.zeros((radius, 2 * wl), BF)

        late.append((s > 0, send(rims.at[d, 0], rimr.at[d, 1], rim_s.at[d, 0], rim_r.at[d, 0], left, s > 0)))
        late.append((s < last, send(rims.at[d, 1], rimr.at[d, 0], rim_s.at[d, 1], rim_r.at[d, 1], right, s < last)))

    def rim_wait(d):
        @pl.when(s < last)
        def _():
            arrived(rimr.at[d, 1], rim_s.at[d, 0], rim_r.at[d, 0], right)

        @pl.when(s > 0)
        def _():
            arrived(rimr.at[d, 0], rim_s.at[d, 1], rim_r.at[d, 1], left)

    def attention_back_rows(d):
        heavy_back_keys(d)
        ds_in = mm(dkvh[mine(d), 256 : 256 + wh], whv[...])
        score = cols[SK, mine(d), :]
        pre_k = row_sum(ds_in * kin[mine(d), :].astype(F32)) * score * (1.0 - score)
        cols[PREK, mine(d), :] = pre_k
        key_rows = mm(dkvh[mine(d), 0:wh], whk[...]) + ds_in * score + pre_k * router_k
        query_rows = mm(dqh[mine(d), 0:wh], whq[...]) + cols[PREQ, mine(d), :] * router_q
        bothr[d, 0:slots, :] = query_rows.astype(BF)
        bothr[d, slots : 2 * slots, :] = key_rows.astype(BF)

    def attention_back_terms(d, h):
        if h == 0:
            rim_wait(d)
            dkvw[d, radius : 2 * radius, :] += rimr[d, 0].astype(F32)
            dkvw[d, rows : rows + radius, :] += rimr[d, 1].astype(F32)
            ar_sent(1, d)
        r = pl.ds(h * half, half)
        dqkv[d, r, wl : 3 * wl] = dkvw[d, pl.ds(h * half + radius, half), :].astype(BF)
        value = mmt(dqkv[d, r, :], wqkv[...]) + mm(pqkt[d, r, :], bothr[d])
        parts[d, r, :] = value.astype(BF)
        ar_start(2, d, h)

    out_copies = []

    def leave(src, dst, i):
        copy = pltpu.make_async_copy(src, dst, out_s.at[i])
        copy.start()
        out_copies.append(copy)

    def token_grad(d, h):
        def body(t):
            r = pl.ds(pl.multiple_of(h * half + t, big), big)
            inv = inva[d, r, :]
            unit = tok[d, r, :].astype(F32) * inv
            w = tot2[d, r, :].astype(F32) * gain_a
            inner = row_sum(w * unit) * (1.0 / width)
            ghf[d, r, :] = ghf[d, r, :] + inv * (w - unit * inner)

        tiles(half, big, body)
        r = pl.ds(h * half, half)
        leave(ghf.at[d, r], gt_o.at[d, r], 3 + 2 * d + h)

    for d in range(docs):

        @step("mixt%d" % d)
        def _(d=d):
            mixed_terms(d)

        @step("mx%d" % d)
        def _(d=d):
            for k in range(1, 4):
                to = (b + k) % 4
                late.append(send(
                    mixb.at[to, d], mixr.at[k - 1, d], mx_s.at[d, k - 1], mx_r.at[d, k - 1], (to, s)
                ))

        @step("mixs%d" % d)
        def _(d=d):
            mixed_start(d)

        @step("mixf%d" % d)
        def _(d=d):
            for k in range(1, 4):
                frm = (b + 4 - k) % 4
                arrived(mixr.at[k - 1, d], mx_s.at[d, k - 1], mx_r.at[d, k - 1], (frm, s))

            def mix_body(t, d=d):
                r = pl.ds(t, 32)
                value = mixa[d, r, :]
                for k in range(3):
                    value = value + mixr[k, d, r, :].astype(F32)
                mixa[d, r, :] = value

            tiles(share, 32, mix_body)
            leave(mixa.at[d], mix_o.at[d], 1 + d)

        for h in range(2):

            @step("hg%d%d" % (d, h))
            def _(d=d, h=h):
                hidden_grad(d, h)

            @step("abt%d%d" % (d, h))
            def _(d=d, h=h):
                attention_back_terms(d, h)

            @step("tok%d%d" % (d, h))
            def _(d=d, h=h):
                token_grad(d, h)

        @step("hb%d" % d)
        def _(d=d):
            heavy_back(d)

        @step("lb%d" % d)
        def _(d=d):
            light_back(d)

        @step("hk%d" % d)
        def _(d=d):
            if d == 0:
                gather_end(1, qall, every)
            gather_end(2 + d, doall, routed(d))
            attention_back_rows(d)

    vlane = lax.broadcasted_iota(jnp.int32, (chunk, 128), 1)
    eye = lax.broadcasted_iota(jnp.int32, (chunk, width), 1) - chunk * s
    eye = eye == lax.broadcasted_iota(jnp.int32, (chunk, width), 0)

    def own_column(row):
        return row_sum(jnp.where(eye, row, 0.0))

    for p in range(len(pieces)):
        steps["rs%de" % p] = functools.partial(rs_end, p)

    @step("gains")
    def _():
        for name in ("gk", "uk"):
            loads[name].wait()
        total = row_sum(packed[:, 0 : 2 * fh_n] * wkeep[...].astype(F32))
        vbuf[:, 0:1] = total + row_sum(
            packed[:, packed_at[3] : packed_at[3] + 2 * fl_n] * wgul[own_rows, :].astype(F32)
        )

    @step("vec")
    def _():
        a_at, q_at = packed_at[4:6]
        va = q_at + 3 * wl + 512
        gf_sum = vbuf[:, 0:1]
        ga_sum = row_sum(packed[:, q_at : q_at + 3 * wl] * wqkv[own_rows, :].astype(F32))
        eye_b = eye.astype(F32).astype(BF)
        for h_at, w in ((a_at + wl + 256, whq), (q_at + 3 * wl, whk), (q_at + 3 * wl + 256, whv)):
            ga_sum = ga_sum + row_sum(packed[:, h_at : h_at + wh] * mmt(eye_b, w[...]))
        vectors = packed[:, va : va + 128]

        def lane_of(i):
            return row_sum(jnp.where(vlane == i, vectors, 0.0))

        ga_sum = ga_sum + own_column(router_q) * lane_of(1) + own_column(router_k) * lane_of(2)
        gf_sum = gf_sum + own_column(router_f) * lane_of(4)
        vectors = jnp.where(vlane == 0, ga_sum / own_column(gain_a), vectors)
        vectors = jnp.where(vlane == 3, gf_sum / own_column(gain_f), vectors)
        vbuf[...] = vectors
        for k in range(1, 4):
            late.append(send(vbuf, vr.at[k - 1], v_s.at[k - 1], v_r.at[k - 1], ((b + k) % 4, s)))

    @step("vece")
    def _():
        for k in range(1, 4):
            arrived(vr.at[k - 1], v_s.at[k - 1], v_r.at[k - 1], ((b + 4 - k) % 4, s))
        vect[...] = (vbuf[...] + vr[0] + vr[1] + vr[2]).T
        leave(vect, vec_o, 0)

    for name in ORDER:
        steps[name]()

    for entry in late:
        if isinstance(entry, tuple):
            pl.when(entry[0])(entry[1].wait_send)
        else:
            entry.wait_send()
    for d in range(docs):
        ar_sent(2, d)
    for copy in out_copies:
        copy.wait()


def kernel_scratch(docs, rows, width, slots, n_seq, wl, wh, fl_n, fh_n):
    nz = n_seq // 2
    chunk = width // n_seq
    routed = docs * slots
    keys = n_seq * slots
    pad = -(-wh // 256) * 256
    ga_n = 4 * wl + 4 * pad + 128
    widths = [fh_n, fh_n, fh_n, 3 * fl_n, wl + 512, 3 * wl + 640]
    h_n, l_n = 3 * fh_n, 3 * fl_n
    radius = WINDOW // 2
    span = rows + 2 * radius
    vmem = [
        ((docs, rows, width), BF), ((docs, rows, width), BF), ((width, 3 * wl), BF), ((4, width, wl), BF),
        ((wh, width), BF), ((wh, width), BF), ((wh, width), BF), ((4, wh, width), BF),
        ((width, 2 * fl_n), BF), ((width, fl_n), BF), ((width, 2 * fh_n), BF), ((width, fh_n), BF),
        ((chunk, 2 * fh_n), BF),
        ((docs, rows, width), BF), ((docs, rows, 1), F32), ((routed, width), BF), ((routed, width), BF),
        ((routed, width), BF), ((docs, rows, wl), BF), ((docs, span, 2 * wl), BF),
        ((docs * rows // WINDOW, 2 * WINDOW, 2 * WINDOW), BF), ((4, docs, rows, wl), BF), ((routed, pad), BF),
        ((n_seq, routed, 2 * pad), BF), ((docs, wh // HD * slots, keys), BF), ((4, routed, pad), BF),
        ((n_seq, routed, pad), BF), ((n_seq, routed, pad), BF), ((routed, width), BF), ((routed, width), BF),
        ((docs, 2 * slots, width), BF),
        ((docs, 2 * slots, rows), BF), ((docs, rows, 2 * slots), BF), ((docs, rows, width), BF),
        ((docs, rows, width), BF), ((docs, rows, width), BF), ((docs, 2, rows // 4, width), BF),
        ((docs, 2, rows // 8, width), BF), ((6, routed, 1), F32),
        ((docs, rows, fl_n), F32), ((routed, fh_n), F32), ((routed, width), BF), ((docs, rows, width), BF),
        ((docs, rows, 1), F32), ((docs, rows, fl_n), BF), ((docs, rows, 2 * fl_n), BF), ((routed, width), BF),
        ((routed, width), BF), ((routed, fh_n), BF), ((routed, 2 * fh_n), BF),
        ((4, docs, width // 4, rows), BF), ((3, docs, width // 4, rows), BF), ((docs, width // 4, rows), F32),
        ((docs, rows, width), F32), ((docs, rows, width), BF), ((docs, rows, wl), BF), ((routed, pad), BF),
        ((routed, width), BF), ((routed, pad), BF), ((docs, span, 2 * wl), F32),
        ((docs, 2, radius, 2 * wl), BF), ((docs, 2, radius, 2 * wl), BF), ((docs, rows, 3 * wl), BF),
        ((routed, 2 * pad), BF),
        ((width, h_n), BF), ((width, l_n), BF),
        *[((nz, chunk, wide), BF) for wide in widths],
        *[((nz - 1, chunk, wide), BF) for wide in widths],
        *[((chunk, wide), BF) for wide in widths],
        ((chunk, h_n + l_n + ga_n), F32), ((chunk, 128), F32), ((3, chunk, 128), F32), ((128, chunk), F32),
    ]
    sems = [
        (18,), (3, 2), (3, 2), (3, 2), (3, 2), (docs, 3), (docs, 3), (3,), (3,),
        (3, docs, 2, 4), (3, docs, 2, 4), (2 + docs, nz), (2 + docs, nz), (2 + docs, nz), (2 + docs, nz),
        (docs, 2), (docs, 2), (docs, 2), (docs, 2), (docs, 3), (docs, 3),
        (6, nz), (6, nz), (6, nz - 1), (6, nz - 1), (6,), (6,), (3,), (3,), (13,),
    ]
    total = 0
    for shape, kind in vmem:
        lanes = -(-shape[-1] // 128) * 128
        total += math.prod(shape[:-1]) * lanes * jnp.dtype(kind).itemsize
    return vmem, sems, total


def shards(sizes, *args):
    (tokens, cotangent, lengths, query_index, key_index, gain_attn, router_query, router_key, wq_light,
     wk_light, wv_light, wo_light, wq_heavy, wk_heavy, wv_heavy, wo_heavy, gain_ffn, router_ffn,
     gate_light, up_light, down_light, gate_heavy, up_heavy, down_heavy) = args
    n_seq = sizes["seq"]
    docs, rows, width = tokens.shape
    slots = query_index.shape[1]
    wl, wh = wq_light.shape[1], wq_heavy.shape[1]
    fl_n, fh_n = gate_light.shape[1], gate_heavy.shape[1]
    dims = (docs, rows, width, slots, n_seq, wl, wh, fl_n, fh_n)
    vmem, sems, total = kernel_scratch(*dims)
    fits = (
        total <= 62 * 2**20
        and sizes["branch"] == 4
        and n_seq == 8
        and width % (16 * n_seq) == 0
        and wl == 2 * HD
        and wh == 3 * HD
        and slots % 16 == 0
        and rows % 256 == 0
    )
    if not fits:
        return plain_shards(*args)
    share = width // 4
    chunk = width // n_seq
    ga_n = 4 * wl + 4 * 256 + 128
    pack_n = 3 * fh_n + 3 * fl_n + ga_n
    in_hbm = [
        tokens, cotangent, wq_light, wk_light, wv_light, wo_light, wq_heavy.T, wk_heavy.T, wv_heavy.T, wo_heavy.T,
        gate_light, up_light, down_light, gate_heavy, up_heavy, down_heavy,
    ]
    whole = pl.BlockSpec(memory_space=pltpu.VMEM)
    outside = pl.BlockSpec(memory_space=pl.ANY)
    grad_tokens, mix, packed, vectors = pl.pallas_call(
        functools.partial(layer_kernel, dims),
        out_shape=[
            jax.ShapeDtypeStruct((docs, rows, width), F32),
            jax.ShapeDtypeStruct((docs, share, rows), F32),
            jax.ShapeDtypeStruct((chunk, pack_n), F32),
            jax.ShapeDtypeStruct((128, chunk), F32),
        ],
        in_specs=[pl.BlockSpec(memory_space=pltpu.SMEM)] + [whole] * 7 + [outside] * 16,
        out_specs=[outside] * 4,
        scratch_shapes=[pltpu.VMEM(shape, kind) for shape, kind in vmem]
        + [pltpu.SemaphoreType.DMA(shape) for shape in sems],
        compiler_params=pltpu.CompilerParams(
            collective_id=0, has_side_effects=True, vmem_limit_bytes=64 * 2**20 - 2**16
        ),
    )(lengths, query_index, key_index, gain_attn, router_query, router_key, gain_ffn, router_ffn, *in_hbm)

    l_at = 3 * fh_n
    a_at = l_at + 3 * fl_n
    q_at = a_at + wl + 512
    parts = [(q_at + i * wl, wl) for i in range(3)] + [(a_at, wl)]
    parts += [(a_at + wl + 256, wh), (q_at + 3 * wl, wh), (q_at + 3 * wl + 256, wh), (a_at + wl, wh)]
    parts += [(l_at + i * fl_n, fl_n) for i in range(3)] + [(i * fh_n, fh_n) for i in range(3)]
    outs = pl.pallas_call(
        functools.partial(hand_out, parts),
        out_shape=[jax.ShapeDtypeStruct(grad_tokens.shape, F32), jax.ShapeDtypeStruct(mix.shape, F32)]
        + [jax.ShapeDtypeStruct((chunk, wide), F32) for at, wide in parts],
        in_specs=[pl.BlockSpec(memory_space=pltpu.HBM)] * 3,
        out_specs=[outside] * 2 + [outside if wide % 128 == 0 else whole for at, wide in parts],
        scratch_shapes=[
            pltpu.SemaphoreType.DMA((3 + docs,)), pltpu.SemaphoreType.DMA((1 + docs + len(parts),)),
            pltpu.VMEM(grad_tokens.shape, F32), pltpu.VMEM(mix.shape, F32), pltpu.VMEM(packed.shape, F32),
        ],
        compiler_params=pltpu.CompilerParams(vmem_limit_bytes=60 * 2**20),
    )(grad_tokens, mix, packed)
    grad_tokens, mix = outs[:2]
    mixed = jnp.swapaxes(mix, 1, 2)
    vec = [vectors[i] for i in range(5)]
    return (mixed, grad_tokens, *vec[:3], *outs[2:10], *vec[3:], *outs[10:])


def hand_out(parts, tokens_in, mix_in, packed_in, tokens_out, mix_out, *rest):
    in_sems, out_sems, tokens, mix, packed = rest[-5:]
    docs = tokens.shape[0]
    arriving = [pltpu.make_async_copy(packed_in, packed, in_sems.at[0])]
    arriving += [pltpu.make_async_copy(tokens_in.at[d], tokens.at[d], in_sems.at[1 + d]) for d in range(docs)]
    arriving += [pltpu.make_async_copy(mix_in, mix, in_sems.at[1 + docs])]
    for copy in arriving:
        copy.start()
    leaving = [pltpu.make_async_copy(mix, mix_out, out_sems.at[0])]
    leaving += [pltpu.make_async_copy(tokens.at[d], tokens_out.at[d], out_sems.at[1 + d]) for d in range(docs)]
    arriving[0].wait()
    for i, (at, wide) in enumerate(parts):
        if wide % 128 == 0:
            copy = pltpu.make_async_copy(packed.at[:, at : at + wide], rest[i], out_sems.at[1 + docs + i])
            copy.start()
            leaving.append(copy)
    for d in range(docs):
        arriving[1 + d].wait()
        leaving[1 + d].start()
    arriving[1 + docs].wait()
    leaving[0].start()
    for i, (at, wide) in enumerate(parts):
        if wide % 128 != 0:
            rest[i][...] = packed[:, at : at + wide]
    for copy in leaving:
        copy.wait()


def solution(mesh):
    return jax.shard_map(
        functools.partial(shards, dict(mesh.shape)),
        mesh=mesh,
        in_specs=(
            P(None, "seq", None),
            P(None, "seq", None),
            P(),
            P(None, "seq"),
            P(None, "seq"),
            P(),
            P(),
            P(),
            P(None, "branch"),
            P(None, "branch"),
            P(None, "branch"),
            P(None, "branch"),
            P(None, "branch"),
            P(None, "branch"),
            P(None, "branch"),
            P(None, "branch"),
            P(),
            P(),
            P(None, "branch"),
            P(None, "branch"),
            P(None, "branch"),
            P(None, "branch"),
            P(None, "branch"),
            P(None, "branch"),
        ),
        out_specs=(
            P(None, "seq", "branch"),
            P(None, "seq", None),
            P("seq"),
            P("seq"),
            P("seq"),
            P("seq", "branch"),
            P("seq", "branch"),
            P("seq", "branch"),
            P("seq", "branch"),
            P("seq", "branch"),
            P("seq", "branch"),
            P("seq", "branch"),
            P("seq", "branch"),
            P("seq"),
            P("seq"),
            P("seq", "branch"),
            P("seq", "branch"),
            P("seq", "branch"),
            P("seq", "branch"),
            P("seq", "branch"),
            P("seq", "branch"),
        ),
        check_vma=False,
    )
```

```python
import functools
import math

import jax
import jax.numpy as jnp
from jax import lax
from jax.experimental import pallas as pl
from jax.experimental.pallas import tpu as pltpu
from jax.sharding import PartitionSpec as P

HD = 64
WINDOW = 128


highest = lax.Precision.HIGHEST
masked_value = -1000000000.0
epsilon = 1e-06


def with_halo(cells, sides, width):
    for axis, dim in sides:
        count = lax.axis_size(axis)
        ends = count - 1
        head = lax.slice_in_dim(cells, 0, width, axis=dim)
        tail = lax.slice_in_dim(cells, cells.shape[dim] - width, cells.shape[dim], axis=dim)
        cells = jnp.concatenate(
            [
                lax.ppermute(tail, axis, [(i, (i + 1) % count) for i in range(ends)]),
                cells,
                lax.ppermute(head, axis, [((i + 1) % count, i) for i in range(ends)]),
            ],
            axis=dim,
        )
    return cells


def project(operand, matrix):
    return jnp.einsum("dsc,ch->dsh", operand, matrix, preferred_element_type=jnp.float32)


def unproject(operand, matrix):
    return jnp.einsum("dsh,ch->dsc", operand, matrix, preferred_element_type=jnp.float32)


def weight_grad(operand, gradient):
    return jnp.einsum("dsc,dsh->ch", operand, gradient, preferred_element_type=jnp.float32)


def pick_rows(selector, values):
    return jnp.einsum("drs,dsc->drc", selector, values, precision=highest)


def put_rows(selector, values):
    return jnp.einsum("drs,drc->dsc", selector, values, precision=highest)


def pick_scalar(selector, values):
    return jnp.einsum("drs,ds->dr", selector, values, precision=highest)


def put_scalar(selector, values):
    return jnp.einsum("drs,dr->ds", selector, values, precision=highest)


def split_heads(values):
    return values.reshape(values.shape[0], values.shape[1], -1, HD)


def attention_scores(queries, keys, mask_bias):
    raw_scores = jnp.einsum("dqhe,dkhe->dhqk", queries, keys, preferred_element_type=jnp.float32)
    return raw_scores * HD ** (-0.5) + mask_bias


def forward_attention(queries, keys, values, mask_bias):
    scores = attention_scores(queries, keys, mask_bias)
    highest_score = jnp.max(scores, axis=-1, keepdims=True)
    exponent = jnp.exp(scores - highest_score)
    totals = jnp.sum(exponent, axis=-1, keepdims=True)
    probs_low = (exponent / totals).astype(jnp.bfloat16)
    result = jnp.einsum("dhqk,dkhe->dqhe", probs_low, values, preferred_element_type=jnp.float32)
    result = result.reshape(result.shape[0], result.shape[1], -1).astype(jnp.bfloat16)
    return (result, highest_score + jnp.log(totals))


def score_grads(queries, keys, values, mask_bias, logsum, grad_out, row_delta):
    probs = jnp.exp(attention_scores(queries, keys, mask_bias) - logsum)
    grad_probs = jnp.einsum("dqhe,dkhe->dhqk", grad_out, values, preferred_element_type=jnp.float32)
    row_delta = jnp.sum(grad_probs * probs, axis=-1, keepdims=True)
    grad_raw = (probs * (grad_probs - row_delta) * HD ** (-0.5)).astype(jnp.bfloat16)
    return (grad_raw, probs.astype(jnp.bfloat16), row_delta)


def contract_query(grad_raw, keys):
    result = jnp.einsum("dhqk,dkhe->dqhe", grad_raw, keys, preferred_element_type=jnp.float32)
    return result.reshape(result.shape[0], result.shape[1], -1)


def contract_key(grad_raw, queries):
    result = jnp.einsum("dhqk,dqhe->dkhe", grad_raw, queries, preferred_element_type=jnp.float32)
    return result.reshape(result.shape[0], result.shape[1], -1)


def geglu_back(gate_vals, up_vals, grad_mid):
    activated, gelu_pull = jax.vjp(jax.nn.gelu, gate_vals.astype(jnp.float32))
    grad_gate = gelu_pull(grad_mid * up_vals.astype(jnp.float32))[0].astype(jnp.bfloat16)
    grad_up = (grad_mid * activated).astype(jnp.bfloat16)
    return (grad_gate, grad_up)


def geglu(gate_vals, up_vals):
    return (jax.nn.gelu(gate_vals.astype(jnp.float32)) * up_vals.astype(jnp.float32)).astype(
        jnp.bfloat16
    )


def plain_shards(
    tokens,
    cotangent,
    lengths,
    query_index,
    key_index,
    gain_attn,
    router_query,
    router_key,
    wq_light,
    wk_light,
    wv_light,
    wo_light,
    wq_heavy,
    wk_heavy,
    wv_heavy,
    wo_heavy,
    gain_ffn,
    router_ffn,
    gate_light,
    up_light,
    down_light,
    gate_heavy,
    up_heavy,
    down_heavy,
):
    documents, local_len, model_width = tokens.shape
    radius = WINDOW // 2
    block_rows = math.gcd(local_len, 512)
    key_span = block_rows + 2 * radius
    offset = lax.axis_index("seq") * local_len
    positions = offset + jnp.arange(local_len, dtype=jnp.int32)
    valid_rows = (positions[None, :] < lengths[:, None]).astype(jnp.float32)[:, :, None]
    pick_query = (query_index[:, :, None] == positions[None, None, :]).astype(jnp.float32)
    pick_key = (key_index[:, :, None] == positions[None, None, :]).astype(jnp.float32)
    inputs = tokens.astype(jnp.float32)
    inv_attn = lax.rsqrt(jnp.mean(inputs * inputs, axis=-1, keepdims=True) + epsilon)
    unit_attn = inputs * inv_attn
    gain_attn_f = gain_attn.astype(jnp.float32)
    normed = unit_attn * gain_attn_f
    normed_low = normed.astype(jnp.bfloat16)
    light_q = project(normed_low, wq_light).astype(jnp.bfloat16)
    light_k = project(normed_low, wk_light).astype(jnp.bfloat16)
    light_v = project(normed_low, wv_light).astype(jnp.bfloat16)
    light_width = light_q.shape[2]
    rim_block = with_halo(jnp.concatenate([light_k, light_v], axis=2), (("seq", 1),), radius)
    wide_k = split_heads(rim_block[:, :, :light_width])
    wide_v = split_heads(rim_block[:, :, light_width:])
    heads_q = split_heads(light_q)
    key_pos = offset - radius + jnp.arange(local_len + 2 * radius, dtype=jnp.int32)
    in_window = (jnp.abs(positions[:, None] - key_pos[None, :]) <= radius)[None]
    in_window = (
        in_window
        & (key_pos[None, None, :] >= 0)
        & (key_pos[None, None, :] < lengths[:, None, None])
    )
    light_bias = jnp.where(in_window, 0.0, masked_value)[:, None]
    piece_out, piece_lse = forward_attention(heads_q, wide_k, wide_v, light_bias)
    router_query_f = router_query.astype(jnp.float32)
    router_key_f = router_key.astype(jnp.float32)
    score_query = pick_scalar(
        pick_query,
        jax.nn.sigmoid(jnp.einsum("dsc,c->ds", normed, router_query_f, precision=highest)),
    )
    score_key = pick_scalar(
        pick_key, jax.nn.sigmoid(jnp.einsum("dsc,c->ds", normed, router_key_f, precision=highest))
    )
    heavy_in = pick_rows(pick_query, normed).astype(jnp.bfloat16)
    key_rows = pick_rows(pick_key, normed)
    key_in = key_rows.astype(jnp.bfloat16)
    scaled_in = (key_rows * score_key[:, :, None]).astype(jnp.bfloat16)
    heavy_q = project(heavy_in, wq_heavy).astype(jnp.bfloat16)
    heavy_k = project(key_in, wk_heavy).astype(jnp.bfloat16)
    heavy_v = project(scaled_in, wv_heavy).astype(jnp.bfloat16)
    heavy_width = heavy_q.shape[2]
    key_alive = (key_index >= 0).astype(jnp.bfloat16)
    routed_kv, alive_all = (
        lax.all_gather(jnp.concatenate([heavy_k, heavy_v], axis=2), "seq", axis=1, tiled=True),
        lax.all_gather(key_alive, "seq", axis=1, tiled=True),
    )
    all_k = routed_kv[:, :, :heavy_width]
    all_v = routed_kv[:, :, heavy_width:]
    heavy_bias = jnp.where(alive_all > 0, 0.0, masked_value)[:, None, None, :]
    heavy_out, heavy_lse = forward_attention(
        split_heads(heavy_q), split_heads(all_k), split_heads(all_v), heavy_bias
    )
    heavy_proj = unproject(heavy_out, wo_heavy)
    light_attn = unproject(piece_out, wo_light) * valid_rows
    heavy_attn = put_rows(pick_query, heavy_proj * score_query[:, :, None])
    attn_total = lax.psum((light_attn + heavy_attn).astype(jnp.bfloat16), "branch").astype(
        jnp.float32
    )
    hidden = inputs + attn_total
    inv_ffn = lax.rsqrt(jnp.mean(hidden * hidden, axis=-1, keepdims=True) + epsilon)
    unit_ffn = hidden * inv_ffn
    gain_ffn_f = gain_ffn.astype(jnp.float32)
    normed_ffn = unit_ffn * gain_ffn_f
    ffn_low = normed_ffn.astype(jnp.bfloat16)
    gate_l = project(ffn_low, gate_light).astype(jnp.bfloat16)
    up_l = project(ffn_low, up_light).astype(jnp.bfloat16)
    middle_l = geglu(gate_l, up_l)
    light_ffn = unproject(middle_l, down_light) * valid_rows
    router_ffn_f = router_ffn.astype(jnp.float32)
    score_ffn = pick_scalar(
        pick_query,
        jax.nn.sigmoid(jnp.einsum("dsc,c->ds", normed_ffn, router_ffn_f, precision=highest)),
    )
    ffn_rows = pick_rows(pick_query, normed_ffn).astype(jnp.bfloat16)
    gate_h = project(ffn_rows, gate_heavy).astype(jnp.bfloat16)
    up_h = project(ffn_rows, up_heavy).astype(jnp.bfloat16)
    middle_h = geglu(gate_h, up_h)
    heavy_fproj = unproject(middle_h, down_heavy)
    heavy_ffn = put_rows(pick_query, heavy_fproj * score_ffn[:, :, None])
    share = model_width // lax.axis_size("branch")
    own_cols = lax.axis_index("branch") * share
    mixed = lax.dynamic_slice_in_dim(hidden, own_cols, share, 2) + lax.psum_scatter(
        (light_ffn + heavy_ffn).astype(jnp.bfloat16), "branch", scatter_dimension=2, tiled=True
    ).astype(jnp.float32)
    grad_out = cotangent.astype(jnp.float32)
    grad_light = (grad_out * valid_rows).astype(jnp.bfloat16)
    grad_down_light = weight_grad(grad_light, middle_l)
    grad_gate_l, grad_up_l = geglu_back(gate_l, up_l, project(grad_light, down_light))
    grad_gate_light = weight_grad(ffn_low, grad_gate_l)
    grad_up_light = weight_grad(ffn_low, grad_up_l)
    grad_rows = pick_rows(pick_query, grad_out)
    grad_heavy = (grad_rows * score_ffn[:, :, None]).astype(jnp.bfloat16)
    score_ffn_part = jnp.sum(grad_rows * heavy_fproj, axis=-1)
    grad_down_heavy = weight_grad(grad_heavy, middle_h)
    grad_gate_h, grad_up_h = geglu_back(gate_h, up_h, project(grad_heavy, down_heavy))
    grad_gate_heavy = weight_grad(ffn_rows, grad_gate_h)
    grad_up_heavy = weight_grad(ffn_rows, grad_up_h)
    heavy_ffn_rows = unproject(grad_gate_h, gate_heavy) + unproject(grad_up_h, up_heavy)
    ffn_part = (
        unproject(grad_gate_l, gate_light)
        + unproject(grad_up_l, up_light)
        + put_rows(pick_query, heavy_ffn_rows)
    )
    grad_normed_ffn, grad_score_ffn = (
        lax.psum(ffn_part.astype(jnp.bfloat16), "branch").astype(jnp.float32),
        lax.psum(score_ffn_part.astype(jnp.bfloat16), "branch").astype(jnp.float32),
    )
    pre_ffn = put_scalar(pick_query, grad_score_ffn * score_ffn * (1.0 - score_ffn))
    grad_normed_ffn = grad_normed_ffn + pre_ffn[:, :, None] * router_ffn_f
    grad_router_ffn = jnp.einsum("ds,dsc->c", pre_ffn, normed_ffn, precision=highest)
    grad_gain_ffn = jnp.sum(grad_normed_ffn * unit_ffn, axis=(0, 1))
    grad_unit_f = grad_normed_ffn * gain_ffn_f
    grad_hidden = grad_out + inv_ffn * (
        grad_unit_f - unit_ffn * jnp.mean(grad_unit_f * unit_ffn, axis=-1, keepdims=True)
    )
    grad_light_attn = (grad_hidden * valid_rows).astype(jnp.bfloat16)
    grad_wo_light = weight_grad(grad_light_attn, piece_out)
    grad_light_out = split_heads(project(grad_light_attn, wo_light).astype(jnp.bfloat16))
    wide_grad = jnp.zeros((documents, local_len + 2 * radius, 2 * light_width), jnp.float32)
    light_raw, light_plow, unused_delta = score_grads(
        heads_q, wide_k, wide_v, light_bias, piece_lse, grad_light_out, None
    )
    query_pieces = contract_query(light_raw, wide_k)
    key_terms = jnp.concatenate(
        [contract_key(light_raw, heads_q), contract_key(light_plow, grad_light_out)], axis=2
    )
    wide_grad = wide_grad.at[:, 0:key_span].add(key_terms)
    grad_light_q = query_pieces.astype(jnp.bfloat16)
    outer_rims = jnp.concatenate(
        [wide_grad[:, :radius], wide_grad[:, radius + local_len :]], axis=1
    )
    returned = with_halo(outer_rims.astype(jnp.bfloat16), (("seq", 1),), radius).astype(
        outer_rims.dtype
    )
    inner = wide_grad[:, radius : radius + local_len]
    inner = inner + jnp.pad(returned[:, :radius], ((0, 0), (0, local_len - radius), (0, 0)))
    inner = inner + jnp.pad(returned[:, 3 * radius :], ((0, 0), (local_len - radius, 0), (0, 0)))
    grad_light_k = inner[:, :, :light_width].astype(jnp.bfloat16)
    grad_light_v = inner[:, :, light_width:].astype(jnp.bfloat16)
    grad_wq_light = weight_grad(normed_low, grad_light_q)
    grad_wk_light = weight_grad(normed_low, grad_light_k)
    grad_wv_light = weight_grad(normed_low, grad_light_v)
    light_part = (
        unproject(grad_light_q, wq_light)
        + unproject(grad_light_k, wk_light)
        + unproject(grad_light_v, wv_light)
    )
    grad_hrows = pick_rows(pick_query, grad_hidden)
    grad_heavy_attn = (grad_hrows * score_query[:, :, None]).astype(jnp.bfloat16)
    score_query_part = jnp.sum(grad_hrows * heavy_proj, axis=-1)
    grad_wo_heavy = weight_grad(grad_heavy_attn, heavy_out)
    grad_heavy_out = project(grad_heavy_attn, wo_heavy).astype(jnp.bfloat16)
    heavy_raw, heavy_plow, heavy_delta = score_grads(
        split_heads(heavy_q),
        split_heads(all_k),
        split_heads(all_v),
        heavy_bias,
        heavy_lse,
        split_heads(grad_heavy_out),
        None,
    )
    grad_heavy_q = contract_query(heavy_raw, split_heads(all_k)).astype(jnp.bfloat16)
    every_kv = jnp.concatenate(
        [
            contract_key(heavy_raw, split_heads(heavy_q)),
            contract_key(heavy_plow, split_heads(grad_heavy_out)),
        ],
        axis=2,
    )
    own_kv = lax.psum_scatter(every_kv, "seq", scatter_dimension=1, tiled=True)
    grad_heavy_k = own_kv[:, :, :heavy_width].astype(jnp.bfloat16)
    grad_heavy_v = own_kv[:, :, heavy_width:].astype(jnp.bfloat16)
    grad_scaled = unproject(grad_heavy_v, wv_heavy)
    score_key_part = jnp.sum(grad_scaled * key_rows, axis=-1)
    grad_key_rows = unproject(grad_heavy_k, wk_heavy) + grad_scaled * score_key[:, :, None]
    grad_wq_heavy = weight_grad(heavy_in, grad_heavy_q)
    grad_wk_heavy = weight_grad(key_in, grad_heavy_k)
    grad_wv_heavy = weight_grad(scaled_in, grad_heavy_v)
    attn_part = (
        light_part
        + put_rows(pick_query, unproject(grad_heavy_q, wq_heavy))
        + put_rows(pick_key, grad_key_rows)
    )
    grad_normed, grad_score_query, grad_score_key = (
        lax.psum(attn_part.astype(jnp.bfloat16), "branch").astype(jnp.float32),
        lax.psum(score_query_part.astype(jnp.bfloat16), "branch").astype(jnp.float32),
        lax.psum(score_key_part.astype(jnp.bfloat16), "branch").astype(jnp.float32),
    )
    pre_query = put_scalar(pick_query, grad_score_query * score_query * (1.0 - score_query))
    pre_key = put_scalar(pick_key, grad_score_key * score_key * (1.0 - score_key))
    grad_normed = (
        grad_normed + pre_query[:, :, None] * router_query_f + pre_key[:, :, None] * router_key_f
    )
    grad_router_query = jnp.einsum("ds,dsc->c", pre_query, normed, precision=highest)
    grad_router_key = jnp.einsum("ds,dsc->c", pre_key, normed, precision=highest)
    grad_gain_attn = jnp.sum(grad_normed * unit_attn, axis=(0, 1))
    grad_unit_a = grad_normed * gain_attn_f
    grad_tokens = grad_hidden + inv_attn * (
        grad_unit_a - unit_attn * jnp.mean(grad_unit_a * unit_attn, axis=-1, keepdims=True)
    )
    names = (
        grad_wq_light, grad_wk_light, grad_wv_light, grad_wo_light,
        grad_wq_heavy, grad_wk_heavy, grad_wv_heavy, grad_wo_heavy,
        grad_gate_light, grad_up_light, grad_down_light,
        grad_gate_heavy, grad_up_heavy, grad_down_heavy,
    )
    vectors = jnp.stack(
        [grad_gain_attn, grad_router_query, grad_router_key, grad_gain_ffn, grad_router_ffn], axis=1
    )
    packed = jnp.concatenate([g.astype(jnp.bfloat16) for g in names + (vectors,)], axis=1)
    summed = lax.psum_scatter(packed, "seq", scatter_dimension=0, tiled=True).astype(jnp.float32)
    widths = [g.shape[1] for g in names]
    cuts = [sum(widths[:i]) for i in range(len(widths) + 1)]
    (
        grad_wq_light, grad_wk_light, grad_wv_light, grad_wo_light,
        grad_wq_heavy, grad_wk_heavy, grad_wv_heavy, grad_wo_heavy,
        grad_gate_light, grad_up_light, grad_down_light,
        grad_gate_heavy, grad_up_heavy, grad_down_heavy,
    ) = [summed[:, cuts[i] : cuts[i + 1]] for i in range(len(widths))]
    grad_gain_attn, grad_router_query, grad_router_key, grad_gain_ffn, grad_router_ffn = [
        summed[:, cuts[-1] + i] for i in range(5)
    ]
    return (
        mixed,
        grad_tokens,
        grad_gain_attn,
        grad_router_query,
        grad_router_key,
        grad_wq_light,
        grad_wk_light,
        grad_wv_light,
        grad_wo_light,
        grad_wq_heavy,
        grad_wk_heavy,
        grad_wv_heavy,
        grad_wo_heavy,
        grad_gain_ffn,
        grad_router_ffn,
        grad_gate_light,
        grad_up_light,
        grad_down_light,
        grad_gate_heavy,
        grad_up_heavy,
        grad_down_heavy,
    )


ORDER = (
    "load", "rowskv", "norm", "pre0", "qkv", "gp0_2", "la0", "gp0_3", "gp0_1", "pre1", "hattn", "predmh",
    "wgp", "la1", "hproj", "nf00", "nf01", "fh0", "fl00", "fl01", "gp1_2", "nf10", "nf11", "fh1", "hgrB1",
    "ar1011_1", "hgrA1", "fl11", "hgrB0", "ar1001_1", "ar1010_1", "ar1011_2", "rs1a", "rs1b", "rs1c",
    "fl10", "hgrA0", "hgrB2", "ar1011_3", "ar1010_2", "hgrA2", "ar1101_1", "ar1110_1", "lgA", "rs0a",
    "ar1111_1", "rs1r", "ar1100_1", "ar1001_2", "ar1000_1", "ar1111_2", "gp1_3", "lgB", "ar1101_2",
    "ar1000_2", "ar1001_3", "ar1011_4", "rs0b", "ar1111_3", "ar1000_3", "rs2d", "ar1100_2", "ar1010_3",
    "ar1001_4", "ar1101_3", "ar1100_3", "rs2a", "rs0c", "ar1110_2", "ar1000_4", "rs0d", "mixt0", "ar1111_4",
    "rs0r", "ar1110_3", "mixt1", "ar1010_4", "mx1", "gp1_1", "mixs0", "hg01", "hg00", "ar1100_4", "hb0",
    "mx0", "ar1110_4", "lb0", "mixs1", "hg11", "rs2b", "gp2_2", "ar1101_4", "hg10", "hb1", "awgA", "rs3a",
    "gp2_3", "lb1", "awgB", "rs3b", "rs3c", "gp3_2", "abt00", "rs2c", "rs4a", "gp3_3", "abt01", "rs2r",
    "gp2_1", "abt10", "abt11", "ar2011_1", "blank", "ar2000_1", "hk0", "rs4b", "gp3_1", "ar2010_1", "hk1",
    "ar2111_1", "rs3r", "ar2101_1", "aqgA", "ar2000_2", "mixf1", "ar2110_1", "ar2001_1", "rs4d", "kar1_1",
    "ar2100_1", "aqgB", "ar2111_2", "rs4c", "kar0_1", "ar2010_2", "rs3d", "rs1d", "kar0_2", "ar2011_2",
    "ar2100_2", "mixf0", "rs1e", "rs5a", "ar2101_2", "ar2110_2", "ar2000_3", "rs5b", "rs5c", "ar2111_3",
    "ar2110_3", "ar2000_4", "ar2111_4", "ar2100_3", "ar2001_2", "ar2011_3", "rs4r", "rs5d", "kar1_2",
    "rs5r", "rs0e", "rs3e", "ar2001_3", "kar1_3", "kar0_3", "kar0_4", "ar2101_3", "ar2100_4", "rs4e",
    "rs2e", "gains", "ar2110_4", "ar2010_3", "rs5e", "vec", "ar2001_4", "tok00", "ar2010_4", "ar2101_4",
    "kar1_4", "ar2011_4", "tok10", "tok01", "tok11", "vece",
)
BF = jnp.bfloat16
F32 = jnp.float32
MESH = pl.DeviceIdType.MESH


def mm(a, b):
    return jnp.dot(a, b, preferred_element_type=F32)


def mmt(a, b):
    return lax.dot_general(a, b, (((1,), (1,)), ((), ())), preferred_element_type=F32)


def tmm(a, b):
    return lax.dot_general(a, b, (((0,), (0,)), ((), ())), preferred_element_type=F32)


def row_sum(values):
    return jnp.sum(values, axis=-1, keepdims=True)


def gelu_parts(v):
    c = math.sqrt(2.0 / math.pi)
    square = v * v
    t = jnp.tanh(c * v * (1.0 + 0.044715 * square))
    act = 0.5 * v * (1.0 + t)
    slope = 0.5 * (1.0 + t) + (0.5 * c) * v * (1.0 - t * t) * (1.0 + 0.134145 * square)
    return act, slope


def layer_kernel(dims, *refs):
    docs, rows, width, slots, n_seq, wl, wh, fl_n, fh_n = dims
    nz = n_seq // 2
    chunk = width // n_seq
    half = rows // 2
    quarter = rows // 4
    radius = WINDOW // 2
    share = width // 4
    it = iter(refs)

    def take(count):
        return [next(it) for _ in range(count)]

    lens, qi, ki, ga_v, rq_v, rk_v, gf_v, rf_v = take(8)
    (tok_h, cot_h, wql_h, wkl_h, wvl_h, wol_h, wqh_h, wkh_h, wvh_h, woh_h,
     gl_h, ul_h, dl_h, gh_h, uh_h, dh_h) = take(16)
    gt_o, mix_o, pack_o, vec_o = take(4)
    (tok, cot, wqkv, wola, whq, whk, whv, woha, wgul, wdl, wguh, wdh, wkeep) = take(13)
    (nl, inva, hin, kin, sin, qbuf, kvw, pbuf, loall, hqx, kvall, ph, hoall, qall, doall, hproj, backr, qrow, kpart, ktot, k1, k2) = take(22)
    (pqk, pqkt, parts, tot1, tot2, r1, r2, cols) = take(8)
    (dm, dmh, grow, fl, invf, mid, dgu, frow, ghr, midh, dguh) = take(11)
    (mixb, mixr, mixa, ghf, ghb, dol, dox, gah, dqh, dkvw, rims, rimr, dqkv, dkvh) = take(14)
    (g_h, g_l, ra, rb, rl, packed, vbuf, vr, vect) = take(2) + [take(6), take(6), take(6)] + take(4)
    g_a = wguh
    (load_s, wg_s, wg_r, wf_s, wf_r, lo_s, lo_r, ho_s, ho_r, ka_s, ka_r, ar_s, ar_r, ag_s, ag_r, fw_s, fw_r, halo_s, halo_r, rim_s, rim_r,
     mx_s, mx_r, wa_s, wa_r, wz_s, wz_r, rl_s, rl_r, v_s, v_r, out_s) = take(32)

    b = lax.axis_index("branch")
    s = lax.axis_index("seq")
    bit_x = b % 2
    bit_y = b // 2
    core = s % 2
    z = s // 2
    offset = s * rows
    dev_x = (b + 1 - 2 * bit_x, s)
    dev_y = (b + 2 - 4 * bit_y, s)
    sibling = (b, s + 1 - 2 * core)

    def zpeer(k):
        return (z + k) % nz

    def same_core(k):
        return (b, 2 * zpeer(k) + core)

    late = []

    def send(src, dst, ssem, rsem, dev, when=None):
        copy = pltpu.make_async_remote_copy(
            src_ref=src, dst_ref=dst, send_sem=ssem, recv_sem=rsem, device_id=dev, device_id_type=MESH
        )
        if when is None:
            copy.start()
        else:
            pl.when(when)(copy.start)
        return copy

    def arrived(dst, ssem, rsem, dev):
        pltpu.make_async_remote_copy(
            src_ref=dst, dst_ref=dst, send_sem=ssem, recv_sem=rsem, device_id=dev, device_id_type=MESH
        ).wait_recv()

    loads = {}

    def load(name, src, dst, i):
        copy = pltpu.make_async_copy(src, dst, load_s.at[i])
        copy.start()
        loads[name] = copy

    load("tok", tok_h, tok, 0)
    load("whq", wqh_h, whq, 1)
    load("whk", wkh_h, whk, 2)
    load("whv", wvh_h, whv, 3)
    load("wq", wql_h, wqkv.at[:, 0:wl], 4)
    load("wk", wkl_h, wqkv.at[:, wl : 2 * wl], 5)
    load("wv", wvl_h, wqkv.at[:, 2 * wl : 3 * wl], 6)
    load("wol", wol_h, wola.at[b], 7)
    load("who", woh_h, woha.at[b], 8)
    load("cot", cot_h, cot, 9)
    load("wdl", dl_h, wdl, 10)
    load("wdh", dh_h, wdh, 11)
    load("gl", gl_h, wgul.at[:, 0:fl_n], 12)
    load("ul", ul_h, wgul.at[:, fl_n : 2 * fl_n], 13)
    load("gh", gh_h, wguh.at[:, 0:fh_n], 14)
    load("uh", uh_h, wguh.at[:, fh_n : 2 * fh_n], 15)
    own_rows = pl.ds(pl.multiple_of(chunk * s, chunk), chunk)
    load("gk", gh_h.at[own_rows], wkeep.at[:, 0:fh_n], 16)
    load("uk", uh_h.at[own_rows], wkeep.at[:, fh_n : 2 * fh_n], 17)

    barrier = pltpu.get_barrier_semaphore()
    for k in range(1, 4):
        pl.semaphore_signal(barrier, inc=1, device_id=((b + k) % 4, s), device_id_type=MESH)

    def greet(k, carry):
        pl.semaphore_signal(barrier, inc=1, device_id=(b, (s + k) % n_seq), device_id_type=MESH)
        return carry

    lax.fori_loop(1, n_seq, greet, 0)
    pl.semaphore_wait(barrier, 3 + n_seq - 1)

    gain_a, router_q, router_k, gain_f, router_f = [
        ref[...].astype(F32).reshape(1, width) for ref in (ga_v, rq_v, rk_v, gf_v, rf_v)
    ]

    def as_column(row):
        count = row.shape[1]
        square = lax.broadcasted_iota(jnp.int32, (count, count), 0)
        same = square == lax.broadcasted_iota(jnp.int32, (count, count), 1)
        return row_sum(jnp.where(same, row.astype(F32), 0.0)).astype(jnp.int32)

    idx_row = [[ref[d : d + 1, :] for ref in (qi, ki)] for d in range(docs)]
    idx_col = [[as_column(row) for row in idx_row[d]] for d in range(docs)]

    def valid_rows(d, first, count):
        at = lax.broadcasted_iota(jnp.int32, (count, 1), 0) + (offset + first)
        return jnp.where(at < lens[d], 1.0, 0.0).astype(F32)

    big = 64

    def tiles(count, size, body):
        def step(t, carry):
            body(pl.multiple_of(t * size, size))
            return carry

        lax.fori_loop(0, count // size, step, 0)

    flights = {}

    def add_rows(src, at, buf, base, dst, count):
        size = min(count, 32)

        def body(t, carry):
            r = pl.multiple_of(t * size, size)
            here = pl.ds(pl.multiple_of(at + r, 16), size)
            value = src[here, :].astype(F32) + buf[pl.ds(pl.multiple_of(base + r, 16), size), :].astype(F32)
            dst[here, :] = value.astype(BF)
            return carry

        lax.fori_loop(0, count // size, body, 0)

    def rows_sum(key, src, dst, b1, b2, ss, rs, base, count, way, src_base=None):
        first, second = ((dev_x, bit_x), (dev_y, bit_y))[:: 1 - 2 * way]
        two, four = count // 2, count // 4
        keep1, send1 = two * first[1], two * (1 - first[1])
        keep2, send2 = keep1 + four * second[1], keep1 + four * (1 - second[1])
        shift = base if src_base is None else src_base

        def rows_at(ref, at, size, frm):
            return ref.at[pl.ds(pl.multiple_of(frm + at, 16), size)]

        def start():
            flights[key, 0] = send(rows_at(src, send1, two, shift), b1, ss.at[0], rs.at[0], first[0])

        def one():
            arrived(b1, ss.at[0], rs.at[0], first[0])
            add_rows(src, shift + send2, b1, send2 - keep1, src, four)
            flights[key, 1] = send(rows_at(src, send2, four, shift), b2, ss.at[1], rs.at[1], second[0])
            add_rows(src, shift + keep2, b1, keep2 - keep1, src, four)

        def two_():
            arrived(b2, ss.at[1], rs.at[1], second[0])
            size = min(four, 32)

            def body(t, carry):
                r = pl.multiple_of(t * size, size)
                value = src[pl.ds(pl.multiple_of(shift + keep2 + r, 16), size), :].astype(F32)
                value = value + b2[pl.ds(r, size), :].astype(F32)
                dst[pl.ds(pl.multiple_of(base + keep2 + r, 16), size), :] = value.astype(BF)
                return carry

            lax.fori_loop(0, four // size, body, 0)
            own = rows_at(dst, keep2, four, base)
            flights[key, 2] = send(own, own, ss.at[2], rs.at[2], second[0])

        def three():
            arrived(rows_at(dst, send2, four, base), ss.at[2], rs.at[2], second[0])
            own = rows_at(dst, keep1, two, base)
            flights[key, 3] = send(own, own, ss.at[3], rs.at[3], first[0])

        def last_():
            arrived(rows_at(dst, send1, two, base), ss.at[3], rs.at[3], first[0])
            flights[key, 0].wait_send()
            flights[key, 1].wait_send()

        return start, one, two_, three, last_

    sums = {}
    for a in (1, 2):
        for d in range(docs):
            for h in range(2):
                for u in range(2):
                    sums[a, d, h, u] = rows_sum(
                        (a, d, h, u), parts.at[d], tot2.at[d], r1.at[d, h, u], r2.at[d, h, u],
                        ar_s.at[a, d, h, u], ar_r.at[a, d, h, u], half * h + quarter * u, quarter, u,
                    )
    for d in range(docs):
        sums[d] = rows_sum(
            d, kpart.at[d], ktot.at[d], k1.at[d], k2.at[d], ka_s.at[d], ka_r.at[d], slots, slots, d, 0
        )

    def ar_start(a, d, h):
        for u in range(2):
            sums[a, d, h, u][0]()

    def ar_sent(a, d):
        for h in range(2):
            for u in range(2):
                flights[(a, d, h, u), 2].wait_send()
                flights[(a, d, h, u), 3].wait_send()

    steps = {}

    def step(name):
        def keep(body):
            steps[name] = body
            return body

        return keep

    def halves(core_of):
        return (
            (wola, pl.ds(pl.multiple_of(width // 2 * core_of, 16), width // 2)),
            (woha, pl.ds(pl.multiple_of(wh // 2 * core_of, 16), wh // 2)),
        )

    @step("load")
    def _():
        loads["wol"].wait()
        loads["who"].wait()
        for k in range(1, 4):
            for i, (ref, part) in enumerate(halves(core)):
                block = ref.at[b, part]
                late.append(send(block, block, wg_s.at[k - 1, i], wg_r.at[k - 1, i], ((b + k) % 4, s)))
        loads["tok"].wait()

    @step("wgp")
    def _():
        for k in range(1, 4):
            frm = (b + 4 - k) % 4
            for i, (ref, part) in enumerate(halves(core)):
                block = ref.at[frm, part]
                arrived(block, wg_s.at[k - 1, i], wg_r.at[k - 1, i], (frm, s))
                late.append(send(block, block, wf_s.at[k - 1, i], wf_r.at[k - 1, i], sibling))

    def projections_wait():
        for k in range(1, 4):
            frm = (b + 4 - k) % 4
            for i, (ref, part) in enumerate(halves(1 - core)):
                arrived(ref.at[frm, part], wf_s.at[k - 1, i], wf_r.at[k - 1, i], sibling)

    @step("norm")
    def _():
        for d in range(docs):

            def norm_body(t, d=d):
                r = pl.ds(t, big)
                x = tok[d, r, :].astype(F32)
                inv = lax.rsqrt(row_sum(x * x) * (1.0 / width) + epsilon)
                inva[d, r, :] = inv
                nl[d, r, :] = (x * inv * gain_a).astype(BF)

            tiles(rows, big, norm_body)

    def selectors():
        for d in range(docs):
            lane_pos = lax.broadcasted_iota(jnp.int32, (slots, rows), 1) + offset
            sub_pos = lax.broadcasted_iota(jnp.int32, (rows, slots), 0) + offset
            for i in range(2):
                here = slice(i * slots, (i + 1) * slots)
                pqk[d, here, :] = jnp.where(idx_col[d][i] == lane_pos, 1.0, 0.0).astype(BF)
                pqkt[d, :, here] = jnp.where(idx_row[d][i] == sub_pos, 1.0, 0.0).astype(BF)

    def alive(d, i):
        return jnp.where(idx_col[d][i] >= 0, 1.0, 0.0).astype(F32)

    SQ, SK, SF, PREQ, PREF, PREK = range(6)

    def mine(d):
        return slice(d * slots, (d + 1) * slots)

    def routed_rows():
        for d in range(docs):
            x = mm(pqk[d], tok[d])
            picked = x * lax.rsqrt(row_sum(x * x) * (1.0 / width) + epsilon) * gain_a
            score_q = jax.nn.sigmoid(row_sum(picked[:slots] * router_q)) * alive(d, 0)
            score_k = jax.nn.sigmoid(row_sum(picked[slots:] * router_k)) * alive(d, 1)
            cols[SQ, mine(d), :] = score_q
            cols[SK, mine(d), :] = score_k
            hin[mine(d), :] = picked[:slots].astype(BF)
            kin[mine(d), :] = picked[slots:].astype(BF)
            sin[mine(d), :] = (picked[slots:] * score_k).astype(BF)
            pad_lane = lax.broadcasted_iota(jnp.int32, (slots, 256 - wh), 1)
            kvall[s, mine(d), wh:256] = jnp.where(
                pad_lane == 0, (1.0 - alive(d, 1)) * masked_value, 0.0
            ).astype(BF)
            kvall[s, mine(d), 256 + wh : 512] = jnp.zeros((slots, 256 - wh), BF)
        loads["whk"].wait()
        kvall[s, :, 0:wh] = mmt(kin[...], whk[...]).astype(BF)
        loads["whv"].wait()
        kvall[s, :, 256 : 256 + wh] = mmt(sin[...], whv[...]).astype(BF)

    at_end = (z == 0) | (z == nz - 1)
    inner = (z > 0) & (z < nz - 1)
    low_side = jnp.where(z < nz // 2, 1, 0)

    def gather_start(g, ref, part):
        block = ref.at[s, part]
        late.append(send(block, block, ag_s.at[g, 0], ag_r.at[g, 0], sibling))
        for k in (2, 1, 3):
            near = (z != 0) if k == 3 else (z != 3) if k == 1 else (z >= 0)
            late.append((near, send(block, block, ag_s.at[g, k], ag_r.at[g, k], same_core(k), near)))

    def gather_pass(g, ref, part, k):
        block = ref.at[2 * zpeer(nz - k) + core, part]
        arrived(block, ag_s.at[g, k], ag_r.at[g, k], same_core(nz - k))
        late.append(send(block, block, fw_s.at[g, k], fw_r.at[g, k], sibling))
        if k == 2:
            onward = (b, 2 * (z + 1 - 2 * low_side) + core)
            slot = 3 - 2 * low_side
            late.append((inner, send(block, block, fw_s.at[g, 0], ag_r.at[g, slot], onward, inner)))

    def gather_end(g, ref, part):
        arrived(ref.at[s + 1 - 2 * core, part], ag_s.at[g, 0], ag_r.at[g, 0], sibling)
        for k in range(1, nz):
            block = ref.at[2 * zpeer(nz - k) + 1 - core, part]
            arrived(block, fw_s.at[g, k], fw_r.at[g, k], sibling)

    def routed(d):
        return pl.ds(d * slots, slots)

    every = pl.ds(0, docs * slots)

    @step("rowskv")
    def _():
        selectors()
        routed_rows()
        gather_start(0, kvall, every)


    last = n_seq - 1
    left = (b, (s + last) % n_seq)
    right = (b, (s + 1) % n_seq)

    @step("qkv")
    def _():
        for name in ("wq", "wk", "wv"):
            loads[name].wait()
        for d in range(docs):

            def qkv_body(t, d=d):
                r = mm(nl[d, pl.ds(t, half), :], wqkv[...]).astype(BF)
                qbuf[d, pl.ds(t, half), :] = r[:, 0:wl]
                kvw[d, pl.ds(pl.multiple_of(t + radius, 32), half), :] = r[:, wl : 3 * wl]

            tiles(rows, half, qkv_body)

            @pl.when(s == 0)
            def _(d=d):
                kvw[d, 0:radius, :] = jnp.zeros((radius, 2 * wl), BF)

            @pl.when(s == last)
            def _(d=d):
                kvw[d, rows + radius : rows + 2 * radius, :] = jnp.zeros((radius, 2 * wl), BF)

            late.append((s > 0, send(
                kvw.at[d, pl.ds(radius, radius)], kvw.at[d, pl.ds(rows + radius, radius)],
                halo_s.at[d, 0], halo_r.at[d, 0], left, s > 0,
            )))
            late.append((s < last, send(
                kvw.at[d, pl.ds(rows, radius)], kvw.at[d, pl.ds(0, radius)],
                halo_s.at[d, 1], halo_r.at[d, 1], right, s < last,
            )))
        loads["whq"].wait()
        hqx[:, 0:wh] = mmt(hin[...], whq[...]).astype(BF)
        pad_lane = lax.broadcasted_iota(jnp.int32, (docs * slots, 256 - wh), 1)
        hqx[:, wh:256] = jnp.where(pad_lane == 0, 8.0, 0.0).astype(BF)

    def halo_wait(d):
        @pl.when(s < last)
        def _():
            arrived(kvw.at[d, pl.ds(rows + radius, radius)], halo_s.at[d, 0], halo_r.at[d, 0], right)

        @pl.when(s > 0)
        def _():
            arrived(kvw.at[d, pl.ds(0, radius)], halo_s.at[d, 1], halo_r.at[d, 1], left)

    blk = WINDOW
    span = 2 * WINDOW
    n_blk = rows // blk

    def two_heads(v):
        lane = lax.broadcasted_iota(jnp.int32, v.shape, 1)
        zero = jnp.zeros_like(v)
        return jnp.concatenate([jnp.where(lane < HD, v, zero), jnp.where(lane < HD, zero, v)], axis=0)

    def one_of_two(v):
        lane = lax.broadcasted_iota(jnp.int32, (blk, 2 * HD), 1)
        return jnp.where(lane < HD, v[:blk], v[blk:])

    def light_attention(d):
        row = lax.broadcasted_iota(jnp.int32, (2 * blk, span), 0) % blk
        col = lax.broadcasted_iota(jnp.int32, (2 * blk, span), 1)
        near = (col >= row) & (col <= row + WINDOW)

        def body(i, carry):
            blocks = [2 * i, 2 * i + 1]
            ats = [pl.multiple_of(j * blk, blk) for j in blocks]
            scores = []
            for at in ats:
                q2 = two_heads(qbuf[d, pl.ds(at, blk), :])
                scores.append(mmt(q2, kvw[d, pl.ds(at, span), 0:wl]))
            probs = []
            for at, score in zip(ats, scores):
                pos = col + (offset + at - radius)
                seen = near & (pos >= 0) & (pos < lens[d])
                e = jnp.where(seen, score * HD ** (-0.5), masked_value)
                e = jnp.exp(e - jnp.max(e, axis=-1, keepdims=True))
                probs.append((e * (1.0 / row_sum(e))).astype(BF))
            for j, at, p in zip(blocks, ats, probs):
                pbuf[d * n_blk + j] = p
                out = one_of_two(mm(p, kvw[d, pl.ds(at, span), wl : 2 * wl]))
                loall[b, d, pl.ds(at, blk), :] = (out * valid_rows(d, at, blk)).astype(BF)
            return carry

        lax.fori_loop(0, n_blk // 2, body, 0)

    def three_heads(v):
        lane = lax.broadcasted_iota(jnp.int32, v.shape, 1)
        zero = jnp.zeros_like(v)
        return jnp.concatenate(
            [jnp.where((lane // HD == h) | (lane >= wh), v, zero) for h in range(wh // HD)], axis=0
        )

    def one_of_three(v):
        lane = lax.broadcasted_iota(jnp.int32, (slots, 256), 1)
        total = jnp.zeros((slots, 256), F32)
        for h in range(wh // HD):
            total = jnp.where(lane // HD == h, v[h * slots : (h + 1) * slots], total)
        return total

    def keys_of(d, at):
        return kvall[:, mine(d), at : at + 256].reshape(n_seq * slots, 256)

    def spread(column):
        lane = lax.broadcasted_iota(jnp.int32, (slots, 256 - wh), 1)
        out = jnp.zeros((slots, 256 - wh), F32)
        for h in range(wh // HD):
            value = column[h * slots : (h + 1) * slots]
            high = value.astype(BF).astype(F32)
            low = value - high
            out = jnp.where(lane == 2 * h, high, jnp.where(lane == 2 * h + 1, low, out))
        return out.astype(BF)

    def own_keys(d, at):
        v = kvall[s, mine(d), at : at + 256]
        lane = lax.broadcasted_iota(jnp.int32, v.shape, 1)
        zero = jnp.zeros_like(v)
        one = jnp.ones_like(v)
        return jnp.concatenate(
            [
                jnp.where(
                    lane // HD == h, v, jnp.where((lane == wh + 2 * h) | (lane == wh + 2 * h + 1), one, zero)
                )
                for h in range(wh // HD)
            ],
            axis=0,
        )

    def heavy_attention(d):
        q3 = three_heads(hqx[mine(d), :])
        scores = mmt(q3, keys_of(d, 0)) * HD ** (-0.5)
        top = jnp.max(scores, axis=-1, keepdims=True)
        e = jnp.exp(scores - top)
        sums = row_sum(e)
        p = (e * (1.0 / sums)).astype(BF)
        ph[d] = p
        qall[s, mine(d), 0:wh] = hqx[mine(d), 0:wh]
        qall[s, mine(d), wh:256] = spread((top + jnp.log(sums)) * -(HD**0.5))
        hoall[b, mine(d), :] = one_of_three(mm(p, keys_of(d, 256))).astype(BF)

    def to_branches(block, ssem, rsem, k):
        return send(block, block, ssem, rsem, ((b + k) % 4, s))

    def from_branch(ref, ssem, rsem, k):
        frm = (b + 4 - k) % 4
        arrived(ref.at[frm], ssem, rsem, (frm, s))

    for d in range(docs):

        @step("la%d" % d)
        def _(d=d):
            halo_wait(d)
            light_attention(d)
            for k in range(1, 4):
                late.append(to_branches(loall.at[b, d], lo_s.at[d, k - 1], lo_r.at[d, k - 1], k))

    @step("hattn")
    def _():
        gather_end(0, kvall, every)
        for d in range(docs):
            heavy_attention(d)
        for k in range(1, 4):
            late.append(to_branches(hoall.at[b], ho_s.at[k - 1], ho_r.at[k - 1], k))
        gather_start(1, qall, every)

    gathers = ((0, kvall, every), (1, qall, every)) + tuple((2 + d, doall, routed(d)) for d in range(docs))
    for g, ref, part in gathers:
        for k in range(1, nz):

            @step("gp%d_%d" % (g, k))
            def _(g=g, ref=ref, part=part, k=k):
                gather_pass(g, ref, part, k)

    @step("hproj")
    def _():
        projections_wait()
        for k in range(1, 4):
            from_branch(hoall, ho_s.at[k - 1], ho_r.at[k - 1], k)
        total = mm(hoall[0, :, 0:wh], woha[0])
        for j in range(1, 4):
            total = total + mm(hoall[j, :, 0:wh], woha[j])
        hproj[...] = (total * cols[SQ]).astype(BF)

    def attention_total(d, h):
        r = pl.ds(h * half, half)
        heads = jnp.concatenate([loall[j, d, r, :] for j in range(4)], axis=1)
        out_weights = jnp.concatenate([wola[j] for j in range(4)], axis=1)
        value = mmt(heads, out_weights) + mm(pqkt[d, r, 0:slots], hproj[mine(d), :])
        tot1[d, r, :] = value.astype(BF)

    def light_pre(d):
        def body(t):
            r = pl.ds(t, half)
            dm[d, r, :] = mm(cot[d, r, :], wdl[...]) * valid_rows(d, t, half)

        tiles(rows, half, body)
        grow[mine(d), :] = mm(pqk[d, 0:slots, :], cot[d]).astype(BF)

    for d in range(docs):

        @step("pre%d" % d)
        def _(d=d):
            if d == 0:
                for name in ("cot", "wdl"):
                    loads[name].wait()
            light_pre(d)

    @step("predmh")
    def _():
        loads["wdh"].wait()
        dmh[...] = mm(grow[...], wdh[...])

    def hidden_rows(d, r):
        return tok[d, r, :].astype(F32) + tot1[d, r, :].astype(F32)

    def ffn_norm(d, h):
        def body(t):
            r = pl.ds(pl.multiple_of(h * half + t, big), big)
            hidden = hidden_rows(d, r)
            inv = lax.rsqrt(row_sum(hidden * hidden) * (1.0 / width) + epsilon)
            invf[d, r, :] = inv
            fl[d, r, :] = (hidden * inv * gain_f).astype(BF)

        tiles(half, big, body)

    for d in range(docs):
        for h in range(2):

            @step("nf%d%d" % (d, h))
            def _(d=d, h=h):
                if h == 0:
                    for k in range(1, 4):
                        frm = (b + 4 - k) % 4
                        arrived(loall.at[frm, d], lo_s.at[d, k - 1], lo_r.at[d, k - 1], (frm, s))
                attention_total(d, h)
                ffn_norm(d, h)

    def ffn_heavy(d):
        rowsf = mm(pqk[d, 0:slots, :], fl[d])
        score = jax.nn.sigmoid(row_sum(rowsf * router_f)) * alive(d, 0)
        cols[SF, mine(d), :] = score
        frow[mine(d), :] = rowsf.astype(BF)
        ghr[mine(d), :] = (grow[mine(d), :].astype(F32) * score).astype(BF)
        size = 512
        dscore = jnp.zeros((slots, 1), F32)
        for t in range(fh_n // size):
            c = slice(t * size, (t + 1) * size)
            c2 = slice(fh_n + t * size, fh_n + (t + 1) * size)
            gate = mm(frow[mine(d), :], wguh[:, c]).astype(BF).astype(F32)
            up = mm(frow[mine(d), :], wguh[:, c2]).astype(BF).astype(F32)
            act, slope = gelu_parts(gate)
            middle = (act * up).astype(BF)
            raw = dmh[mine(d), c]
            grad_mid = raw * score
            midh[mine(d), c] = middle
            dguh[mine(d), c] = (grad_mid * up * slope).astype(BF)
            dguh[mine(d), c2] = (grad_mid * act).astype(BF)
            dscore = dscore + row_sum(middle.astype(F32) * raw)
        pre = dscore * score * (1.0 - score)
        cols[PREF, mine(d), :] = pre
        backr[mine(d), :] = (mmt(dguh[mine(d), :], wguh[...]) + pre * router_f).astype(BF)

    for d in range(docs):

        @step("fh%d" % d)
        def _(d=d):
            if d == 0:
                for name in ("gh", "uh"):
                    loads[name].wait()
            ffn_heavy(d)


    def ffn_light(d, h):
        r = pl.ds(h * half, half)
        gu = mm(fl[d, r, :], wgul[...]).astype(BF)
        gate = gu[:, 0:fl_n].astype(F32)
        up = gu[:, fl_n : 2 * fl_n].astype(F32)
        act, slope = gelu_parts(gate)
        mid[d, r, :] = (act * up * valid_rows(d, h * half, half)).astype(BF)
        grad_mid = dm[d, r, :]
        dgu[d, r, 0:fl_n] = (grad_mid * up * slope).astype(BF)
        dgu[d, r, fl_n : 2 * fl_n] = (grad_mid * act).astype(BF)
        value = mmt(dgu[d, r, :], wgul[...]) + mm(pqkt[d, r, 0:slots], backr[mine(d), :])
        parts[d, r, :] = value.astype(BF)
        ar_start(1, d, h)

    for d in range(docs):
        for h in range(2):

            @step("fl%d%d" % (d, h))
            def _(d=d, h=h):
                if d == 0 and h == 0:
                    for name in ("gl", "ul"):
                        loads[name].wait()
                ffn_light(d, h)

            for a in (1, 2):
                for u in range(2):
                    for i in range(1, 5):
                        steps["ar%d%d%d%d_%d" % (a, d, h, u, i)] = sums[a, d, h, u][i]
        for i in range(1, 5):
            steps["kar%d_%d" % (d, i)] = sums[d][i]

    pieces = (
        (g_h, 0, fh_n), (g_h, fh_n, fh_n), (g_h, 2 * fh_n, fh_n), (g_l, 0, 3 * fl_n),
        (g_a, 0, wl + 2 * wh), (g_a, wl + 2 * wh, 3 * wl + 2 * wh + 128),
    )
    packed_at = [sum(piece[2] for piece in pieces[:p]) for p in range(len(pieces))]

    def chunk_rows(zz, cc):
        return pl.ds(pl.multiple_of(chunk * (2 * zz + cc), chunk), chunk)

    def chunk_of(p, zz, cc):
        grad, base, wide = pieces[p]
        return grad.at[chunk_rows(zz, cc), pl.ds(base, wide)]

    def rs_start(p, t):
        for zz in (2 * t, 2 * t + 1):
            late.append(send(
                chunk_of(p, zz, 1 - core), ra[p].at[zz], wa_s.at[p, zz], wa_r.at[p, zz], sibling
            ))

    def add_chunk(p, zz, other):
        grad, base, wide = pieces[p]

        def add_body(t, carry):
            r = pl.ds(pl.multiple_of(chunk * (2 * zz + core) + 16 * t, 16), 16)
            value = grad[r, base : base + wide].astype(F32)
            value = value + other[pl.ds(pl.multiple_of(16 * t, 16), 16), :].astype(F32)
            grad[r, base : base + wide] = value.astype(BF)
            return carry

        lax.fori_loop(0, chunk // 16, add_body, 0)

    def rs_direct(p, k, when):
        late.append((when, send(
            chunk_of(p, zpeer(k), core), rb[p].at[k - 1], wz_s.at[p, k - 1], wz_r.at[p, k - 1],
            same_core(k), when,
        )))

    def rs_own(p, k):
        zz = zpeer(k)
        arrived(ra[p].at[zz], wa_s.at[p, zz], wa_r.at[p, zz], sibling)
        add_chunk(p, zz, ra[p].at[zz])

    def rs_far(p):
        k = 1 + 2 * low_side
        rs_own(p, k)
        neighbour = (b, 2 * (z + 2 * low_side - 1) + core)
        late.append((at_end, send(
            chunk_of(p, zpeer(k), core), rl[p], rl_s.at[p], rl_r.at[p], neighbour, at_end
        )))
        rs_direct(p, k, inner)

    def rs_two(p):
        rs_own(p, 2)
        rs_direct(p, 2, at_end)

    def rs_near(p):
        k = 3 - 2 * low_side
        rs_own(p, k)
        rs_direct(p, k, z >= 0)

    def rs_relay(p):
        @pl.when(inner)
        def _():
            arrived(rl[p], rl_s.at[p], rl_r.at[p], same_core(1))
            add_chunk(p, zpeer(2), rl[p])

        rs_direct(p, 2, inner)

    for p in range(len(pieces)):
        steps["rs%da" % p] = functools.partial(rs_far, p)
        steps["rs%db" % p] = functools.partial(rs_two, p)
        steps["rs%dc" % p] = functools.partial(rs_near, p)
        steps["rs%dd" % p] = functools.partial(rs_own, p, nz)
        steps["rs%dr" % p] = functools.partial(rs_relay, p)

    def rs_end(p):
        grad, base, wide = pieces[p]
        for k, when in ((1, z > 0), (2, z >= 0), (3, z < nz - 1)):

            @pl.when(when)
            def _(k=k):
                arrived(rb[p].at[k - 1], wz_s.at[p, k - 1], wz_r.at[p, k - 1], same_core(nz - k))

        at = packed_at[p]

        def add_body(t, carry):
            r = pl.ds(pl.multiple_of(16 * t, 16), 16)
            value = grad[pl.ds(pl.multiple_of(chunk * s + 16 * t, 16), 16), base : base + wide].astype(F32)
            for k in range(1, nz):
                value = value + rb[p][k - 1, r, :].astype(F32)
            packed[r, at : at + wide] = value
            return carry

        lax.fori_loop(0, chunk // 16, add_body, 0)
        leave(packed.at[:, at : at + wide], pack_o.at[:, at : at + wide], 7 + p)

    @step("blank")
    def _():
        ktot[:, 0:slots, :] = jnp.zeros((docs, slots, width), BF)

        @pl.when(z == 0)
        def _():
            for buf in rb:
                buf[0] = jnp.zeros(buf.shape[1:], BF)

        @pl.when(z == nz - 1)
        def _():
            for buf in rb:
                buf[2] = jnp.zeros(buf.shape[1:], BF)

    def half_features(t):
        return slice(t * (width // 2), (t + 1) * (width // 2))

    def heavy_ffn_grads(t, p):
        size = 512
        f = half_features(t)
        src, gr, first = ((frow, dguh, 0), (frow, dguh, fh_n), (ghr, midh, 0))[p]
        left_t = src[:, f].T

        def body(i, carry):
            c = pl.ds(pl.multiple_of(first + i * size, size), size)
            o = pl.ds(pl.multiple_of(p * fh_n + i * size, size), size)
            g_h[f, o] = mm(left_t, gr[:, c]).astype(BF)
            return carry

        lax.fori_loop(0, fh_n // size, body, 0)

    def light_grad(t, src, gr, ref, base):
        f = half_features(t)
        wide = gr.shape[2]
        value = tmm(src[:, :, f].reshape(docs * rows, width // 2), gr[...].reshape(docs * rows, wide))
        ref[f, base : base + wide] = value.astype(BF)

    def rows_grads(t, pairs, at):
        f = half_features(t)
        value = jnp.concatenate([tmm(src[:, f], gr) for src, gr in pairs], axis=1)
        g_a[f, at : at + 2 * wh] = value.astype(BF)

    def early_grads(t):
        light_grad(t, ghb, loall.at[b], g_a, 0)
        rows_grads(t, ((gah, hoall[b, :, 0:wh]), (hin, dqh[:, 0:wh])), wl)

    def late_grads(t):
        f = half_features(t)
        at = wl + 2 * wh
        light_grad(t, nl, dqkv, g_a, at)
        rows_grads(t, ((kin, dkvh[:, 0:wh]), (sin, dkvh[:, 256 : 256 + wh])), at + 3 * wl)
        lane = lax.broadcasted_iota(jnp.int32, (docs * slots, 128), 1)
        vectors = jnp.zeros((width // 2, 128), F32)
        for src, which, at_lane in ((hin, PREQ, 1), (kin, PREK, 2), (frow, PREF, 4)):
            vectors = vectors + tmm(src[:, f], jnp.where(lane == at_lane, cols[which], 0.0).astype(BF))
        at = at + 3 * wl + 2 * wh
        g_a[f, at : at + 128] = vectors.astype(BF)

    for t in range(2):

        for p in range(3):

            @step("hgr%s%d" % ("AB"[t], p))
            def _(t=t, p=p):
                heavy_ffn_grads(t, p)
                rs_start(p, t)

        @step("lg" + "AB"[t])
        def _(t=t):
            light_grad(t, fl, dgu, g_l, 0)
            light_grad(t, cot, mid, g_l, 2 * fl_n)
            rs_start(3, t)

        @step("awg" + "AB"[t])
        def _(t=t):
            early_grads(t)
            rs_start(4, t)

        @step("aqg" + "AB"[t])
        def _(t=t):
            late_grads(t)
            rs_start(5, t)

    def mixed_terms(d):
        for t in range(2):
            w = half_features(t)
            heavy = (mmt(midh[mine(d), :], wdh[w, :]) * cols[SF, mine(d), :]).astype(BF)
            value = mmt(wdl[w, :], mid[d]) + tmm(heavy, pqk[d, 0:slots, :])
            for j in range(2):
                mixb[2 * t + j, d] = value[j * share : (j + 1) * share].astype(BF)

    def mixed_start(d):
        column = lax.broadcasted_iota(jnp.int32, (share, width), 1) - b * share
        own = jnp.where(column == lax.broadcasted_iota(jnp.int32, (share, width), 0), 1.0, 0.0).astype(BF)
        mixa[d] = mmt(own, tok[d]) + mmt(own, tot1[d]) + mixb[b, d].astype(F32)

    def hidden_grad(d, h):
        def body(t):
            r = pl.ds(pl.multiple_of(h * half + t, big), big)
            unit = hidden_rows(d, r) * invf[d, r, :]
            w = tot2[d, r, :].astype(F32) * gain_f
            inner = row_sum(w * unit) * (1.0 / width)
            value = cot[d, r, :].astype(F32) + invf[d, r, :] * (w - unit * inner)
            ghf[d, r, :] = value
            ghb[d, r, :] = value.astype(BF)

        tiles(half, big, body)

    def heavy_back(d):
        picked = mm(pqk[d, 0:slots, :], ghb[d])
        score = cols[SQ, mine(d), :]
        gah[mine(d), :] = (picked * score).astype(BF)
        raw = mmt(picked.astype(BF), woha[b])
        pre = row_sum(hoall[b, mine(d), 0:wh].astype(F32) * raw) * score * (1.0 - score)
        cols[PREQ, mine(d), :] = pre
        dox[mine(d), 0:wh] = (raw * score).astype(BF)
        dox[mine(d), wh:256] = jnp.zeros((slots, 256 - wh), BF)
        do3 = three_heads(dox[mine(d), :])
        pf = ph[d].astype(F32)
        dp = mmt(do3, keys_of(d, 256))
        delta = row_sum(dp * pf)
        doall[s, mine(d), 0:wh] = dox[mine(d), 0:wh]
        doall[s, mine(d), wh:256] = spread(-delta)
        gather_start(2 + d, doall, routed(d))
        ds = (pf * (dp - delta) * HD ** (-0.5)).astype(BF)
        dqh[mine(d), :] = one_of_three(mm(ds, keys_of(d, 0))).astype(BF)
        query_rows = mm(dqh[mine(d), 0:wh], whq[...]) + cols[PREQ, mine(d), :] * router_q
        qrow[mine(d), :] = query_rows.astype(BF)

    def heavy_back_keys(d):
        q = qall[:, mine(d), :].reshape(n_seq * slots, 256)
        do = doall[:, mine(d), :].reshape(n_seq * slots, 256)
        live = jnp.concatenate([alive(d, 1)] * (wh // HD), axis=0) > 0
        p = jnp.exp(jnp.where(live, mmt(own_keys(d, 0), q) * HD ** (-0.5), masked_value))
        ds = (p * mmt(own_keys(d, 256), do) * HD ** (-0.5)).astype(BF)
        dkvh[mine(d), 0:256] = one_of_three(mm(ds, q)).astype(BF)
        dkvh[mine(d), 256:512] = one_of_three(mm(p.astype(BF), do)).astype(BF)

    def light_back(d):
        dkvw[d] = jnp.zeros((rows + 2 * radius, 2 * wl), F32)

        def dol_body(t):
            r = pl.ds(t, half)
            dol[d, r, :] = (mm(ghb[d, r, :], wola[b]) * valid_rows(d, t, half)).astype(BF)

        tiles(rows, half, dol_body)

        def body(i, carry):
            blocks = [2 * i, 2 * i + 1]
            ats = [pl.multiple_of(j * blk, blk) for j in blocks]
            do2s = [two_heads(dol[d, pl.ds(at, blk), :]) for at in ats]
            dps = [mmt(do2, kvw[d, pl.ds(at, span), wl : 2 * wl]) for at, do2 in zip(ats, do2s)]
            grads_s = []
            for j, dp in zip(blocks, dps):
                pf = pbuf[d * n_blk + j].astype(F32)
                grads_s.append((pf * (dp - row_sum(dp * pf)) * HD ** (-0.5)).astype(BF))
            for j, at, do2, ds in zip(blocks, ats, do2s, grads_s):
                q2 = two_heads(qbuf[d, pl.ds(at, blk), :])
                dqkv[d, pl.ds(at, blk), 0:wl] = one_of_two(mm(ds, kvw[d, pl.ds(at, span), 0:wl])).astype(BF)
                dkvw[d, pl.ds(at, span), 0:wl] += tmm(ds, q2)
                dkvw[d, pl.ds(at, span), wl : 2 * wl] += tmm(pbuf[d * n_blk + j], do2)
            return carry

        lax.fori_loop(0, n_blk // 2, body, 0)
        rims[d, 0] = dkvw[d, 0:radius, :].astype(BF)
        rims[d, 1] = dkvw[d, rows + radius : rows + 2 * radius, :].astype(BF)

        @pl.when(s == 0)
        def _():
            rimr[d, 0] = jnp.zeros((radius, 2 * wl), BF)

        @pl.when(s == last)
        def _():
            rimr[d, 1] = jnp.zeros((radius, 2 * wl), BF)

        late.append((s > 0, send(rims.at[d, 0], rimr.at[d, 1], rim_s.at[d, 0], rim_r.at[d, 0], left, s > 0)))
        late.append((s < last, send(rims.at[d, 1], rimr.at[d, 0], rim_s.at[d, 1], rim_r.at[d, 1], right, s < last)))

    def rim_wait(d):
        @pl.when(s < last)
        def _():
            arrived(rimr.at[d, 1], rim_s.at[d, 0], rim_r.at[d, 0], right)

        @pl.when(s > 0)
        def _():
            arrived(rimr.at[d, 0], rim_s.at[d, 1], rim_r.at[d, 1], left)

    def attention_back_rows(d):
        heavy_back_keys(d)
        ds_in = mm(dkvh[mine(d), 256 : 256 + wh], whv[...])
        score = cols[SK, mine(d), :]
        pre_k = row_sum(ds_in * kin[mine(d), :].astype(F32)) * score * (1.0 - score)
        cols[PREK, mine(d), :] = pre_k
        key_rows = mm(dkvh[mine(d), 0:wh], whk[...]) + ds_in * score + pre_k * router_k
        kpart[d] = key_rows.astype(BF)
        sums[d][0]()

    def attention_back_terms(d, h):
        if h == 0:
            rim_wait(d)
            dkvw[d, radius : 2 * radius, :] += rimr[d, 0].astype(F32)
            dkvw[d, rows : rows + radius, :] += rimr[d, 1].astype(F32)
            ar_sent(1, d)
        r = pl.ds(h * half, half)
        dqkv[d, r, wl : 3 * wl] = dkvw[d, pl.ds(h * half + radius, half), :].astype(BF)
        value = mmt(dqkv[d, r, :], wqkv[...]) + mm(pqkt[d, r, 0:slots], qrow[mine(d), :])
        parts[d, r, :] = value.astype(BF)
        ar_start(2, d, h)

    out_copies = []

    def leave(src, dst, i):
        copy = pltpu.make_async_copy(src, dst, out_s.at[i])
        copy.start()
        out_copies.append(copy)

    def token_grad(d, h):
        def body(t):
            r = pl.ds(pl.multiple_of(h * half + t, big), big)
            inv = inva[d, r, :]
            unit = tok[d, r, :].astype(F32) * inv
            w = (tot2[d, r, :].astype(F32) + mm(pqkt[d, r, :], ktot[d])) * gain_a
            inner = row_sum(w * unit) * (1.0 / width)
            ghf[d, r, :] = ghf[d, r, :] + inv * (w - unit * inner)

        tiles(half, big, body)
        r = pl.ds(h * half, half)
        leave(ghf.at[d, r], gt_o.at[d, r], 3 + 2 * d + h)

    for d in range(docs):

        @step("mixt%d" % d)
        def _(d=d):
            mixed_terms(d)

        @step("mx%d" % d)
        def _(d=d):
            for k in range(1, 4):
                to = (b + k) % 4
                late.append(send(
                    mixb.at[to, d], mixr.at[k - 1, d], mx_s.at[d, k - 1], mx_r.at[d, k - 1], (to, s)
                ))

        @step("mixs%d" % d)
        def _(d=d):
            mixed_start(d)

        @step("mixf%d" % d)
        def _(d=d):
            for k in range(1, 4):
                frm = (b + 4 - k) % 4
                arrived(mixr.at[k - 1, d], mx_s.at[d, k - 1], mx_r.at[d, k - 1], (frm, s))

            def mix_body(t, d=d):
                r = pl.ds(t, 32)
                value = mixa[d, r, :]
                for k in range(3):
                    value = value + mixr[k, d, r, :].astype(F32)
                mixa[d, r, :] = value

            tiles(share, 32, mix_body)
            leave(mixa.at[d], mix_o.at[d], 1 + d)

        for h in range(2):

            @step("hg%d%d" % (d, h))
            def _(d=d, h=h):
                hidden_grad(d, h)

            @step("abt%d%d" % (d, h))
            def _(d=d, h=h):
                attention_back_terms(d, h)

            @step("tok%d%d" % (d, h))
            def _(d=d, h=h):
                token_grad(d, h)

        @step("hb%d" % d)
        def _(d=d):
            heavy_back(d)

        @step("lb%d" % d)
        def _(d=d):
            light_back(d)

        @step("hk%d" % d)
        def _(d=d):
            if d == 0:
                gather_end(1, qall, every)
            gather_end(2 + d, doall, routed(d))
            attention_back_rows(d)

    vlane = lax.broadcasted_iota(jnp.int32, (chunk, 128), 1)
    eye = lax.broadcasted_iota(jnp.int32, (chunk, width), 1) - chunk * s
    eye = eye == lax.broadcasted_iota(jnp.int32, (chunk, width), 0)

    def own_column(row):
        return row_sum(jnp.where(eye, row, 0.0))

    for p in range(len(pieces)):
        steps["rs%de" % p] = functools.partial(rs_end, p)

    @step("gains")
    def _():
        for name in ("gk", "uk"):
            loads[name].wait()
        total = row_sum(packed[:, 0 : 2 * fh_n] * wkeep[...].astype(F32))
        vbuf[:, 0:1] = total + row_sum(
            packed[:, packed_at[3] : packed_at[3] + 2 * fl_n] * wgul[own_rows, :].astype(F32)
        )

    @step("vec")
    def _():
        a_at, q_at = packed_at[4:6]
        va = q_at + 3 * wl + 2 * wh
        gf_sum = vbuf[:, 0:1]
        ga_sum = row_sum(packed[:, q_at : q_at + 3 * wl] * wqkv[own_rows, :].astype(F32))
        eye_b = eye.astype(F32).astype(BF)
        for h_at, w in ((a_at + wl + wh, whq), (q_at + 3 * wl, whk), (q_at + 3 * wl + wh, whv)):
            ga_sum = ga_sum + row_sum(packed[:, h_at : h_at + wh] * mmt(eye_b, w[...]))
        vectors = packed[:, va : va + 128]

        def lane_of(i):
            return row_sum(jnp.where(vlane == i, vectors, 0.0))

        ga_sum = ga_sum + own_column(router_q) * lane_of(1) + own_column(router_k) * lane_of(2)
        gf_sum = gf_sum + own_column(router_f) * lane_of(4)
        vectors = jnp.where(vlane == 0, ga_sum / own_column(gain_a), vectors)
        vectors = jnp.where(vlane == 3, gf_sum / own_column(gain_f), vectors)
        vbuf[...] = vectors
        for k in range(1, 4):
            late.append(send(vbuf, vr.at[k - 1], v_s.at[k - 1], v_r.at[k - 1], ((b + k) % 4, s)))

    @step("vece")
    def _():
        for k in range(1, 4):
            arrived(vr.at[k - 1], v_s.at[k - 1], v_r.at[k - 1], ((b + 4 - k) % 4, s))
        vect[...] = (vbuf[...] + vr[0] + vr[1] + vr[2]).T
        leave(vect, vec_o, 0)

    for name in ORDER:
        steps[name]()

    for entry in late:
        if isinstance(entry, tuple):
            pl.when(entry[0])(entry[1].wait_send)
        else:
            entry.wait_send()
    for d in range(docs):
        ar_sent(2, d)
        flights[d, 2].wait_send()
        flights[d, 3].wait_send()
    for copy in out_copies:
        copy.wait()


def kernel_scratch(docs, rows, width, slots, n_seq, wl, wh, fl_n, fh_n):
    nz = n_seq // 2
    chunk = width // n_seq
    routed = docs * slots
    keys = n_seq * slots
    pad = -(-wh // 256) * 256
    ga_n = 4 * wl + 4 * wh + 128
    widths = [fh_n, fh_n, fh_n, 3 * fl_n, wl + 2 * wh, 3 * wl + 2 * wh + 128]
    h_n, l_n = 3 * fh_n, 3 * fl_n
    radius = WINDOW // 2
    span = rows + 2 * radius
    vmem = [
        ((docs, rows, width), BF), ((docs, rows, width), BF), ((width, 3 * wl), BF), ((4, width, wl), BF),
        ((wh, width), BF), ((wh, width), BF), ((wh, width), BF), ((4, wh, width), BF),
        ((width, 2 * fl_n), BF), ((width, fl_n), BF), ((width, 2 * fh_n), BF), ((width, fh_n), BF),
        ((chunk, 2 * fh_n), BF),
        ((docs, rows, width), BF), ((docs, rows, 1), F32), ((routed, width), BF), ((routed, width), BF),
        ((routed, width), BF), ((docs, rows, wl), BF), ((docs, span, 2 * wl), BF),
        ((docs * rows // WINDOW, 2 * WINDOW, 2 * WINDOW), BF), ((4, docs, rows, wl), BF), ((routed, pad), BF),
        ((n_seq, routed, 2 * pad), BF), ((docs, wh // HD * slots, keys), BF), ((4, routed, pad), BF),
        ((n_seq, routed, pad), BF), ((n_seq, routed, pad), BF), ((routed, width), BF), ((routed, width), BF),
        ((routed, width), BF), ((docs, slots, width), BF), ((docs, 2 * slots, width), BF),
        ((docs, slots // 2, width), BF), ((docs, slots // 4, width), BF),
        ((docs, 2 * slots, rows), BF), ((docs, rows, 2 * slots), BF), ((docs, rows, width), BF),
        ((docs, rows, width), BF), ((docs, rows, width), BF), ((docs, 2, 2, rows // 8, width), BF),
        ((docs, 2, 2, rows // 16, width), BF), ((6, routed, 1), F32),
        ((docs, rows, fl_n), F32), ((routed, fh_n), F32), ((routed, width), BF), ((docs, rows, width), BF),
        ((docs, rows, 1), F32), ((docs, rows, fl_n), BF), ((docs, rows, 2 * fl_n), BF), ((routed, width), BF),
        ((routed, width), BF), ((routed, fh_n), BF), ((routed, 2 * fh_n), BF),
        ((4, docs, width // 4, rows), BF), ((3, docs, width // 4, rows), BF), ((docs, width // 4, rows), F32),
        ((docs, rows, width), F32), ((docs, rows, width), BF), ((docs, rows, wl), BF), ((routed, pad), BF),
        ((routed, width), BF), ((routed, pad), BF), ((docs, span, 2 * wl), F32),
        ((docs, 2, radius, 2 * wl), BF), ((docs, 2, radius, 2 * wl), BF), ((docs, rows, 3 * wl), BF),
        ((routed, 2 * pad), BF),
        ((width, h_n), BF), ((width, l_n), BF),
        *[((nz, chunk, wide), BF) for wide in widths],
        *[((nz - 1, chunk, wide), BF) for wide in widths],
        *[((chunk, wide), BF) for wide in widths],
        ((chunk, h_n + l_n + ga_n), F32), ((chunk, 128), F32), ((3, chunk, 128), F32), ((128, chunk), F32),
    ]
    sems = [
        (18,), (3, 2), (3, 2), (3, 2), (3, 2), (docs, 3), (docs, 3), (3,), (3,),
        (docs, 4), (docs, 4), (3, docs, 2, 2, 4), (3, docs, 2, 2, 4), (2 + docs, nz), (2 + docs, nz), (2 + docs, nz), (2 + docs, nz),
        (docs, 2), (docs, 2), (docs, 2), (docs, 2), (docs, 3), (docs, 3),
        (6, nz), (6, nz), (6, nz - 1), (6, nz - 1), (6,), (6,), (3,), (3,), (13,),
    ]
    total = 0
    for shape, kind in vmem:
        lanes = -(-shape[-1] // 128) * 128
        total += math.prod(shape[:-1]) * lanes * jnp.dtype(kind).itemsize
    return vmem, sems, total


def shards(sizes, *args):
    (tokens, cotangent, lengths, query_index, key_index, gain_attn, router_query, router_key, wq_light,
     wk_light, wv_light, wo_light, wq_heavy, wk_heavy, wv_heavy, wo_heavy, gain_ffn, router_ffn,
     gate_light, up_light, down_light, gate_heavy, up_heavy, down_heavy) = args
    n_seq = sizes["seq"]
    docs, rows, width = tokens.shape
    slots = query_index.shape[1]
    wl, wh = wq_light.shape[1], wq_heavy.shape[1]
    fl_n, fh_n = gate_light.shape[1], gate_heavy.shape[1]
    dims = (docs, rows, width, slots, n_seq, wl, wh, fl_n, fh_n)
    vmem, sems, total = kernel_scratch(*dims)
    fits = (
        total <= 62 * 2**20
        and sizes["branch"] == 4
        and n_seq == 8
        and width % (16 * n_seq) == 0
        and wl == 2 * HD
        and wh == 3 * HD
        and slots % 16 == 0
        and rows % 256 == 0
    )
    if not fits:
        return plain_shards(*args)
    share = width // 4
    chunk = width // n_seq
    ga_n = 4 * wl + 4 * wh + 128
    pack_n = 3 * fh_n + 3 * fl_n + ga_n
    in_hbm = [
        tokens, cotangent, wq_light, wk_light, wv_light, wo_light, wq_heavy.T, wk_heavy.T, wv_heavy.T, wo_heavy.T,
        gate_light, up_light, down_light, gate_heavy, up_heavy, down_heavy,
    ]
    whole = pl.BlockSpec(memory_space=pltpu.VMEM)
    outside = pl.BlockSpec(memory_space=pl.ANY)
    grad_tokens, mix, packed, vectors = pl.pallas_call(
        functools.partial(layer_kernel, dims),
        out_shape=[
            jax.ShapeDtypeStruct((docs, rows, width), F32),
            jax.ShapeDtypeStruct((docs, share, rows), F32),
            jax.ShapeDtypeStruct((chunk, pack_n), F32),
            jax.ShapeDtypeStruct((128, chunk), F32),
        ],
        in_specs=[pl.BlockSpec(memory_space=pltpu.SMEM)] + [whole] * 7 + [outside] * 16,
        out_specs=[outside] * 4,
        scratch_shapes=[pltpu.VMEM(shape, kind) for shape, kind in vmem]
        + [pltpu.SemaphoreType.DMA(shape) for shape in sems],
        compiler_params=pltpu.CompilerParams(
            collective_id=0, has_side_effects=True, vmem_limit_bytes=64 * 2**20 - 2**16
        ),
    )(lengths, query_index, key_index, gain_attn, router_query, router_key, gain_ffn, router_ffn, *in_hbm)

    l_at = 3 * fh_n
    a_at = l_at + 3 * fl_n
    q_at = a_at + wl + 2 * wh
    parts = [(q_at + i * wl, wl) for i in range(3)] + [(a_at, wl)]
    parts += [(a_at + wl + wh, wh), (q_at + 3 * wl, wh), (q_at + 3 * wl + wh, wh), (a_at + wl, wh)]
    parts += [(l_at + i * fl_n, fl_n) for i in range(3)] + [(i * fh_n, fh_n) for i in range(3)]
    outs = pl.pallas_call(
        functools.partial(hand_out, parts),
        out_shape=[jax.ShapeDtypeStruct(grad_tokens.shape, F32), jax.ShapeDtypeStruct(mix.shape, F32)]
        + [jax.ShapeDtypeStruct((chunk, wide), F32) for at, wide in parts],
        in_specs=[pl.BlockSpec(memory_space=pltpu.HBM)] * 3,
        out_specs=[outside] * 2 + [outside if wide % 128 == 0 else whole for at, wide in parts],
        scratch_shapes=[
            pltpu.SemaphoreType.DMA((3 + docs,)), pltpu.SemaphoreType.DMA((1 + docs + len(parts),)),
            pltpu.VMEM(grad_tokens.shape, F32), pltpu.VMEM(mix.shape, F32), pltpu.VMEM(packed.shape, F32),
        ],
        compiler_params=pltpu.CompilerParams(vmem_limit_bytes=60 * 2**20),
    )(grad_tokens, mix, packed)
    grad_tokens, mix = outs[:2]
    mixed = jnp.swapaxes(mix, 1, 2)
    vec = [vectors[i] for i in range(5)]
    return (mixed, grad_tokens, *vec[:3], *outs[2:10], *vec[3:], *outs[10:])


def hand_out(parts, tokens_in, mix_in, packed_in, tokens_out, mix_out, *rest):
    in_sems, out_sems, tokens, mix, packed = rest[-5:]
    docs = tokens.shape[0]
    arriving = [pltpu.make_async_copy(packed_in, packed, in_sems.at[0])]
    arriving += [pltpu.make_async_copy(tokens_in.at[d], tokens.at[d], in_sems.at[1 + d]) for d in range(docs)]
    arriving += [pltpu.make_async_copy(mix_in, mix, in_sems.at[1 + docs])]
    for copy in arriving:
        copy.start()
    leaving = [pltpu.make_async_copy(mix, mix_out, out_sems.at[0])]
    leaving += [pltpu.make_async_copy(tokens.at[d], tokens_out.at[d], out_sems.at[1 + d]) for d in range(docs)]
    arriving[0].wait()
    for i, (at, wide) in enumerate(parts):
        if wide % 128 == 0:
            copy = pltpu.make_async_copy(packed.at[:, at : at + wide], rest[i], out_sems.at[1 + docs + i])
            copy.start()
            leaving.append(copy)
    for d in range(docs):
        arriving[1 + d].wait()
        leaving[1 + d].start()
    arriving[1 + docs].wait()
    leaving[0].start()
    for i, (at, wide) in enumerate(parts):
        if wide % 128 != 0:
            rest[i][...] = packed[:, at : at + wide]
    for copy in leaving:
        copy.wait()


def solution(mesh):
    return jax.shard_map(
        functools.partial(shards, dict(mesh.shape)),
        mesh=mesh,
        in_specs=(
            P(None, "seq", None),
            P(None, "seq", None),
            P(),
            P(None, "seq"),
            P(None, "seq"),
            P(),
            P(),
            P(),
            P(None, "branch"),
            P(None, "branch"),
            P(None, "branch"),
            P(None, "branch"),
            P(None, "branch"),
            P(None, "branch"),
            P(None, "branch"),
            P(None, "branch"),
            P(),
            P(),
            P(None, "branch"),
            P(None, "branch"),
            P(None, "branch"),
            P(None, "branch"),
            P(None, "branch"),
            P(None, "branch"),
        ),
        out_specs=(
            P(None, "seq", "branch"),
            P(None, "seq", None),
            P("seq"),
            P("seq"),
            P("seq"),
            P("seq", "branch"),
            P("seq", "branch"),
            P("seq", "branch"),
            P("seq", "branch"),
            P("seq", "branch"),
            P("seq", "branch"),
            P("seq", "branch"),
            P("seq", "branch"),
            P("seq"),
            P("seq"),
            P("seq", "branch"),
            P("seq", "branch"),
            P("seq", "branch"),
            P("seq", "branch"),
            P("seq", "branch"),
            P("seq", "branch"),
        ),
        check_vma=False,
    )
```

```python
import functools
import math

import jax
import jax.numpy as jnp
from jax import lax
from jax.experimental import pallas as pl
from jax.experimental.pallas import tpu as pltpu
from jax.sharding import PartitionSpec as P

HD = 64
WINDOW = 128


highest = lax.Precision.HIGHEST
masked_value = -1000000000.0
epsilon = 1e-06


def with_halo(cells, sides, width):
    for axis, dim in sides:
        count = lax.axis_size(axis)
        ends = count - 1
        head = lax.slice_in_dim(cells, 0, width, axis=dim)
        tail = lax.slice_in_dim(cells, cells.shape[dim] - width, cells.shape[dim], axis=dim)
        cells = jnp.concatenate(
            [
                lax.ppermute(tail, axis, [(i, (i + 1) % count) for i in range(ends)]),
                cells,
                lax.ppermute(head, axis, [((i + 1) % count, i) for i in range(ends)]),
            ],
            axis=dim,
        )
    return cells


def project(operand, matrix):
    return jnp.einsum("dsc,ch->dsh", operand, matrix, preferred_element_type=jnp.float32)


def unproject(operand, matrix):
    return jnp.einsum("dsh,ch->dsc", operand, matrix, preferred_element_type=jnp.float32)


def weight_grad(operand, gradient):
    return jnp.einsum("dsc,dsh->ch", operand, gradient, preferred_element_type=jnp.float32)


def pick_rows(selector, values):
    return jnp.einsum("drs,dsc->drc", selector, values, precision=highest)


def put_rows(selector, values):
    return jnp.einsum("drs,drc->dsc", selector, values, precision=highest)


def pick_scalar(selector, values):
    return jnp.einsum("drs,ds->dr", selector, values, precision=highest)


def put_scalar(selector, values):
    return jnp.einsum("drs,dr->ds", selector, values, precision=highest)


def split_heads(values):
    return values.reshape(values.shape[0], values.shape[1], -1, HD)


def attention_scores(queries, keys, mask_bias):
    raw_scores = jnp.einsum("dqhe,dkhe->dhqk", queries, keys, preferred_element_type=jnp.float32)
    return raw_scores * HD ** (-0.5) + mask_bias


def forward_attention(queries, keys, values, mask_bias):
    scores = attention_scores(queries, keys, mask_bias)
    highest_score = jnp.max(scores, axis=-1, keepdims=True)
    exponent = jnp.exp(scores - highest_score)
    totals = jnp.sum(exponent, axis=-1, keepdims=True)
    probs_low = (exponent / totals).astype(jnp.bfloat16)
    result = jnp.einsum("dhqk,dkhe->dqhe", probs_low, values, preferred_element_type=jnp.float32)
    result = result.reshape(result.shape[0], result.shape[1], -1).astype(jnp.bfloat16)
    return (result, highest_score + jnp.log(totals))


def score_grads(queries, keys, values, mask_bias, logsum, grad_out, row_delta):
    probs = jnp.exp(attention_scores(queries, keys, mask_bias) - logsum)
    grad_probs = jnp.einsum("dqhe,dkhe->dhqk", grad_out, values, preferred_element_type=jnp.float32)
    row_delta = jnp.sum(grad_probs * probs, axis=-1, keepdims=True)
    grad_raw = (probs * (grad_probs - row_delta) * HD ** (-0.5)).astype(jnp.bfloat16)
    return (grad_raw, probs.astype(jnp.bfloat16), row_delta)


def contract_query(grad_raw, keys):
    result = jnp.einsum("dhqk,dkhe->dqhe", grad_raw, keys, preferred_element_type=jnp.float32)
    return result.reshape(result.shape[0], result.shape[1], -1)


def contract_key(grad_raw, queries):
    result = jnp.einsum("dhqk,dqhe->dkhe", grad_raw, queries, preferred_element_type=jnp.float32)
    return result.reshape(result.shape[0], result.shape[1], -1)


def geglu_back(gate_vals, up_vals, grad_mid):
    activated, gelu_pull = jax.vjp(jax.nn.gelu, gate_vals.astype(jnp.float32))
    grad_gate = gelu_pull(grad_mid * up_vals.astype(jnp.float32))[0].astype(jnp.bfloat16)
    grad_up = (grad_mid * activated).astype(jnp.bfloat16)
    return (grad_gate, grad_up)


def geglu(gate_vals, up_vals):
    return (jax.nn.gelu(gate_vals.astype(jnp.float32)) * up_vals.astype(jnp.float32)).astype(
        jnp.bfloat16
    )


def plain_shards(
    tokens,
    cotangent,
    lengths,
    query_index,
    key_index,
    gain_attn,
    router_query,
    router_key,
    wq_light,
    wk_light,
    wv_light,
    wo_light,
    wq_heavy,
    wk_heavy,
    wv_heavy,
    wo_heavy,
    gain_ffn,
    router_ffn,
    gate_light,
    up_light,
    down_light,
    gate_heavy,
    up_heavy,
    down_heavy,
):
    documents, local_len, model_width = tokens.shape
    radius = WINDOW // 2
    block_rows = math.gcd(local_len, 512)
    key_span = block_rows + 2 * radius
    offset = lax.axis_index("seq") * local_len
    positions = offset + jnp.arange(local_len, dtype=jnp.int32)
    valid_rows = (positions[None, :] < lengths[:, None]).astype(jnp.float32)[:, :, None]
    pick_query = (query_index[:, :, None] == positions[None, None, :]).astype(jnp.float32)
    pick_key = (key_index[:, :, None] == positions[None, None, :]).astype(jnp.float32)
    inputs = tokens.astype(jnp.float32)
    inv_attn = lax.rsqrt(jnp.mean(inputs * inputs, axis=-1, keepdims=True) + epsilon)
    unit_attn = inputs * inv_attn
    gain_attn_f = gain_attn.astype(jnp.float32)
    normed = unit_attn * gain_attn_f
    normed_low = normed.astype(jnp.bfloat16)
    light_q = project(normed_low, wq_light).astype(jnp.bfloat16)
    light_k = project(normed_low, wk_light).astype(jnp.bfloat16)
    light_v = project(normed_low, wv_light).astype(jnp.bfloat16)
    light_width = light_q.shape[2]
    rim_block = with_halo(jnp.concatenate([light_k, light_v], axis=2), (("seq", 1),), radius)
    wide_k = split_heads(rim_block[:, :, :light_width])
    wide_v = split_heads(rim_block[:, :, light_width:])
    heads_q = split_heads(light_q)
    key_pos = offset - radius + jnp.arange(local_len + 2 * radius, dtype=jnp.int32)
    in_window = (jnp.abs(positions[:, None] - key_pos[None, :]) <= radius)[None]
    in_window = (
        in_window
        & (key_pos[None, None, :] >= 0)
        & (key_pos[None, None, :] < lengths[:, None, None])
    )
    light_bias = jnp.where(in_window, 0.0, masked_value)[:, None]
    piece_out, piece_lse = forward_attention(heads_q, wide_k, wide_v, light_bias)
    router_query_f = router_query.astype(jnp.float32)
    router_key_f = router_key.astype(jnp.float32)
    score_query = pick_scalar(
        pick_query,
        jax.nn.sigmoid(jnp.einsum("dsc,c->ds", normed, router_query_f, precision=highest)),
    )
    score_key = pick_scalar(
        pick_key, jax.nn.sigmoid(jnp.einsum("dsc,c->ds", normed, router_key_f, precision=highest))
    )
    heavy_in = pick_rows(pick_query, normed).astype(jnp.bfloat16)
    key_rows = pick_rows(pick_key, normed)
    key_in = key_rows.astype(jnp.bfloat16)
    scaled_in = (key_rows * score_key[:, :, None]).astype(jnp.bfloat16)
    heavy_q = project(heavy_in, wq_heavy).astype(jnp.bfloat16)
    heavy_k = project(key_in, wk_heavy).astype(jnp.bfloat16)
    heavy_v = project(scaled_in, wv_heavy).astype(jnp.bfloat16)
    heavy_width = heavy_q.shape[2]
    key_alive = (key_index >= 0).astype(jnp.bfloat16)
    routed_kv, alive_all = (
        lax.all_gather(jnp.concatenate([heavy_k, heavy_v], axis=2), "seq", axis=1, tiled=True),
        lax.all_gather(key_alive, "seq", axis=1, tiled=True),
    )
    all_k = routed_kv[:, :, :heavy_width]
    all_v = routed_kv[:, :, heavy_width:]
    heavy_bias = jnp.where(alive_all > 0, 0.0, masked_value)[:, None, None, :]
    heavy_out, heavy_lse = forward_attention(
        split_heads(heavy_q), split_heads(all_k), split_heads(all_v), heavy_bias
    )
    heavy_proj = unproject(heavy_out, wo_heavy)
    light_attn = unproject(piece_out, wo_light) * valid_rows
    heavy_attn = put_rows(pick_query, heavy_proj * score_query[:, :, None])
    attn_total = lax.psum((light_attn + heavy_attn).astype(jnp.bfloat16), "branch").astype(
        jnp.float32
    )
    hidden = inputs + attn_total
    inv_ffn = lax.rsqrt(jnp.mean(hidden * hidden, axis=-1, keepdims=True) + epsilon)
    unit_ffn = hidden * inv_ffn
    gain_ffn_f = gain_ffn.astype(jnp.float32)
    normed_ffn = unit_ffn * gain_ffn_f
    ffn_low = normed_ffn.astype(jnp.bfloat16)
    gate_l = project(ffn_low, gate_light).astype(jnp.bfloat16)
    up_l = project(ffn_low, up_light).astype(jnp.bfloat16)
    middle_l = geglu(gate_l, up_l)
    light_ffn = unproject(middle_l, down_light) * valid_rows
    router_ffn_f = router_ffn.astype(jnp.float32)
    score_ffn = pick_scalar(
        pick_query,
        jax.nn.sigmoid(jnp.einsum("dsc,c->ds", normed_ffn, router_ffn_f, precision=highest)),
    )
    ffn_rows = pick_rows(pick_query, normed_ffn).astype(jnp.bfloat16)
    gate_h = project(ffn_rows, gate_heavy).astype(jnp.bfloat16)
    up_h = project(ffn_rows, up_heavy).astype(jnp.bfloat16)
    middle_h = geglu(gate_h, up_h)
    heavy_fproj = unproject(middle_h, down_heavy)
    heavy_ffn = put_rows(pick_query, heavy_fproj * score_ffn[:, :, None])
    share = model_width // lax.axis_size("branch")
    own_cols = lax.axis_index("branch") * share
    mixed = lax.dynamic_slice_in_dim(hidden, own_cols, share, 2) + lax.psum_scatter(
        (light_ffn + heavy_ffn).astype(jnp.bfloat16), "branch", scatter_dimension=2, tiled=True
    ).astype(jnp.float32)
    grad_out = cotangent.astype(jnp.float32)
    grad_light = (grad_out * valid_rows).astype(jnp.bfloat16)
    grad_down_light = weight_grad(grad_light, middle_l)
    grad_gate_l, grad_up_l = geglu_back(gate_l, up_l, project(grad_light, down_light))
    grad_gate_light = weight_grad(ffn_low, grad_gate_l)
    grad_up_light = weight_grad(ffn_low, grad_up_l)
    grad_rows = pick_rows(pick_query, grad_out)
    grad_heavy = (grad_rows * score_ffn[:, :, None]).astype(jnp.bfloat16)
    score_ffn_part = jnp.sum(grad_rows * heavy_fproj, axis=-1)
    grad_down_heavy = weight_grad(grad_heavy, middle_h)
    grad_gate_h, grad_up_h = geglu_back(gate_h, up_h, project(grad_heavy, down_heavy))
    grad_gate_heavy = weight_grad(ffn_rows, grad_gate_h)
    grad_up_heavy = weight_grad(ffn_rows, grad_up_h)
    heavy_ffn_rows = unproject(grad_gate_h, gate_heavy) + unproject(grad_up_h, up_heavy)
    ffn_part = (
        unproject(grad_gate_l, gate_light)
        + unproject(grad_up_l, up_light)
        + put_rows(pick_query, heavy_ffn_rows)
    )
    grad_normed_ffn, grad_score_ffn = (
        lax.psum(ffn_part.astype(jnp.bfloat16), "branch").astype(jnp.float32),
        lax.psum(score_ffn_part.astype(jnp.bfloat16), "branch").astype(jnp.float32),
    )
    pre_ffn = put_scalar(pick_query, grad_score_ffn * score_ffn * (1.0 - score_ffn))
    grad_normed_ffn = grad_normed_ffn + pre_ffn[:, :, None] * router_ffn_f
    grad_router_ffn = jnp.einsum("ds,dsc->c", pre_ffn, normed_ffn, precision=highest)
    grad_gain_ffn = jnp.sum(grad_normed_ffn * unit_ffn, axis=(0, 1))
    grad_unit_f = grad_normed_ffn * gain_ffn_f
    grad_hidden = grad_out + inv_ffn * (
        grad_unit_f - unit_ffn * jnp.mean(grad_unit_f * unit_ffn, axis=-1, keepdims=True)
    )
    grad_light_attn = (grad_hidden * valid_rows).astype(jnp.bfloat16)
    grad_wo_light = weight_grad(grad_light_attn, piece_out)
    grad_light_out = split_heads(project(grad_light_attn, wo_light).astype(jnp.bfloat16))
    wide_grad = jnp.zeros((documents, local_len + 2 * radius, 2 * light_width), jnp.float32)
    light_raw, light_plow, unused_delta = score_grads(
        heads_q, wide_k, wide_v, light_bias, piece_lse, grad_light_out, None
    )
    query_pieces = contract_query(light_raw, wide_k)
    key_terms = jnp.concatenate(
        [contract_key(light_raw, heads_q), contract_key(light_plow, grad_light_out)], axis=2
    )
    wide_grad = wide_grad.at[:, 0:key_span].add(key_terms)
    grad_light_q = query_pieces.astype(jnp.bfloat16)
    outer_rims = jnp.concatenate(
        [wide_grad[:, :radius], wide_grad[:, radius + local_len :]], axis=1
    )
    returned = with_halo(outer_rims.astype(jnp.bfloat16), (("seq", 1),), radius).astype(
        outer_rims.dtype
    )
    inner = wide_grad[:, radius : radius + local_len]
    inner = inner + jnp.pad(returned[:, :radius], ((0, 0), (0, local_len - radius), (0, 0)))
    inner = inner + jnp.pad(returned[:, 3 * radius :], ((0, 0), (local_len - radius, 0), (0, 0)))
    grad_light_k = inner[:, :, :light_width].astype(jnp.bfloat16)
    grad_light_v = inner[:, :, light_width:].astype(jnp.bfloat16)
    grad_wq_light = weight_grad(normed_low, grad_light_q)
    grad_wk_light = weight_grad(normed_low, grad_light_k)
    grad_wv_light = weight_grad(normed_low, grad_light_v)
    light_part = (
        unproject(grad_light_q, wq_light)
        + unproject(grad_light_k, wk_light)
        + unproject(grad_light_v, wv_light)
    )
    grad_hrows = pick_rows(pick_query, grad_hidden)
    grad_heavy_attn = (grad_hrows * score_query[:, :, None]).astype(jnp.bfloat16)
    score_query_part = jnp.sum(grad_hrows * heavy_proj, axis=-1)
    grad_wo_heavy = weight_grad(grad_heavy_attn, heavy_out)
    grad_heavy_out = project(grad_heavy_attn, wo_heavy).astype(jnp.bfloat16)
    heavy_raw, heavy_plow, heavy_delta = score_grads(
        split_heads(heavy_q),
        split_heads(all_k),
        split_heads(all_v),
        heavy_bias,
        heavy_lse,
        split_heads(grad_heavy_out),
        None,
    )
    grad_heavy_q = contract_query(heavy_raw, split_heads(all_k)).astype(jnp.bfloat16)
    every_kv = jnp.concatenate(
        [
            contract_key(heavy_raw, split_heads(heavy_q)),
            contract_key(heavy_plow, split_heads(grad_heavy_out)),
        ],
        axis=2,
    )
    own_kv = lax.psum_scatter(every_kv, "seq", scatter_dimension=1, tiled=True)
    grad_heavy_k = own_kv[:, :, :heavy_width].astype(jnp.bfloat16)
    grad_heavy_v = own_kv[:, :, heavy_width:].astype(jnp.bfloat16)
    grad_scaled = unproject(grad_heavy_v, wv_heavy)
    score_key_part = jnp.sum(grad_scaled * key_rows, axis=-1)
    grad_key_rows = unproject(grad_heavy_k, wk_heavy) + grad_scaled * score_key[:, :, None]
    grad_wq_heavy = weight_grad(heavy_in, grad_heavy_q)
    grad_wk_heavy = weight_grad(key_in, grad_heavy_k)
    grad_wv_heavy = weight_grad(scaled_in, grad_heavy_v)
    attn_part = (
        light_part
        + put_rows(pick_query, unproject(grad_heavy_q, wq_heavy))
        + put_rows(pick_key, grad_key_rows)
    )
    grad_normed, grad_score_query, grad_score_key = (
        lax.psum(attn_part.astype(jnp.bfloat16), "branch").astype(jnp.float32),
        lax.psum(score_query_part.astype(jnp.bfloat16), "branch").astype(jnp.float32),
        lax.psum(score_key_part.astype(jnp.bfloat16), "branch").astype(jnp.float32),
    )
    pre_query = put_scalar(pick_query, grad_score_query * score_query * (1.0 - score_query))
    pre_key = put_scalar(pick_key, grad_score_key * score_key * (1.0 - score_key))
    grad_normed = (
        grad_normed + pre_query[:, :, None] * router_query_f + pre_key[:, :, None] * router_key_f
    )
    grad_router_query = jnp.einsum("ds,dsc->c", pre_query, normed, precision=highest)
    grad_router_key = jnp.einsum("ds,dsc->c", pre_key, normed, precision=highest)
    grad_gain_attn = jnp.sum(grad_normed * unit_attn, axis=(0, 1))
    grad_unit_a = grad_normed * gain_attn_f
    grad_tokens = grad_hidden + inv_attn * (
        grad_unit_a - unit_attn * jnp.mean(grad_unit_a * unit_attn, axis=-1, keepdims=True)
    )
    names = (
        grad_wq_light, grad_wk_light, grad_wv_light, grad_wo_light,
        grad_wq_heavy, grad_wk_heavy, grad_wv_heavy, grad_wo_heavy,
        grad_gate_light, grad_up_light, grad_down_light,
        grad_gate_heavy, grad_up_heavy, grad_down_heavy,
    )
    vectors = jnp.stack(
        [grad_gain_attn, grad_router_query, grad_router_key, grad_gain_ffn, grad_router_ffn], axis=1
    )
    packed = jnp.concatenate([g.astype(jnp.bfloat16) for g in names + (vectors,)], axis=1)
    summed = lax.psum_scatter(packed, "seq", scatter_dimension=0, tiled=True).astype(jnp.float32)
    widths = [g.shape[1] for g in names]
    cuts = [sum(widths[:i]) for i in range(len(widths) + 1)]
    (
        grad_wq_light, grad_wk_light, grad_wv_light, grad_wo_light,
        grad_wq_heavy, grad_wk_heavy, grad_wv_heavy, grad_wo_heavy,
        grad_gate_light, grad_up_light, grad_down_light,
        grad_gate_heavy, grad_up_heavy, grad_down_heavy,
    ) = [summed[:, cuts[i] : cuts[i + 1]] for i in range(len(widths))]
    grad_gain_attn, grad_router_query, grad_router_key, grad_gain_ffn, grad_router_ffn = [
        summed[:, cuts[-1] + i] for i in range(5)
    ]
    return (
        mixed,
        grad_tokens,
        grad_gain_attn,
        grad_router_query,
        grad_router_key,
        grad_wq_light,
        grad_wk_light,
        grad_wv_light,
        grad_wo_light,
        grad_wq_heavy,
        grad_wk_heavy,
        grad_wv_heavy,
        grad_wo_heavy,
        grad_gain_ffn,
        grad_router_ffn,
        grad_gate_light,
        grad_up_light,
        grad_down_light,
        grad_gate_heavy,
        grad_up_heavy,
        grad_down_heavy,
    )


ORDER = (
    "load", "rowskv", "norm", "pre0", "qkv", "pre1", "gp0_2", "la0", "predmh", "gp0_1", "gp0_3", "hattn",
    "wgp", "la1", "hproj", "nf00", "nf01", "fh0", "fl00", "fl01", "nf10", "nf11", "fh1", "hgrB1",
    "ar1000_1", "ar1011_1", "hgrA1", "fl11", "hgrA0", "ar1011_2", "rs1a", "rs1b", "fl10", "rs1c",
    "ar1010_1", "ar1001_1", "hgrB2", "ar1111_1", "hgrB0", "ar1000_2", "ar1110_1", "ar1001_2", "ar1010_2",
    "ar1101_1", "rs1r", "mixt1", "ar1100_1", "ar1010_3", "rs0d", "mixs1", "ar1001_3", "ar1110_2",
    "ar1101_2", "rs0a", "lgB", "ar1100_2", "ar1011_3", "rs0b", "mixt0", "ar1111_2", "ar1110_3", "hgrA2",
    "ar1100_3", "ar1111_3", "gp1_2", "ar1101_3", "ar1000_3", "rs0c", "mx0", "rs0r", "mixs0", "lgA",
    "ar1000_4", "ar1110_4", "mx1", "ar1001_4", "ar1111_4", "hg00", "ar1010_4", "ar1011_4", "ar1101_4",
    "hg01", "ar1100_4", "rs2a", "hg11", "hg10", "hb1", "lb1", "lb0", "hb0", "rs2b", "rs2c", "rs2r", "abt10",
    "rs3a", "gp1_3", "rs3b", "abt11", "gp1_1", "gp2_2", "awgA", "abt00", "gp3_2", "awgB", "abt01", "rs4a",
    "gp2_1", "gp3_3", "ar2000_1", "ar2001_1", "ar2110_1", "rs3c", "mixf0", "rs1d", "ar2100_1", "ar2111_1",
    "rs3r", "gp2_3", "blank", "ar2010_1", "gp3_1", "ar2101_1", "ar2000_2", "ar2011_1", "hk0", "hk1", "aqgA",
    "rs0e", "rs4b", "rs4r", "aqgB", "ar2011_2", "rs4d", "ar2000_3", "kar0_1", "rs2d", "ar2010_2", "rs3d",
    "ar2101_2", "rs1e", "rs5a", "ar2100_2", "kar0_2", "ar2110_2", "rs5d", "ar2011_3", "rs4c", "rs5b",
    "rs5c", "kar1_1", "ar2100_3", "rs3e", "kar0_3", "kar1_2", "ar2001_2", "rs2e", "ar2101_3", "rs5r",
    "gains", "ar2111_2", "rs4e", "ar2001_3", "kar1_3", "ar2111_3", "ar2010_3", "ar2110_3", "kar1_4",
    "kar0_4", "ar2100_4", "rs5e", "vec", "ar2111_4", "ar2000_4", "ar2001_4", "ar2011_4", "ar2101_4",
    "ar2010_4", "mixf1", "tok10", "tok00", "ar2110_4", "tok11", "tok01", "vece",
)
BF = jnp.bfloat16
F32 = jnp.float32
MESH = pl.DeviceIdType.MESH


def mm(a, b):
    return jnp.dot(a, b, preferred_element_type=F32)


def mmt(a, b):
    return lax.dot_general(a, b, (((1,), (1,)), ((), ())), preferred_element_type=F32)


def tmm(a, b):
    return lax.dot_general(a, b, (((0,), (0,)), ((), ())), preferred_element_type=F32)


def row_sum(values):
    return jnp.sum(values, axis=-1, keepdims=True)


def gelu_parts(v):
    c = math.sqrt(2.0 / math.pi)
    square = v * v
    t = jnp.tanh(c * v * (1.0 + 0.044715 * square))
    act = 0.5 * v * (1.0 + t)
    slope = 0.5 * (1.0 + t) + (0.5 * c) * v * (1.0 - t * t) * (1.0 + 0.134145 * square)
    return act, slope


def layer_kernel(dims, *refs):
    docs, rows, width, slots, n_seq, wl, wh, fl_n, fh_n = dims
    nz = n_seq // 2
    chunk = width // n_seq
    half = rows // 2
    quarter = rows // 4
    radius = WINDOW // 2
    share = width // 4
    it = iter(refs)

    def take(count):
        return [next(it) for _ in range(count)]

    lens, qi, ki, ga_v, rq_v, rk_v, gf_v, rf_v = take(8)
    (tok_h, cot_h, wql_h, wkl_h, wvl_h, wol_h, wqh_h, wkh_h, wvh_h, woh_h,
     gl_h, ul_h, dl_h, gh_h, uh_h, dh_h) = take(16)
    gt_o, mix_o, pack_o, vec_o = take(4)
    (tok, cot, wqkv, wola, whq, whk, whv, woha, wgul, wdl, wguh, wdh, wkeep) = take(13)
    (nl, inva, hin, kin, sin, qbuf, kvw, pbuf, loall, hqx, kvall, ph, hoall, qall, doall, hproj, backr, qrow, kpart, ktot, k1, k2) = take(22)
    (pqk, pqkt, parts, tot1, tot2, r1, r2, cols) = take(8)
    (dm, dmh, grow, fl, invf, mid, dgu, frow, ghr, midh, dguh) = take(11)
    (mixb, mixr, mixa, ghf, ghb, dol, dox, gah, dqh, dkvw, rims, rimr, dqkv, dkvh) = take(14)
    (g_h, g_l, ra, rb, rl, packed, vbuf, vr, vect) = take(2) + [take(6), take(6), take(6)] + take(4)
    g_a = wguh
    (load_s, wg_s, wg_r, wf_s, wf_r, lo_s, lo_r, ho_s, ho_r, ka_s, ka_r, ar_s, ar_r, ag_s, ag_r, fw_s, fw_r, halo_s, halo_r, rim_s, rim_r,
     mx_s, mx_r, wa_s, wa_r, wz_s, wz_r, rl_s, rl_r, v_s, v_r, out_s) = take(32)

    b = lax.axis_index("branch")
    s = lax.axis_index("seq")
    bit_x = b % 2
    bit_y = b // 2
    core = s % 2
    z = s // 2
    offset = s * rows
    dev_x = (b + 1 - 2 * bit_x, s)
    dev_y = (b + 2 - 4 * bit_y, s)
    sibling = (b, s + 1 - 2 * core)

    def zpeer(k):
        return (z + k) % nz

    def same_core(k):
        return (b, 2 * zpeer(k) + core)

    late = []

    def send(src, dst, ssem, rsem, dev, when=None):
        copy = pltpu.make_async_remote_copy(
            src_ref=src, dst_ref=dst, send_sem=ssem, recv_sem=rsem, device_id=dev, device_id_type=MESH
        )
        if when is None:
            copy.start()
        else:
            pl.when(when)(copy.start)
        return copy

    def arrived(dst, ssem, rsem, dev):
        pltpu.make_async_remote_copy(
            src_ref=dst, dst_ref=dst, send_sem=ssem, recv_sem=rsem, device_id=dev, device_id_type=MESH
        ).wait_recv()

    loads = {}

    def load(name, src, dst, i):
        copy = pltpu.make_async_copy(src, dst, load_s.at[i])
        copy.start()
        loads[name] = copy

    load("tok", tok_h, tok, 0)
    load("whq", wqh_h, whq, 1)
    load("whk", wkh_h, whk, 2)
    load("whv", wvh_h, whv, 3)
    load("wq", wql_h, wqkv.at[:, 0:wl], 4)
    load("wk", wkl_h, wqkv.at[:, wl : 2 * wl], 5)
    load("wv", wvl_h, wqkv.at[:, 2 * wl : 3 * wl], 6)
    load("wol", wol_h, wola.at[b], 7)
    load("who", woh_h, woha.at[b], 8)
    load("cot", cot_h, cot, 9)
    load("wdl", dl_h, wdl, 10)
    load("wdh", dh_h, wdh, 11)
    load("gl", gl_h, wgul.at[:, 0:fl_n], 12)
    load("ul", ul_h, wgul.at[:, fl_n : 2 * fl_n], 13)
    load("gh", gh_h, wguh.at[:, 0:fh_n], 14)
    load("uh", uh_h, wguh.at[:, fh_n : 2 * fh_n], 15)
    own_rows = pl.ds(pl.multiple_of(chunk * s, chunk), chunk)
    load("gk", gh_h.at[own_rows], wkeep.at[:, 0:fh_n], 16)
    load("uk", uh_h.at[own_rows], wkeep.at[:, fh_n : 2 * fh_n], 17)

    barrier = pltpu.get_barrier_semaphore()
    for k in range(1, 4):
        pl.semaphore_signal(barrier, inc=1, device_id=((b + k) % 4, s), device_id_type=MESH)

    def greet(k, carry):
        pl.semaphore_signal(barrier, inc=1, device_id=(b, (s + k) % n_seq), device_id_type=MESH)
        return carry

    lax.fori_loop(1, n_seq, greet, 0)
    pl.semaphore_wait(barrier, 3 + n_seq - 1)

    gain_a, router_q, router_k, gain_f, router_f = [
        ref[...].astype(F32).reshape(1, width) for ref in (ga_v, rq_v, rk_v, gf_v, rf_v)
    ]

    def as_column(row):
        count = row.shape[1]
        square = lax.broadcasted_iota(jnp.int32, (count, count), 0)
        same = square == lax.broadcasted_iota(jnp.int32, (count, count), 1)
        return row_sum(jnp.where(same, row.astype(F32), 0.0)).astype(jnp.int32)

    idx_row = [[ref[d : d + 1, :] for ref in (qi, ki)] for d in range(docs)]
    idx_col = [[as_column(row) for row in idx_row[d]] for d in range(docs)]

    def valid_rows(d, first, count):
        at = lax.broadcasted_iota(jnp.int32, (count, 1), 0) + (offset + first)
        return jnp.where(at < lens[d], 1.0, 0.0).astype(F32)

    big = 128

    def tiles(count, size, body):
        def step(t, carry):
            body(pl.multiple_of(t * size, size))
            return carry

        lax.fori_loop(0, count // size, step, 0)

    flights = {}

    def add_rows(src, at, buf, base, dst, count):
        size = min(count, 32)

        def body(t, carry):
            r = pl.multiple_of(t * size, size)
            here = pl.ds(pl.multiple_of(at + r, 16), size)
            value = src[here, :].astype(F32) + buf[pl.ds(pl.multiple_of(base + r, 16), size), :].astype(F32)
            dst[here, :] = value.astype(BF)
            return carry

        lax.fori_loop(0, count // size, body, 0)

    def rows_sum(key, src, dst, b1, b2, ss, rs, base, count, way, src_base=None):
        first, second = ((dev_x, bit_x), (dev_y, bit_y))[:: 1 - 2 * way]
        two, four = count // 2, count // 4
        keep1, send1 = two * first[1], two * (1 - first[1])
        keep2, send2 = keep1 + four * second[1], keep1 + four * (1 - second[1])
        shift = base if src_base is None else src_base

        def rows_at(ref, at, size, frm):
            return ref.at[pl.ds(pl.multiple_of(frm + at, 16), size)]

        def start():
            flights[key, 0] = send(rows_at(src, send1, two, shift), b1, ss.at[0], rs.at[0], first[0])

        def one():
            arrived(b1, ss.at[0], rs.at[0], first[0])
            add_rows(src, shift + send2, b1, send2 - keep1, src, four)
            flights[key, 1] = send(rows_at(src, send2, four, shift), b2, ss.at[1], rs.at[1], second[0])
            add_rows(src, shift + keep2, b1, keep2 - keep1, src, four)

        def two_():
            arrived(b2, ss.at[1], rs.at[1], second[0])
            size = min(four, 32)

            def body(t, carry):
                r = pl.multiple_of(t * size, size)
                value = src[pl.ds(pl.multiple_of(shift + keep2 + r, 16), size), :].astype(F32)
                value = value + b2[pl.ds(r, size), :].astype(F32)
                dst[pl.ds(pl.multiple_of(base + keep2 + r, 16), size), :] = value.astype(BF)
                return carry

            lax.fori_loop(0, four // size, body, 0)
            own = rows_at(dst, keep2, four, base)
            flights[key, 2] = send(own, own, ss.at[2], rs.at[2], second[0])

        def three():
            arrived(rows_at(dst, send2, four, base), ss.at[2], rs.at[2], second[0])
            own = rows_at(dst, keep1, two, base)
            flights[key, 3] = send(own, own, ss.at[3], rs.at[3], first[0])

        def last_():
            arrived(rows_at(dst, send1, two, base), ss.at[3], rs.at[3], first[0])
            flights[key, 0].wait_send()
            flights[key, 1].wait_send()

        return start, one, two_, three, last_

    sums = {}
    for a in (1, 2):
        for d in range(docs):
            for h in range(2):
                for u in range(2):
                    sums[a, d, h, u] = rows_sum(
                        (a, d, h, u), parts.at[d], tot2.at[d], r1.at[d, h, u], r2.at[d, h, u],
                        ar_s.at[a, d, h, u], ar_r.at[a, d, h, u], half * h + quarter * u, quarter, u,
                    )
    for d in range(docs):
        sums[d] = rows_sum(
            d, kpart.at[d], ktot.at[d], k1.at[d], k2.at[d], ka_s.at[d], ka_r.at[d], slots, slots, d, 0
        )

    def ar_start(a, d, h):
        for u in range(2):
            sums[a, d, h, u][0]()

    def ar_sent(a, d):
        for h in range(2):
            for u in range(2):
                flights[(a, d, h, u), 2].wait_send()
                flights[(a, d, h, u), 3].wait_send()

    steps = {}

    def step(name):
        def keep(body):
            steps[name] = body
            return body

        return keep

    def halves(core_of):
        return (
            (wola, pl.ds(pl.multiple_of(width // 2 * core_of, 16), width // 2)),
            (woha, pl.ds(pl.multiple_of(wh // 2 * core_of, 16), wh // 2)),
        )

    @step("load")
    def _():
        loads["wol"].wait()
        loads["who"].wait()
        for k in range(1, 4):
            for i, (ref, part) in enumerate(halves(core)):
                block = ref.at[b, part]
                late.append(send(block, block, wg_s.at[k - 1, i], wg_r.at[k - 1, i], ((b + k) % 4, s)))
        loads["tok"].wait()

    @step("wgp")
    def _():
        for k in range(1, 4):
            frm = (b + 4 - k) % 4
            for i, (ref, part) in enumerate(halves(core)):
                block = ref.at[frm, part]
                arrived(block, wg_s.at[k - 1, i], wg_r.at[k - 1, i], (frm, s))
                late.append(send(block, block, wf_s.at[k - 1, i], wf_r.at[k - 1, i], sibling))

    def projections_wait():
        for k in range(1, 4):
            frm = (b + 4 - k) % 4
            for i, (ref, part) in enumerate(halves(1 - core)):
                arrived(ref.at[frm, part], wf_s.at[k - 1, i], wf_r.at[k - 1, i], sibling)

    @step("norm")
    def _():
        for d in range(docs):

            def norm_body(t, d=d):
                r = pl.ds(t, big)
                x = tok[d, r, :].astype(F32)
                inv = lax.rsqrt(row_sum(x * x) * (1.0 / width) + epsilon)
                inva[d, r, :] = inv
                nl[d, r, :] = (x * inv * gain_a).astype(BF)

            tiles(rows, big, norm_body)

    def selectors():
        for d in range(docs):
            lane_pos = lax.broadcasted_iota(jnp.int32, (slots, rows), 1) + offset
            sub_pos = lax.broadcasted_iota(jnp.int32, (rows, slots), 0) + offset
            for i in range(2):
                here = slice(i * slots, (i + 1) * slots)
                pqk[d, here, :] = jnp.where(idx_col[d][i] == lane_pos, 1.0, 0.0).astype(BF)
                pqkt[d, :, here] = jnp.where(idx_row[d][i] == sub_pos, 1.0, 0.0).astype(BF)

    def alive(d, i):
        return jnp.where(idx_col[d][i] >= 0, 1.0, 0.0).astype(F32)

    SQ, SK, SF, PREQ, PREF, PREK = range(6)

    def mine(d):
        return slice(d * slots, (d + 1) * slots)

    def routed_rows():
        for d in range(docs):
            x = mm(pqk[d], tok[d])
            picked = x * lax.rsqrt(row_sum(x * x) * (1.0 / width) + epsilon) * gain_a
            score_q = jax.nn.sigmoid(row_sum(picked[:slots] * router_q)) * alive(d, 0)
            score_k = jax.nn.sigmoid(row_sum(picked[slots:] * router_k)) * alive(d, 1)
            cols[SQ, mine(d), :] = score_q
            cols[SK, mine(d), :] = score_k
            hin[mine(d), :] = picked[:slots].astype(BF)
            kin[mine(d), :] = picked[slots:].astype(BF)
            sin[mine(d), :] = (picked[slots:] * score_k).astype(BF)
            pad_lane = lax.broadcasted_iota(jnp.int32, (slots, 256 - wh), 1)
            kvall[s, mine(d), wh:256] = jnp.where(
                pad_lane == 0, (1.0 - alive(d, 1)) * masked_value, 0.0
            ).astype(BF)
            kvall[s, mine(d), 256 + wh : 512] = jnp.zeros((slots, 256 - wh), BF)
        loads["whk"].wait()
        kvall[s, :, 0:wh] = mmt(kin[...], whk[...]).astype(BF)
        loads["whv"].wait()
        kvall[s, :, 256 : 256 + wh] = mmt(sin[...], whv[...]).astype(BF)

    at_end = (z == 0) | (z == nz - 1)
    inner = (z > 0) & (z < nz - 1)
    low_side = jnp.where(z < nz // 2, 1, 0)

    def gather_start(g, ref, part):
        block = ref.at[s, part]
        late.append(send(block, block, ag_s.at[g, 0], ag_r.at[g, 0], sibling))
        for k in (2, 1, 3):
            near = (z != 0) if k == 3 else (z != 3) if k == 1 else (z >= 0)
            late.append((near, send(block, block, ag_s.at[g, k], ag_r.at[g, k], same_core(k), near)))

    def gather_pass(g, ref, part, k):
        block = ref.at[2 * zpeer(nz - k) + core, part]
        arrived(block, ag_s.at[g, k], ag_r.at[g, k], same_core(nz - k))
        late.append(send(block, block, fw_s.at[g, k], fw_r.at[g, k], sibling))
        if k == 2:
            onward = (b, 2 * (z + 1 - 2 * low_side) + core)
            slot = 3 - 2 * low_side
            late.append((inner, send(block, block, fw_s.at[g, 0], ag_r.at[g, slot], onward, inner)))

    def gather_end(g, ref, part):
        arrived(ref.at[s + 1 - 2 * core, part], ag_s.at[g, 0], ag_r.at[g, 0], sibling)
        for k in range(1, nz):
            block = ref.at[2 * zpeer(nz - k) + 1 - core, part]
            arrived(block, fw_s.at[g, k], fw_r.at[g, k], sibling)

    def routed(d):
        return pl.ds(d * slots, slots)

    every = pl.ds(0, docs * slots)

    @step("rowskv")
    def _():
        selectors()
        routed_rows()
        gather_start(0, kvall, every)


    last = n_seq - 1
    left = (b, (s + last) % n_seq)
    right = (b, (s + 1) % n_seq)

    @step("qkv")
    def _():
        for name in ("wq", "wk", "wv"):
            loads[name].wait()
        for d in range(docs):

            def qkv_body(t, d=d):
                r = mm(nl[d, pl.ds(t, half), :], wqkv[...]).astype(BF)
                qbuf[d, pl.ds(t, half), :] = r[:, 0:wl]
                kvw[d, pl.ds(pl.multiple_of(t + radius, 32), half), :] = r[:, wl : 3 * wl]

            tiles(rows, half, qkv_body)

            @pl.when(s == 0)
            def _(d=d):
                kvw[d, 0:radius, :] = jnp.zeros((radius, 2 * wl), BF)

            @pl.when(s == last)
            def _(d=d):
                kvw[d, rows + radius : rows + 2 * radius, :] = jnp.zeros((radius, 2 * wl), BF)

            late.append((s > 0, send(
                kvw.at[d, pl.ds(radius, radius)], kvw.at[d, pl.ds(rows + radius, radius)],
                halo_s.at[d, 0], halo_r.at[d, 0], left, s > 0,
            )))
            late.append((s < last, send(
                kvw.at[d, pl.ds(rows, radius)], kvw.at[d, pl.ds(0, radius)],
                halo_s.at[d, 1], halo_r.at[d, 1], right, s < last,
            )))
        loads["whq"].wait()
        hqx[:, 0:wh] = mmt(hin[...], whq[...]).astype(BF)
        pad_lane = lax.broadcasted_iota(jnp.int32, (docs * slots, 256 - wh), 1)
        hqx[:, wh:256] = jnp.where(pad_lane == 0, 8.0, 0.0).astype(BF)

    def halo_wait(d):
        @pl.when(s < last)
        def _():
            arrived(kvw.at[d, pl.ds(rows + radius, radius)], halo_s.at[d, 0], halo_r.at[d, 0], right)

        @pl.when(s > 0)
        def _():
            arrived(kvw.at[d, pl.ds(0, radius)], halo_s.at[d, 1], halo_r.at[d, 1], left)

    blk = WINDOW
    span = 2 * WINDOW
    n_blk = rows // blk

    def two_heads(v):
        lane = lax.broadcasted_iota(jnp.int32, v.shape, 1)
        zero = jnp.zeros_like(v)
        return jnp.concatenate([jnp.where(lane < HD, v, zero), jnp.where(lane < HD, zero, v)], axis=0)

    def one_of_two(v):
        lane = lax.broadcasted_iota(jnp.int32, (blk, 2 * HD), 1)
        return jnp.where(lane < HD, v[:blk], v[blk:])

    def light_attention(d):
        row = lax.broadcasted_iota(jnp.int32, (2 * blk, span), 0) % blk
        col = lax.broadcasted_iota(jnp.int32, (2 * blk, span), 1)
        near = (col >= row) & (col <= row + WINDOW)

        def body(i, carry):
            blocks = [2 * i, 2 * i + 1]
            ats = [pl.multiple_of(j * blk, blk) for j in blocks]
            scores = []
            for at in ats:
                q2 = two_heads(qbuf[d, pl.ds(at, blk), :])
                scores.append(mmt(q2, kvw[d, pl.ds(at, span), 0:wl]))
            probs = []
            for at, score in zip(ats, scores):
                pos = col + (offset + at - radius)
                seen = near & (pos >= 0) & (pos < lens[d])
                e = jnp.where(seen, score * HD ** (-0.5), masked_value)
                e = jnp.exp(e - jnp.max(e, axis=-1, keepdims=True))
                probs.append((e * (1.0 / row_sum(e))).astype(BF))
            for j, at, p in zip(blocks, ats, probs):
                pbuf[d * n_blk + j] = p
                out = one_of_two(mm(p, kvw[d, pl.ds(at, span), wl : 2 * wl]))
                loall[b, d, pl.ds(at, blk), :] = (out * valid_rows(d, at, blk)).astype(BF)
            return carry

        lax.fori_loop(0, n_blk // 2, body, 0)

    def three_heads(v):
        lane = lax.broadcasted_iota(jnp.int32, v.shape, 1)
        zero = jnp.zeros_like(v)
        return jnp.concatenate(
            [jnp.where((lane // HD == h) | (lane >= wh), v, zero) for h in range(wh // HD)], axis=0
        )

    def one_of_three(v):
        lane = lax.broadcasted_iota(jnp.int32, (slots, 256), 1)
        total = jnp.zeros((slots, 256), F32)
        for h in range(wh // HD):
            total = jnp.where(lane // HD == h, v[h * slots : (h + 1) * slots], total)
        return total

    def keys_of(d, at):
        return kvall[:, mine(d), at : at + 256].reshape(n_seq * slots, 256)

    def spread(column):
        lane = lax.broadcasted_iota(jnp.int32, (slots, 256 - wh), 1)
        out = jnp.zeros((slots, 256 - wh), F32)
        for h in range(wh // HD):
            value = column[h * slots : (h + 1) * slots]
            high = value.astype(BF).astype(F32)
            low = value - high
            out = jnp.where(lane == 2 * h, high, jnp.where(lane == 2 * h + 1, low, out))
        return out.astype(BF)

    def own_keys(d, at):
        v = kvall[s, mine(d), at : at + 256]
        lane = lax.broadcasted_iota(jnp.int32, v.shape, 1)
        zero = jnp.zeros_like(v)
        one = jnp.ones_like(v)
        return jnp.concatenate(
            [
                jnp.where(
                    lane // HD == h, v, jnp.where((lane == wh + 2 * h) | (lane == wh + 2 * h + 1), one, zero)
                )
                for h in range(wh // HD)
            ],
            axis=0,
        )

    def heavy_attention(d):
        q3 = three_heads(hqx[mine(d), :])
        scores = mmt(q3, keys_of(d, 0)) * HD ** (-0.5)
        top = jnp.max(scores, axis=-1, keepdims=True)
        e = jnp.exp(scores - top)
        sums = row_sum(e)
        p = (e * (1.0 / sums)).astype(BF)
        ph[d] = p
        qall[s, mine(d), 0:wh] = hqx[mine(d), 0:wh]
        qall[s, mine(d), wh:256] = spread((top + jnp.log(sums)) * -(HD**0.5))
        hoall[b, mine(d), :] = one_of_three(mm(p, keys_of(d, 256))).astype(BF)

    def to_branches(block, ssem, rsem, k):
        return send(block, block, ssem, rsem, ((b + k) % 4, s))

    def from_branch(ref, ssem, rsem, k):
        frm = (b + 4 - k) % 4
        arrived(ref.at[frm], ssem, rsem, (frm, s))

    for d in range(docs):

        @step("la%d" % d)
        def _(d=d):
            halo_wait(d)
            light_attention(d)
            for k in range(1, 4):
                late.append(to_branches(loall.at[b, d], lo_s.at[d, k - 1], lo_r.at[d, k - 1], k))

    @step("hattn")
    def _():
        gather_end(0, kvall, every)
        for d in range(docs):
            heavy_attention(d)
        for k in range(1, 4):
            late.append(to_branches(hoall.at[b], ho_s.at[k - 1], ho_r.at[k - 1], k))
        gather_start(1, qall, every)

    gathers = ((0, kvall, every), (1, qall, every)) + tuple((2 + d, doall, routed(d)) for d in range(docs))
    for g, ref, part in gathers:
        for k in range(1, nz):

            @step("gp%d_%d" % (g, k))
            def _(g=g, ref=ref, part=part, k=k):
                gather_pass(g, ref, part, k)

    @step("hproj")
    def _():
        projections_wait()
        for k in range(1, 4):
            from_branch(hoall, ho_s.at[k - 1], ho_r.at[k - 1], k)
        total = mm(hoall[0, :, 0:wh], woha[0])
        for j in range(1, 4):
            total = total + mm(hoall[j, :, 0:wh], woha[j])
        hproj[...] = (total * cols[SQ]).astype(BF)

    def attention_total(d, h):
        r = pl.ds(h * half, half)
        heads = jnp.concatenate([loall[j, d, r, :] for j in range(4)], axis=1)
        out_weights = jnp.concatenate([wola[j] for j in range(4)], axis=1)
        value = mmt(heads, out_weights) + mm(pqkt[d, r, 0:slots], hproj[mine(d), :])
        tot1[d, r, :] = value.astype(BF)

    def light_pre(d):
        def body(t):
            r = pl.ds(t, half)
            dm[d, r, :] = mm(cot[d, r, :], wdl[...]) * valid_rows(d, t, half)

        tiles(rows, half, body)
        grow[mine(d), :] = mm(pqk[d, 0:slots, :], cot[d]).astype(BF)

    for d in range(docs):

        @step("pre%d" % d)
        def _(d=d):
            if d == 0:
                for name in ("cot", "wdl"):
                    loads[name].wait()
            light_pre(d)

    @step("predmh")
    def _():
        loads["wdh"].wait()
        dmh[...] = mm(grow[...], wdh[...])

    def hidden_rows(d, r):
        return tok[d, r, :].astype(F32) + tot1[d, r, :].astype(F32)

    def ffn_norm(d, h):
        def body(t):
            r = pl.ds(pl.multiple_of(h * half + t, big), big)
            hidden = hidden_rows(d, r)
            inv = lax.rsqrt(row_sum(hidden * hidden) * (1.0 / width) + epsilon)
            invf[d, r, :] = inv
            fl[d, r, :] = (hidden * inv * gain_f).astype(BF)

        tiles(half, big, body)

    for d in range(docs):
        for h in range(2):

            @step("nf%d%d" % (d, h))
            def _(d=d, h=h):
                if h == 0:
                    for k in range(1, 4):
                        frm = (b + 4 - k) % 4
                        arrived(loall.at[frm, d], lo_s.at[d, k - 1], lo_r.at[d, k - 1], (frm, s))
                attention_total(d, h)
                ffn_norm(d, h)

    def ffn_heavy(d):
        rowsf = mm(pqk[d, 0:slots, :], fl[d])
        score = jax.nn.sigmoid(row_sum(rowsf * router_f)) * alive(d, 0)
        cols[SF, mine(d), :] = score
        frow[mine(d), :] = rowsf.astype(BF)
        ghr[mine(d), :] = (grow[mine(d), :].astype(F32) * score).astype(BF)
        size = 512
        dscore = jnp.zeros((slots, 1), F32)
        for t in range(fh_n // size):
            c = slice(t * size, (t + 1) * size)
            c2 = slice(fh_n + t * size, fh_n + (t + 1) * size)
            gate = mm(frow[mine(d), :], wguh[:, c]).astype(BF).astype(F32)
            up = mm(frow[mine(d), :], wguh[:, c2]).astype(BF).astype(F32)
            act, slope = gelu_parts(gate)
            middle = (act * up).astype(BF)
            raw = dmh[mine(d), c]
            grad_mid = raw * score
            midh[mine(d), c] = middle
            dguh[mine(d), c] = (grad_mid * up * slope).astype(BF)
            dguh[mine(d), c2] = (grad_mid * act).astype(BF)
            dscore = dscore + row_sum(middle.astype(F32) * raw)
        pre = dscore * score * (1.0 - score)
        cols[PREF, mine(d), :] = pre
        backr[mine(d), :] = (mmt(dguh[mine(d), :], wguh[...]) + pre * router_f).astype(BF)

    for d in range(docs):

        @step("fh%d" % d)
        def _(d=d):
            if d == 0:
                for name in ("gh", "uh"):
                    loads[name].wait()
            ffn_heavy(d)


    def ffn_light(d, h):
        r = pl.ds(h * half, half)
        gu = mm(fl[d, r, :], wgul[...]).astype(BF)
        gate = gu[:, 0:fl_n].astype(F32)
        up = gu[:, fl_n : 2 * fl_n].astype(F32)
        act, slope = gelu_parts(gate)
        mid[d, r, :] = (act * up * valid_rows(d, h * half, half)).astype(BF)
        grad_mid = dm[d, r, :]
        dgu[d, r, 0:fl_n] = (grad_mid * up * slope).astype(BF)
        dgu[d, r, fl_n : 2 * fl_n] = (grad_mid * act).astype(BF)
        value = mmt(dgu[d, r, :], wgul[...]) + mm(pqkt[d, r, 0:slots], backr[mine(d), :])
        parts[d, r, :] = value.astype(BF)
        ar_start(1, d, h)

    for d in range(docs):
        for h in range(2):

            @step("fl%d%d" % (d, h))
            def _(d=d, h=h):
                if d == 0 and h == 0:
                    for name in ("gl", "ul"):
                        loads[name].wait()
                ffn_light(d, h)

            for a in (1, 2):
                for u in range(2):
                    for i in range(1, 5):
                        steps["ar%d%d%d%d_%d" % (a, d, h, u, i)] = sums[a, d, h, u][i]
        for i in range(1, 5):
            steps["kar%d_%d" % (d, i)] = sums[d][i]

    pieces = (
        (g_h, 0, fh_n), (g_h, fh_n, fh_n), (g_h, 2 * fh_n, fh_n), (g_l, 0, 3 * fl_n),
        (g_a, 0, wl + 2 * wh), (g_a, wl + 2 * wh, 3 * wl + 2 * wh + 128),
    )
    packed_at = [sum(piece[2] for piece in pieces[:p]) for p in range(len(pieces))]

    def chunk_rows(zz, cc):
        return pl.ds(pl.multiple_of(chunk * (2 * zz + cc), chunk), chunk)

    def chunk_of(p, zz, cc):
        grad, base, wide = pieces[p]
        return grad.at[chunk_rows(zz, cc), pl.ds(base, wide)]

    def rs_start(p, t):
        for zz in (2 * t, 2 * t + 1):
            late.append(send(
                chunk_of(p, zz, 1 - core), ra[p].at[zz], wa_s.at[p, zz], wa_r.at[p, zz], sibling
            ))

    def add_chunk(p, zz, other):
        grad, base, wide = pieces[p]

        def add_body(t, carry):
            r = pl.ds(pl.multiple_of(chunk * (2 * zz + core) + 16 * t, 16), 16)
            value = grad[r, base : base + wide].astype(F32)
            value = value + other[pl.ds(pl.multiple_of(16 * t, 16), 16), :].astype(F32)
            grad[r, base : base + wide] = value.astype(BF)
            return carry

        lax.fori_loop(0, chunk // 16, add_body, 0)

    def rs_direct(p, k, when):
        late.append((when, send(
            chunk_of(p, zpeer(k), core), rb[p].at[k - 1], wz_s.at[p, k - 1], wz_r.at[p, k - 1],
            same_core(k), when,
        )))

    def rs_own(p, k):
        zz = zpeer(k)
        arrived(ra[p].at[zz], wa_s.at[p, zz], wa_r.at[p, zz], sibling)
        add_chunk(p, zz, ra[p].at[zz])

    def rs_far(p):
        k = 1 + 2 * low_side
        rs_own(p, k)
        neighbour = (b, 2 * (z + 2 * low_side - 1) + core)
        late.append((at_end, send(
            chunk_of(p, zpeer(k), core), rl[p], rl_s.at[p], rl_r.at[p], neighbour, at_end
        )))
        rs_direct(p, k, inner)

    def rs_two(p):
        rs_own(p, 2)
        rs_direct(p, 2, at_end)

    def rs_near(p):
        k = 3 - 2 * low_side
        rs_own(p, k)
        rs_direct(p, k, z >= 0)

    def rs_relay(p):
        @pl.when(inner)
        def _():
            arrived(rl[p], rl_s.at[p], rl_r.at[p], same_core(1))
            add_chunk(p, zpeer(2), rl[p])

        rs_direct(p, 2, inner)

    for p in range(len(pieces)):
        steps["rs%da" % p] = functools.partial(rs_far, p)
        steps["rs%db" % p] = functools.partial(rs_two, p)
        steps["rs%dc" % p] = functools.partial(rs_near, p)
        steps["rs%dd" % p] = functools.partial(rs_own, p, nz)
        steps["rs%dr" % p] = functools.partial(rs_relay, p)

    def rs_end(p):
        grad, base, wide = pieces[p]
        for k, when in ((1, z > 0), (2, z >= 0), (3, z < nz - 1)):

            @pl.when(when)
            def _(k=k):
                arrived(rb[p].at[k - 1], wz_s.at[p, k - 1], wz_r.at[p, k - 1], same_core(nz - k))

        at = packed_at[p]

        def add_body(t, carry):
            r = pl.ds(pl.multiple_of(16 * t, 16), 16)
            value = grad[pl.ds(pl.multiple_of(chunk * s + 16 * t, 16), 16), base : base + wide].astype(F32)
            for k in range(1, nz):
                value = value + rb[p][k - 1, r, :].astype(F32)
            packed[r, at : at + wide] = value
            return carry

        lax.fori_loop(0, chunk // 16, add_body, 0)
        leave(packed.at[:, at : at + wide], pack_o.at[:, at : at + wide], 7 + p)

    @step("blank")
    def _():
        ktot[:, 0:slots, :] = jnp.zeros((docs, slots, width), BF)

        @pl.when(z == 0)
        def _():
            for buf in rb:
                buf[0] = jnp.zeros(buf.shape[1:], BF)

        @pl.when(z == nz - 1)
        def _():
            for buf in rb:
                buf[2] = jnp.zeros(buf.shape[1:], BF)

    def half_features(t):
        return slice(t * (width // 2), (t + 1) * (width // 2))

    def heavy_ffn_grads(t, p):
        size = 512
        f = half_features(t)
        src, gr, first = ((frow, dguh, 0), (frow, dguh, fh_n), (ghr, midh, 0))[p]
        left_t = src[:, f].T

        def body(i, carry):
            c = pl.ds(pl.multiple_of(first + i * size, size), size)
            o = pl.ds(pl.multiple_of(p * fh_n + i * size, size), size)
            g_h[f, o] = mm(left_t, gr[:, c]).astype(BF)
            return carry

        lax.fori_loop(0, fh_n // size, body, 0)

    def light_grad(t, src, gr, ref, base):
        f = half_features(t)
        wide = gr.shape[2]
        value = tmm(src[:, :, f].reshape(docs * rows, width // 2), gr[...].reshape(docs * rows, wide))
        ref[f, base : base + wide] = value.astype(BF)

    def rows_grads(t, pairs, at):
        f = half_features(t)
        value = jnp.concatenate([tmm(src[:, f], gr) for src, gr in pairs], axis=1)
        g_a[f, at : at + 2 * wh] = value.astype(BF)

    def early_grads(t):
        light_grad(t, ghb, loall.at[b], g_a, 0)
        rows_grads(t, ((gah, hoall[b, :, 0:wh]), (hin, dqh[:, 0:wh])), wl)

    def late_grads(t):
        f = half_features(t)
        at = wl + 2 * wh
        light_grad(t, nl, dqkv, g_a, at)
        rows_grads(t, ((kin, dkvh[:, 0:wh]), (sin, dkvh[:, 256 : 256 + wh])), at + 3 * wl)
        lane = lax.broadcasted_iota(jnp.int32, (docs * slots, 128), 1)
        vectors = jnp.zeros((width // 2, 128), F32)
        for src, which, at_lane in ((hin, PREQ, 1), (kin, PREK, 2), (frow, PREF, 4)):
            vectors = vectors + tmm(src[:, f], jnp.where(lane == at_lane, cols[which], 0.0).astype(BF))
        at = at + 3 * wl + 2 * wh
        g_a[f, at : at + 128] = vectors.astype(BF)

    for t in range(2):

        for p in range(3):

            @step("hgr%s%d" % ("AB"[t], p))
            def _(t=t, p=p):
                heavy_ffn_grads(t, p)
                rs_start(p, t)

        @step("lg" + "AB"[t])
        def _(t=t):
            light_grad(t, fl, dgu, g_l, 0)
            light_grad(t, cot, mid, g_l, 2 * fl_n)
            rs_start(3, t)

        @step("awg" + "AB"[t])
        def _(t=t):
            early_grads(t)
            rs_start(4, t)

        @step("aqg" + "AB"[t])
        def _(t=t):
            late_grads(t)
            rs_start(5, t)

    def mixed_terms(d):
        for t in range(2):
            w = half_features(t)
            heavy = (mmt(midh[mine(d), :], wdh[w, :]) * cols[SF, mine(d), :]).astype(BF)
            value = mmt(wdl[w, :], mid[d]) + tmm(heavy, pqk[d, 0:slots, :])
            for j in range(2):
                mixb[2 * t + j, d] = value[j * share : (j + 1) * share].astype(BF)

    def mixed_start(d):
        column = lax.broadcasted_iota(jnp.int32, (share, width), 1) - b * share
        own = jnp.where(column == lax.broadcasted_iota(jnp.int32, (share, width), 0), 1.0, 0.0).astype(BF)
        mixa[d] = mmt(own, tok[d]) + mmt(own, tot1[d]) + mixb[b, d].astype(F32)

    def hidden_grad(d, h):
        def body(t):
            r = pl.ds(pl.multiple_of(h * half + t, big), big)
            unit = hidden_rows(d, r) * invf[d, r, :]
            w = tot2[d, r, :].astype(F32) * gain_f
            inner = row_sum(w * unit) * (1.0 / width)
            value = cot[d, r, :].astype(F32) + invf[d, r, :] * (w - unit * inner)
            ghf[d, r, :] = value
            ghb[d, r, :] = value.astype(BF)

        tiles(half, big, body)

    def heavy_back(d):
        picked = mm(pqk[d, 0:slots, :], ghb[d])
        score = cols[SQ, mine(d), :]
        gah[mine(d), :] = (picked * score).astype(BF)
        raw = mmt(picked.astype(BF), woha[b])
        pre = row_sum(hoall[b, mine(d), 0:wh].astype(F32) * raw) * score * (1.0 - score)
        cols[PREQ, mine(d), :] = pre
        dox[mine(d), 0:wh] = (raw * score).astype(BF)
        dox[mine(d), wh:256] = jnp.zeros((slots, 256 - wh), BF)
        do3 = three_heads(dox[mine(d), :])
        pf = ph[d].astype(F32)
        dp = mmt(do3, keys_of(d, 256))
        delta = row_sum(dp * pf)
        doall[s, mine(d), 0:wh] = dox[mine(d), 0:wh]
        doall[s, mine(d), wh:256] = spread(-delta)
        gather_start(2 + d, doall, routed(d))
        ds = (pf * (dp - delta) * HD ** (-0.5)).astype(BF)
        dqh[mine(d), :] = one_of_three(mm(ds, keys_of(d, 0))).astype(BF)
        query_rows = mm(dqh[mine(d), 0:wh], whq[...]) + cols[PREQ, mine(d), :] * router_q
        qrow[mine(d), :] = query_rows.astype(BF)

    def heavy_back_keys(d):
        q = qall[:, mine(d), :].reshape(n_seq * slots, 256)
        do = doall[:, mine(d), :].reshape(n_seq * slots, 256)
        live = jnp.concatenate([alive(d, 1)] * (wh // HD), axis=0) > 0
        p = jnp.exp(jnp.where(live, mmt(own_keys(d, 0), q) * HD ** (-0.5), masked_value))
        ds = (p * mmt(own_keys(d, 256), do) * HD ** (-0.5)).astype(BF)
        dkvh[mine(d), 0:256] = one_of_three(mm(ds, q)).astype(BF)
        dkvh[mine(d), 256:512] = one_of_three(mm(p.astype(BF), do)).astype(BF)

    def light_back(d):
        dkvw[d] = jnp.zeros((rows + 2 * radius, 2 * wl), F32)

        def dol_body(t):
            r = pl.ds(t, half)
            dol[d, r, :] = (mm(ghb[d, r, :], wola[b]) * valid_rows(d, t, half)).astype(BF)

        tiles(rows, half, dol_body)

        def body(i, carry):
            blocks = [2 * i, 2 * i + 1]
            ats = [pl.multiple_of(j * blk, blk) for j in blocks]
            do2s = [two_heads(dol[d, pl.ds(at, blk), :]) for at in ats]
            dps = [mmt(do2, kvw[d, pl.ds(at, span), wl : 2 * wl]) for at, do2 in zip(ats, do2s)]
            grads_s = []
            for j, dp in zip(blocks, dps):
                pf = pbuf[d * n_blk + j].astype(F32)
                grads_s.append((pf * (dp - row_sum(dp * pf)) * HD ** (-0.5)).astype(BF))
            for j, at, do2, ds in zip(blocks, ats, do2s, grads_s):
                q2 = two_heads(qbuf[d, pl.ds(at, blk), :])
                dqkv[d, pl.ds(at, blk), 0:wl] = one_of_two(mm(ds, kvw[d, pl.ds(at, span), 0:wl])).astype(BF)
                dkvw[d, pl.ds(at, span), 0:wl] += tmm(ds, q2)
                dkvw[d, pl.ds(at, span), wl : 2 * wl] += tmm(pbuf[d * n_blk + j], do2)
            return carry

        lax.fori_loop(0, n_blk // 2, body, 0)
        rims[d, 0] = dkvw[d, 0:radius, :].astype(BF)
        rims[d, 1] = dkvw[d, rows + radius : rows + 2 * radius, :].astype(BF)

        @pl.when(s == 0)
        def _():
            rimr[d, 0] = jnp.zeros((radius, 2 * wl), BF)

        @pl.when(s == last)
        def _():
            rimr[d, 1] = jnp.zeros((radius, 2 * wl), BF)

        late.append((s > 0, send(rims.at[d, 0], rimr.at[d, 1], rim_s.at[d, 0], rim_r.at[d, 0], left, s > 0)))
        late.append((s < last, send(rims.at[d, 1], rimr.at[d, 0], rim_s.at[d, 1], rim_r.at[d, 1], right, s < last)))

    def rim_wait(d):
        @pl.when(s < last)
        def _():
            arrived(rimr.at[d, 1], rim_s.at[d, 0], rim_r.at[d, 0], right)

        @pl.when(s > 0)
        def _():
            arrived(rimr.at[d, 0], rim_s.at[d, 1], rim_r.at[d, 1], left)

    def attention_back_rows(d):
        heavy_back_keys(d)
        ds_in = mm(dkvh[mine(d), 256 : 256 + wh], whv[...])
        score = cols[SK, mine(d), :]
        pre_k = row_sum(ds_in * kin[mine(d), :].astype(F32)) * score * (1.0 - score)
        cols[PREK, mine(d), :] = pre_k
        key_rows = mm(dkvh[mine(d), 0:wh], whk[...]) + ds_in * score + pre_k * router_k
        kpart[d] = key_rows.astype(BF)
        sums[d][0]()

    def attention_back_terms(d, h):
        if h == 0:
            rim_wait(d)
            dkvw[d, radius : 2 * radius, :] += rimr[d, 0].astype(F32)
            dkvw[d, rows : rows + radius, :] += rimr[d, 1].astype(F32)
            ar_sent(1, d)
        r = pl.ds(h * half, half)
        dqkv[d, r, wl : 3 * wl] = dkvw[d, pl.ds(h * half + radius, half), :].astype(BF)
        value = mmt(dqkv[d, r, :], wqkv[...]) + mm(pqkt[d, r, 0:slots], qrow[mine(d), :])
        parts[d, r, :] = value.astype(BF)
        ar_start(2, d, h)

    out_copies = []

    def leave(src, dst, i):
        copy = pltpu.make_async_copy(src, dst, out_s.at[i])
        copy.start()
        out_copies.append(copy)

    def token_grad(d, h):
        def body(t):
            r = pl.ds(pl.multiple_of(h * half + t, big), big)
            inv = inva[d, r, :]
            unit = tok[d, r, :].astype(F32) * inv
            w = (tot2[d, r, :].astype(F32) + mm(pqkt[d, r, :], ktot[d])) * gain_a
            inner = row_sum(w * unit) * (1.0 / width)
            ghf[d, r, :] = ghf[d, r, :] + inv * (w - unit * inner)

        tiles(half, big, body)
        r = pl.ds(h * half, half)
        leave(ghf.at[d, r], gt_o.at[d, r], 3 + 2 * d + h)

    for d in range(docs):

        @step("mixt%d" % d)
        def _(d=d):
            mixed_terms(d)

        @step("mx%d" % d)
        def _(d=d):
            for k in range(1, 4):
                to = (b + k) % 4
                late.append(send(
                    mixb.at[to, d], mixr.at[k - 1, d], mx_s.at[d, k - 1], mx_r.at[d, k - 1], (to, s)
                ))

        @step("mixs%d" % d)
        def _(d=d):
            mixed_start(d)

        @step("mixf%d" % d)
        def _(d=d):
            for k in range(1, 4):
                frm = (b + 4 - k) % 4
                arrived(mixr.at[k - 1, d], mx_s.at[d, k - 1], mx_r.at[d, k - 1], (frm, s))

            def mix_body(t, d=d):
                r = pl.ds(t, 32)
                value = mixa[d, r, :]
                for k in range(3):
                    value = value + mixr[k, d, r, :].astype(F32)
                mixa[d, r, :] = value

            tiles(share, 32, mix_body)
            leave(mixa.at[d], mix_o.at[d], 1 + d)

        for h in range(2):

            @step("hg%d%d" % (d, h))
            def _(d=d, h=h):
                hidden_grad(d, h)

            @step("abt%d%d" % (d, h))
            def _(d=d, h=h):
                attention_back_terms(d, h)

            @step("tok%d%d" % (d, h))
            def _(d=d, h=h):
                token_grad(d, h)

        @step("hb%d" % d)
        def _(d=d):
            heavy_back(d)

        @step("lb%d" % d)
        def _(d=d):
            light_back(d)

        @step("hk%d" % d)
        def _(d=d):
            if d == 0:
                gather_end(1, qall, every)
            gather_end(2 + d, doall, routed(d))
            attention_back_rows(d)

    vlane = lax.broadcasted_iota(jnp.int32, (chunk, 128), 1)
    eye = lax.broadcasted_iota(jnp.int32, (chunk, width), 1) - chunk * s
    eye = eye == lax.broadcasted_iota(jnp.int32, (chunk, width), 0)

    def own_column(row):
        return row_sum(jnp.where(eye, row, 0.0))

    for p in range(len(pieces)):
        steps["rs%de" % p] = functools.partial(rs_end, p)

    @step("gains")
    def _():
        for name in ("gk", "uk"):
            loads[name].wait()
        total = row_sum(packed[:, 0 : 2 * fh_n] * wkeep[...].astype(F32))
        vbuf[:, 0:1] = total + row_sum(
            packed[:, packed_at[3] : packed_at[3] + 2 * fl_n] * wgul[own_rows, :].astype(F32)
        )

    @step("vec")
    def _():
        a_at, q_at = packed_at[4:6]
        va = q_at + 3 * wl + 2 * wh
        gf_sum = vbuf[:, 0:1]
        ga_sum = row_sum(packed[:, q_at : q_at + 3 * wl] * wqkv[own_rows, :].astype(F32))
        eye_b = eye.astype(F32).astype(BF)
        for h_at, w in ((a_at + wl + wh, whq), (q_at + 3 * wl, whk), (q_at + 3 * wl + wh, whv)):
            ga_sum = ga_sum + row_sum(packed[:, h_at : h_at + wh] * mmt(eye_b, w[...]))
        vectors = packed[:, va : va + 128]

        def lane_of(i):
            return row_sum(jnp.where(vlane == i, vectors, 0.0))

        ga_sum = ga_sum + own_column(router_q) * lane_of(1) + own_column(router_k) * lane_of(2)
        gf_sum = gf_sum + own_column(router_f) * lane_of(4)
        vectors = jnp.where(vlane == 0, ga_sum / own_column(gain_a), vectors)
        vectors = jnp.where(vlane == 3, gf_sum / own_column(gain_f), vectors)
        vbuf[...] = vectors
        for k in range(1, 4):
            late.append(send(vbuf, vr.at[k - 1], v_s.at[k - 1], v_r.at[k - 1], ((b + k) % 4, s)))

    @step("vece")
    def _():
        for k in range(1, 4):
            arrived(vr.at[k - 1], v_s.at[k - 1], v_r.at[k - 1], ((b + 4 - k) % 4, s))
        vect[...] = (vbuf[...] + vr[0] + vr[1] + vr[2]).T
        leave(vect, vec_o, 0)

    for name in ORDER:
        steps[name]()

    for entry in late:
        if isinstance(entry, tuple):
            pl.when(entry[0])(entry[1].wait_send)
        else:
            entry.wait_send()
    for d in range(docs):
        ar_sent(2, d)
        flights[d, 2].wait_send()
        flights[d, 3].wait_send()
    for copy in out_copies:
        copy.wait()


def kernel_scratch(docs, rows, width, slots, n_seq, wl, wh, fl_n, fh_n):
    nz = n_seq // 2
    chunk = width // n_seq
    routed = docs * slots
    keys = n_seq * slots
    pad = -(-wh // 256) * 256
    ga_n = 4 * wl + 4 * wh + 128
    widths = [fh_n, fh_n, fh_n, 3 * fl_n, wl + 2 * wh, 3 * wl + 2 * wh + 128]
    h_n, l_n = 3 * fh_n, 3 * fl_n
    radius = WINDOW // 2
    span = rows + 2 * radius
    vmem = [
        ((docs, rows, width), BF), ((docs, rows, width), BF), ((width, 3 * wl), BF), ((4, width, wl), BF),
        ((wh, width), BF), ((wh, width), BF), ((wh, width), BF), ((4, wh, width), BF),
        ((width, 2 * fl_n), BF), ((width, fl_n), BF), ((width, 2 * fh_n), BF), ((width, fh_n), BF),
        ((chunk, 2 * fh_n), BF),
        ((docs, rows, width), BF), ((docs, rows, 1), F32), ((routed, width), BF), ((routed, width), BF),
        ((routed, width), BF), ((docs, rows, wl), BF), ((docs, span, 2 * wl), BF),
        ((docs * rows // WINDOW, 2 * WINDOW, 2 * WINDOW), BF), ((4, docs, rows, wl), BF), ((routed, pad), BF),
        ((n_seq, routed, 2 * pad), BF), ((docs, wh // HD * slots, keys), BF), ((4, routed, pad), BF),
        ((n_seq, routed, pad), BF), ((n_seq, routed, pad), BF), ((routed, width), BF), ((routed, width), BF),
        ((routed, width), BF), ((docs, slots, width), BF), ((docs, 2 * slots, width), BF),
        ((docs, slots // 2, width), BF), ((docs, slots // 4, width), BF),
        ((docs, 2 * slots, rows), BF), ((docs, rows, 2 * slots), BF), ((docs, rows, width), BF),
        ((docs, rows, width), BF), ((docs, rows, width), BF), ((docs, 2, 2, rows // 8, width), BF),
        ((docs, 2, 2, rows // 16, width), BF), ((6, routed, 1), F32),
        ((docs, rows, fl_n), F32), ((routed, fh_n), F32), ((routed, width), BF), ((docs, rows, width), BF),
        ((docs, rows, 1), F32), ((docs, rows, fl_n), BF), ((docs, rows, 2 * fl_n), BF), ((routed, width), BF),
        ((routed, width), BF), ((routed, fh_n), BF), ((routed, 2 * fh_n), BF),
        ((4, docs, width // 4, rows), BF), ((3, docs, width // 4, rows), BF), ((docs, width // 4, rows), F32),
        ((docs, rows, width), F32), ((docs, rows, width), BF), ((docs, rows, wl), BF), ((routed, pad), BF),
        ((routed, width), BF), ((routed, pad), BF), ((docs, span, 2 * wl), F32),
        ((docs, 2, radius, 2 * wl), BF), ((docs, 2, radius, 2 * wl), BF), ((docs, rows, 3 * wl), BF),
        ((routed, 2 * pad), BF),
        ((width, h_n), BF), ((width, l_n), BF),
        *[((nz, chunk, wide), BF) for wide in widths],
        *[((nz - 1, chunk, wide), BF) for wide in widths],
        *[((chunk, wide), BF) for wide in widths],
        ((chunk, h_n + l_n + ga_n), F32), ((chunk, 128), F32), ((3, chunk, 128), F32), ((128, chunk), F32),
    ]
    sems = [
        (18,), (3, 2), (3, 2), (3, 2), (3, 2), (docs, 3), (docs, 3), (3,), (3,),
        (docs, 4), (docs, 4), (3, docs, 2, 2, 4), (3, docs, 2, 2, 4), (2 + docs, nz), (2 + docs, nz), (2 + docs, nz), (2 + docs, nz),
        (docs, 2), (docs, 2), (docs, 2), (docs, 2), (docs, 3), (docs, 3),
        (6, nz), (6, nz), (6, nz - 1), (6, nz - 1), (6,), (6,), (3,), (3,), (13,),
    ]
    total = 0
    for shape, kind in vmem:
        lanes = -(-shape[-1] // 128) * 128
        total += math.prod(shape[:-1]) * lanes * jnp.dtype(kind).itemsize
    return vmem, sems, total


def shards(sizes, *args):
    (tokens, cotangent, lengths, query_index, key_index, gain_attn, router_query, router_key, wq_light,
     wk_light, wv_light, wo_light, wq_heavy, wk_heavy, wv_heavy, wo_heavy, gain_ffn, router_ffn,
     gate_light, up_light, down_light, gate_heavy, up_heavy, down_heavy) = args
    n_seq = sizes["seq"]
    docs, rows, width = tokens.shape
    slots = query_index.shape[1]
    wl, wh = wq_light.shape[1], wq_heavy.shape[1]
    fl_n, fh_n = gate_light.shape[1], gate_heavy.shape[1]
    dims = (docs, rows, width, slots, n_seq, wl, wh, fl_n, fh_n)
    vmem, sems, total = kernel_scratch(*dims)
    fits = (
        total <= 62 * 2**20
        and sizes["branch"] == 4
        and n_seq == 8
        and width % (16 * n_seq) == 0
        and wl == 2 * HD
        and wh == 3 * HD
        and slots % 16 == 0
        and rows % 256 == 0
    )
    if not fits:
        return plain_shards(*args)
    share = width // 4
    chunk = width // n_seq
    ga_n = 4 * wl + 4 * wh + 128
    pack_n = 3 * fh_n + 3 * fl_n + ga_n
    in_hbm = [
        tokens, cotangent, wq_light, wk_light, wv_light, wo_light, wq_heavy.T, wk_heavy.T, wv_heavy.T, wo_heavy.T,
        gate_light, up_light, down_light, gate_heavy, up_heavy, down_heavy,
    ]
    whole = pl.BlockSpec(memory_space=pltpu.VMEM)
    outside = pl.BlockSpec(memory_space=pl.ANY)
    grad_tokens, mix, packed, vectors = pl.pallas_call(
        functools.partial(layer_kernel, dims),
        out_shape=[
            jax.ShapeDtypeStruct((docs, rows, width), F32),
            jax.ShapeDtypeStruct((docs, share, rows), F32),
            jax.ShapeDtypeStruct((chunk, pack_n), F32),
            jax.ShapeDtypeStruct((128, chunk), F32),
        ],
        in_specs=[pl.BlockSpec(memory_space=pltpu.SMEM)] + [whole] * 7 + [outside] * 16,
        out_specs=[outside] * 4,
        scratch_shapes=[pltpu.VMEM(shape, kind) for shape, kind in vmem]
        + [pltpu.SemaphoreType.DMA(shape) for shape in sems],
        compiler_params=pltpu.CompilerParams(
            collective_id=0, has_side_effects=True, vmem_limit_bytes=64 * 2**20 - 2**16
        ),
    )(lengths, query_index, key_index, gain_attn, router_query, router_key, gain_ffn, router_ffn, *in_hbm)

    l_at = 3 * fh_n
    a_at = l_at + 3 * fl_n
    q_at = a_at + wl + 2 * wh
    parts = [(q_at + i * wl, wl) for i in range(3)] + [(a_at, wl)]
    parts += [(a_at + wl + wh, wh), (q_at + 3 * wl, wh), (q_at + 3 * wl + wh, wh), (a_at + wl, wh)]
    parts += [(l_at + i * fl_n, fl_n) for i in range(3)] + [(i * fh_n, fh_n) for i in range(3)]
    outs = pl.pallas_call(
        functools.partial(hand_out, parts),
        out_shape=[jax.ShapeDtypeStruct(grad_tokens.shape, F32), jax.ShapeDtypeStruct(mix.shape, F32)]
        + [jax.ShapeDtypeStruct((chunk, wide), F32) for at, wide in parts],
        in_specs=[pl.BlockSpec(memory_space=pltpu.HBM)] * 3,
        out_specs=[outside] * 2 + [outside if wide % 128 == 0 else whole for at, wide in parts],
        scratch_shapes=[
            pltpu.SemaphoreType.DMA((3 + docs,)), pltpu.SemaphoreType.DMA((1 + docs + len(parts),)),
            pltpu.VMEM(grad_tokens.shape, F32), pltpu.VMEM(mix.shape, F32), pltpu.VMEM(packed.shape, F32),
        ],
        compiler_params=pltpu.CompilerParams(vmem_limit_bytes=60 * 2**20),
    )(grad_tokens, mix, packed)
    grad_tokens, mix = outs[:2]
    mixed = jnp.swapaxes(mix, 1, 2)
    vec = [vectors[i] for i in range(5)]
    return (mixed, grad_tokens, *vec[:3], *outs[2:10], *vec[3:], *outs[10:])


def hand_out(parts, tokens_in, mix_in, packed_in, tokens_out, mix_out, *rest):
    in_sems, out_sems, tokens, mix, packed = rest[-5:]
    docs = tokens.shape[0]
    arriving = [pltpu.make_async_copy(packed_in, packed, in_sems.at[0])]
    arriving += [pltpu.make_async_copy(tokens_in.at[d], tokens.at[d], in_sems.at[1 + d]) for d in range(docs)]
    arriving += [pltpu.make_async_copy(mix_in, mix, in_sems.at[1 + docs])]
    for copy in arriving:
        copy.start()
    leaving = [pltpu.make_async_copy(mix, mix_out, out_sems.at[0])]
    leaving += [pltpu.make_async_copy(tokens.at[d], tokens_out.at[d], out_sems.at[1 + d]) for d in range(docs)]
    arriving[0].wait()
    for i, (at, wide) in enumerate(parts):
        if wide % 128 == 0:
            copy = pltpu.make_async_copy(packed.at[:, at : at + wide], rest[i], out_sems.at[1 + docs + i])
            copy.start()
            leaving.append(copy)
    for d in range(docs):
        arriving[1 + d].wait()
        leaving[1 + d].start()
    arriving[1 + docs].wait()
    leaving[0].start()
    for i, (at, wide) in enumerate(parts):
        if wide % 128 != 0:
            rest[i][...] = packed[:, at : at + wide]
    for copy in leaving:
        copy.wait()


def solution(mesh):
    return jax.shard_map(
        functools.partial(shards, dict(mesh.shape)),
        mesh=mesh,
        in_specs=(
            P(None, "seq", None),
            P(None, "seq", None),
            P(),
            P(None, "seq"),
            P(None, "seq"),
            P(),
            P(),
            P(),
            P(None, "branch"),
            P(None, "branch"),
            P(None, "branch"),
            P(None, "branch"),
            P(None, "branch"),
            P(None, "branch"),
            P(None, "branch"),
            P(None, "branch"),
            P(),
            P(),
            P(None, "branch"),
            P(None, "branch"),
            P(None, "branch"),
            P(None, "branch"),
            P(None, "branch"),
            P(None, "branch"),
        ),
        out_specs=(
            P(None, "seq", "branch"),
            P(None, "seq", None),
            P("seq"),
            P("seq"),
            P("seq"),
            P("seq", "branch"),
            P("seq", "branch"),
            P("seq", "branch"),
            P("seq", "branch"),
            P("seq", "branch"),
            P("seq", "branch"),
            P("seq", "branch"),
            P("seq", "branch"),
            P("seq"),
            P("seq"),
            P("seq", "branch"),
            P("seq", "branch"),
            P("seq", "branch"),
            P("seq", "branch"),
            P("seq", "branch"),
            P("seq", "branch"),
        ),
        check_vma=False,
    )
```
